32 devices in a mesh: dp: 8 (over y, x, core), fsdp: 4 (over z).
Axes of the slice: x: 2, y: 2, z: 4, core: 2. Of those that a mesh axis runs over, the one named last changes fastest.
Arguments:
- tokens: bfloat16 [8, 1024, 2048], P('dp', 'fsdp'), may hold values from -6 to 6
- doc_lengths: int32 [8, 8], P('dp'), may hold values from 1 to 512, as said below
- norm_gain: bfloat16 [2048], P(('dp', 'fsdp')), may hold values from 0.099609375 to 1.8984375
- w_query: bfloat16 [2048, 1024], P(('dp', 'fsdp')), may hold values from -0.125 to 0.125
- w_key: bfloat16 [2048, 1024], P(('dp', 'fsdp')), may hold values from -0.125 to 0.125
- w_value: bfloat16 [2048, 2048], P(('dp', 'fsdp')), may hold values from -0.125 to 0.125
- w_outgate: bfloat16 [2048, 2048], P(('dp', 'fsdp')), may hold values from -0.125 to 0.125
- w_lowrank: bfloat16 [2048, 16], P(('dp', 'fsdp')), may hold values from -0.125 to 0.125
- w_gaterank: bfloat16 [16, 1024], P(None, ('dp', 'fsdp')), may hold values from -1.5 to 1.5
- gate_bias: bfloat16 [1024], P(('dp', 'fsdp')), may hold values from -1 to 7
- head_gain: bfloat16 [512], P(('dp', 'fsdp')), may hold values from 0.099609375 to 1.8984375
- w_output: bfloat16 [2048, 2048], P(('dp', 'fsdp')), may hold values from -0.25 to 0.25
- ffn_gain: bfloat16 [2048], P(('dp', 'fsdp')), may hold values from 0.099609375 to 1.8984375
- w_gate: bfloat16 [2048, 5632], P(('dp', 'fsdp')), may hold values from -0.125 to 0.125
- w_up: bfloat16 [2048, 5632], P(('dp', 'fsdp')), may hold values from -0.125 to 0.125
- w_down: bfloat16 [5632, 2048], P(('dp', 'fsdp')), may hold values from -0.15625 to 0.15625
- cotangent: bfloat16 [8, 1024, 2048], P('dp', 'fsdp'), may hold values from -6 to 6
Outputs:
- output: bfloat16 [8, 1024, 2048], P('dp', 'fsdp')
- tokens_grad: bfloat16 [8, 1024, 2048], P('dp', 'fsdp')
- norm_gain_grad: float32 [2048], P(('dp', 'fsdp'))
- w_query_grad: float32 [2048, 1024], P(('dp', 'fsdp'))
- w_key_grad: float32 [2048, 1024], P(('dp', 'fsdp'))
- w_value_grad: float32 [2048, 2048], P(('dp', 'fsdp'))
- w_outgate_grad: float32 [2048, 2048], P(('dp', 'fsdp'))
- w_lowrank_grad: float32 [2048, 16], P(('dp', 'fsdp'))
- w_gaterank_grad: float32 [16, 1024], P(None, ('dp', 'fsdp'))
- gate_bias_grad: float32 [1024], P(('dp', 'fsdp'))
- head_gain_grad: float32 [512], P(('dp', 'fsdp'))
- w_output_grad: float32 [2048, 2048], P(('dp', 'fsdp'))
- ffn_gain_grad: float32 [2048], P(('dp', 'fsdp'))
- w_gate_grad: float32 [2048, 5632], P(('dp', 'fsdp'))
- w_up_grad: float32 [2048, 5632], P(('dp', 'fsdp'))
- w_down_grad: float32 [5632, 2048], P(('dp', 'fsdp'))
The draws below stay inside these ranges and needn't reach their ends.
Inputs may be any that keep to these rules, and one draw needn't show every extreme that they name: `doc_lengths`: each row lists, in order, the lengths of the 7 documents packed into one sequence, each of 60 to 512 tokens with one of exactly 512, then the padding at the sequence's end, 1 to 59 tokens; a row sums to 1024.
All inputs are finite; a program needn't handle non-finite values.
Results may differ from the reference program's by a relative error of at most 0.018.
Values may be sent and summed in bfloat16 or wider, within the bound.
A program may use at most 328 MiB of HBM per device.

```python
import jax
import jax.numpy as jnp
from jax import lax

D = 2048
H = 4
DK = 256
DV = 512
R = 16
FF = 5632
C = 64
LEN = 1024
DOCS = 8
DOC_MAX = 512
DOC_MIN = 60
KD = 1024
VD = 2048
SEQS = 8


def draw_doc_lengths(key, part):
    key = jax.random.fold_in(key, 5)
    first_key, second_key, third_key = jax.random.split(key, 3)
    row_count = SEQS
    row_index = jnp.arange(row_count, dtype=jnp.int32)
    padding = jax.random.randint(first_key, (row_count,), 1, DOC_MIN, dtype=jnp.int32).astype(jnp.int32)
    padding = jnp.where(row_index == 0, jnp.int32(1), padding).astype(jnp.int32)
    extra = (jnp.int32(LEN - DOC_MAX - (DOCS - 2) * DOC_MIN) - padding).astype(jnp.int32)
    shares_w = jax.random.randint(second_key, (row_count, DOCS - 2), 1, 100, dtype=jnp.int32).astype(jnp.int32)
    weight_total = jnp.sum(shares_w, axis=1, keepdims=True, dtype=jnp.int32).astype(jnp.int32)
    shares = (extra[:, None] * shares_w // weight_total).astype(jnp.int32)
    column = jnp.arange(DOCS - 2, dtype=jnp.int32)
    rest = (extra - jnp.sum(shares, axis=1, dtype=jnp.int32)).astype(jnp.int32)
    shares = (shares + (column[None, :] == 0).astype(jnp.int32) * rest[:, None]).astype(jnp.int32)
    small_docs = (DOC_MIN + shares).astype(jnp.int32)
    place = jax.random.randint(third_key, (row_count,), 0, DOCS - 1, dtype=jnp.int32).astype(jnp.int32)
    slot = jnp.arange(DOCS - 1, dtype=jnp.int32)
    source = jnp.clip(slot[None, :] - (slot[None, :] > place[:, None]).astype(jnp.int32), 0, DOCS - 3).astype(jnp.int32)
    picked = jnp.take_along_axis(small_docs, source, axis=1).astype(jnp.int32)
    documents = jnp.where(slot[None, :] == place[:, None], jnp.int32(DOC_MAX), picked).astype(jnp.int32)
    return jnp.concatenate([documents, padding[:, None]], axis=1).astype(jnp.int32)


def block_scale(stream_key, shape, shards, low, largest):
    def one(axis_at, parts):
        draws = jax.random.uniform(jax.random.fold_in(jax.random.fold_in(stream_key, 6), axis_at), (parts,), jnp.float32, low / len(shards), largest / len(shards))
        return jnp.repeat(jnp.exp(draws), shape[axis_at] // parts).reshape((-1,) + (1,) * (len(shape) - axis_at - 1))

    level = one(*shards[0])
    for cut in shards[1:]:
        level = level * one(*cut)
    return level


def gaussian(stream_key, extent, deviation, limit, cuts=(), held_as=jnp.bfloat16):
    values = jax.random.normal(stream_key, extent, jnp.float32) * deviation
    if len(cuts) > 0:
        values = block_scale(stream_key, extent, cuts, -0.22, 0.18) * values
    return jnp.clip(values, min=-limit, max=limit).astype(held_as)


def setup_inputs(seed: int = 0) -> dict:
    key_of = jax.random.split(jax.random.key(seed), 18)
    return {
        "tokens": gaussian(key_of[0], (SEQS, LEN, D), 1.0, 6.0, ((0, 8), (1, 4))),
        "doc_lengths": draw_doc_lengths(jax.random.fold_in(key_of[17], 71), 0),
        "norm_gain": jnp.clip(1.0 + 0.18 * jax.random.normal(key_of[2], (D,), jnp.float32), 0.099609375, 1.8984375).astype(jnp.bfloat16),
        "w_query": gaussian(key_of[3], (D, KD), D ** -0.5, 0.125, ((0, 32),)),
        "w_key": gaussian(key_of[4], (D, KD), D ** -0.5, 0.125, ((0, 32),)),
        "w_value": gaussian(key_of[5], (D, VD), D ** -0.5, 0.125, ((0, 32),)),
        "w_outgate": gaussian(key_of[6], (D, VD), D ** -0.5, 0.125, ((0, 32),)),
        "w_lowrank": gaussian(key_of[7], (D, R), D ** -0.5, 0.125, ((0, 32),)),
        "w_gaterank": gaussian(key_of[8], (R, KD), R ** -0.5, 1.5, ((1, 32),)),
        "gate_bias": jnp.clip(-1.0 + 8.0 * jax.random.uniform(key_of[9], (KD,), jnp.float32) ** block_scale(key_of[9], (KD,), ((0, 32),), -0.2, 0.2), -1.0, 7.0).astype(jnp.bfloat16),
        "head_gain": jnp.clip(1.0 + 0.18 * jax.random.normal(key_of[10], (DV,), jnp.float32), 0.099609375, 1.8984375).astype(jnp.bfloat16),
        "w_output": gaussian(key_of[11], (VD, D), (VD // 4) ** -0.5, 0.25, ((0, 32),)),
        "ffn_gain": jnp.clip(1.0 + 0.18 * jax.random.normal(key_of[12], (D,), jnp.float32), 0.099609375, 1.8984375).astype(jnp.bfloat16),
        "w_gate": gaussian(key_of[13], (D, FF), D ** -0.5, 0.125, ((0, 32),)),
        "w_up": gaussian(key_of[14], (D, FF), D ** -0.5, 0.125, ((0, 32),)),
        "w_down": gaussian(key_of[15], (FF, D), (FF // 4) ** -0.5, 0.15625, ((0, 32),)),
        "cotangent": gaussian(key_of[16], (SEQS, LEN, D), 1.0, 6.0, ((0, 8), (1, 4))),
    }


@jax.custom_vjp
def low(v):
    return lax.optimization_barrier(v.astype(jnp.bfloat16)).astype(jnp.float32)

@jax.custom_vjp
def low_back(v):
    return v

def low_keep(v):
    return (low(v), None)

def low_pass(kept, grad):
    return (grad,)

def back_keep(v):
    return (v, None)

def back_low(kept, grad):
    return (low(grad),)
low.defvjp(low_keep, low_pass)
low_back.defvjp(back_keep, back_low)
EPS = 1e-05
HEAD_EPS = 1.0
PRECISION_FULL = lax.Precision.HIGHEST

def matmul_high(left_op, right_op):
    return jnp.dot(left_op, right_op, precision=PRECISION_FULL, preferred_element_type=jnp.float32)

def rms_norm(values, gain_vec, epsilon):
    return values * lax.rsqrt(lax.optimization_barrier(jnp.mean(values * values, axis=-1, keepdims=True)) + epsilon) * gain_vec

def tables(lengths):
    doc_ends = jnp.cumsum(lengths.astype(jnp.int32), axis=-1, dtype=jnp.int32).astype(jnp.int32)
    places = jnp.arange(LEN, dtype=jnp.int32)
    segment = lax.optimization_barrier(jnp.sum((places[None, :, None] >= doc_ends[:, None, :]).astype(jnp.int32), axis=-1, dtype=jnp.int32)).astype(jnp.int32)
    previous = lax.optimization_barrier(jnp.sum((places[None, :, None] - 1 >= doc_ends[:, None, :]).astype(jnp.int32), axis=-1, dtype=jnp.int32)).astype(jnp.int32)
    return (segment, previous)

def block_step(carry_state, pieces):
    query_rows, key_rows, value_matrix_rows, log_rates, segment, before = pieces
    block_len = log_rates.shape[2]
    float_type = log_rates.dtype
    zero_like = jnp.zeros((), float_type)
    one_like = jnp.ones((), float_type)
    places = jnp.arange(block_len, dtype=jnp.int32)
    cum_logs = jnp.cumsum(log_rates, axis=2)
    same_doc = (segment[:, :, None] == segment[:, None, :]) & (places[:, None] >= places[None, :])[None]
    allowed = same_doc[:, None, :, :, None]
    weights = jnp.where(allowed, jnp.exp(jnp.where(allowed, cum_logs[:, :, :, None, :] - cum_logs[:, :, None, :, :], zero_like)), zero_like)
    scores = lax.optimization_barrier(jnp.sum(query_rows[:, :, :, None, :] * key_rows[:, :, None, :, :] * weights, axis=-1))
    carried = jnp.where(segment == before[:, None], one_like, zero_like)
    scaled_query_rows = query_rows * jnp.exp(cum_logs) * carried[:, None, :, None]
    layer_result = jnp.einsum('ghij,ghjv->ghiv', scores, value_matrix_rows, precision=PRECISION_FULL)
    layer_result = layer_result + jnp.einsum('ghik,ghkv->ghiv', scaled_query_rows, carry_state, precision=PRECISION_FULL)
    last_cum = cum_logs[:, :, -1, :]
    tail_mask = jnp.where(segment == segment[:, -1:], one_like, zero_like)
    scaled_key_rows = key_rows * jnp.exp(last_cum[:, :, None, :] - cum_logs) * tail_mask[:, None, :, None]
    link_flag = jnp.where(segment[:, -1] == before, one_like, zero_like)
    decays = jnp.exp(last_cum) * link_flag[:, None, None]
    carry_state = decays[..., None] * carry_state + jnp.einsum('ghjk,ghjv->ghkv', scaled_key_rows, value_matrix_rows, precision=PRECISION_FULL)
    return (carry_state, layer_result)

def layer(params, block_in, segment, previous):
    norm_one, query_w, key_w, value_w, outgate_w, lowrank_w, gaterank_w, bias_vec, headgain_w, output_w, norm_two, gate_w, up_w, down_w = params
    group_size = block_in.shape[0]
    float_type = block_in.dtype
    zero_like = jnp.zeros((), float_type)
    one_like = jnp.ones((), float_type)
    live = jnp.where(segment != DOCS - 1, one_like, zero_like).reshape(-1, 1, 1)
    inputs = block_in.reshape(-1, D)
    normed = low(rms_norm(inputs, norm_one, EPS))
    query_rows = low_back(matmul_high(normed, query_w)) * DK ** (-0.5)
    key_rows = low_back(matmul_high(normed, key_w))
    value_matrix_rows = low_back(matmul_high(normed, value_w))
    outgate = low_back(matmul_high(normed, outgate_w))
    lowrank = low_back(matmul_high(normed, lowrank_w))
    log_rates = jax.nn.log_sigmoid(matmul_high(lowrank, gaterank_w) + bias_vec) / 16.0
    block_count = LEN // C

    def split_heads(matrix):
        inner = matrix.shape[-1] // H
        return matrix.reshape(group_size, block_count, C, H, inner).transpose(1, 0, 3, 2, 4)
    seg_blocks = segment.reshape(group_size, block_count, C).transpose(1, 0, 2).astype(jnp.int32)
    before = previous[:, ::C].T.astype(jnp.int32)
    initial = jnp.zeros((group_size, H, DK, DV), float_type)
    _, attended = lax.scan(jax.checkpoint(block_step), initial, (split_heads(query_rows), split_heads(key_rows), split_heads(value_matrix_rows), split_heads(log_rates), seg_blocks, before))
    attended = attended.transpose(1, 0, 3, 2, 4).reshape(-1, H, DV) * live
    headed = rms_norm(attended, headgain_w, HEAD_EPS)
    gated = low(headed.reshape(-1, H * DV) * jax.nn.silu(outgate))
    hidden = inputs + low_back(matmul_high(gated, output_w))
    normed_two = low(rms_norm(hidden, norm_two, EPS))
    gate_pre = low_back(matmul_high(normed_two, gate_w))
    up_pre = low_back(matmul_high(normed_two, up_w))
    activated = low(jax.nn.silu(gate_pre) * up_pre)
    layer_result = hidden + low_back(matmul_high(activated, down_w))
    return layer_result.reshape(block_in.shape)

def reference(tokens, doc_lengths, norm_gain, w_query, w_key, w_value, w_outgate, w_lowrank, w_gaterank, gate_bias, head_gain, w_output, ffn_gain, w_gate, w_up, w_down, cotangent):
    params = (norm_gain.astype(jnp.float32), w_query.astype(jnp.float32), w_key.astype(jnp.float32), w_value.astype(jnp.float32), w_outgate.astype(jnp.float32), w_lowrank.astype(jnp.float32), w_gaterank.astype(jnp.float32), gate_bias.astype(jnp.float32), head_gain.astype(jnp.float32), w_output.astype(jnp.float32), ffn_gain.astype(jnp.float32), w_gate.astype(jnp.float32), w_up.astype(jnp.float32), w_down.astype(jnp.float32))
    group_count = SEQS // 4
    segment_all, previous_all = tables(doc_lengths.astype(jnp.int32))
    segment_all = segment_all.astype(jnp.int32).reshape(group_count, 4, LEN)
    previous_all = previous_all.astype(jnp.int32).reshape(group_count, 4, LEN)

    def whole(weights_all, inputs_all):
        stacked = inputs_all.reshape(group_count, 4, LEN, D)

        def run_group(triple):
            return jax.checkpoint(lambda block_in: layer(weights_all, block_in, triple[1], triple[2]))(triple[0])
        return lax.map(run_group, (stacked, segment_all, previous_all)).reshape(SEQS, LEN, D)
    layer_result, pullback = jax.vjp(whole, params, tokens.astype(jnp.float32))
    grads, tokens_grad = pullback(cotangent.astype(jnp.float32))
    return (layer_result.astype(jnp.bfloat16), tokens_grad.astype(jnp.bfloat16), grads[0], grads[1], grads[2], grads[3], grads[4], grads[5], grads[6], grads[7], grads[8], grads[9], grads[10], grads[11], grads[12], grads[13])
```

```python
import jax
import jax.numpy as jnp
from jax import lax
from jax.sharding import Mesh
from jax.sharding import PartitionSpec as P

H = 4
DK = 256
DV = 512
CORES = 2
DOCS = 8

EPS = 1e-05
HEAD_EPS = 1.0
HIGHEST = lax.Precision.HIGHEST
F32 = jnp.float32
BF16 = jnp.bfloat16

SHARE = ("rep", "core", "fsdp")
EVERY = ("rep", "head", "core", "fsdp")


def dot(a, b, dims, precision=None):
    return lax.dot_general(a, b, (dims, ((), ())), precision=precision, preferred_element_type=F32)


def matmul(a, b):
    return dot(a, b, ((1,), (0,)))


def rows_product(a, b):
    return dot(a, b, ((0,), (0,)))


def back_product(a, b):
    return dot(a, b, ((1,), (1,)))


def batched(form, a, b):
    return jnp.einsum(form, a, b, preferred_element_type=F32)


def rms_scale(values, epsilon):
    return lax.rsqrt(jnp.mean(values * values, axis=-1, keepdims=True) + epsilon)


def rms_back(upstream, values, scale):
    return scale * upstream - values * scale**3 * jnp.mean(upstream * values, axis=-1, keepdims=True)


def share_rows(part):
    spread = jnp.broadcast_to(part[None], (H,) + part.shape)
    whole = lax.all_to_all(spread, "head", split_axis=0, concat_axis=0, tiled=True)
    return whole.reshape(-1, part.shape[-1])


def sum_rows(partial):
    pieces = partial.astype(BF16).reshape(H, -1, partial.shape[-1])
    pieces = lax.all_to_all(pieces, "head", split_axis=0, concat_axis=0, tiled=True)
    return jnp.sum(pieces.astype(F32), axis=0)


def level_sums(length):
    rows = jnp.arange(length)[:, None]
    cols = jnp.arange(length)[None, :]
    sums, pairs = [], []
    step = 1
    while step < length:
        bound = rows // (2 * step) * (2 * step) + step - 1
        upper = rows > bound
        sums.append(jnp.where(upper, (cols > bound) & (cols <= rows), (cols > rows) & (cols <= bound)))
        pairs.append(upper & (cols // (2 * step) == rows // (2 * step)) & (cols <= bound))
        step *= 2
    sums.append(cols <= rows)
    sums.append(cols > rows)
    return jnp.stack(sums), jnp.stack(pairs)


def chain_before(decay, state, backward):
    count = lax.axis_size("fsdp")
    place = lax.axis_index("fsdp")
    decays = lax.all_gather(decay.astype(BF16), "fsdp")
    states = lax.all_gather(state.astype(BF16), "fsdp")
    total = jnp.zeros_like(state)
    for step in range(count - 1):
        source = count - 1 - step if backward else step
        ahead = source > place if backward else source < place
        joined = decays[source].astype(F32)[..., None] * total + states[source].astype(F32)
        total = jnp.where(ahead, joined, total)
    return total


def per_device(
    tokens,
    doc_lengths,
    norm_gain,
    w_query,
    w_key,
    w_value,
    w_outgate,
    w_lowrank,
    w_gaterank,
    gate_bias,
    head_gain,
    w_output,
    ffn_gain,
    w_gate,
    w_up,
    w_down,
    cotangent,
):
    seqs_here, length, width = tokens.shape
    reps = lax.axis_size("rep")
    parts = lax.axis_size("fsdp")
    devices = reps * H * CORES * parts
    here = lax.axis_index("head")
    key_dim, value_dim = DK, DV
    rank = w_lowrank.shape[1]
    rows = width // devices
    count = H * seqs_here

    def to_shared(a):
        shaped = a.reshape(a.shape[0], reps, H, CORES * parts, rows)
        return shaped.transpose(0, 1, 3, 2, 4).reshape(a.shape)

    def from_shared(a):
        shaped = a.reshape(a.shape[0], reps, CORES * parts, H, rows)
        return shaped.transpose(0, 1, 3, 2, 4).reshape(a.shape)

    def gather_columns(w):
        moved = lax.all_to_all(w.transpose(1, 0, 2), "head", split_axis=0, concat_axis=0, tiled=True)
        return lax.all_gather(moved.reshape(-1, w.shape[2]), SHARE, axis=0, tiled=True)

    def scatter_columns(g):
        g = g.astype(BF16)
        for axis in SHARE:
            g = lax.psum_scatter(g, axis, scatter_dimension=0, tiled=True)
        moved = lax.all_to_all(g.reshape(H, rows, -1), "head", split_axis=0, concat_axis=0, tiled=True)
        return moved.transpose(1, 0, 2).astype(F32)

    def gather_part(w):
        if reps == 1:
            return lax.all_gather(w, SHARE, axis=0, tiled=True)
        whole = lax.all_gather(w, EVERY, axis=0, tiled=True)
        size = whole.shape[0] // H
        return lax.dynamic_slice_in_dim(whole, here * size, size, 0)

    def scatter_part(g):
        g = g.astype(BF16)
        if reps == 1:
            for axis in SHARE:
                g = lax.psum_scatter(g, axis, scatter_dimension=0, tiled=True)
            return g.astype(F32)
        whole = jnp.zeros((H * g.shape[0], g.shape[1]), BF16)
        whole = lax.dynamic_update_slice_in_dim(whole, g, here * g.shape[0], 0)
        return lax.psum_scatter(whole, EVERY, scatter_dimension=0, tiled=True).astype(F32)

    small = (
        norm_gain,
        ffn_gain,
        gate_bias,
        head_gain,
        w_gaterank.reshape(-1),
    )
    sizes = [a.shape[0] for a in small]
    packed = jnp.concatenate(small).reshape(1, -1)
    packed = lax.all_gather(packed, EVERY, axis=0, tiled=True).astype(F32)
    gain_one, gain_two, bias, gain_head, gaterank = jnp.split(
        packed, [sum(sizes[:i]) for i in range(1, len(sizes))], axis=1
    )
    gain_one, gain_two, bias, gain_head = (
        gain_one.reshape(-1),
        gain_two.reshape(-1),
        bias.reshape(-1),
        gain_head.reshape(-1),
    )
    gaterank = gaterank.reshape(devices, rank, -1).transpose(1, 0, 2).reshape(rank, -1)
    bias = lax.dynamic_slice_in_dim(bias, here * key_dim, key_dim, 0)
    gaterank = lax.dynamic_slice_in_dim(gaterank, here * key_dim, key_dim, 1)
    lengths = lax.all_gather(doc_lengths, "head", axis=0, tiled=True)

    mix_w = gather_columns(
        jnp.concatenate(
            [
                w_query.reshape(rows, H, key_dim),
                w_key.reshape(rows, H, key_dim),
                w_value.reshape(rows, H, value_dim),
                w_outgate.reshape(rows, H, value_dim),
                jnp.broadcast_to(w_lowrank[:, None, :], (rows, H, rank)),
            ],
            axis=2,
        )
    )
    output_w = gather_part(w_output)
    gate_w = gather_columns(w_gate.reshape(rows, H, -1))
    up_w = gather_columns(w_up.reshape(rows, H, -1))
    down_w = gather_part(w_down)

    offset = lax.axis_index("fsdp") * length
    doc_ends = jnp.cumsum(lengths, axis=-1)
    places = offset + jnp.arange(length, dtype=jnp.int32)
    segment = jnp.sum((places[None, :, None] >= doc_ends[:, None, :]).astype(jnp.int32), axis=-1)
    before = jnp.sum((offset - 1 >= doc_ends).astype(jnp.int32), axis=-1)
    live = (segment != DOCS - 1).astype(F32)[:, :, None]
    same = segment[:, :, None] == segment[:, None, :]
    tail = (segment == segment[:, -1:]).astype(F32)[:, :, None]
    carried = (segment == before[:, None]).astype(F32)[:, :, None]
    link = (segment[:, -1] == before).astype(F32)[:, None]

    inputs = tokens.reshape(-1, width).astype(F32)
    scale_one = rms_scale(inputs, EPS)
    normed = share_rows(to_shared((inputs * scale_one * gain_one).astype(BF16)))
    mixed = matmul(normed, mix_w)
    edges = [key_dim, 2 * key_dim, 2 * key_dim + value_dim, 2 * key_dim + 2 * value_dim]
    query, key, value, outgate, lowrank = jnp.split(mixed, edges, axis=1)
    query_scale = key_dim ** (-0.5)
    query = (query * query_scale).reshape(count, length, key_dim)
    key = key.reshape(count, length, key_dim)
    value = value.astype(BF16).reshape(count, length, value_dim)
    logits = dot(lowrank, gaterank, ((1,), (0,)), HIGHEST) + bias
    rates = (jax.nn.log_sigmoid(logits) / 16.0).reshape(count, length, key_dim)

    sums, pairs = level_sums(length)
    sums = sums.astype(BF16)
    levels = pairs.shape[0]
    high = rates.astype(BF16)
    low = (rates - high.astype(F32)).astype(BF16)
    decayed = jnp.exp(batched("sim,bmk->bsik", sums, high) + batched("sim,bmk->bsik", sums, low))
    level_decay = decayed[:, :levels]
    from_start = decayed[:, levels] * carried
    to_end = decayed[:, levels + 1] * tail
    decay = decayed[:, levels, -1] * link

    mask = pairs[None] & same[:, None]
    level_query = (query[:, None] * level_decay).astype(BF16)
    level_key = (key[:, None] * level_decay).astype(BF16)
    own = (jnp.arange(length)[:, None] == jnp.arange(length)[None, :])[None]
    scores = jnp.sum(
        jnp.where(mask, batched("bsik,bsjk->bsij", level_query, level_key), 0.0), axis=1
    ) + jnp.where(own, jnp.sum(query * key, axis=-1)[:, :, None], 0.0)
    scores = scores.astype(BF16)
    start_query = (query * from_start).astype(BF16)
    end_key = (key * to_end).astype(BF16)
    local_end = batched("bjk,bjv->bkv", end_key, value)
    entering = chain_before(decay, local_end, False).astype(BF16)
    attended = (
        batched("bij,bjv->biv", scores, value) + batched("bik,bkv->biv", start_query, entering)
    ) * live
    attended = attended.reshape(-1, value_dim)
    scale_head = rms_scale(attended, HEAD_EPS)
    headed = attended * scale_head * gain_head
    sig_out = jax.nn.sigmoid(outgate)
    swish = outgate * sig_out
    gated = (headed * swish).astype(BF16)
    hidden = inputs + sum_rows(matmul(gated, output_w))

    scale_two = rms_scale(hidden, EPS)
    normed_two = share_rows(to_shared((hidden * scale_two * gain_two).astype(BF16)))
    gate_pre = matmul(normed_two, gate_w)
    up_pre = matmul(normed_two, up_w)
    sig_gate = jax.nn.sigmoid(gate_pre)
    activated = (gate_pre * sig_gate * up_pre).astype(BF16)
    output = (hidden + sum_rows(matmul(activated, down_w))).astype(BF16).reshape(tokens.shape)

    cot_rows = cotangent.reshape(-1, width)
    cot_shared = share_rows(cot_rows)
    grad_act = back_product(cot_shared, down_w)
    grad_up = (grad_act * gate_pre * sig_gate).astype(BF16)
    grad_gate = (grad_act * up_pre * sig_gate * (1.0 + gate_pre * (1.0 - sig_gate))).astype(BF16)
    grad_normed_two = from_shared(
        sum_rows(back_product(grad_gate, gate_w) + back_product(grad_up, up_w))
    )
    w_down_grad = scatter_part(rows_product(activated, cot_shared))
    w_gate_grad = scatter_columns(rows_product(normed_two, grad_gate))
    w_up_grad = scatter_columns(rows_product(normed_two, grad_up))
    grad_gain_two = jnp.sum(grad_normed_two * hidden * scale_two, axis=0)
    grad_hidden = cot_rows.astype(F32) + rms_back(grad_normed_two * gain_two, hidden, scale_two)

    branch = share_rows(grad_hidden.astype(BF16))
    grad_gated = back_product(branch, output_w)
    w_output_grad = scatter_part(rows_product(gated, branch))
    grad_outgate = grad_gated * headed * sig_out * (1.0 + outgate * (1.0 - sig_out))
    grad_headed = grad_gated * swish
    grad_gain_head = jnp.sum(grad_headed * attended * scale_head, axis=0)
    grad_attended = rms_back(grad_headed * gain_head, attended, scale_head)
    grad_attended = (grad_attended.reshape(count, length, value_dim) * live).astype(BF16)

    leaving = batched("bik,biv->bkv", start_query, grad_attended)
    ending = chain_before(decay, leaving, True).astype(BF16)
    grad_scores = jnp.where(same, batched("biv,bjv->bij", grad_attended, value), 0.0)
    grad_value = batched("bij,biv->bjv", scores, grad_attended) + batched(
        "bjk,bkv->bjv", end_key, ending
    )
    grad_own = jnp.sum(jnp.where(own, grad_scores, 0.0), axis=-1)[:, :, None]
    level_scores = jnp.where(pairs[None], grad_scores[:, None], 0.0).astype(BF16)
    level_grad_query = batched("bsij,bsjk->bsik", level_scores, level_key)
    level_grad_key = batched("bsij,bsik->bsjk", level_scores, level_query)
    start_grad = batched("biv,bkv->bik", grad_attended, entering)
    end_grad = batched("bjv,bkv->bjk", value, ending)
    grad_query = (
        jnp.sum(level_grad_query * level_decay, axis=1) + grad_own * key + start_grad * from_start
    )
    grad_key = jnp.sum(level_grad_key * level_decay, axis=1) + grad_own * query + end_grad * to_end
    flows = jnp.concatenate(
        [
            level_grad_query * level_query + level_grad_key * level_key,
            (start_grad * start_query)[:, None],
            (end_grad * end_key)[:, None],
        ],
        axis=1,
    ).astype(BF16)
    through = decay * jnp.sum(ending.astype(F32) * entering.astype(F32), axis=-1)
    grad_rates = batched("sim,bsik->bmk", sums, flows) + through[:, None, :]
    grad_logits = grad_rates.reshape(-1, key_dim) / 16.0 * jax.nn.sigmoid(-logits)
    grad_bias = jnp.sum(grad_logits, axis=0)
    grad_gaterank = dot(lowrank, grad_logits, ((0,), (0,)), HIGHEST)
    grad_lowrank = dot(grad_logits, gaterank, ((1,), (1,)), HIGHEST)
    grad_mixed = jnp.concatenate(
        [
            grad_query.reshape(-1, key_dim) * query_scale,
            grad_key.reshape(-1, key_dim),
            grad_value.reshape(-1, value_dim),
            grad_outgate,
            grad_lowrank,
        ],
        axis=1,
    ).astype(BF16)
    grad_normed = from_shared(sum_rows(back_product(grad_mixed, mix_w)))
    grad_mix_w = scatter_columns(rows_product(normed, grad_mixed))
    grad_gain_one = jnp.sum(grad_normed * inputs * scale_one, axis=0)
    tokens_grad = grad_hidden + rms_back(grad_normed * gain_one, inputs, scale_one)
    tokens_grad = tokens_grad.astype(BF16).reshape(tokens.shape)

    query_g, key_g, value_g, outgate_g, lowrank_g = jnp.split(grad_mix_w, edges, axis=2)

    def place(g, axis):
        shape = list(g.shape)
        shape[axis] *= H
        return lax.dynamic_update_slice_in_dim(jnp.zeros(shape, F32), g, here * key_dim, axis)

    small_grads = jnp.concatenate(
        [
            grad_gain_one.reshape(devices, -1),
            grad_gain_two.reshape(devices, -1),
            place(grad_bias, 0).reshape(devices, -1),
            grad_gain_head.reshape(devices, -1),
            place(grad_gaterank, 1)
            .reshape(rank, devices, -1)
            .transpose(1, 0, 2)
            .reshape(devices, -1),
        ],
        axis=1,
    )
    small_grads = lax.all_to_all(small_grads, EVERY, split_axis=0, concat_axis=0, tiled=True)
    small_grads = jnp.sum(small_grads, axis=0)
    norm_g, ffn_g, bias_g, head_g, gaterank_g = jnp.split(
        small_grads, [sum(sizes[:i]) for i in range(1, len(sizes))]
    )
    return (
        output,
        tokens_grad,
        norm_g,
        query_g.reshape(w_query.shape),
        key_g.reshape(w_key.shape),
        value_g.reshape(w_value.shape),
        outgate_g.reshape(w_outgate.shape),
        jnp.sum(lowrank_g, axis=1),
        gaterank_g.reshape(w_gaterank.shape),
        bias_g,
        head_g,
        w_output_grad,
        ffn_g,
        w_gate_grad.reshape(w_gate.shape),
        w_up_grad.reshape(w_up.shape),
        w_down_grad,
    )


def solution(mesh):
    dp, parts = mesh.shape["dp"], mesh.shape["fsdp"]
    fine = Mesh(mesh.devices.reshape(dp // (H * CORES), H, CORES, parts), EVERY)
    seq = ("rep", "head", "core")
    rows, vector = P(EVERY, None), P(EVERY)
    activations = P(seq, "fsdp", None)
    columns = P(None, EVERY)
    return jax.shard_map(
        per_device,
        mesh=fine,
        in_specs=(
            activations,
            P(seq, None),
            vector,
            rows,
            rows,
            rows,
            rows,
            rows,
            columns,
            vector,
            vector,
            rows,
            vector,
            rows,
            rows,
            rows,
            activations,
        ),
        out_specs=(
            activations,
            activations,
            vector,
            rows,
            rows,
            rows,
            rows,
            rows,
            columns,
            vector,
            vector,
            rows,
            vector,
            rows,
            rows,
            rows,
        ),
        check_vma=False,
    )
```

```python
import functools

import jax
import jax.experimental.pallas as pl
import jax.experimental.pallas.tpu as pltpu
import jax.numpy as jnp
from jax import lax
from jax.sharding import Mesh
from jax.sharding import PartitionSpec as P

H = 4
DK = 256
DV = 512
CORES = 2
DOCS = 8
PIECES = 2
LANES = 128

EPS = 1e-05
HEAD_EPS = 1.0
HIGHEST = lax.Precision.HIGHEST
F32 = jnp.float32
BF16 = jnp.bfloat16

SHARE = ("rep", "core", "fsdp")
EVERY = ("rep", "head", "core", "fsdp")


def dot(a, b, dims, precision=None):
    return lax.dot_general(a, b, (dims, ((), ())), precision=precision, preferred_element_type=F32)


def after(value, *others):
    return lax.optimization_barrier((value,) + others)


def matmul(a, b):
    return dot(a, b, ((1,), (0,)))


def rows_product(a, b):
    return dot(a, b, ((0,), (0,)))


def back_product(a, b):
    return dot(a, b, ((1,), (1,)))


def batched(form, a, b):
    return jnp.einsum(form, a, b, preferred_element_type=F32)


def rms_scale(values, epsilon):
    return lax.rsqrt(jnp.mean(values * values, axis=-1, keepdims=True) + epsilon)


def rms_back(upstream, values, scale):
    return scale * upstream - values * scale**3 * jnp.mean(upstream * values, axis=-1, keepdims=True)


def share_rows(part):
    spread = jnp.broadcast_to(part[None], (H,) + part.shape)
    whole = lax.all_to_all(spread, "head", split_axis=0, concat_axis=0, tiled=True)
    return whole.reshape(-1, part.shape[-1])


def move_rows(partial):
    pieces = partial.astype(BF16).reshape(H, -1, partial.shape[-1])
    return lax.all_to_all(pieces, "head", split_axis=0, concat_axis=0, tiled=True)


def sum_rows(partial):
    return jnp.sum(move_rows(partial).astype(F32), axis=0)


def level_sums(length):
    rows = jnp.arange(length)[:, None]
    cols = jnp.arange(length)[None, :]
    sums, pairs = [], []
    step = 1
    while step < length:
        bound = rows // (2 * step) * (2 * step) + step - 1
        upper = rows > bound
        sums.append(jnp.where(upper, (cols > bound) & (cols <= rows), (cols > rows) & (cols <= bound)))
        pairs.append(upper & (cols // (2 * step) == rows // (2 * step)) & (cols <= bound))
        step *= 2
    sums.append(cols <= rows)
    sums.append(cols > rows)
    return jnp.stack(sums), jnp.stack(pairs)


def log_sigmoid(x):
    return jnp.minimum(x, 0.0) - jnp.log1p(jnp.exp(-jnp.abs(x)))


def state_copy(send, recv, send_sem, recv_sem, seq, piece, target):
    size = send.shape[1] // PIECES
    part = pl.ds(piece * size, size)
    return pltpu.make_async_remote_copy(
        src_ref=send.at[seq, part],
        dst_ref=recv.at[seq, part],
        send_sem=send_sem.at[seq, piece],
        recv_sem=recv_sem.at[seq, piece],
        device_id={"fsdp": target},
        device_id_type=pl.DeviceIdType.MESH,
    )


def greet_neighbours(place, parts):
    barrier = pltpu.get_barrier_semaphore()
    for near, there in ((place - 1, place > 0), (place + 1, place < parts - 1)):

        @pl.when(there)
        def _(near=near):
            pl.semaphore_signal(
                barrier,
                inc=1,
                device_id={"fsdp": lax.rem(near + parts, parts)},
                device_id_type=pl.DeviceIdType.MESH,
            )

    peers = (place > 0).astype(jnp.int32) + (place < parts - 1).astype(jnp.int32)
    pl.semaphore_wait(barrier, peers)


def pass_state(s, first, last, target, decay, local, send, recv, send_sem, recv_sem):
    size = send.shape[1] // PIECES
    for piece in range(PIECES):
        part = pl.ds(piece * size, size)
        copy = state_copy(send, recv, send_sem, recv_sem, s, piece, target)

        @pl.when(jnp.logical_not(first))
        def _(copy=copy):
            copy.wait_recv()

        @pl.when(jnp.logical_not(last))
        def _(copy=copy, part=part):
            joined = decay * recv[s, part].astype(F32) + local[s, part]
            send[s, part] = joined.astype(BF16)
            copy.start()


def finish_states(count, last, target, send, recv, send_sem, recv_sem):
    @pl.when(jnp.logical_not(last))
    def _():
        def one(s, carry):
            for piece in range(PIECES):
                state_copy(send, recv, send_sem, recv_sem, s, piece, target).wait_send()
            return carry

        lax.fori_loop(0, count, one, 0)


def split_rates(logits):
    rates = log_sigmoid(logits) / 16.0
    high = rates.astype(BF16)
    return high, (rates - high.astype(F32)).astype(BF16)


def decayed(sums, high, low):
    return jnp.exp(matmul(sums, high) + matmul(sums, low))


def forward_kernel(
    key_dim,
    value_dim,
    mixed_ref,
    bias_ref,
    gaterank_ref,
    gain_ref,
    marks_ref,
    segment_ref,
    sums_ref,
    pairs_ref,
    gated_ref,
    attended_ref,
    logits_ref,
    scores_ref,
    start_ref,
    end_ref,
    decay_ref,
    enter_ref,
    local_ref,
    send_ref,
    recv_ref,
    send_sem,
    recv_sem,
):
    count, _, length = segment_ref.shape
    levels = pairs_ref.shape[0]
    parts, place = lax.axis_size("fsdp"), lax.axis_index("fsdp")
    first, last, target = place == 0, place == parts - 1, lax.rem(place + 1, parts)
    rank = gaterank_ref.shape[0]
    scale = key_dim ** (-0.5)
    value_at = 2 * key_dim
    gate_at = value_at + value_dim
    rank_at = gate_at + value_dim

    greet_neighbours(place, parts)

    @pl.when(first)
    def _():
        recv_ref[...] = jnp.zeros_like(recv_ref)

    def rows_of(s):
        return pl.ds(pl.multiple_of(s * length, length), length)

    def ends(s, carry):
        rows = rows_of(s)
        lowrank = mixed_ref[rows, pl.ds(rank_at, rank)]
        logits = dot(lowrank, gaterank_ref[...], ((1,), (0,)), HIGHEST) + bias_ref[...]
        logits_ref[rows, :] = logits
        high, low = split_rates(logits)
        from_start = decayed(sums_ref[levels], high, low)
        to_end = decayed(sums_ref[levels + 1], high, low)
        marks = marks_ref[rows, :]
        decay_ref[s] = from_start[length - 1 :, :] * marks[:1, 4:5]
        query = mixed_ref[rows, pl.ds(0, key_dim)] * scale
        key = mixed_ref[rows, pl.ds(key_dim, key_dim)]
        start_ref[rows, :] = (query * (from_start * marks[:, 1:2])).astype(BF16)
        end_key = (key * (to_end * marks[:, 2:3])).astype(BF16)
        end_ref[rows, :] = end_key
        value = mixed_ref[rows, pl.ds(value_at, value_dim)].astype(BF16)
        local_ref[s] = rows_product(value, end_key)
        return carry

    lax.fori_loop(0, count, ends, 0)

    def mix(s, carry):
        rows = rows_of(s)
        pass_state(
            s, first, last, target, decay_ref[s], local_ref, send_ref, recv_ref, send_sem, recv_sem
        )
        query = mixed_ref[rows, pl.ds(0, key_dim)] * scale
        key = mixed_ref[rows, pl.ds(key_dim, key_dim)]
        high, low = split_rates(logits_ref[rows, :])
        scores = jnp.zeros((length, length), F32)
        for level in range(levels):
            decay = decayed(sums_ref[level], high, low)
            pair = back_product((query * decay).astype(BF16), (key * decay).astype(BF16))
            scores += pair * pairs_ref[level].astype(F32)
        row = lax.broadcasted_iota(jnp.int32, (length, length), 0)
        col = lax.broadcasted_iota(jnp.int32, (length, length), 1)
        own = jnp.sum(query * key, axis=1, keepdims=True)
        scores += jnp.where(row == col, own, 0.0)
        marks = marks_ref[rows, :]
        scores = jnp.where(marks[:, 0:1] == segment_ref[s], scores, 0.0).astype(BF16)
        scores_ref[s] = scores
        value = mixed_ref[rows, pl.ds(value_at, value_dim)].astype(BF16)
        attended = matmul(scores, value) + back_product(start_ref[rows, :], recv_ref[s])
        attended = attended * marks[:, 3:4]
        attended_ref[rows, :] = attended
        headed = attended * rms_scale(attended, HEAD_EPS) * gain_ref[...]
        outgate = mixed_ref[rows, pl.ds(gate_at, value_dim)]
        gated_ref[rows, :] = (headed * (outgate * jax.nn.sigmoid(outgate))).astype(BF16)
        enter_ref[s] = recv_ref[s]
        return carry

    lax.fori_loop(0, count, mix, 0)
    finish_states(count, last, target, send_ref, recv_ref, send_sem, recv_sem)


def backward_kernel(
    key_dim,
    value_dim,
    mixed_ref,
    logits_ref,
    scores_ref,
    start_ref,
    end_ref,
    decay_ref,
    enter_ref,
    attended_ref,
    upstream_ref,
    gaterank_ref,
    gain_ref,
    marks_ref,
    segment_ref,
    sums_ref,
    pairs_ref,
    grad_ref,
    gain_grad_ref,
    bias_grad_ref,
    gaterank_grad_ref,
    out_ref,
    local_ref,
    send_ref,
    recv_ref,
    send_sem,
    recv_sem,
):
    count, _, length = segment_ref.shape
    levels = pairs_ref.shape[0]
    parts, place = lax.axis_size("fsdp"), lax.axis_index("fsdp")
    first, last, target = place == parts - 1, place == 0, lax.rem(place + parts - 1, parts)
    rank = gaterank_ref.shape[0]
    scale = key_dim ** (-0.5)
    value_at = 2 * key_dim
    gate_at = value_at + value_dim
    rank_at = gate_at + value_dim

    greet_neighbours(place, parts)

    @pl.when(first)
    def _():
        recv_ref[...] = jnp.zeros_like(recv_ref)

    gain_grad_ref[...] = jnp.zeros_like(gain_grad_ref)
    bias_grad_ref[...] = jnp.zeros_like(bias_grad_ref)
    gaterank_grad_ref[...] = jnp.zeros_like(gaterank_grad_ref)

    def rows_of(s):
        return pl.ds(pl.multiple_of(s * length, length), length)

    def heads(s, carry):
        rows = rows_of(s)
        upstream = upstream_ref[rows, :]
        attended = attended_ref[rows, :]
        outgate = mixed_ref[rows, pl.ds(gate_at, value_dim)]
        gain = gain_ref[...]
        norm = rms_scale(attended, HEAD_EPS)
        normed = attended * norm
        sig = jax.nn.sigmoid(outgate)
        grad_gate = upstream * (normed * gain) * sig * (1.0 + outgate * (1.0 - sig))
        grad_ref[rows, pl.ds(gate_at, value_dim)] = grad_gate.astype(BF16)
        grad_headed = upstream * (outgate * sig)
        gain_grad_ref[...] += jnp.sum(grad_headed * normed, axis=0, keepdims=True)
        grad_out = rms_back(grad_headed * gain, attended, norm) * marks_ref[rows, pl.ds(3, 1)]
        grad_out = grad_out.astype(BF16)
        out_ref[rows, :] = grad_out
        local_ref[s] = rows_product(grad_out, start_ref[rows, :])
        return carry

    lax.fori_loop(0, count, heads, 0)

    def mix(s, carry):
        rows = rows_of(s)
        decay_row = decay_ref[s]
        pass_state(
            s, first, last, target, decay_row, local_ref, send_ref, recv_ref, send_sem, recv_sem
        )
        query = mixed_ref[rows, pl.ds(0, key_dim)] * scale
        key = mixed_ref[rows, pl.ds(key_dim, key_dim)]
        value = mixed_ref[rows, pl.ds(value_at, value_dim)].astype(BF16)
        marks = marks_ref[rows, :]
        logits = logits_ref[rows, :]
        high, low = split_rates(logits)
        grad_out = out_ref[rows, :]
        row = lax.broadcasted_iota(jnp.int32, (length, length), 0)
        col = lax.broadcasted_iota(jnp.int32, (length, length), 1)
        pair_grads = back_product(grad_out, value)
        pair_grads = jnp.where(marks[:, 0:1] == segment_ref[s], pair_grads, 0.0)
        own = jnp.sum(jnp.where(row == col, pair_grads, 0.0), axis=1, keepdims=True)
        grad_query = own * key
        grad_key = own * query
        grad_rates = jnp.zeros((length, key_dim), F32)
        for level in range(levels):
            decay = decayed(sums_ref[level], high, low)
            level_query = (query * decay).astype(BF16)
            level_key = (key * decay).astype(BF16)
            level_pairs = (pair_grads * pairs_ref[level].astype(F32)).astype(BF16)
            level_grad_query = matmul(level_pairs, level_key)
            level_grad_key = rows_product(level_pairs, level_query)
            grad_query += level_grad_query * decay
            grad_key += level_grad_key * decay
            flow = level_grad_query * level_query.astype(F32)
            flow += level_grad_key * level_key.astype(F32)
            grad_rates += rows_product(sums_ref[level], flow.astype(BF16))
        ending = recv_ref[s]
        entering = enter_ref[s]
        start_query = start_ref[rows, :]
        end_key = end_ref[rows, :]
        start_grad = matmul(grad_out, entering)
        end_grad = matmul(value, ending)
        grad_query += start_grad * (decayed(sums_ref[levels], high, low) * marks[:, 1:2])
        grad_key += end_grad * (decayed(sums_ref[levels + 1], high, low) * marks[:, 2:3])
        grad_rates += rows_product(
            sums_ref[levels], (start_grad * start_query.astype(F32)).astype(BF16)
        )
        grad_rates += rows_product(
            sums_ref[levels + 1], (end_grad * end_key.astype(F32)).astype(BF16)
        )
        grad_rates += decay_row * jnp.sum(
            ending.astype(F32) * entering.astype(F32), axis=0, keepdims=True
        )
        grad_value = rows_product(scores_ref[s], grad_out) + back_product(end_key, ending)
        grad_ref[rows, pl.ds(0, key_dim)] = (grad_query * scale).astype(BF16)
        grad_ref[rows, pl.ds(key_dim, key_dim)] = grad_key.astype(BF16)
        grad_ref[rows, pl.ds(value_at, value_dim)] = grad_value.astype(BF16)
        grad_logits = grad_rates / 16.0 * jax.nn.sigmoid(-logits)
        bias_grad_ref[...] += jnp.sum(grad_logits, axis=0, keepdims=True)
        lowrank = mixed_ref[rows, pl.ds(rank_at, rank)]
        gaterank_grad_ref[...] += dot(lowrank, grad_logits, ((0,), (0,)), HIGHEST)
        grad_lowrank = dot(grad_logits, gaterank_ref[...], ((1,), (1,)), HIGHEST)
        rest = grad_ref.shape[1] - rank_at - rank
        grad_ref[rows, pl.ds(rank_at, rank + rest)] = jnp.concatenate(
            [grad_lowrank, jnp.zeros((length, rest), F32)], axis=1
        ).astype(BF16)
        return carry

    lax.fori_loop(0, count, mix, 0)
    finish_states(count, last, target, send_ref, recv_ref, send_sem, recv_sem)


def state_scratch(count, value_dim, key_dim):
    return [
        pltpu.VMEM((count, value_dim, key_dim), F32),
        pltpu.VMEM((count, value_dim, key_dim), BF16),
        pltpu.VMEM((count, value_dim, key_dim), BF16),
        pltpu.SemaphoreType.DMA((count, PIECES)),
        pltpu.SemaphoreType.DMA((count, PIECES)),
    ]


def kernel_params(number):
    return pltpu.CompilerParams(
        collective_id=number, has_side_effects=True, vmem_limit_bytes=52 * 2**20
    )


def mix_forward(mixed, bias, gaterank, gain, marks, segment, sums, pairs, key_dim, value_dim):
    rows = mixed.shape[0]
    count, _, length = segment.shape
    shapes = (
        ((rows, value_dim), BF16),
        ((rows, value_dim), F32),
        ((rows, key_dim), F32),
        ((count, length, length), BF16),
        ((rows, key_dim), BF16),
        ((rows, key_dim), BF16),
        ((count, 1, key_dim), F32),
        ((count, value_dim, key_dim), BF16),
    )
    whole = pl.BlockSpec(memory_space=pltpu.VMEM)
    return pl.pallas_call(
        functools.partial(forward_kernel, key_dim, value_dim),
        out_shape=[jax.ShapeDtypeStruct(*s) for s in shapes],
        in_specs=[whole] * 8,
        out_specs=[whole] * len(shapes),
        scratch_shapes=state_scratch(count, value_dim, key_dim),
        compiler_params=kernel_params(1),
        cost_estimate=pl.CostEstimate(flops=5 * 10**10, bytes_accessed=10**7, transcendentals=0),
        name="mix_forward",
    )(mixed, bias, gaterank, gain, marks, segment, sums, pairs)


def mix_backward(
    mixed, kept, upstream, gaterank, gain, marks, segment, sums, pairs, key_dim, value_dim
):
    rows = mixed.shape[0]
    count = segment.shape[0]
    shapes = (
        (mixed.shape, BF16),
        ((1, value_dim), F32),
        ((1, key_dim), F32),
        (gaterank.shape, F32),
    )
    attended, logits, scores, start, end, decay, enter = kept
    whole = pl.BlockSpec(memory_space=pltpu.VMEM)
    return pl.pallas_call(
        functools.partial(backward_kernel, key_dim, value_dim),
        out_shape=[jax.ShapeDtypeStruct(*s) for s in shapes],
        in_specs=[whole] * 15,
        out_specs=[whole] * len(shapes),
        scratch_shapes=[pltpu.VMEM((rows, value_dim), BF16)]
        + state_scratch(count, value_dim, key_dim),
        compiler_params=kernel_params(2),
        cost_estimate=pl.CostEstimate(flops=8 * 10**10, bytes_accessed=10**7, transcendentals=0),
        name="mix_backward",
    )(
        mixed,
        logits,
        scores,
        start,
        end,
        decay,
        enter,
        attended,
        upstream,
        gaterank,
        gain,
        marks,
        segment,
        sums,
        pairs,
    )


def per_device(
    tokens,
    doc_lengths,
    norm_gain,
    w_query,
    w_key,
    w_value,
    w_outgate,
    w_lowrank,
    w_gaterank,
    gate_bias,
    head_gain,
    w_output,
    ffn_gain,
    w_gate,
    w_up,
    w_down,
    cotangent,
):
    seqs_here, length, width = tokens.shape
    reps = lax.axis_size("rep")
    parts = lax.axis_size("fsdp")
    devices = reps * H * CORES * parts
    here = lax.axis_index("head")
    key_dim, value_dim = DK, DV
    rank = w_lowrank.shape[1]
    rows = width // devices
    count = H * seqs_here

    rank_at = 2 * key_dim + 2 * value_dim

    def to_shared(a):
        shaped = a.reshape(a.shape[0], reps, H, CORES * parts, rows)
        return shaped.transpose(0, 1, 3, 2, 4).reshape(a.shape)

    def from_shared(a):
        shaped = a.reshape(a.shape[0], reps, CORES * parts, H, rows)
        return shaped.transpose(0, 1, 3, 2, 4).reshape(a.shape)

    def core_sum(g):
        halves = g.reshape(CORES, -1, g.shape[-1])
        core = lax.axis_index("core")
        other = lax.ppermute(halves[1 - core], "core", ((0, 1), (1, 0)))
        return (halves[core].astype(F32) + other.astype(F32)).astype(BF16)

    def pair_rows(g):
        if reps > 1:
            g = lax.psum_scatter(g, "rep", scatter_dimension=0, tiled=True)
        return core_sum(g)

    def scatter_rows(g):
        return lax.psum_scatter(g, "fsdp", scatter_dimension=0, tiled=True)

    def gather_columns(w):
        moved = lax.all_to_all(w.transpose(1, 0, 2), "head", split_axis=0, concat_axis=0, tiled=True)
        return lax.all_gather(moved.reshape(-1, w.shape[2]), SHARE, axis=0, tiled=True)

    def to_columns(g):
        moved = lax.all_to_all(g.reshape(H, rows, -1), "head", split_axis=0, concat_axis=0, tiled=True)
        return moved.transpose(1, 0, 2).astype(F32)

    def gather_part(w):
        if reps == 1:
            return lax.all_gather(w, SHARE, axis=0, tiled=True)
        whole = lax.all_gather(w, EVERY, axis=0, tiled=True)
        size = whole.shape[0] // H
        return lax.dynamic_slice_in_dim(whole, here * size, size, 0)

    def pair_part(g):
        return core_sum(g) if reps == 1 else g

    def scatter_part(g):
        if reps == 1:
            return lax.psum_scatter(g, "fsdp", scatter_dimension=0, tiled=True)
        whole = jnp.zeros((H * g.shape[0], g.shape[1]), BF16)
        whole = lax.dynamic_update_slice_in_dim(whole, g, here * g.shape[0], 0)
        return lax.psum_scatter(whole, EVERY, scatter_dimension=0, tiled=True)

    def with_gain(w, gain):
        return (w.astype(F32) * gain.astype(F32)[:, None]).astype(BF16)

    small = (
        gate_bias,
        head_gain,
        w_gaterank.reshape(-1),
        (doc_lengths // 16).astype(BF16).reshape(-1),
        (doc_lengths % 16).astype(BF16).reshape(-1),
    )
    sizes = [a.shape[0] for a in small]
    small = jnp.concatenate(small)
    small = jnp.pad(small, (0, rows * rank - small.shape[0])).reshape(rows, rank)

    mix_w = gather_columns(
        jnp.concatenate(
            [
                with_gain(w_query, norm_gain).reshape(rows, H, key_dim),
                with_gain(w_key, norm_gain).reshape(rows, H, key_dim),
                with_gain(w_value, norm_gain).reshape(rows, H, value_dim),
                with_gain(w_outgate, norm_gain).reshape(rows, H, value_dim),
                jnp.broadcast_to(with_gain(w_lowrank, norm_gain)[:, None, :], (rows, H, rank)),
                jnp.broadcast_to(small[:, None, :], (rows, H, rank)),
                jnp.zeros((rows, H, -(rank_at + 2 * rank) % LANES), BF16),
            ],
            axis=2,
        )
    )
    output_w = gather_part(w_output)

    small = mix_w[:, rank_at + rank : rank_at + 2 * rank].astype(F32)
    small = small.reshape(reps, CORES * parts, H, rows * rank).transpose(0, 2, 1, 3)
    bias, gain_head, gaterank, long, short = jnp.split(
        small[..., : sum(sizes)], [sum(sizes[:i]) for i in range(1, len(sizes))], axis=3
    )
    gaterank = gaterank.reshape(devices, rank, -1).transpose(1, 0, 2).reshape(rank, -1)
    bias = lax.dynamic_slice_in_dim(bias.reshape(1, -1), here * key_dim, key_dim, 1)
    gaterank = lax.dynamic_slice_in_dim(gaterank, here * key_dim, key_dim, 1)
    gain_head = gain_head.reshape(1, -1)
    lengths = (long * 16.0 + short).reshape(reps, H, CORES, parts, seqs_here, DOCS)
    lengths = lengths[lax.axis_index("rep"), :, lax.axis_index("core"), 0]
    lengths = lengths.reshape(count, DOCS).astype(jnp.int32)

    offset = lax.axis_index("fsdp") * length
    doc_ends = jnp.cumsum(lengths, axis=-1)
    places = offset + jnp.arange(length, dtype=jnp.int32)
    segment = jnp.sum((places[None, :, None] >= doc_ends[:, None, :]).astype(jnp.int32), axis=-1)
    before = jnp.sum((offset - 1 >= doc_ends).astype(jnp.int32), axis=-1)[:, None]
    last = segment[:, -1:]
    marks = jnp.stack(
        [
            segment,
            segment == before,
            segment == last,
            segment != DOCS - 1,
            jnp.broadcast_to(last == before, segment.shape),
        ],
        axis=2,
    )
    marks = jnp.pad(marks.astype(F32).reshape(count * length, 5), ((0, 0), (0, 3)))
    segment = segment.astype(F32).reshape(count, 1, length)

    inputs = tokens.reshape(-1, width).astype(F32)
    scale_one = rms_scale(inputs, EPS)
    normed = share_rows(to_shared((inputs * scale_one).astype(BF16)))
    normed, w_gate_late, w_up_late, w_down_late = after(normed, w_gate, w_up, w_down)
    gate_w = gather_columns(with_gain(w_gate_late, ffn_gain).reshape(rows, H, -1))
    up_w = gather_columns(with_gain(w_up_late, ffn_gain).reshape(rows, H, -1))
    down_w = gather_part(w_down_late)
    mixed = matmul(normed, mix_w)
    sums, pairs = level_sums(length)
    sums, pairs = sums.astype(BF16), pairs.astype(BF16)
    gated, *kept = mix_forward(
        mixed, bias, gaterank, gain_head, marks, segment, sums, pairs, key_dim, value_dim
    )
    cot_rows = cotangent.reshape(-1, width)
    gated, cot_shared = after(gated, share_rows(cot_rows))
    hidden = inputs + sum_rows(matmul(gated, output_w))

    scale_two = rms_scale(hidden, EPS)
    normed_two = share_rows(to_shared((hidden * scale_two).astype(BF16)))
    gate_pre = matmul(normed_two, gate_w)
    up_pre = matmul(normed_two, up_w)
    sig_gate = jax.nn.sigmoid(gate_pre)
    activated = (gate_pre * sig_gate * up_pre).astype(BF16)

    grad_down_w = rows_product(activated, cot_shared).astype(BF16)
    down_w, grad_down_w = after(down_w, grad_down_w)
    grad_act = back_product(cot_shared, down_w)
    grad_up = (grad_act * gate_pre * sig_gate).astype(BF16)
    grad_gate = (grad_act * up_pre * sig_gate * (1.0 + gate_pre * (1.0 - sig_gate))).astype(BF16)
    grad_gate, grad_up, grad_down_w = after(grad_gate, grad_up, pair_part(grad_down_w))
    partial = (back_product(grad_gate, gate_w) + back_product(grad_up, up_w)).astype(BF16)
    grad_gate, grad_up, partial = after(grad_gate, grad_up, partial)
    grad_gate_w = pair_rows(rows_product(normed_two, grad_gate).astype(BF16))
    grad_up_w = pair_rows(rows_product(normed_two, grad_up).astype(BF16))
    down_partial = matmul(activated, down_w).astype(BF16)
    pieces = move_rows(partial)
    pieces, grad_gate_w, down_partial = after(pieces, grad_gate_w, down_partial)
    grad_normed_two = from_shared(jnp.sum(pieces.astype(F32), axis=0))
    grad_down_w = scatter_part(grad_down_w)
    grad_gate_w = scatter_rows(grad_gate_w)
    grad_up_w = scatter_rows(grad_up_w)
    grad_gain_two = jnp.sum(grad_normed_two * hidden * scale_two, axis=0)
    grad_hidden = cot_rows.astype(F32) + rms_back(grad_normed_two, hidden, scale_two)

    branch = share_rows(grad_hidden.astype(BF16))
    branch, down_partial = after(branch, down_partial)
    grad_output_w = pair_part(rows_product(gated, branch).astype(BF16))
    grad_gated = back_product(branch, output_w)
    grad_gated, grad_output_w = after(grad_gated, grad_output_w)
    grad_output_w = scatter_part(grad_output_w)
    pieces = move_rows(down_partial)
    grad_mixed, grad_gain_head, grad_bias, grad_gaterank = mix_backward(
        mixed,
        kept,
        grad_gated,
        gaterank,
        gain_head,
        marks,
        segment,
        sums,
        pairs,
        key_dim,
        value_dim,
    )
    grad_mixed, pieces, grad_down_w, grad_gate_w, grad_output_w = after(
        grad_mixed, pieces, grad_down_w, grad_gate_w, grad_output_w
    )
    output = (hidden + jnp.sum(pieces.astype(F32), axis=0)).astype(BF16).reshape(tokens.shape)
    grad_mix_w = pair_rows(rows_product(normed, grad_mixed).astype(BF16))
    grad_mixed, grad_mix_w = after(grad_mixed, grad_mix_w)
    partial = back_product(grad_mixed, mix_w).astype(BF16)
    grad_mix_w = scatter_rows(grad_mix_w)
    w_gate_grad = to_columns(grad_gate_w)
    w_up_grad = to_columns(grad_up_w)
    pieces = move_rows(partial)
    pieces, w_gate_grad, w_up_grad = after(pieces, w_gate_grad, w_up_grad)
    grad_normed = from_shared(jnp.sum(pieces.astype(F32), axis=0))
    grad_mix_w = to_columns(grad_mix_w)
    grad_gain_one = jnp.sum(grad_normed * inputs * scale_one, axis=0)
    tokens_grad = grad_hidden + rms_back(grad_normed, inputs, scale_one)
    tokens_grad = tokens_grad.astype(BF16).reshape(tokens.shape)

    edges = [key_dim, 2 * key_dim, 2 * key_dim + value_dim, rank_at, rank_at + rank]
    query_g, key_g, value_g, outgate_g, lowrank_g, _ = jnp.split(grad_mix_w, edges, axis=2)
    gain_one = norm_gain.astype(F32)
    gain_two = ffn_gain.astype(F32)

    def scaled(g, gain, w):
        return g.reshape(w.shape) * gain[:, None]

    def place(g, axis):
        shape = list(g.shape)
        shape[axis] *= H
        return lax.dynamic_update_slice_in_dim(jnp.zeros(shape, F32), g, here * key_dim, axis)

    small_grads = jnp.concatenate(
        [
            grad_gain_one.reshape(devices, -1),
            grad_gain_two.reshape(devices, -1),
            place(grad_bias.reshape(-1), 0).reshape(devices, -1),
            grad_gain_head.reshape(devices, -1),
            place(grad_gaterank, 1)
            .reshape(rank, devices, -1)
            .transpose(1, 0, 2)
            .reshape(devices, -1),
        ],
        axis=1,
    )
    small_grads = lax.all_to_all(small_grads, EVERY, split_axis=0, concat_axis=0, tiled=True)
    small_grads = jnp.sum(small_grads, axis=0)
    sizes = [norm_gain.shape[0], ffn_gain.shape[0], gate_bias.shape[0], head_gain.shape[0]]
    norm_g, ffn_g, bias_g, head_g, gaterank_g = jnp.split(
        small_grads, [sum(sizes[: i + 1]) for i in range(len(sizes))]
    )
    return (
        output,
        tokens_grad,
        norm_g / gain_one,
        scaled(query_g, gain_one, w_query),
        scaled(key_g, gain_one, w_key),
        scaled(value_g, gain_one, w_value),
        scaled(outgate_g, gain_one, w_outgate),
        scaled(jnp.sum(lowrank_g, axis=1), gain_one, w_lowrank),
        gaterank_g.reshape(w_gaterank.shape),
        bias_g,
        head_g,
        grad_output_w.astype(F32),
        ffn_g / gain_two,
        scaled(w_gate_grad, gain_two, w_gate),
        scaled(w_up_grad, gain_two, w_up),
        grad_down_w.astype(F32),
    )


def solution(mesh):
    dp, parts = mesh.shape["dp"], mesh.shape["fsdp"]
    fine = Mesh(mesh.devices.reshape(dp // (H * CORES), H, CORES, parts), EVERY)
    seq = ("rep", "head", "core")
    rows, vector = P(EVERY, None), P(EVERY)
    activations = P(seq, "fsdp", None)
    columns = P(None, EVERY)
    return jax.shard_map(
        per_device,
        mesh=fine,
        in_specs=(
            activations,
            P(seq, None),
            vector,
            rows,
            rows,
            rows,
            rows,
            rows,
            columns,
            vector,
            vector,
            rows,
            vector,
            rows,
            rows,
            rows,
            activations,
        ),
        out_specs=(
            activations,
            activations,
            vector,
            rows,
            rows,
            rows,
            rows,
            rows,
            columns,
            vector,
            vector,
            rows,
            vector,
            rows,
            rows,
            rows,
        ),
        check_vma=False,
    )
```

```python
import functools

import jax
import jax.experimental.pallas as pl
import jax.experimental.pallas.tpu as pltpu
import jax.numpy as jnp
from jax import lax
from jax.sharding import Mesh
from jax.sharding import PartitionSpec as P

H = 4
DK = 256
DV = 512
CORES = 2
DOCS = 8
PIECES = 2
LANES = 128
CHUNKS = 8

EPS = 1e-05
HEAD_EPS = 1.0
HIGHEST = lax.Precision.HIGHEST
F32 = jnp.float32
BF16 = jnp.bfloat16

SHARE = ("rep", "core", "fsdp")
EVERY = ("rep", "head", "core", "fsdp")


def dot(a, b, dims, precision=None):
    return lax.dot_general(a, b, (dims, ((), ())), precision=precision, preferred_element_type=F32)


def after(value, *others):
    return lax.optimization_barrier((value,) + others)


def matmul(a, b):
    return dot(a, b, ((1,), (0,)))


def rows_product(a, b):
    return dot(a, b, ((0,), (0,)))


def back_product(a, b):
    return dot(a, b, ((1,), (1,)))


def batched(form, a, b):
    return jnp.einsum(form, a, b, preferred_element_type=F32)


def rms_scale(values, epsilon):
    return lax.rsqrt(jnp.mean(values * values, axis=-1, keepdims=True) + epsilon)


def rms_back(upstream, values, scale):
    return scale * upstream - values * scale**3 * jnp.mean(upstream * values, axis=-1, keepdims=True)


def share_rows(part):
    spread = jnp.broadcast_to(part[None], (H,) + part.shape)
    whole = lax.all_to_all(spread, "head", split_axis=0, concat_axis=0, tiled=True)
    return whole.reshape(-1, part.shape[-1])


def move_rows(partial):
    pieces = partial.astype(BF16).reshape(H, -1, partial.shape[-1])
    return lax.all_to_all(pieces, "head", split_axis=0, concat_axis=0, tiled=True)


def sum_rows(partial):
    return jnp.sum(move_rows(partial).astype(F32), axis=0)


def level_sums(length):
    rows = jnp.arange(length)[:, None]
    cols = jnp.arange(length)[None, :]
    sums, pairs = [], []
    step = 1
    while step < length:
        bound = rows // (2 * step) * (2 * step) + step - 1
        upper = rows > bound
        sums.append(jnp.where(upper, (cols > bound) & (cols <= rows), (cols > rows) & (cols <= bound)))
        pairs.append(upper & (cols // (2 * step) == rows // (2 * step)) & (cols <= bound))
        step *= 2
    sums.append(cols <= rows)
    sums.append(cols > rows)
    return jnp.stack(sums), jnp.stack(pairs)


def log_sigmoid(x):
    return jnp.minimum(x, 0.0) - jnp.log1p(jnp.exp(-jnp.abs(x)))


def state_copy(send, recv, send_sem, recv_sem, seq, piece, target):
    size = send.shape[1] // PIECES
    part = pl.ds(piece * size, size)
    return pltpu.make_async_remote_copy(
        src_ref=send.at[seq, part],
        dst_ref=recv.at[seq, part],
        send_sem=send_sem.at[seq, piece],
        recv_sem=recv_sem.at[seq, piece],
        device_id={"fsdp": target},
        device_id_type=pl.DeviceIdType.MESH,
    )


def greet_neighbours(place, parts):
    barrier = pltpu.get_barrier_semaphore()
    for near, there in ((place - 1, place > 0), (place + 1, place < parts - 1)):

        @pl.when(there)
        def _(near=near):
            pl.semaphore_signal(
                barrier,
                inc=1,
                device_id={"fsdp": lax.rem(near + parts, parts)},
                device_id_type=pl.DeviceIdType.MESH,
            )

    peers = (place > 0).astype(jnp.int32) + (place < parts - 1).astype(jnp.int32)
    pl.semaphore_wait(barrier, peers)


def pass_state(s, first, last, target, decay, local, send, recv, send_sem, recv_sem):
    size = send.shape[1] // PIECES
    for piece in range(PIECES):
        part = pl.ds(piece * size, size)
        copy = state_copy(send, recv, send_sem, recv_sem, s, piece, target)

        @pl.when(jnp.logical_not(first))
        def _(copy=copy):
            copy.wait_recv()

        @pl.when(jnp.logical_not(jnp.logical_or(first, last)))
        def _(copy=copy, part=part):
            joined = decay * recv[s, part].astype(F32) + local[s, part]
            send[s, part] = joined.astype(BF16)
            copy.start()


def start_state(s, first, last, target, local, send, recv, send_sem, recv_sem):
    @pl.when(jnp.logical_and(first, jnp.logical_not(last)))
    def _():
        send[s] = local[s].astype(BF16)
        for piece in range(PIECES):
            state_copy(send, recv, send_sem, recv_sem, s, piece, target).start()


def finish_states(count, last, target, send, recv, send_sem, recv_sem):
    @pl.when(jnp.logical_not(last))
    def _():
        def one(s, carry):
            for piece in range(PIECES):
                state_copy(send, recv, send_sem, recv_sem, s, piece, target).wait_send()
            return carry

        lax.fori_loop(0, count, one, 0)


def split_rates(logits):
    rates = log_sigmoid(logits) / 16.0
    high = rates.astype(BF16)
    return high, (rates - high.astype(F32)).astype(BF16)


def decayed(sums, high, low):
    return jnp.exp(matmul(sums, high) + matmul(sums, low))


def forward_kernel(
    key_dim,
    value_dim,
    mixed_ref,
    bias_ref,
    gaterank_ref,
    gain_ref,
    marks_ref,
    segment_ref,
    sums_ref,
    pairs_ref,
    gated_ref,
    attended_ref,
    logits_ref,
    scores_ref,
    start_ref,
    end_ref,
    decay_ref,
    enter_ref,
    local_ref,
    send_ref,
    recv_ref,
    send_sem,
    recv_sem,
):
    count, _, length = segment_ref.shape
    levels = pairs_ref.shape[0]
    parts, place = lax.axis_size("fsdp"), lax.axis_index("fsdp")
    first, last, target = place == 0, place == parts - 1, lax.rem(place + 1, parts)
    rank = gaterank_ref.shape[0]
    scale = key_dim ** (-0.5)
    value_at = 2 * key_dim
    gate_at = value_at + value_dim
    rank_at = gate_at + value_dim

    greet_neighbours(place, parts)

    @pl.when(first)
    def _():
        recv_ref[...] = jnp.zeros_like(recv_ref)

    def rows_of(s):
        return pl.ds(pl.multiple_of(s * length, length), length)

    def ends(s, carry):
        rows = rows_of(s)
        lowrank = mixed_ref[rows, pl.ds(rank_at, rank)]
        logits = dot(lowrank, gaterank_ref[...], ((1,), (0,)), HIGHEST) + bias_ref[...]
        logits_ref[rows, :] = logits
        high, low = split_rates(logits)
        from_start = decayed(sums_ref[levels], high, low)
        to_end = decayed(sums_ref[levels + 1], high, low)
        marks = marks_ref[rows, :]
        decay_ref[s] = from_start[length - 1 :, :] * marks[:1, 4:5]
        query = mixed_ref[rows, pl.ds(0, key_dim)] * scale
        key = mixed_ref[rows, pl.ds(key_dim, key_dim)]
        start_ref[rows, :] = (query * (from_start * marks[:, 1:2])).astype(BF16)
        end_key = (key * (to_end * marks[:, 2:3])).astype(BF16)
        end_ref[rows, :] = end_key
        value = mixed_ref[rows, pl.ds(value_at, value_dim)].astype(BF16)
        local_ref[s] = rows_product(value, end_key)
        start_state(s, first, last, target, local_ref, send_ref, recv_ref, send_sem, recv_sem)
        return carry

    lax.fori_loop(0, count, ends, 0)

    def mix(s, carry):
        rows = rows_of(s)
        pass_state(
            s, first, last, target, decay_ref[s], local_ref, send_ref, recv_ref, send_sem, recv_sem
        )
        query = mixed_ref[rows, pl.ds(0, key_dim)] * scale
        key = mixed_ref[rows, pl.ds(key_dim, key_dim)]
        high, low = split_rates(logits_ref[rows, :])
        scores = jnp.zeros((length, length), F32)
        for level in range(levels):
            decay = decayed(sums_ref[level], high, low)
            pair = back_product((query * decay).astype(BF16), (key * decay).astype(BF16))
            scores += pair * pairs_ref[level].astype(F32)
        row = lax.broadcasted_iota(jnp.int32, (length, length), 0)
        col = lax.broadcasted_iota(jnp.int32, (length, length), 1)
        own = jnp.sum(query * key, axis=1, keepdims=True)
        scores += jnp.where(row == col, own, 0.0)
        marks = marks_ref[rows, :]
        scores = jnp.where(marks[:, 0:1] == segment_ref[s], scores, 0.0).astype(BF16)
        scores_ref[s] = scores
        value = mixed_ref[rows, pl.ds(value_at, value_dim)].astype(BF16)
        attended = matmul(scores, value) + back_product(start_ref[rows, :], recv_ref[s])
        attended = attended * marks[:, 3:4]
        attended_ref[rows, :] = attended
        headed = attended * rms_scale(attended, HEAD_EPS) * gain_ref[...]
        outgate = mixed_ref[rows, pl.ds(gate_at, value_dim)]
        gated_ref[rows, :] = (headed * (outgate * jax.nn.sigmoid(outgate))).astype(BF16)
        enter_ref[s] = recv_ref[s]
        return carry

    lax.fori_loop(0, count, mix, 0)
    finish_states(count, last, target, send_ref, recv_ref, send_sem, recv_sem)


def backward_kernel(
    key_dim,
    value_dim,
    mixed_ref,
    logits_ref,
    scores_ref,
    start_ref,
    end_ref,
    decay_ref,
    enter_ref,
    attended_ref,
    upstream_ref,
    gaterank_ref,
    gain_ref,
    marks_ref,
    segment_ref,
    sums_ref,
    pairs_ref,
    grad_ref,
    gain_grad_ref,
    bias_grad_ref,
    gaterank_grad_ref,
    out_ref,
    local_ref,
    send_ref,
    recv_ref,
    send_sem,
    recv_sem,
):
    count, _, length = segment_ref.shape
    levels = pairs_ref.shape[0]
    parts, place = lax.axis_size("fsdp"), lax.axis_index("fsdp")
    first, last, target = place == parts - 1, place == 0, lax.rem(place + parts - 1, parts)
    rank = gaterank_ref.shape[0]
    scale = key_dim ** (-0.5)
    value_at = 2 * key_dim
    gate_at = value_at + value_dim
    rank_at = gate_at + value_dim

    greet_neighbours(place, parts)

    @pl.when(first)
    def _():
        recv_ref[...] = jnp.zeros_like(recv_ref)

    gain_grad_ref[...] = jnp.zeros_like(gain_grad_ref)
    bias_grad_ref[...] = jnp.zeros_like(bias_grad_ref)
    gaterank_grad_ref[...] = jnp.zeros_like(gaterank_grad_ref)

    def rows_of(s):
        return pl.ds(pl.multiple_of(s * length, length), length)

    def heads(s, carry):
        rows = rows_of(s)
        upstream = upstream_ref[rows, :]
        attended = attended_ref[rows, :]
        outgate = mixed_ref[rows, pl.ds(gate_at, value_dim)]
        gain = gain_ref[...]
        norm = rms_scale(attended, HEAD_EPS)
        normed = attended * norm
        sig = jax.nn.sigmoid(outgate)
        grad_gate = upstream * (normed * gain) * sig * (1.0 + outgate * (1.0 - sig))
        grad_ref[rows, pl.ds(gate_at, value_dim)] = grad_gate.astype(BF16)
        grad_headed = upstream * (outgate * sig)
        gain_grad_ref[...] += jnp.sum(grad_headed * normed, axis=0, keepdims=True)
        grad_out = rms_back(grad_headed * gain, attended, norm) * marks_ref[rows, pl.ds(3, 1)]
        grad_out = grad_out.astype(BF16)
        out_ref[rows, :] = grad_out
        local_ref[s] = rows_product(grad_out, start_ref[rows, :])
        start_state(s, first, last, target, local_ref, send_ref, recv_ref, send_sem, recv_sem)
        return carry

    lax.fori_loop(0, count, heads, 0)

    def mix(s, carry):
        rows = rows_of(s)
        decay_row = decay_ref[s]
        pass_state(
            s, first, last, target, decay_row, local_ref, send_ref, recv_ref, send_sem, recv_sem
        )
        query = mixed_ref[rows, pl.ds(0, key_dim)] * scale
        key = mixed_ref[rows, pl.ds(key_dim, key_dim)]
        value = mixed_ref[rows, pl.ds(value_at, value_dim)].astype(BF16)
        marks = marks_ref[rows, :]
        logits = logits_ref[rows, :]
        high, low = split_rates(logits)
        grad_out = out_ref[rows, :]
        row = lax.broadcasted_iota(jnp.int32, (length, length), 0)
        col = lax.broadcasted_iota(jnp.int32, (length, length), 1)
        pair_grads = back_product(grad_out, value)
        pair_grads = jnp.where(marks[:, 0:1] == segment_ref[s], pair_grads, 0.0)
        own = jnp.sum(jnp.where(row == col, pair_grads, 0.0), axis=1, keepdims=True)
        grad_query = own * key
        grad_key = own * query
        grad_rates = jnp.zeros((length, key_dim), F32)
        for level in range(levels):
            decay = decayed(sums_ref[level], high, low)
            level_query = (query * decay).astype(BF16)
            level_key = (key * decay).astype(BF16)
            level_pairs = (pair_grads * pairs_ref[level].astype(F32)).astype(BF16)
            level_grad_query = matmul(level_pairs, level_key)
            level_grad_key = rows_product(level_pairs, level_query)
            grad_query += level_grad_query * decay
            grad_key += level_grad_key * decay
            flow = level_grad_query * level_query.astype(F32)
            flow += level_grad_key * level_key.astype(F32)
            grad_rates += rows_product(sums_ref[level], flow.astype(BF16))
        ending = recv_ref[s]
        entering = enter_ref[s]
        start_query = start_ref[rows, :]
        end_key = end_ref[rows, :]
        start_grad = matmul(grad_out, entering)
        end_grad = matmul(value, ending)
        grad_query += start_grad * (decayed(sums_ref[levels], high, low) * marks[:, 1:2])
        grad_key += end_grad * (decayed(sums_ref[levels + 1], high, low) * marks[:, 2:3])
        grad_rates += rows_product(
            sums_ref[levels], (start_grad * start_query.astype(F32)).astype(BF16)
        )
        grad_rates += rows_product(
            sums_ref[levels + 1], (end_grad * end_key.astype(F32)).astype(BF16)
        )
        grad_rates += decay_row * jnp.sum(
            ending.astype(F32) * entering.astype(F32), axis=0, keepdims=True
        )
        grad_value = rows_product(scores_ref[s], grad_out) + back_product(end_key, ending)
        grad_ref[rows, pl.ds(0, key_dim)] = (grad_query * scale).astype(BF16)
        grad_ref[rows, pl.ds(key_dim, key_dim)] = grad_key.astype(BF16)
        grad_ref[rows, pl.ds(value_at, value_dim)] = grad_value.astype(BF16)
        grad_logits = grad_rates / 16.0 * jax.nn.sigmoid(-logits)
        bias_grad_ref[...] += jnp.sum(grad_logits, axis=0, keepdims=True)
        lowrank = mixed_ref[rows, pl.ds(rank_at, rank)]
        gaterank_grad_ref[...] += dot(lowrank, grad_logits, ((0,), (0,)), HIGHEST)
        grad_lowrank = dot(grad_logits, gaterank_ref[...], ((1,), (1,)), HIGHEST)
        rest = grad_ref.shape[1] - rank_at - rank
        grad_ref[rows, pl.ds(rank_at, rank + rest)] = jnp.concatenate(
            [grad_lowrank, jnp.zeros((length, rest), F32)], axis=1
        ).astype(BF16)
        return carry

    lax.fori_loop(0, count, mix, 0)
    finish_states(count, last, target, send_ref, recv_ref, send_sem, recv_sem)


def state_scratch(count, value_dim, key_dim):
    return [
        pltpu.VMEM((count, value_dim, key_dim), F32),
        pltpu.VMEM((count, value_dim, key_dim), BF16),
        pltpu.VMEM((count, value_dim, key_dim), BF16),
        pltpu.SemaphoreType.DMA((count, PIECES)),
        pltpu.SemaphoreType.DMA((count, PIECES)),
    ]


def kernel_params(number, mebibytes=44):
    return pltpu.CompilerParams(
        collective_id=number, has_side_effects=True, vmem_limit_bytes=mebibytes * 2**20
    )


def head_copy(src, dst, send_sem, recv_sem, target):
    return pltpu.make_async_remote_copy(
        src_ref=src,
        dst_ref=dst,
        send_sem=send_sem,
        recv_sem=recv_sem,
        device_id={"head": target},
        device_id_type=pl.DeviceIdType.MESH,
    )


def greet_heads(targets):
    barrier = pltpu.get_barrier_semaphore()
    for target in targets:
        pl.semaphore_signal(
            barrier, inc=1, device_id={"head": target}, device_id_type=pl.DeviceIdType.MESH
        )
    pl.semaphore_wait(barrier, len(targets))


def square(me):
    return me + 1 - 2 * lax.rem(me, 2), me + 2 - 4 * (me // 2), H - 1 - me


def move_columns(weights, gain, out_ref, send_ref, send_sem, recv_sem, own_sem):
    me = lax.axis_index("head")
    place = 0
    for w in weights:
        n = w.shape[1] // H
        for h in range(H):
            part = w[:, pl.ds(h * n, n)].astype(F32) * gain
            send_ref[h, :, pl.ds(place, n)] = part.astype(BF16)
        place += n
    copies = []
    for ahead in range(1, H):
        peer = lax.rem(me + ahead, H)
        copy = head_copy(
            send_ref.at[peer],
            out_ref.at[me],
            send_sem.at[ahead],
            recv_sem.at[ahead],
            peer,
        )
        copy.start()
        copies.append(copy)
    own = pltpu.make_async_copy(send_ref.at[me], out_ref.at[me], own_sem)
    own.start()
    return copies + [own]


def mix_weights_kernel(*refs):
    *weights, extra_ref, gain_ref, out_ref, send_ref, send_sem, recv_sem, own_sem = refs
    me = lax.axis_index("head")
    greet_heads([lax.rem(me + ahead, H) for ahead in range(1, H)])
    spare = extra_ref.shape[1]
    for h in range(H):
        send_ref[h, :, pl.ds(send_ref.shape[2] - spare, spare)] = extra_ref[...]
    gain = gain_ref[...].astype(F32)
    for copy in move_columns(weights, gain, out_ref, send_ref, send_sem, recv_sem, own_sem):
        copy.wait()


def mix_weights(weights, extra, gain):
    rows = extra.shape[0]
    n = sum(w.shape[1] for w in weights) // H + extra.shape[1]
    return pl.pallas_call(
        mix_weights_kernel,
        out_shape=jax.ShapeDtypeStruct((H, rows, n), BF16),
        in_specs=[pl.BlockSpec(memory_space=pltpu.VMEM)] * (len(weights) + 2),
        out_specs=pl.BlockSpec(memory_space=pl.ANY),
        scratch_shapes=[
            pltpu.VMEM((H, rows, n), BF16),
            pltpu.SemaphoreType.DMA((H,)),
            pltpu.SemaphoreType.DMA((H,)),
            pltpu.SemaphoreType.DMA,
        ],
        compiler_params=kernel_params(3, 16),
        cost_estimate=pl.CostEstimate(flops=10**10, bytes_accessed=10**6, transcendentals=0),
        name="mix_weights",
    )(*weights, extra, gain)


class Share:
    def __init__(self, mine_ref, out_ref, send_sem, recv_sem, own_sem):
        self.refs = mine_ref, out_ref, send_sem, recv_sem, own_sem
        self.me = lax.axis_index("head")
        self.size = mine_ref.shape[0] // CHUNKS

    def copy(self, c, kind):
        mine, out, send_sem, recv_sem, _ = self.refs
        sides = square(self.me)[:2]
        rows = pl.ds(c * self.size, self.size)
        if kind < 2:
            src, dst, target = mine.at[rows], out.at[self.me, rows], sides[kind]
        else:
            origin, target = (sides[0], sides[1]) if c % 2 == 0 else (sides[1], sides[0])
            src = dst = out.at[origin, rows]
        return head_copy(src, dst, send_sem.at[c, kind], recv_sem.at[c, kind], target)

    def own(self, c):
        mine, out, _, _, own_sem = self.refs
        rows = pl.ds(c * self.size, self.size)
        return pltpu.make_async_copy(mine.at[rows], out.at[self.me, rows], own_sem.at[c])

    def start(self, c):
        self.copy(c, 0).start()
        self.copy(c, 1).start()
        self.own(c).start()

    def forward(self, c):
        self.copy(c, c % 2).wait_recv()
        self.copy(c, 2).start()

    def finish(self):
        for c in range(CHUNKS):
            self.copy(c, 1 - c % 2).wait_recv()
            self.copy(c, 2).wait_recv()
            self.own(c).wait()
            for kind in range(3):
                self.copy(c, kind).wait_send()


def share_scratch(rows, width):
    return [
        pltpu.VMEM((rows, width), BF16),
        pltpu.SemaphoreType.DMA((CHUNKS, 3)),
        pltpu.SemaphoreType.DMA((CHUNKS, 3)),
        pltpu.SemaphoreType.DMA((CHUNKS,)),
    ]


def share_kernel(
    tokens_ref,
    gate_ref,
    up_ref,
    gain_ref,
    out_ref,
    moved_ref,
    mine_ref,
    share_send,
    share_recv,
    share_own,
    send_ref,
    send_sem,
    recv_sem,
    own_sem,
):
    me = lax.axis_index("head")
    greet_heads([lax.rem(me + ahead, H) for ahead in range(1, H)])
    share = Share(mine_ref, out_ref, share_send, share_recv, share_own)
    for c in range(CHUNKS):
        rows = pl.ds(c * share.size, share.size)
        x = tokens_ref[rows, :].astype(F32)
        mine_ref[rows, :] = (x * rms_scale(x, EPS)).astype(BF16)
        share.start(c)
    gain = gain_ref[...].astype(F32)
    copies = move_columns(
        [gate_ref, up_ref], gain, moved_ref, send_ref, send_sem, recv_sem, own_sem
    )
    for c in range(CHUNKS):
        share.forward(c)
    share.finish()
    for copy in copies:
        copy.wait()


def share_tokens(tokens, w_gate, w_up, gain):
    rows, n = w_gate.shape[0], 2 * w_gate.shape[1] // H
    return pl.pallas_call(
        share_kernel,
        out_shape=[
            jax.ShapeDtypeStruct((H,) + tokens.shape, BF16),
            jax.ShapeDtypeStruct((H, rows, n), BF16),
        ],
        in_specs=[pl.BlockSpec(memory_space=pltpu.VMEM)] * 4,
        out_specs=[pl.BlockSpec(memory_space=pl.ANY)] * 2,
        scratch_shapes=share_scratch(*tokens.shape)
        + [
            pltpu.VMEM((H, rows, n), BF16),
            pltpu.SemaphoreType.DMA((H,)),
            pltpu.SemaphoreType.DMA((H,)),
            pltpu.SemaphoreType.DMA,
        ],
        compiler_params=kernel_params(4, 16),
        cost_estimate=pl.CostEstimate(flops=5 * 10**10, bytes_accessed=10**6, transcendentals=0),
        name="share_tokens",
    )(tokens, w_gate, w_up, gain)


def turn_rows(
    partial_ref,
    first_ref,
    relay_ref,
    second_ref,
    pass_ref,
    send_sem,
    recv_sem,
    done,
    share=None,
    fillers=(),
):
    me = lax.axis_index("head")
    side = square(me)
    far = side[2]
    size = first_ref.shape[0] // CHUNKS
    steps = CHUNKS + 3
    fillers = list(fillers)

    def copies(c):
        one, two = (side[0], side[1]) if c % 2 == 0 else (side[1], side[0])
        rows = pl.ds(c * size, size)
        sems = [(send_sem.at[c, kind], recv_sem.at[c, kind]) for kind in range(3)]
        return (
            head_copy(partial_ref.at[far, rows], relay_ref.at[rows], *sems[0], one),
            head_copy(partial_ref.at[one, rows], first_ref.at[rows], *sems[1], one),
            head_copy(pass_ref.at[rows], second_ref.at[rows], *sems[2], two),
            two,
            rows,
        )

    for c in range(CHUNKS):
        relay, first, *_ = copies(c)
        relay.start()
        first.start()
    for step in range(steps):
        for filler in fillers[step * len(fillers) // steps : (step + 1) * len(fillers) // steps]:
            filler()
        if step < CHUNKS:
            relay, _, second, two, rows = copies(step)
            relay.wait_recv()
            both = partial_ref[two, rows, :].astype(F32) + relay_ref[rows, :].astype(F32)
            pass_ref[rows, :] = both.astype(BF16)
            second.start()
        if 1 <= step <= CHUNKS:
            _, first, second, _, rows = copies(step - 1)
            first.wait_recv()
            second.wait_recv()
            total = partial_ref[me, rows, :].astype(F32) + first_ref[rows, :].astype(F32)
            made = done(rows, total + second_ref[rows, :].astype(F32))
            if share is not None:
                share.refs[0][rows, :] = made
                share.start(step - 1)
        if step >= 3 and share is not None:
            share.forward(step - 3)
    if share is not None:
        share.finish()
    for c in range(CHUNKS):
        for copy in copies(c)[:3]:
            copy.wait_send()


def turn_scratch(rows, width):
    return [pltpu.VMEM((rows, width), BF16) for _ in range(4)] + [
        pltpu.SemaphoreType.DMA((CHUNKS, 3)),
        pltpu.SemaphoreType.DMA((CHUNKS, 3)),
    ]


def hidden_kernel(partial_ref, tokens_ref, hidden_ref, out_ref, *scratch):
    greet_heads(square(lax.axis_index("head"))[:2])
    mine_ref, *sems = scratch[6:]

    def done(rows, total):
        hidden = tokens_ref[rows, :].astype(F32) + total
        hidden_ref[rows, :] = hidden
        return (hidden * rms_scale(hidden, EPS)).astype(BF16)

    turn_rows(partial_ref, *scratch[:6], done, Share(mine_ref, out_ref, *sems))


def share_hidden(partial, tokens):
    whole = pl.BlockSpec(memory_space=pltpu.VMEM)
    return pl.pallas_call(
        hidden_kernel,
        out_shape=[
            jax.ShapeDtypeStruct(tokens.shape, F32),
            jax.ShapeDtypeStruct((H,) + tokens.shape, BF16),
        ],
        in_specs=[whole] * 2,
        out_specs=[whole, pl.BlockSpec(memory_space=pl.ANY)],
        scratch_shapes=turn_scratch(*tokens.shape) + share_scratch(*tokens.shape),
        compiler_params=kernel_params(5, 24),
        cost_estimate=pl.CostEstimate(flops=8 * 10**10, bytes_accessed=10**7, transcendentals=0),
        name="share_hidden",
    )(partial, tokens)


class PairProduct:
    def __init__(self, left_ref, right_ref, out_ref, give_ref, take_ref, send_sem, recv_sem):
        self.refs = left_ref, right_ref, out_ref, give_ref, take_ref, send_sem, recv_sem
        self.core = lax.axis_index("core")
        self.groups, self.rows, width = out_ref.shape
        self.cut = width // 2 if width % (2 * LANES) == 0 else width

    def product(self, group, core, at):
        left, right, *_ = self.refs
        start = pl.multiple_of((group * CORES + core) * self.rows, LANES)
        return rows_product(left[:, pl.ds(start, self.rows)], right[:, pl.ds(at, self.cut)])

    def copy(self, group):
        _, _, _, give, take, send_sem, recv_sem = self.refs
        return pltpu.make_async_remote_copy(
            src_ref=give.at[group],
            dst_ref=take.at[group],
            send_sem=send_sem.at[group],
            recv_sem=recv_sem.at[group],
            device_id={"core": 1 - self.core},
            device_id_type=pl.DeviceIdType.MESH,
        )

    def give(self, group, at):
        out, give = self.refs[2:4]
        give[group, :, pl.ds(at, self.cut)] = self.product(group, 1 - self.core, at).astype(BF16)
        if at + self.cut == out.shape[2]:
            self.copy(group).start()

    def keep(self, group, at):
        out, _, take = self.refs[2:5]
        if at == 0:
            self.copy(group).wait_recv()
        both = self.product(group, self.core, at)
        both += take[group, :, pl.ds(at, self.cut)].astype(F32)
        out[group, :, pl.ds(at, self.cut)] = both.astype(BF16)

    def steps(self):
        places = [
            (group, at)
            for group in range(self.groups)
            for at in range(0, self.refs[2].shape[2], self.cut)
        ]
        return [functools.partial(self.give, *place) for place in places] + [
            functools.partial(self.keep, *place) for place in places
        ]

    def finish(self):
        for group in range(self.groups):
            self.copy(group).wait_send()


def pair_shape(left, right, groups):
    return (groups, left.shape[1] // (CORES * groups), right.shape[1])


def pair_scratch(shape):
    return [
        pltpu.VMEM(shape, BF16),
        pltpu.VMEM(shape, BF16),
        pltpu.SemaphoreType.DMA((shape[0],)),
        pltpu.SemaphoreType.DMA((shape[0],)),
    ]


def greet_square_and_core():
    barrier = pltpu.get_barrier_semaphore()
    for side in square(lax.axis_index("head"))[:2]:
        pl.semaphore_signal(
            barrier, inc=1, device_id={"head": side}, device_id_type=pl.DeviceIdType.MESH
        )
    other = 1 - lax.axis_index("core")
    pl.semaphore_signal(
        barrier, inc=1, device_id={"core": other}, device_id_type=pl.DeviceIdType.MESH
    )
    pl.semaphore_wait(barrier, 3)


def pair_kernel(left_ref, right_ref, out_ref, *scratch):
    barrier = pltpu.get_barrier_semaphore()
    other = 1 - lax.axis_index("core")
    pl.semaphore_signal(
        barrier, inc=1, device_id={"core": other}, device_id_type=pl.DeviceIdType.MESH
    )
    pl.semaphore_wait(barrier, 1)
    pair = PairProduct(left_ref, right_ref, out_ref, *scratch)
    for step in pair.steps():
        step()
    pair.finish()


def pair_product(left, right, groups):
    shape = pair_shape(left, right, groups)
    whole = pl.BlockSpec(memory_space=pltpu.VMEM)
    return pl.pallas_call(
        pair_kernel,
        out_shape=jax.ShapeDtypeStruct(shape, BF16),
        in_specs=[whole] * 2,
        out_specs=whole,
        scratch_shapes=pair_scratch(shape),
        compiler_params=kernel_params(7, 32),
        cost_estimate=pl.CostEstimate(flops=10**10, bytes_accessed=10**7, transcendentals=0),
        name="pair_product",
    )(left, right)


def branch_kernel(
    partial_ref,
    hidden_ref,
    upstream_ref,
    left_ref,
    right_ref,
    grad_ref,
    gain_grad_ref,
    pair_ref,
    out_ref,
    *scratch,
):
    greet_square_and_core()
    mine_ref, *sems = scratch[6:10]
    gain_grad_ref[...] = jnp.zeros_like(gain_grad_ref)
    pair = PairProduct(left_ref, right_ref, pair_ref, *scratch[10:])

    def done(rows, total):
        hidden = hidden_ref[rows, :]
        scale = rms_scale(hidden, EPS)
        gain_grad_ref[...] += jnp.sum(total * hidden * scale, axis=0, keepdims=True)
        grad = upstream_ref[rows, :].astype(F32) + rms_back(total, hidden, scale)
        grad_ref[rows, :] = grad
        return grad.astype(BF16)

    share = Share(mine_ref, out_ref, *sems)
    turn_rows(partial_ref, *scratch[:6], done, share, pair.steps())
    pair.finish()


def share_branch(partial, hidden, upstream, left, right, groups):
    whole = pl.BlockSpec(memory_space=pltpu.VMEM)
    shape = pair_shape(left, right, groups)
    return pl.pallas_call(
        branch_kernel,
        out_shape=[
            jax.ShapeDtypeStruct(hidden.shape, F32),
            jax.ShapeDtypeStruct((1, hidden.shape[1]), F32),
            jax.ShapeDtypeStruct(shape, BF16),
            jax.ShapeDtypeStruct((H,) + hidden.shape, BF16),
        ],
        in_specs=[whole] * 5,
        out_specs=[whole] * 3 + [pl.BlockSpec(memory_space=pl.ANY)],
        scratch_shapes=turn_scratch(*hidden.shape)
        + share_scratch(*hidden.shape)
        + pair_scratch(shape),
        compiler_params=kernel_params(6, 54),
        cost_estimate=pl.CostEstimate(flops=8 * 10**10, bytes_accessed=10**7, transcendentals=0),
        name="share_branch",
    )(partial, hidden, upstream, left, right)


def tokens_kernel(partial_ref, tokens_ref, upstream_ref, grad_ref, gain_grad_ref, *scratch):
    greet_heads(square(lax.axis_index("head"))[:2])
    gain_grad_ref[...] = jnp.zeros_like(gain_grad_ref)

    def done(rows, total):
        tokens = tokens_ref[rows, :].astype(F32)
        scale = rms_scale(tokens, EPS)
        gain_grad_ref[...] += jnp.sum(total * tokens * scale, axis=0, keepdims=True)
        grad = upstream_ref[rows, :] + rms_back(total, tokens, scale)
        grad_ref[rows, :] = grad.astype(BF16)

    turn_rows(partial_ref, *scratch, done)


def tokens_back(partial, tokens, upstream):
    whole = pl.BlockSpec(memory_space=pltpu.VMEM)
    return pl.pallas_call(
        tokens_kernel,
        out_shape=[
            jax.ShapeDtypeStruct(tokens.shape, BF16),
            jax.ShapeDtypeStruct((1, tokens.shape[1]), F32),
        ],
        in_specs=[whole] * 3,
        out_specs=[whole] * 2,
        scratch_shapes=turn_scratch(*tokens.shape),
        compiler_params=kernel_params(8, 24),
        cost_estimate=pl.CostEstimate(flops=4 * 10**10, bytes_accessed=10**7, transcendentals=0),
        name="tokens_back",
    )(partial, tokens, upstream)


def mix_forward(mixed, bias, gaterank, gain, marks, segment, sums, pairs, key_dim, value_dim):
    rows = mixed.shape[0]
    count, _, length = segment.shape
    shapes = (
        ((rows, value_dim), BF16),
        ((rows, value_dim), F32),
        ((rows, key_dim), F32),
        ((count, length, length), BF16),
        ((rows, key_dim), BF16),
        ((rows, key_dim), BF16),
        ((count, 1, key_dim), F32),
        ((count, value_dim, key_dim), BF16),
    )
    whole = pl.BlockSpec(memory_space=pltpu.VMEM)
    return pl.pallas_call(
        functools.partial(forward_kernel, key_dim, value_dim),
        out_shape=[jax.ShapeDtypeStruct(*s) for s in shapes],
        in_specs=[whole] * 8,
        out_specs=[whole] * len(shapes),
        scratch_shapes=state_scratch(count, value_dim, key_dim),
        compiler_params=kernel_params(1),
        cost_estimate=pl.CostEstimate(flops=5 * 10**10, bytes_accessed=10**7, transcendentals=0),
        name="mix_forward",
    )(mixed, bias, gaterank, gain, marks, segment, sums, pairs)


def mix_backward(
    mixed, kept, upstream, gaterank, gain, marks, segment, sums, pairs, key_dim, value_dim
):
    rows = mixed.shape[0]
    count = segment.shape[0]
    shapes = (
        (mixed.shape, BF16),
        ((1, value_dim), F32),
        ((1, key_dim), F32),
        (gaterank.shape, F32),
    )
    attended, logits, scores, start, end, decay, enter = kept
    whole = pl.BlockSpec(memory_space=pltpu.VMEM)
    return pl.pallas_call(
        functools.partial(backward_kernel, key_dim, value_dim),
        out_shape=[jax.ShapeDtypeStruct(*s) for s in shapes],
        in_specs=[whole] * 15,
        out_specs=[whole] * len(shapes),
        scratch_shapes=[pltpu.VMEM((rows, value_dim), BF16)]
        + state_scratch(count, value_dim, key_dim),
        compiler_params=kernel_params(2),
        cost_estimate=pl.CostEstimate(flops=8 * 10**10, bytes_accessed=10**7, transcendentals=0),
        name="mix_backward",
    )(
        mixed,
        logits,
        scores,
        start,
        end,
        decay,
        enter,
        attended,
        upstream,
        gaterank,
        gain,
        marks,
        segment,
        sums,
        pairs,
    )


def per_device(
    tokens,
    doc_lengths,
    norm_gain,
    w_query,
    w_key,
    w_value,
    w_outgate,
    w_lowrank,
    w_gaterank,
    gate_bias,
    head_gain,
    w_output,
    ffn_gain,
    w_gate,
    w_up,
    w_down,
    cotangent,
):
    seqs_here, length, width = tokens.shape
    reps = lax.axis_size("rep")
    parts = lax.axis_size("fsdp")
    devices = reps * H * CORES * parts
    here = lax.axis_index("head")
    key_dim, value_dim = DK, DV
    rank = w_lowrank.shape[1]
    rows = width // devices
    count = H * seqs_here

    rank_at = 2 * key_dim + 2 * value_dim

    def core_sum(g):
        halves = g.reshape(g.shape[0], CORES, -1, g.shape[-1])
        core = lax.axis_index("core")
        other = lax.ppermute(halves[:, 1 - core], "core", ((0, 1), (1, 0)))
        return (halves[:, core].astype(F32) + other.astype(F32)).astype(BF16)

    def scatter_rows(g):
        if reps > 1:
            g = lax.psum_scatter(g, "rep", scatter_dimension=0, tiled=True)
        return lax.psum_scatter(g, "fsdp", scatter_dimension=1, tiled=True)

    def gather_columns(moved):
        whole = lax.all_gather(moved, ("core", "fsdp"), axis=1, tiled=True)
        if reps > 1:
            whole = lax.all_gather(whole, "rep", axis=0, tiled=False)
        return whole.reshape(width, -1)

    def to_columns(g):
        moved = lax.all_to_all(g, "head", split_axis=0, concat_axis=0, tiled=True)
        return moved.transpose(1, 0, 2).astype(F32)

    def gather_part(w):
        if reps == 1:
            return lax.all_gather(w, SHARE, axis=0, tiled=True)
        whole = lax.all_gather(w, EVERY, axis=0, tiled=True)
        size = whole.shape[0] // H
        return lax.dynamic_slice_in_dim(whole, here * size, size, 0)

    def pair_part(g):
        return core_sum(g[None])[0] if reps == 1 else g

    def scatter_part(g):
        if reps == 1:
            return lax.psum_scatter(g, "fsdp", scatter_dimension=0, tiled=True)
        whole = jnp.zeros((H * g.shape[0], g.shape[1]), BF16)
        whole = lax.dynamic_update_slice_in_dim(whole, g, here * g.shape[0], 0)
        return lax.psum_scatter(whole, EVERY, scatter_dimension=0, tiled=True)

    rank_at = 2 * key_dim + 2 * value_dim

    def with_gain(w, gain):
        return (w.astype(F32) * gain.astype(F32)[:, None]).astype(BF16)

    small = (
        w_gaterank,
        gate_bias.reshape(1, -1),
        head_gain.reshape(1, -1),
        (doc_lengths // 16).astype(BF16).reshape(1, -1),
        (doc_lengths % 16).astype(BF16).reshape(1, -1),
    )
    edges = [rank]
    extra = jnp.pad(with_gain(w_lowrank, norm_gain), ((0, 0), (0, LANES - rank)))
    for piece in small:
        high, wide = piece.shape
        extra += jnp.pad(piece, ((0, rows - high), (edges[-1], LANES - edges[-1] - wide)))
        edges.append(edges[-1] + wide)

    mix_moved = mix_weights((w_query, w_key, w_value, w_outgate), extra, norm_gain[:, None])
    inputs = tokens.reshape(-1, width)
    inputs, _ = after(inputs, mix_moved)
    output_w = gather_part(w_output)
    mix_moved, output_w = after(mix_moved, output_w)
    mix_w = gather_columns(mix_moved)
    normed, ffn_moved = share_tokens(inputs, w_gate, w_up, ffn_gain[:, None])
    normed = normed.reshape(-1, width)
    ffn_w = gather_columns(ffn_moved)
    normed, w_down = after(normed, w_down)
    down_w = gather_part(w_down)

    small = mix_w[:, rank_at:].astype(F32).reshape(devices, rows, LANES)
    gaterank, bias, gain_head, long, short = (
        small[:, : rank if i == 0 else 1, edges[i] : edges[i + 1]] for i in range(len(edges) - 1)
    )
    gaterank = gaterank.transpose(1, 0, 2).reshape(rank, -1)
    bias = lax.dynamic_slice_in_dim(bias.reshape(1, -1), here * key_dim, key_dim, 1)
    gaterank = lax.dynamic_slice_in_dim(gaterank, here * key_dim, key_dim, 1)
    gain_head = gain_head.reshape(1, -1)
    lengths = (long * 16.0 + short).reshape(reps, H, CORES, parts, seqs_here, DOCS)
    lengths = lengths[lax.axis_index("rep"), :, lax.axis_index("core"), 0]
    lengths = lengths.reshape(count, DOCS).astype(jnp.int32)

    offset = lax.axis_index("fsdp") * length
    doc_ends = jnp.cumsum(lengths, axis=-1)
    places = offset + jnp.arange(length, dtype=jnp.int32)
    segment = jnp.sum((places[None, :, None] >= doc_ends[:, None, :]).astype(jnp.int32), axis=-1)
    before = jnp.sum((offset - 1 >= doc_ends).astype(jnp.int32), axis=-1)[:, None]
    last = segment[:, -1:]
    marks = jnp.stack(
        [
            segment,
            segment == before,
            segment == last,
            segment != DOCS - 1,
            jnp.broadcast_to(last == before, segment.shape),
        ],
        axis=2,
    )
    marks = jnp.pad(marks.astype(F32).reshape(count * length, 5), ((0, 0), (0, 3)))
    segment = segment.astype(F32).reshape(count, 1, length)

    mixed = matmul(normed, mix_w)
    sums, pairs = level_sums(length)
    sums, pairs = sums.astype(BF16), pairs.astype(BF16)
    gated, *kept = mix_forward(
        mixed, bias, gaterank, gain_head, marks, segment, sums, pairs, key_dim, value_dim
    )
    cot_rows = cotangent.reshape(-1, width)
    gated, cot_shared = after(gated, share_rows(cot_rows))
    partial = matmul(gated, output_w).astype(BF16).reshape(H, -1, width)
    hidden, normed_two = share_hidden(partial, inputs)
    normed_two = normed_two.reshape(-1, width)

    gate_pre, up_pre = jnp.split(matmul(normed_two, ffn_w), 2, axis=1)
    sig_gate = jax.nn.sigmoid(gate_pre)
    activated = (gate_pre * sig_gate * up_pre).astype(BF16)

    grad_down_w = rows_product(activated, cot_shared).astype(BF16)
    down_w, grad_down_w = after(down_w, grad_down_w)
    grad_act = back_product(cot_shared, down_w)
    grad_up = grad_act * gate_pre * sig_gate
    grad_gate = grad_act * up_pre * sig_gate * (1.0 + gate_pre * (1.0 - sig_gate))
    grad_pre = jnp.concatenate([grad_gate, grad_up], axis=1).astype(BF16)
    grad_pre, grad_down_w = after(grad_pre, pair_part(grad_down_w))
    grad_down_w = scatter_part(grad_down_w)
    partial = back_product(grad_pre, ffn_w).astype(BF16)
    down_partial = matmul(activated, down_w).astype(BF16)

    grad_hidden, grad_gain_two, grad_ffn_w, branch = share_branch(
        partial.reshape(H, -1, width), hidden, cot_rows, normed_two, grad_pre, reps * H
    )
    grad_ffn_w = scatter_rows(grad_ffn_w)
    branch = branch.reshape(-1, width)
    grad_output_w = pair_part(rows_product(gated, branch).astype(BF16))
    grad_gated = back_product(branch, output_w)
    grad_gated, grad_output_w, grad_down_w = after(grad_gated, grad_output_w, grad_down_w)
    grad_output_w = scatter_part(grad_output_w)
    pieces = move_rows(down_partial)
    grad_mixed, grad_gain_head, grad_bias, grad_gaterank = mix_backward(
        mixed,
        kept,
        grad_gated,
        gaterank,
        gain_head,
        marks,
        segment,
        sums,
        pairs,
        key_dim,
        value_dim,
    )
    grad_mixed, pieces, grad_down_w, grad_output_w = after(
        grad_mixed, pieces, grad_down_w, grad_output_w
    )
    output = (hidden + jnp.sum(pieces.astype(F32), axis=0)).astype(BF16).reshape(tokens.shape)
    grad_mix_w = pair_product(normed, grad_mixed, reps * H)
    grad_mixed, grad_mix_w = after(grad_mixed, grad_mix_w)
    partial = back_product(grad_mixed, mix_w).astype(BF16)
    grad_mix_w = scatter_rows(grad_mix_w)
    tokens_grad, grad_gain_one = tokens_back(partial.reshape(H, -1, width), inputs, grad_hidden)
    tokens_grad = tokens_grad.reshape(tokens.shape)
    w_gate_grad, w_up_grad = jnp.split(to_columns(grad_ffn_w), 2, axis=2)
    grad_mix_w = to_columns(grad_mix_w)

    edges = [key_dim, 2 * key_dim, 2 * key_dim + value_dim, rank_at, rank_at + rank]
    query_g, key_g, value_g, outgate_g, lowrank_g, _ = jnp.split(grad_mix_w, edges, axis=2)
    gain_one = norm_gain.astype(F32)
    gain_two = ffn_gain.astype(F32)

    def scaled(g, gain, w):
        return g.reshape(w.shape) * gain[:, None]

    def place(g, axis):
        shape = list(g.shape)
        shape[axis] *= H
        return lax.dynamic_update_slice_in_dim(jnp.zeros(shape, F32), g, here * key_dim, axis)

    small_grads = jnp.concatenate(
        [
            grad_gain_one.reshape(devices, -1),
            grad_gain_two.reshape(devices, -1),
            place(grad_bias.reshape(-1), 0).reshape(devices, -1),
            grad_gain_head.reshape(devices, -1),
            place(grad_gaterank, 1)
            .reshape(rank, devices, -1)
            .transpose(1, 0, 2)
            .reshape(devices, -1),
        ],
        axis=1,
    )
    small_grads = lax.all_to_all(small_grads, EVERY, split_axis=0, concat_axis=0, tiled=True)
    small_grads = jnp.sum(small_grads, axis=0)
    sizes = [norm_gain.shape[0], ffn_gain.shape[0], gate_bias.shape[0], head_gain.shape[0]]
    norm_g, ffn_g, bias_g, head_g, gaterank_g = jnp.split(
        small_grads, [sum(sizes[: i + 1]) for i in range(len(sizes))]
    )
    return (
        output,
        tokens_grad,
        norm_g / gain_one,
        scaled(query_g, gain_one, w_query),
        scaled(key_g, gain_one, w_key),
        scaled(value_g, gain_one, w_value),
        scaled(outgate_g, gain_one, w_outgate),
        scaled(jnp.sum(lowrank_g, axis=1), gain_one, w_lowrank),
        gaterank_g.reshape(w_gaterank.shape),
        bias_g,
        head_g,
        grad_output_w.astype(F32),
        ffn_g / gain_two,
        scaled(w_gate_grad, gain_two, w_gate),
        scaled(w_up_grad, gain_two, w_up),
        grad_down_w.astype(F32),
    )


def solution(mesh):
    dp, parts = mesh.shape["dp"], mesh.shape["fsdp"]
    fine = Mesh(mesh.devices.reshape(dp // (H * CORES), H, CORES, parts), EVERY)
    seq = ("rep", "head", "core")
    rows, vector = P(EVERY, None), P(EVERY)
    activations = P(seq, "fsdp", None)
    columns = P(None, EVERY)
    return jax.shard_map(
        per_device,
        mesh=fine,
        in_specs=(
            activations,
            P(seq, None),
            vector,
            rows,
            rows,
            rows,
            rows,
            rows,
            columns,
            vector,
            vector,
            rows,
            vector,
            rows,
            rows,
            rows,
            activations,
        ),
        out_specs=(
            activations,
            activations,
            vector,
            rows,
            rows,
            rows,
            rows,
            rows,
            columns,
            vector,
            vector,
            rows,
            vector,
            rows,
            rows,
            rows,
        ),
        check_vma=False,
    )
```

```python
import functools

import jax
import jax.experimental.pallas as pl
import jax.experimental.pallas.tpu as pltpu
import jax.numpy as jnp
from jax import lax
from jax.sharding import Mesh
from jax.sharding import PartitionSpec as P

H = 4
DK = 256
DV = 512
CORES = 2
DOCS = 8
PIECES = 2
LANES = 128
CHUNKS = 8

EPS = 1e-05
HEAD_EPS = 1.0
HIGHEST = lax.Precision.HIGHEST
F32 = jnp.float32
BF16 = jnp.bfloat16

SHARE = ("rep", "core", "fsdp")
EVERY = ("rep", "head", "core", "fsdp")


def dot(a, b, dims, precision=None):
    return lax.dot_general(a, b, (dims, ((), ())), precision=precision, preferred_element_type=F32)


def after(value, *others):
    return lax.optimization_barrier((value,) + others)


def matmul(a, b):
    return dot(a, b, ((1,), (0,)))


def rows_product(a, b):
    return dot(a, b, ((0,), (0,)))


def back_product(a, b):
    return dot(a, b, ((1,), (1,)))


def batched(form, a, b):
    return jnp.einsum(form, a, b, preferred_element_type=F32)


def rms_scale(values, epsilon):
    return lax.rsqrt(jnp.mean(values * values, axis=-1, keepdims=True) + epsilon)


def rms_back(upstream, values, scale):
    return scale * upstream - values * scale**3 * jnp.mean(upstream * values, axis=-1, keepdims=True)


def share_rows(part):
    spread = jnp.broadcast_to(part[None], (H,) + part.shape)
    whole = lax.all_to_all(spread, "head", split_axis=0, concat_axis=0, tiled=True)
    return whole.reshape(-1, part.shape[-1])


def move_rows(partial):
    pieces = partial.astype(BF16).reshape(H, -1, partial.shape[-1])
    return lax.all_to_all(pieces, "head", split_axis=0, concat_axis=0, tiled=True)


def sum_rows(partial):
    return jnp.sum(move_rows(partial).astype(F32), axis=0)


def level_sums(length):
    rows = jnp.arange(length)[:, None]
    cols = jnp.arange(length)[None, :]
    sums, pairs = [], []
    step = 1
    while step < length:
        bound = rows // (2 * step) * (2 * step) + step - 1
        upper = rows > bound
        sums.append(jnp.where(upper, (cols > bound) & (cols <= rows), (cols > rows) & (cols <= bound)))
        pairs.append(upper & (cols // (2 * step) == rows // (2 * step)) & (cols <= bound))
        step *= 2
    sums.append(cols <= rows)
    sums.append(cols > rows)
    return jnp.stack(sums), jnp.stack(pairs)


def log_sigmoid(x):
    return jnp.minimum(x, 0.0) - jnp.log1p(jnp.exp(-jnp.abs(x)))


def state_copy(send, recv, send_sem, recv_sem, seq, piece, target):
    size = send.shape[1] // PIECES
    part = pl.ds(piece * size, size)
    return pltpu.make_async_remote_copy(
        src_ref=send.at[seq, part],
        dst_ref=recv.at[seq, part],
        send_sem=send_sem.at[seq, piece],
        recv_sem=recv_sem.at[seq, piece],
        device_id={"fsdp": target},
        device_id_type=pl.DeviceIdType.MESH,
    )


def greet_neighbours(place, parts):
    barrier = pltpu.get_barrier_semaphore()
    for near, there in ((place - 1, place > 0), (place + 1, place < parts - 1)):

        @pl.when(there)
        def _(near=near):
            pl.semaphore_signal(
                barrier,
                inc=1,
                device_id={"fsdp": lax.rem(near + parts, parts)},
                device_id_type=pl.DeviceIdType.MESH,
            )

    peers = (place > 0).astype(jnp.int32) + (place < parts - 1).astype(jnp.int32)
    pl.semaphore_wait(barrier, peers)


def pass_state(s, first, last, target, decay, local, send, recv, send_sem, recv_sem):
    size = send.shape[1] // PIECES
    for piece in range(PIECES):
        part = pl.ds(piece * size, size)
        copy = state_copy(send, recv, send_sem, recv_sem, s, piece, target)

        @pl.when(jnp.logical_not(first))
        def _(copy=copy):
            copy.wait_recv()

        @pl.when(jnp.logical_not(jnp.logical_or(first, last)))
        def _(copy=copy, part=part):
            joined = decay * recv[s, part].astype(F32) + local[s, part]
            send[s, part] = joined.astype(BF16)
            copy.start()


def start_state(s, first, last, target, local, send, recv, send_sem, recv_sem):
    @pl.when(jnp.logical_and(first, jnp.logical_not(last)))
    def _():
        send[s] = local[s].astype(BF16)
        for piece in range(PIECES):
            state_copy(send, recv, send_sem, recv_sem, s, piece, target).start()


def finish_states(count, last, target, send, recv, send_sem, recv_sem):
    @pl.when(jnp.logical_not(last))
    def _():
        def one(s, carry):
            for piece in range(PIECES):
                state_copy(send, recv, send_sem, recv_sem, s, piece, target).wait_send()
            return carry

        lax.fori_loop(0, count, one, 0)


def split_rates(logits):
    rates = log_sigmoid(logits) / 16.0
    high = rates.astype(BF16)
    return high, (rates - high.astype(F32)).astype(BF16)


def decayed(sums, high, low):
    return jnp.exp(matmul(sums, high) + matmul(sums, low))


def forward_kernel(
    key_dim,
    value_dim,
    mixed_ref,
    bias_ref,
    gaterank_ref,
    gain_ref,
    marks_ref,
    segment_ref,
    sums_ref,
    pairs_ref,
    gated_ref,
    *refs,
):
    kept, (attended_ref, logits_ref, scores_ref, start_ref, end_ref, decay_ref) = refs[:7], refs[7:13]
    local_ref, send_ref, recv_ref, send_sem, recv_sem, keep_sem = refs[13:]
    count, _, length = segment_ref.shape
    levels = pairs_ref.shape[0]
    parts, place = lax.axis_size("fsdp"), lax.axis_index("fsdp")
    first, last, target = place == 0, place == parts - 1, lax.rem(place + 1, parts)

    def rows_of(s):
        return pl.ds(pl.multiple_of(s * length, length), length)

    def keeps(s, kinds):
        held = (attended_ref, logits_ref, scores_ref, start_ref, end_ref, decay_ref, recv_ref)
        rows = rows_of(s)
        for kind in kinds:
            at = rows if len(held[kind].shape) == 2 else s
            yield pltpu.make_async_copy(held[kind].at[at], kept[kind].at[at], keep_sem.at[s, kind])

    def finish_keeps(s, carry):
        for copy in keeps(s, range(7)):
            copy.wait()
        return carry

    rank = gaterank_ref.shape[0]
    scale = key_dim ** (-0.5)
    value_at = 2 * key_dim
    gate_at = value_at + value_dim
    rank_at = gate_at + value_dim

    greet_neighbours(place, parts)

    @pl.when(first)
    def _():
        recv_ref[...] = jnp.zeros_like(recv_ref)

    def ends(s, carry):
        rows = rows_of(s)
        lowrank = mixed_ref[rows, pl.ds(rank_at, rank)]
        logits = dot(lowrank, gaterank_ref[...], ((1,), (0,)), HIGHEST) + bias_ref[...]
        logits_ref[rows, :] = logits
        high, low = split_rates(logits)
        from_start = decayed(sums_ref[levels], high, low)
        to_end = decayed(sums_ref[levels + 1], high, low)
        marks = marks_ref[rows, :]
        decay_ref[s] = from_start[length - 1 :, :] * marks[:1, 4:5]
        query = mixed_ref[rows, pl.ds(0, key_dim)] * scale
        key = mixed_ref[rows, pl.ds(key_dim, key_dim)]
        start_ref[rows, :] = (query * (from_start * marks[:, 1:2])).astype(BF16)
        end_key = (key * (to_end * marks[:, 2:3])).astype(BF16)
        end_ref[rows, :] = end_key
        value = mixed_ref[rows, pl.ds(value_at, value_dim)].astype(BF16)
        local_ref[s] = rows_product(value, end_key)
        start_state(s, first, last, target, local_ref, send_ref, recv_ref, send_sem, recv_sem)
        for copy in keeps(s, (1, 3, 4, 5)):
            copy.start()
        return carry

    lax.fori_loop(0, count, ends, 0)

    def mix(s, carry):
        rows = rows_of(s)
        pass_state(
            s, first, last, target, decay_ref[s], local_ref, send_ref, recv_ref, send_sem, recv_sem
        )
        query = mixed_ref[rows, pl.ds(0, key_dim)] * scale
        key = mixed_ref[rows, pl.ds(key_dim, key_dim)]
        high, low = split_rates(logits_ref[rows, :])
        scores = jnp.zeros((length, length), F32)
        for level in range(levels):
            decay = decayed(sums_ref[level], high, low)
            pair = back_product((query * decay).astype(BF16), (key * decay).astype(BF16))
            scores += pair * pairs_ref[level].astype(F32)
        row = lax.broadcasted_iota(jnp.int32, (length, length), 0)
        col = lax.broadcasted_iota(jnp.int32, (length, length), 1)
        own = jnp.sum(query * key, axis=1, keepdims=True)
        scores += jnp.where(row == col, own, 0.0)
        marks = marks_ref[rows, :]
        scores = jnp.where(marks[:, 0:1] == segment_ref[s], scores, 0.0).astype(BF16)
        scores_ref[s] = scores
        value = mixed_ref[rows, pl.ds(value_at, value_dim)].astype(BF16)
        attended = matmul(scores, value) + back_product(start_ref[rows, :], recv_ref[s])
        attended = attended * marks[:, 3:4]
        attended_ref[rows, :] = attended
        headed = attended * rms_scale(attended, HEAD_EPS) * gain_ref[...]
        outgate = mixed_ref[rows, pl.ds(gate_at, value_dim)]
        gated_ref[rows, :] = (headed * (outgate * jax.nn.sigmoid(outgate))).astype(BF16)
        for copy in keeps(s, (0, 2, 6)):
            copy.start()
        return carry

    lax.fori_loop(0, count, mix, 0)
    finish_states(count, last, target, send_ref, recv_ref, send_sem, recv_sem)
    lax.fori_loop(0, count, finish_keeps, 0)


def backward_kernel(
    key_dim,
    value_dim,
    *refs,
):
    given, refs = refs[:9], refs[9:]
    gaterank_ref, gain_ref, marks_ref, segment_ref, sums_ref, pairs_ref, *refs = refs
    grad_ref, gain_grad_ref, bias_grad_ref, gaterank_grad_ref, *refs = refs
    held, refs = refs[:9], refs[9:]
    mixed_ref, upstream_ref, attended_ref, start_ref, *rest_refs = held
    logits_ref, scores_ref, end_ref, decay_ref, enter_ref = rest_refs
    out_ref, local_ref, send_ref, recv_ref, send_sem, recv_sem, take_sem = refs
    count, _, length = segment_ref.shape

    def rows_of(s):
        return pl.ds(pl.multiple_of(s * length, length), length)

    def takes(s, kinds):
        rows = rows_of(s)
        for kind in kinds:
            at = rows if len(held[kind].shape) == 2 else s
            yield pltpu.make_async_copy(given[kind].at[at], held[kind].at[at], take_sem.at[s, kind])

    def start_takes(s, carry):
        for copy in takes(s, range(9)):
            copy.start()
        return carry

    lax.fori_loop(0, count, start_takes, 0)
    levels = pairs_ref.shape[0]
    parts, place = lax.axis_size("fsdp"), lax.axis_index("fsdp")
    first, last, target = place == parts - 1, place == 0, lax.rem(place + parts - 1, parts)
    rank = gaterank_ref.shape[0]
    scale = key_dim ** (-0.5)
    value_at = 2 * key_dim
    gate_at = value_at + value_dim
    rank_at = gate_at + value_dim

    greet_neighbours(place, parts)

    @pl.when(first)
    def _():
        recv_ref[...] = jnp.zeros_like(recv_ref)

    gain_grad_ref[...] = jnp.zeros_like(gain_grad_ref)
    bias_grad_ref[...] = jnp.zeros_like(bias_grad_ref)
    gaterank_grad_ref[...] = jnp.zeros_like(gaterank_grad_ref)

    def heads(s, carry):
        rows = rows_of(s)
        for copy in takes(s, range(4)):
            copy.wait()
        upstream = upstream_ref[rows, :]
        attended = attended_ref[rows, :]
        outgate = mixed_ref[rows, pl.ds(gate_at, value_dim)]
        gain = gain_ref[...]
        norm = rms_scale(attended, HEAD_EPS)
        normed = attended * norm
        sig = jax.nn.sigmoid(outgate)
        grad_gate = upstream * (normed * gain) * sig * (1.0 + outgate * (1.0 - sig))
        grad_ref[rows, pl.ds(gate_at, value_dim)] = grad_gate.astype(BF16)
        grad_headed = upstream * (outgate * sig)
        gain_grad_ref[...] += jnp.sum(grad_headed * normed, axis=0, keepdims=True)
        grad_out = rms_back(grad_headed * gain, attended, norm) * marks_ref[rows, pl.ds(3, 1)]
        grad_out = grad_out.astype(BF16)
        out_ref[rows, :] = grad_out
        local_ref[s] = rows_product(grad_out, start_ref[rows, :])
        start_state(s, first, last, target, local_ref, send_ref, recv_ref, send_sem, recv_sem)
        return carry

    lax.fori_loop(0, count, heads, 0)

    def mix(s, carry):
        rows = rows_of(s)
        for copy in takes(s, range(4, 9)):
            copy.wait()
        decay_row = decay_ref[s]
        pass_state(
            s, first, last, target, decay_row, local_ref, send_ref, recv_ref, send_sem, recv_sem
        )
        query = mixed_ref[rows, pl.ds(0, key_dim)] * scale
        key = mixed_ref[rows, pl.ds(key_dim, key_dim)]
        value = mixed_ref[rows, pl.ds(value_at, value_dim)].astype(BF16)
        marks = marks_ref[rows, :]
        logits = logits_ref[rows, :]
        high, low = split_rates(logits)
        grad_out = out_ref[rows, :]
        row = lax.broadcasted_iota(jnp.int32, (length, length), 0)
        col = lax.broadcasted_iota(jnp.int32, (length, length), 1)
        pair_grads = back_product(grad_out, value)
        pair_grads = jnp.where(marks[:, 0:1] == segment_ref[s], pair_grads, 0.0)
        own = jnp.sum(jnp.where(row == col, pair_grads, 0.0), axis=1, keepdims=True)
        grad_query = own * key
        grad_key = own * query
        grad_rates = jnp.zeros((length, key_dim), F32)
        for level in range(levels):
            decay = decayed(sums_ref[level], high, low)
            level_query = (query * decay).astype(BF16)
            level_key = (key * decay).astype(BF16)
            level_pairs = (pair_grads * pairs_ref[level].astype(F32)).astype(BF16)
            level_grad_query = matmul(level_pairs, level_key)
            level_grad_key = rows_product(level_pairs, level_query)
            grad_query += level_grad_query * decay
            grad_key += level_grad_key * decay
            flow = level_grad_query * level_query.astype(F32)
            flow += level_grad_key * level_key.astype(F32)
            grad_rates += rows_product(sums_ref[level], flow.astype(BF16))
        ending = recv_ref[s]
        entering = enter_ref[s]
        start_query = start_ref[rows, :]
        end_key = end_ref[rows, :]
        start_grad = matmul(grad_out, entering)
        end_grad = matmul(value, ending)
        grad_query += start_grad * (decayed(sums_ref[levels], high, low) * marks[:, 1:2])
        grad_key += end_grad * (decayed(sums_ref[levels + 1], high, low) * marks[:, 2:3])
        grad_rates += rows_product(
            sums_ref[levels], (start_grad * start_query.astype(F32)).astype(BF16)
        )
        grad_rates += rows_product(
            sums_ref[levels + 1], (end_grad * end_key.astype(F32)).astype(BF16)
        )
        grad_rates += decay_row * jnp.sum(
            ending.astype(F32) * entering.astype(F32), axis=0, keepdims=True
        )
        grad_value = rows_product(scores_ref[s], grad_out) + back_product(end_key, ending)
        grad_ref[rows, pl.ds(0, key_dim)] = (grad_query * scale).astype(BF16)
        grad_ref[rows, pl.ds(key_dim, key_dim)] = grad_key.astype(BF16)
        grad_ref[rows, pl.ds(value_at, value_dim)] = grad_value.astype(BF16)
        grad_logits = grad_rates / 16.0 * jax.nn.sigmoid(-logits)
        bias_grad_ref[...] += jnp.sum(grad_logits, axis=0, keepdims=True)
        lowrank = mixed_ref[rows, pl.ds(rank_at, rank)]
        gaterank_grad_ref[...] += dot(lowrank, grad_logits, ((0,), (0,)), HIGHEST)
        grad_lowrank = dot(grad_logits, gaterank_ref[...], ((1,), (1,)), HIGHEST)
        rest = grad_ref.shape[1] - rank_at - rank
        grad_ref[rows, pl.ds(rank_at, rank + rest)] = jnp.concatenate(
            [grad_lowrank, jnp.zeros((length, rest), F32)], axis=1
        ).astype(BF16)
        return carry

    lax.fori_loop(0, count, mix, 0)
    finish_states(count, last, target, send_ref, recv_ref, send_sem, recv_sem)


def state_scratch(count, value_dim, key_dim):
    return [
        pltpu.VMEM((count, value_dim, key_dim), F32),
        pltpu.VMEM((count, value_dim, key_dim), BF16),
        pltpu.VMEM((count, value_dim, key_dim), BF16),
        pltpu.SemaphoreType.DMA((count, PIECES)),
        pltpu.SemaphoreType.DMA((count, PIECES)),
    ]


def kernel_params(number, mebibytes=44):
    return pltpu.CompilerParams(
        collective_id=number, has_side_effects=True, vmem_limit_bytes=mebibytes * 2**20
    )


def head_copy(src, dst, send_sem, recv_sem, target):
    return pltpu.make_async_remote_copy(
        src_ref=src,
        dst_ref=dst,
        send_sem=send_sem,
        recv_sem=recv_sem,
        device_id={"head": target},
        device_id_type=pl.DeviceIdType.MESH,
    )


def greet_heads(targets):
    barrier = pltpu.get_barrier_semaphore()
    for target in targets:
        pl.semaphore_signal(
            barrier, inc=1, device_id={"head": target}, device_id_type=pl.DeviceIdType.MESH
        )
    pl.semaphore_wait(barrier, len(targets))


def square(me):
    return me + 1 - 2 * lax.rem(me, 2), me + 2 - 4 * (me // 2), H - 1 - me


def move_columns(weights, gain, out_ref, send_ref, send_sem, recv_sem, own_sem):
    me = lax.axis_index("head")
    place = 0
    for w in weights:
        n = w.shape[1] // H
        for h in range(H):
            part = w[:, pl.ds(h * n, n)].astype(F32) * gain
            send_ref[h, :, pl.ds(place, n)] = part.astype(BF16)
        place += n
    copies = []
    for ahead in range(1, H):
        peer = lax.rem(me + ahead, H)
        copy = head_copy(
            send_ref.at[peer],
            out_ref.at[me],
            send_sem.at[ahead],
            recv_sem.at[ahead],
            peer,
        )
        copy.start()
        copies.append(copy)
    own = pltpu.make_async_copy(send_ref.at[me], out_ref.at[me], own_sem)
    own.start()
    return copies + [own]


def mix_weights_kernel(*refs):
    *weights, extra_ref, gain_ref, out_ref, send_ref, send_sem, recv_sem, own_sem = refs
    me = lax.axis_index("head")
    greet_heads([lax.rem(me + ahead, H) for ahead in range(1, H)])
    spare = extra_ref.shape[1]
    for h in range(H):
        send_ref[h, :, pl.ds(send_ref.shape[2] - spare, spare)] = extra_ref[...]
    gain = gain_ref[...].astype(F32)
    for copy in move_columns(weights, gain, out_ref, send_ref, send_sem, recv_sem, own_sem):
        copy.wait()


def mix_weights(weights, extra, gain):
    rows = extra.shape[0]
    n = sum(w.shape[1] for w in weights) // H + extra.shape[1]
    return pl.pallas_call(
        mix_weights_kernel,
        out_shape=jax.ShapeDtypeStruct((H, rows, n), BF16),
        in_specs=[pl.BlockSpec(memory_space=pltpu.VMEM)] * (len(weights) + 2),
        out_specs=pl.BlockSpec(memory_space=pl.ANY),
        scratch_shapes=[
            pltpu.VMEM((H, rows, n), BF16),
            pltpu.SemaphoreType.DMA((H,)),
            pltpu.SemaphoreType.DMA((H,)),
            pltpu.SemaphoreType.DMA,
        ],
        compiler_params=kernel_params(3, 16),
        cost_estimate=pl.CostEstimate(flops=10**10, bytes_accessed=10**6, transcendentals=0),
        name="mix_weights",
    )(*weights, extra, gain)


class Share:
    def __init__(self, mine_ref, out_ref, send_sem, recv_sem, own_sem):
        self.refs = mine_ref, out_ref, send_sem, recv_sem, own_sem
        self.me = lax.axis_index("head")
        self.size = mine_ref.shape[0] // CHUNKS

    def copy(self, c, kind):
        mine, out, send_sem, recv_sem, _ = self.refs
        sides = square(self.me)[:2]
        rows = pl.ds(c * self.size, self.size)
        if kind < 2:
            src, dst, target = mine.at[rows], out.at[self.me, rows], sides[kind]
        else:
            origin, target = (sides[0], sides[1]) if c % 2 == 0 else (sides[1], sides[0])
            src = dst = out.at[origin, rows]
        return head_copy(src, dst, send_sem.at[c, kind], recv_sem.at[c, kind], target)

    def own(self, c):
        mine, out, _, _, own_sem = self.refs
        rows = pl.ds(c * self.size, self.size)
        return pltpu.make_async_copy(mine.at[rows], out.at[self.me, rows], own_sem.at[c])

    def start(self, c):
        self.copy(c, 0).start()
        self.copy(c, 1).start()
        self.own(c).start()

    def forward(self, c):
        self.copy(c, c % 2).wait_recv()
        self.copy(c, 2).start()

    def finish(self):
        for c in range(CHUNKS):
            self.copy(c, 1 - c % 2).wait_recv()
            self.copy(c, 2).wait_recv()
            self.own(c).wait()
            for kind in range(3):
                self.copy(c, kind).wait_send()


def share_scratch(rows, width):
    return [
        pltpu.VMEM((rows, width), BF16),
        pltpu.SemaphoreType.DMA((CHUNKS, 3)),
        pltpu.SemaphoreType.DMA((CHUNKS, 3)),
        pltpu.SemaphoreType.DMA((CHUNKS,)),
    ]


def share_kernel(
    tokens_ref,
    gate_ref,
    up_ref,
    gain_ref,
    out_ref,
    moved_ref,
    mine_ref,
    share_send,
    share_recv,
    share_own,
    send_ref,
    send_sem,
    recv_sem,
    own_sem,
):
    me = lax.axis_index("head")
    greet_heads([lax.rem(me + ahead, H) for ahead in range(1, H)])
    share = Share(mine_ref, out_ref, share_send, share_recv, share_own)
    for c in range(CHUNKS):
        rows = pl.ds(c * share.size, share.size)
        x = tokens_ref[rows, :].astype(F32)
        mine_ref[rows, :] = (x * rms_scale(x, EPS)).astype(BF16)
        share.start(c)
    gain = gain_ref[...].astype(F32)
    copies = move_columns(
        [gate_ref, up_ref], gain, moved_ref, send_ref, send_sem, recv_sem, own_sem
    )
    for c in range(CHUNKS):
        share.forward(c)
    share.finish()
    for copy in copies:
        copy.wait()


def share_tokens(tokens, w_gate, w_up, gain):
    rows, n = w_gate.shape[0], 2 * w_gate.shape[1] // H
    return pl.pallas_call(
        share_kernel,
        out_shape=[
            jax.ShapeDtypeStruct((H,) + tokens.shape, BF16),
            jax.ShapeDtypeStruct((H, rows, n), BF16),
        ],
        in_specs=[pl.BlockSpec(memory_space=pltpu.VMEM)] * 4,
        out_specs=[pl.BlockSpec(memory_space=pl.ANY)] * 2,
        scratch_shapes=share_scratch(*tokens.shape)
        + [
            pltpu.VMEM((H, rows, n), BF16),
            pltpu.SemaphoreType.DMA((H,)),
            pltpu.SemaphoreType.DMA((H,)),
            pltpu.SemaphoreType.DMA,
        ],
        compiler_params=kernel_params(4, 16),
        cost_estimate=pl.CostEstimate(flops=5 * 10**10, bytes_accessed=10**6, transcendentals=0),
        name="share_tokens",
    )(tokens, w_gate, w_up, gain)


def turn_rows(
    partial_ref,
    first_ref,
    relay_ref,
    second_ref,
    pass_ref,
    send_sem,
    recv_sem,
    done,
    share=None,
    fillers=(),
):
    me = lax.axis_index("head")
    side = square(me)
    far = side[2]
    size = first_ref.shape[0] // CHUNKS
    steps = CHUNKS + 3
    fillers = list(fillers)

    def copies(c):
        one, two = (side[0], side[1]) if c % 2 == 0 else (side[1], side[0])
        rows = pl.ds(c * size, size)
        sems = [(send_sem.at[c, kind], recv_sem.at[c, kind]) for kind in range(3)]
        return (
            head_copy(partial_ref.at[far, rows], relay_ref.at[rows], *sems[0], one),
            head_copy(partial_ref.at[one, rows], first_ref.at[rows], *sems[1], one),
            head_copy(pass_ref.at[rows], second_ref.at[rows], *sems[2], two),
            two,
            rows,
        )

    for c in range(CHUNKS):
        relay, first, *_ = copies(c)
        relay.start()
        first.start()
    for step in range(steps):
        for filler in fillers[step * len(fillers) // steps : (step + 1) * len(fillers) // steps]:
            filler()
        if step < CHUNKS:
            relay, _, second, two, rows = copies(step)
            relay.wait_recv()
            both = partial_ref[two, rows, :].astype(F32) + relay_ref[rows, :].astype(F32)
            pass_ref[rows, :] = both.astype(BF16)
            second.start()
        if 1 <= step <= CHUNKS:
            _, first, second, _, rows = copies(step - 1)
            first.wait_recv()
            second.wait_recv()
            total = partial_ref[me, rows, :].astype(F32) + first_ref[rows, :].astype(F32)
            made = done(rows, total + second_ref[rows, :].astype(F32))
            if share is not None:
                share.refs[0][rows, :] = made
                share.start(step - 1)
        if step >= 3 and share is not None:
            share.forward(step - 3)
    if share is not None:
        share.finish()
    for c in range(CHUNKS):
        for copy in copies(c)[:3]:
            copy.wait_send()


def turn_scratch(rows, width):
    return [pltpu.VMEM((rows, width), BF16) for _ in range(4)] + [
        pltpu.SemaphoreType.DMA((CHUNKS, 3)),
        pltpu.SemaphoreType.DMA((CHUNKS, 3)),
    ]


def hidden_kernel(partial_ref, tokens_ref, hidden_ref, out_ref, *scratch):
    greet_heads(square(lax.axis_index("head"))[:2])
    mine_ref, *sems = scratch[6:]

    def done(rows, total):
        hidden = tokens_ref[rows, :].astype(F32) + total
        hidden_ref[rows, :] = hidden
        return (hidden * rms_scale(hidden, EPS)).astype(BF16)

    turn_rows(partial_ref, *scratch[:6], done, Share(mine_ref, out_ref, *sems))


def share_hidden(partial, tokens):
    whole = pl.BlockSpec(memory_space=pltpu.VMEM)
    return pl.pallas_call(
        hidden_kernel,
        out_shape=[
            jax.ShapeDtypeStruct(tokens.shape, F32),
            jax.ShapeDtypeStruct((H,) + tokens.shape, BF16),
        ],
        in_specs=[whole] * 2,
        out_specs=[whole, pl.BlockSpec(memory_space=pl.ANY)],
        scratch_shapes=turn_scratch(*tokens.shape) + share_scratch(*tokens.shape),
        compiler_params=kernel_params(5, 24),
        cost_estimate=pl.CostEstimate(flops=8 * 10**10, bytes_accessed=10**7, transcendentals=0),
        name="share_hidden",
    )(partial, tokens)


class PairProduct:
    def __init__(self, left_ref, right_ref, out_ref, give_ref, take_ref, send_sem, recv_sem, own_sem):
        self.refs = left_ref, right_ref, out_ref, give_ref, take_ref
        self.sems = send_sem, recv_sem, own_sem
        self.core = lax.axis_index("core")
        self.groups, self.rows, self.width = out_ref.shape
        self.cut = self.width // 2 if self.width % (2 * LANES) == 0 else self.width

    def product(self, group, core, at):
        left, right, *_ = self.refs
        start = pl.multiple_of((group * CORES + core) * self.rows, LANES)
        return rows_product(left[:, pl.ds(start, self.rows)], right[:, pl.ds(at, self.cut)])

    def copy(self, group):
        give, take = self.refs[3:]
        return pltpu.make_async_remote_copy(
            src_ref=give.at[group],
            dst_ref=take.at[group],
            send_sem=self.sems[0].at[group],
            recv_sem=self.sems[1].at[group],
            device_id={"core": 1 - self.core},
            device_id_type=pl.DeviceIdType.MESH,
        )

    def store(self, group):
        return pltpu.make_async_copy(
            self.refs[3].at[group], self.refs[2].at[group], self.sems[2].at[group]
        )

    def give(self, group, at):
        product = self.product(group, 1 - self.core, at)
        self.refs[3][group, :, pl.ds(at, self.cut)] = product.astype(BF16)
        if at + self.cut == self.width:
            self.copy(group).start()

    def keep(self, group, at):
        give, take = self.refs[3:]
        if at == 0:
            self.copy(group).wait()
        both = self.product(group, self.core, at)
        both += take[group, :, pl.ds(at, self.cut)].astype(F32)
        give[group, :, pl.ds(at, self.cut)] = both.astype(BF16)
        if at + self.cut == self.width:
            self.store(group).start()

    def steps(self):
        places = [
            (group, at) for group in range(self.groups) for at in range(0, self.width, self.cut)
        ]
        return [functools.partial(self.give, *place) for place in places] + [
            functools.partial(self.keep, *place) for place in places
        ]

    def finish(self):
        for group in range(self.groups):
            self.store(group).wait()


def pair_shape(left, right, groups):
    return (groups, left.shape[1] // (CORES * groups), right.shape[1])


def pair_scratch(shape):
    return [
        pltpu.VMEM(shape, BF16),
        pltpu.VMEM(shape, BF16),
        pltpu.SemaphoreType.DMA((shape[0],)),
        pltpu.SemaphoreType.DMA((shape[0],)),
        pltpu.SemaphoreType.DMA((shape[0],)),
    ]


def greet_square_and_core():
    barrier = pltpu.get_barrier_semaphore()
    for side in square(lax.axis_index("head"))[:2]:
        pl.semaphore_signal(
            barrier, inc=1, device_id={"head": side}, device_id_type=pl.DeviceIdType.MESH
        )
    other = 1 - lax.axis_index("core")
    pl.semaphore_signal(
        barrier, inc=1, device_id={"core": other}, device_id_type=pl.DeviceIdType.MESH
    )
    pl.semaphore_wait(barrier, 3)


def pair_kernel(left_ref, right_ref, out_ref, *scratch):
    barrier = pltpu.get_barrier_semaphore()
    other = 1 - lax.axis_index("core")
    pl.semaphore_signal(
        barrier, inc=1, device_id={"core": other}, device_id_type=pl.DeviceIdType.MESH
    )
    pl.semaphore_wait(barrier, 1)
    pair = PairProduct(left_ref, right_ref, out_ref, *scratch)
    for step in pair.steps():
        step()
    pair.finish()


def pair_product(left, right, groups):
    shape = pair_shape(left, right, groups)
    whole = pl.BlockSpec(memory_space=pltpu.VMEM)
    return pl.pallas_call(
        pair_kernel,
        out_shape=jax.ShapeDtypeStruct(shape, BF16),
        in_specs=[whole] * 2,
        out_specs=pl.BlockSpec(memory_space=pl.ANY),
        scratch_shapes=pair_scratch(shape),
        compiler_params=kernel_params(7, 32),
        cost_estimate=pl.CostEstimate(flops=10**10, bytes_accessed=10**7, transcendentals=0),
        name="pair_product",
    )(left, right)


def branch_kernel(
    partial_ref,
    hidden_ref,
    upstream_ref,
    left_ref,
    right_ref,
    active_ref,
    down_ref,
    grad_ref,
    gain_grad_ref,
    down_out_ref,
    pair_ref,
    out_ref,
    *scratch,
):
    greet_square_and_core()
    mine_ref, *sems = scratch[6:10]
    gain_grad_ref[...] = jnp.zeros_like(gain_grad_ref)
    pair = PairProduct(left_ref, right_ref, pair_ref, *scratch[10:])

    def done(rows, total):
        hidden = hidden_ref[rows, :]
        scale = rms_scale(hidden, EPS)
        gain_grad_ref[...] += jnp.sum(total * hidden * scale, axis=0, keepdims=True)
        grad = upstream_ref[rows, :].astype(F32) + rms_back(total, hidden, scale)
        grad_ref[rows, :] = grad
        return grad.astype(BF16)

    def down(at):
        rows = pl.ds(at, LANES)
        down_out_ref[rows, :] = matmul(active_ref[rows, :], down_ref[...]).astype(BF16)

    share = Share(mine_ref, out_ref, *sems)
    fillers = pair.steps()
    fillers += [functools.partial(down, at) for at in range(0, active_ref.shape[0], LANES)]
    turn_rows(partial_ref, *scratch[:6], done, share, fillers)
    pair.finish()


def share_branch(partial, hidden, upstream, left, right, active, down, groups):
    whole = pl.BlockSpec(memory_space=pltpu.VMEM)
    shape = pair_shape(left, right, groups)
    return pl.pallas_call(
        branch_kernel,
        out_shape=[
            jax.ShapeDtypeStruct(hidden.shape, F32),
            jax.ShapeDtypeStruct((1, hidden.shape[1]), F32),
            jax.ShapeDtypeStruct((active.shape[0], down.shape[1]), BF16),
            jax.ShapeDtypeStruct(shape, BF16),
            jax.ShapeDtypeStruct((H,) + hidden.shape, BF16),
        ],
        in_specs=[whole] * 7,
        out_specs=[whole] * 3 + [pl.BlockSpec(memory_space=pl.ANY)] * 2,
        scratch_shapes=turn_scratch(*hidden.shape)
        + share_scratch(*hidden.shape)
        + pair_scratch(shape),
        compiler_params=kernel_params(6, 54),
        cost_estimate=pl.CostEstimate(flops=8 * 10**10, bytes_accessed=10**7, transcendentals=0),
        name="share_branch",
    )(partial, hidden, upstream, left, right, active, down)


def tokens_kernel(partial_ref, tokens_ref, upstream_ref, grad_ref, gain_grad_ref, *scratch):
    greet_heads(square(lax.axis_index("head"))[:2])
    gain_grad_ref[...] = jnp.zeros_like(gain_grad_ref)

    def done(rows, total):
        tokens = tokens_ref[rows, :].astype(F32)
        scale = rms_scale(tokens, EPS)
        gain_grad_ref[...] += jnp.sum(total * tokens * scale, axis=0, keepdims=True)
        grad = upstream_ref[rows, :] + rms_back(total, tokens, scale)
        grad_ref[rows, :] = grad.astype(BF16)

    turn_rows(partial_ref, *scratch, done)


def tokens_back(partial, tokens, upstream):
    whole = pl.BlockSpec(memory_space=pltpu.VMEM)
    return pl.pallas_call(
        tokens_kernel,
        out_shape=[
            jax.ShapeDtypeStruct(tokens.shape, BF16),
            jax.ShapeDtypeStruct((1, tokens.shape[1]), F32),
        ],
        in_specs=[whole] * 3,
        out_specs=[whole] * 2,
        scratch_shapes=turn_scratch(*tokens.shape),
        compiler_params=kernel_params(8, 24),
        cost_estimate=pl.CostEstimate(flops=4 * 10**10, bytes_accessed=10**7, transcendentals=0),
        name="tokens_back",
    )(partial, tokens, upstream)


def hidden_units_kernel(cot_ref, down_ref, pre_ref, out_ref):
    units = down_ref.shape[0]
    grad = back_product(cot_ref[...], down_ref[...])
    gate, up = pre_ref[:, pl.ds(0, units)], pre_ref[:, pl.ds(units, units)]
    sig = jax.nn.sigmoid(gate)
    grad_sig = grad * sig
    out_ref[:, pl.ds(0, units)] = (grad_sig * up * (1.0 + gate * (1.0 - sig))).astype(BF16)
    out_ref[:, pl.ds(units, units)] = (grad_sig * gate).astype(BF16)


def hidden_units_back(cot, down, pre):
    rows, width = cot.shape
    size = 2 * LANES

    def rows_block(n):
        return pl.BlockSpec((size, n), lambda i: (i, 0))

    return pl.pallas_call(
        hidden_units_kernel,
        grid=(rows // size,),
        out_shape=jax.ShapeDtypeStruct(pre.shape, BF16),
        in_specs=[
            rows_block(width),
            pl.BlockSpec(down.shape, lambda i: (0, 0)),
            rows_block(pre.shape[1]),
        ],
        out_specs=rows_block(pre.shape[1]),
        compiler_params=pltpu.CompilerParams(vmem_limit_bytes=40 * 2**20),
        cost_estimate=pl.CostEstimate(flops=10**10, bytes_accessed=10**7, transcendentals=0),
        name="hidden_units_back",
    )(cot, down, pre)


def columns_kernel(g_ref, out_ref, send_sem, recv_sem, own_sem):
    me = lax.axis_index("head")
    peers = [lax.rem(me + ahead, H) for ahead in range(1, H)]
    greet_heads(peers)
    copies = [
        head_copy(g_ref.at[peer], out_ref.at[me], send_sem.at[ahead], recv_sem.at[ahead], peer)
        for ahead, peer in enumerate(peers)
    ]
    copies.append(pltpu.make_async_copy(g_ref.at[me], out_ref.at[me], own_sem))
    for copy in copies:
        copy.start()
    for copy in copies:
        copy.wait()


def columns_back(g, number):
    return pl.pallas_call(
        columns_kernel,
        out_shape=jax.ShapeDtypeStruct(g.shape, BF16),
        in_specs=[pl.BlockSpec(memory_space=pl.ANY)],
        out_specs=pl.BlockSpec(memory_space=pl.ANY),
        scratch_shapes=[
            pltpu.SemaphoreType.DMA((H,)),
            pltpu.SemaphoreType.DMA((H,)),
            pltpu.SemaphoreType.DMA,
        ],
        compiler_params=kernel_params(number, 16),
        cost_estimate=pl.CostEstimate(flops=10**10, bytes_accessed=10**6, transcendentals=0),
        name="columns_back",
    )(g)


def mix_forward(mixed, bias, gaterank, gain, marks, segment, sums, pairs, key_dim, value_dim):
    rows = mixed.shape[0]
    count, _, length = segment.shape
    shapes = (
        ((rows, value_dim), BF16),
        ((rows, value_dim), F32),
        ((rows, key_dim), F32),
        ((count, length, length), BF16),
        ((rows, key_dim), BF16),
        ((rows, key_dim), BF16),
        ((count, 1, key_dim), F32),
        ((count, value_dim, key_dim), BF16),
    )
    whole = pl.BlockSpec(memory_space=pltpu.VMEM)
    return pl.pallas_call(
        functools.partial(forward_kernel, key_dim, value_dim),
        out_shape=[jax.ShapeDtypeStruct(*s) for s in shapes],
        in_specs=[whole] * 8,
        out_specs=[whole] + [pl.BlockSpec(memory_space=pl.ANY)] * (len(shapes) - 1),
        scratch_shapes=[pltpu.VMEM(*s) for s in shapes[1:-1]]
        + state_scratch(count, value_dim, key_dim)
        + [pltpu.SemaphoreType.DMA((count, 7))],
        compiler_params=kernel_params(1, 30),
        cost_estimate=pl.CostEstimate(flops=5 * 10**10, bytes_accessed=10**7, transcendentals=0),
        name="mix_forward",
    )(mixed, bias, gaterank, gain, marks, segment, sums, pairs)


def mix_backward(
    mixed, kept, upstream, gaterank, gain, marks, segment, sums, pairs, key_dim, value_dim
):
    rows = mixed.shape[0]
    count = segment.shape[0]
    shapes = (
        (mixed.shape, BF16),
        ((1, value_dim), F32),
        ((1, key_dim), F32),
        (gaterank.shape, F32),
    )
    attended, logits, scores, start, end, decay, enter = kept
    given = (mixed, upstream, attended, start, logits, scores, end, decay, enter)
    whole = pl.BlockSpec(memory_space=pltpu.VMEM)
    return pl.pallas_call(
        functools.partial(backward_kernel, key_dim, value_dim),
        out_shape=[jax.ShapeDtypeStruct(*s) for s in shapes],
        in_specs=[pl.BlockSpec(memory_space=pl.ANY)] * 9 + [whole] * 6,
        out_specs=[whole] * len(shapes),
        scratch_shapes=[pltpu.VMEM(a.shape, a.dtype) for a in given]
        + [pltpu.VMEM((rows, value_dim), BF16)]
        + state_scratch(count, value_dim, key_dim)
        + [pltpu.SemaphoreType.DMA((count, 9))],
        compiler_params=kernel_params(2, 36),
        cost_estimate=pl.CostEstimate(flops=8 * 10**10, bytes_accessed=10**7, transcendentals=0),
        name="mix_backward",
    )(
        *given,
        gaterank,
        gain,
        marks,
        segment,
        sums,
        pairs,
    )


def per_device(
    tokens,
    doc_lengths,
    norm_gain,
    w_query,
    w_key,
    w_value,
    w_outgate,
    w_lowrank,
    w_gaterank,
    gate_bias,
    head_gain,
    w_output,
    ffn_gain,
    w_gate,
    w_up,
    w_down,
    cotangent,
):
    seqs_here, length, width = tokens.shape
    reps = lax.axis_size("rep")
    parts = lax.axis_size("fsdp")
    devices = reps * H * CORES * parts
    here = lax.axis_index("head")
    key_dim, value_dim = DK, DV
    rank = w_lowrank.shape[1]
    rows = width // devices
    count = H * seqs_here

    rank_at = 2 * key_dim + 2 * value_dim

    def core_sum(g):
        halves = g.reshape(g.shape[0], CORES, -1, g.shape[-1])
        core = lax.axis_index("core")
        other = lax.ppermute(halves[:, 1 - core], "core", ((0, 1), (1, 0)))
        return (halves[:, core].astype(F32) + other.astype(F32)).astype(BF16)

    def scatter_rows(g):
        if reps > 1:
            g = lax.psum_scatter(g, "rep", scatter_dimension=0, tiled=True)
        return lax.psum_scatter(g, "fsdp", scatter_dimension=1, tiled=True)

    def gather_columns(moved):
        whole = lax.all_gather(moved, ("core", "fsdp"), axis=1, tiled=True)
        if reps > 1:
            whole = lax.all_gather(whole, "rep", axis=0, tiled=False)
        return whole.reshape(width, -1)

    def gather_part(w):
        if reps == 1:
            return lax.all_gather(w, SHARE, axis=0, tiled=True)
        whole = lax.all_gather(w, EVERY, axis=0, tiled=True)
        size = whole.shape[0] // H
        return lax.dynamic_slice_in_dim(whole, here * size, size, 0)

    def pair_part(g):
        return core_sum(g[None])[0] if reps == 1 else g

    def scatter_part(g):
        if reps == 1:
            return lax.psum_scatter(g, "fsdp", scatter_dimension=0, tiled=True)
        whole = jnp.zeros((H * g.shape[0], g.shape[1]), BF16)
        whole = lax.dynamic_update_slice_in_dim(whole, g, here * g.shape[0], 0)
        return lax.psum_scatter(whole, EVERY, scatter_dimension=0, tiled=True)

    rank_at = 2 * key_dim + 2 * value_dim

    def with_gain(w, gain):
        return (w.astype(F32) * gain.astype(F32)[:, None]).astype(BF16)

    small = (
        w_gaterank,
        gate_bias.reshape(1, -1),
        head_gain.reshape(1, -1),
        (doc_lengths // 16).astype(BF16).reshape(1, -1),
        (doc_lengths % 16).astype(BF16).reshape(1, -1),
    )
    edges = [rank]
    extra = jnp.pad(with_gain(w_lowrank, norm_gain), ((0, 0), (0, LANES - rank)))
    for piece in small:
        high, wide = piece.shape
        extra += jnp.pad(piece, ((0, rows - high), (edges[-1], LANES - edges[-1] - wide)))
        edges.append(edges[-1] + wide)

    mix_moved = mix_weights((w_query, w_key, w_value, w_outgate), extra, norm_gain[:, None])
    inputs = tokens.reshape(-1, width)
    inputs, _ = after(inputs, mix_moved)
    output_w = gather_part(w_output)
    mix_moved, output_w = after(mix_moved, output_w)
    mix_w = gather_columns(mix_moved)
    w_down, _ = after(w_down, mix_moved)
    down_w = gather_part(w_down)
    normed, ffn_moved = share_tokens(inputs, w_gate, w_up, ffn_gain[:, None])
    normed = normed.reshape(-1, width)

    small = mix_w[:, rank_at:].astype(F32).reshape(devices, rows, LANES)
    gaterank, bias, gain_head, long, short = (
        small[:, : rank if i == 0 else 1, edges[i] : edges[i + 1]] for i in range(len(edges) - 1)
    )
    gaterank = gaterank.transpose(1, 0, 2).reshape(rank, -1)
    bias = lax.dynamic_slice_in_dim(bias.reshape(1, -1), here * key_dim, key_dim, 1)
    gaterank = lax.dynamic_slice_in_dim(gaterank, here * key_dim, key_dim, 1)
    gain_head = gain_head.reshape(1, -1)
    lengths = (long * 16.0 + short).reshape(reps, H, CORES, parts, seqs_here, DOCS)
    lengths = lengths[lax.axis_index("rep"), :, lax.axis_index("core"), 0]
    lengths = lengths.reshape(count, DOCS).astype(jnp.int32)

    offset = lax.axis_index("fsdp") * length
    doc_ends = jnp.cumsum(lengths, axis=-1)
    places = offset + jnp.arange(length, dtype=jnp.int32)
    segment = jnp.sum((places[None, :, None] >= doc_ends[:, None, :]).astype(jnp.int32), axis=-1)
    before = jnp.sum((offset - 1 >= doc_ends).astype(jnp.int32), axis=-1)[:, None]
    last = segment[:, -1:]
    marks = jnp.stack(
        [
            segment,
            segment == before,
            segment == last,
            segment != DOCS - 1,
            jnp.broadcast_to(last == before, segment.shape),
        ],
        axis=2,
    )
    marks = jnp.pad(marks.astype(F32).reshape(count * length, 5), ((0, 0), (0, 3)))
    segment = segment.astype(F32).reshape(count, 1, length)

    mixed = matmul(normed, mix_w)
    sums, pairs = level_sums(length)
    sums, pairs = sums.astype(BF16), pairs.astype(BF16)
    gated, *kept = mix_forward(
        mixed, bias, gaterank, gain_head, marks, segment, sums, pairs, key_dim, value_dim
    )
    cot_rows, _ = after(cotangent.reshape(-1, width), normed)
    gated, cot_shared, down_w = after(gated, share_rows(cot_rows), down_w)
    ffn_moved, _ = after(ffn_moved, gated)
    ffn_w = gather_columns(ffn_moved)
    partial = matmul(gated, output_w).astype(BF16).reshape(H, -1, width)
    hidden, normed_two = share_hidden(partial, inputs)
    normed_two = normed_two.reshape(-1, width)

    pre = matmul(normed_two, ffn_w)
    gate_pre, up_pre = jnp.split(pre, 2, axis=1)
    sig_gate = jax.nn.sigmoid(gate_pre)
    activated = (gate_pre * sig_gate * up_pre).astype(BF16)

    grad_down_w = rows_product(activated, cot_shared).astype(BF16)
    down_w, grad_down_w = after(down_w, grad_down_w)
    grad_pre = hidden_units_back(cot_shared, down_w, pre)
    grad_pre, grad_down_w = after(grad_pre, pair_part(grad_down_w))
    grad_down_w = scatter_part(grad_down_w)
    partial = back_product(grad_pre, ffn_w).astype(BF16)

    grad_hidden, grad_gain_two, down_partial, grad_ffn_w, branch = share_branch(
        partial.reshape(H, -1, width),
        hidden,
        cot_rows,
        normed_two,
        grad_pre,
        activated,
        down_w,
        reps * H,
    )
    grad_ffn_w = scatter_rows(grad_ffn_w)
    branch = branch.reshape(-1, width)
    grad_gated = back_product(branch, output_w)
    gated, grad_gated = after(gated, grad_gated)
    grad_output_w = pair_part(rows_product(gated, branch).astype(BF16))
    grad_gated, grad_output_w, grad_down_w = after(grad_gated, grad_output_w, grad_down_w)
    grad_output_w = scatter_part(grad_output_w)
    pieces = move_rows(down_partial)
    grad_mixed, grad_gain_head, grad_bias, grad_gaterank = mix_backward(
        mixed,
        kept,
        grad_gated,
        gaterank,
        gain_head,
        marks,
        segment,
        sums,
        pairs,
        key_dim,
        value_dim,
    )
    grad_mixed, pieces, grad_down_w = after(grad_mixed, pieces, grad_down_w)
    output = (hidden + jnp.sum(pieces.astype(F32), axis=0)).astype(BF16).reshape(tokens.shape)
    grad_mix_w = pair_product(normed, grad_mixed, reps * H)
    grad_mixed, grad_mix_w = after(grad_mixed, grad_mix_w)
    partial = back_product(grad_mixed, mix_w).astype(BF16)
    grad_mix_w = scatter_rows(grad_mix_w)
    grad_ffn_w = columns_back(grad_ffn_w, 9)
    partial, grad_ffn_w, grad_output_w = after(partial, grad_ffn_w, grad_output_w)
    tokens_grad, grad_gain_one = tokens_back(partial.reshape(H, -1, width), inputs, grad_hidden)
    tokens_grad = tokens_grad.reshape(tokens.shape)

    def weight_grad(moved, gain, start, w):
        n = w.shape[1] // H
        whole = moved[:, :, start : start + n].transpose(1, 0, 2).reshape(rows, -1)
        return whole.astype(F32) * gain.astype(F32)[:, None]

    w_gate_grad = weight_grad(grad_ffn_w, ffn_gain, 0, w_gate)
    w_up_grad = weight_grad(grad_ffn_w, ffn_gain, w_gate.shape[1] // H, w_up)
    grad_mix_w = columns_back(grad_mix_w, 10)
    query_g = weight_grad(grad_mix_w, norm_gain, 0, w_query)
    key_g = weight_grad(grad_mix_w, norm_gain, key_dim, w_key)
    value_g = weight_grad(grad_mix_w, norm_gain, 2 * key_dim, w_value)
    outgate_g = weight_grad(grad_mix_w, norm_gain, 2 * key_dim + value_dim, w_outgate)
    lowrank_g = grad_mix_w[:, :, rank_at : rank_at + rank].astype(F32)
    lowrank_g = jnp.sum(lowrank_g, axis=0) * norm_gain.astype(F32)[:, None]

    def place(g, axis):
        shape = list(g.shape)
        shape[axis] *= H
        return lax.dynamic_update_slice_in_dim(jnp.zeros(shape, F32), g, here * key_dim, axis)

    small_grads = jnp.concatenate(
        [
            grad_gain_one.reshape(devices, -1),
            grad_gain_two.reshape(devices, -1),
            place(grad_bias.reshape(-1), 0).reshape(devices, -1),
            grad_gain_head.reshape(devices, -1),
            place(grad_gaterank, 1)
            .reshape(rank, devices, -1)
            .transpose(1, 0, 2)
            .reshape(devices, -1),
        ],
        axis=1,
    )
    small_grads = lax.all_to_all(small_grads, EVERY, split_axis=0, concat_axis=0, tiled=True)
    small_grads = jnp.sum(small_grads, axis=0)
    sizes = [norm_gain.shape[0], ffn_gain.shape[0], gate_bias.shape[0], head_gain.shape[0]]
    norm_g, ffn_g, bias_g, head_g, gaterank_g = jnp.split(
        small_grads, [sum(sizes[: i + 1]) for i in range(len(sizes))]
    )
    return (
        output,
        tokens_grad,
        norm_g / norm_gain.astype(F32),
        query_g,
        key_g,
        value_g,
        outgate_g,
        lowrank_g,
        gaterank_g.reshape(w_gaterank.shape),
        bias_g,
        head_g,
        grad_output_w.astype(F32),
        ffn_g / ffn_gain.astype(F32),
        w_gate_grad,
        w_up_grad,
        grad_down_w.astype(F32),
    )


def solution(mesh):
    dp, parts = mesh.shape["dp"], mesh.shape["fsdp"]
    fine = Mesh(mesh.devices.reshape(dp // (H * CORES), H, CORES, parts), EVERY)
    seq = ("rep", "head", "core")
    rows, vector = P(EVERY, None), P(EVERY)
    activations = P(seq, "fsdp", None)
    columns = P(None, EVERY)
    return jax.shard_map(
        per_device,
        mesh=fine,
        in_specs=(
            activations,
            P(seq, None),
            vector,
            rows,
            rows,
            rows,
            rows,
            rows,
            columns,
            vector,
            vector,
            rows,
            vector,
            rows,
            rows,
            rows,
            activations,
        ),
        out_specs=(
            activations,
            activations,
            vector,
            rows,
            rows,
            rows,
            rows,
            rows,
            columns,
            vector,
            vector,
            rows,
            vector,
            rows,
            rows,
            rows,
        ),
        check_vma=False,
    )
```

```python
import functools

import jax
import jax.experimental.pallas as pl
import jax.experimental.pallas.tpu as pltpu
import jax.numpy as jnp
from jax import lax
from jax.sharding import Mesh
from jax.sharding import PartitionSpec as P

H = 4
DK = 256
DV = 512
CORES = 2
DOCS = 8
PIECES = 2
LANES = 128
CHUNKS = 8

EPS = 1e-05
HEAD_EPS = 1.0
HIGHEST = lax.Precision.HIGHEST
F32 = jnp.float32
BF16 = jnp.bfloat16

SHARE = ("rep", "core", "fsdp")
EVERY = ("rep", "head", "core", "fsdp")


def dot(a, b, dims, precision=None):
    return lax.dot_general(a, b, (dims, ((), ())), precision=precision, preferred_element_type=F32)


def after(value, *others):
    return lax.optimization_barrier((value,) + others)


def matmul(a, b):
    return dot(a, b, ((1,), (0,)))


def rows_product(a, b):
    return dot(a, b, ((0,), (0,)))


def back_product(a, b):
    return dot(a, b, ((1,), (1,)))


def batched(form, a, b):
    return jnp.einsum(form, a, b, preferred_element_type=F32)


def rms_scale(values, epsilon):
    return lax.rsqrt(jnp.mean(values * values, axis=-1, keepdims=True) + epsilon)


def rms_back(upstream, values, scale):
    return scale * upstream - values * scale**3 * jnp.mean(upstream * values, axis=-1, keepdims=True)


def share_rows(part):
    spread = jnp.broadcast_to(part[None], (H,) + part.shape)
    whole = lax.all_to_all(spread, "head", split_axis=0, concat_axis=0, tiled=True)
    return whole.reshape(-1, part.shape[-1])


def move_rows(partial):
    pieces = partial.astype(BF16).reshape(H, -1, partial.shape[-1])
    return lax.all_to_all(pieces, "head", split_axis=0, concat_axis=0, tiled=True)


def sum_rows(partial):
    return jnp.sum(move_rows(partial).astype(F32), axis=0)


def level_sums(length):
    rows = jnp.arange(length)[:, None]
    cols = jnp.arange(length)[None, :]
    sums, pairs = [], []
    step = 1
    while step < length:
        bound = rows // (2 * step) * (2 * step) + step - 1
        upper = rows > bound
        sums.append(jnp.where(upper, (cols > bound) & (cols <= rows), (cols > rows) & (cols <= bound)))
        pairs.append(upper & (cols // (2 * step) == rows // (2 * step)) & (cols <= bound))
        step *= 2
    sums.append(cols <= rows)
    sums.append(cols > rows)
    return jnp.stack(sums), jnp.stack(pairs)


def log_sigmoid(x):
    return jnp.minimum(x, 0.0) - jnp.log1p(jnp.exp(-jnp.abs(x)))


def state_copy(send, recv, send_sem, recv_sem, seq, piece, target):
    size = send.shape[1] // PIECES
    part = pl.ds(piece * size, size)
    return pltpu.make_async_remote_copy(
        src_ref=send.at[seq, part],
        dst_ref=recv.at[seq, part],
        send_sem=send_sem.at[seq, piece],
        recv_sem=recv_sem.at[seq, piece],
        device_id={"fsdp": target},
        device_id_type=pl.DeviceIdType.MESH,
    )


def greet_neighbours(place, parts):
    barrier = pltpu.get_barrier_semaphore()
    for near, there in ((place - 1, place > 0), (place + 1, place < parts - 1)):

        @pl.when(there)
        def _(near=near):
            pl.semaphore_signal(
                barrier,
                inc=1,
                device_id={"fsdp": lax.rem(near + parts, parts)},
                device_id_type=pl.DeviceIdType.MESH,
            )

    peers = (place > 0).astype(jnp.int32) + (place < parts - 1).astype(jnp.int32)
    pl.semaphore_wait(barrier, peers)


def pass_state(s, first, last, target, decay, local, send, recv, send_sem, recv_sem):
    size = send.shape[1] // PIECES
    for piece in range(PIECES):
        part = pl.ds(piece * size, size)
        copy = state_copy(send, recv, send_sem, recv_sem, s, piece, target)

        @pl.when(jnp.logical_not(first))
        def _(copy=copy):
            copy.wait_recv()

        @pl.when(jnp.logical_not(jnp.logical_or(first, last)))
        def _(copy=copy, part=part):
            joined = decay * recv[s, part].astype(F32) + local[s, part]
            send[s, part] = joined.astype(BF16)
            copy.start()


def start_state(s, first, last, target, local, send, recv, send_sem, recv_sem):
    @pl.when(jnp.logical_and(first, jnp.logical_not(last)))
    def _():
        send[s] = local[s].astype(BF16)
        for piece in range(PIECES):
            state_copy(send, recv, send_sem, recv_sem, s, piece, target).start()


def finish_states(count, last, target, send, recv, send_sem, recv_sem):
    @pl.when(jnp.logical_not(last))
    def _():
        def one(s, carry):
            for piece in range(PIECES):
                state_copy(send, recv, send_sem, recv_sem, s, piece, target).wait_send()
            return carry

        lax.fori_loop(0, count, one, 0)


def split_rates(logits):
    rates = log_sigmoid(logits) / 16.0
    high = rates.astype(BF16)
    return high, (rates - high.astype(F32)).astype(BF16)


def decayed(sums, high, low):
    return jnp.exp(matmul(sums, high) + matmul(sums, low))


def forward_kernel(
    key_dim,
    value_dim,
    mixed_ref,
    bias_ref,
    gaterank_ref,
    gain_ref,
    marks_ref,
    segment_ref,
    sums_ref,
    pairs_ref,
    gated_ref,
    *refs,
):
    kept, (attended_ref, logits_ref, scores_ref, start_ref, end_ref, decay_ref) = refs[:7], refs[7:13]
    local_ref, send_ref, recv_ref, send_sem, recv_sem, keep_sem = refs[13:]
    count, _, length = segment_ref.shape
    levels = pairs_ref.shape[0]
    parts, place = lax.axis_size("fsdp"), lax.axis_index("fsdp")
    first, last, target = place == 0, place == parts - 1, lax.rem(place + 1, parts)

    def rows_of(s):
        return pl.ds(pl.multiple_of(s * length, length), length)

    def keeps(s, kinds):
        held = (attended_ref, logits_ref, scores_ref, start_ref, end_ref, decay_ref, recv_ref)
        rows = rows_of(s)
        for kind in kinds:
            at = rows if len(held[kind].shape) == 2 else s
            yield pltpu.make_async_copy(held[kind].at[at], kept[kind].at[at], keep_sem.at[s, kind])

    def finish_keeps(s, carry):
        for copy in keeps(s, range(7)):
            copy.wait()
        return carry

    rank = gaterank_ref.shape[0]
    scale = key_dim ** (-0.5)
    value_at = 2 * key_dim
    gate_at = value_at + value_dim
    rank_at = gate_at + value_dim

    greet_neighbours(place, parts)

    @pl.when(first)
    def _():
        recv_ref[...] = jnp.zeros_like(recv_ref)

    def ends(s, carry):
        rows = rows_of(s)
        lowrank = mixed_ref[rows, pl.ds(rank_at, rank)]
        logits = dot(lowrank, gaterank_ref[...], ((1,), (0,)), HIGHEST) + bias_ref[...]
        logits_ref[rows, :] = logits
        high, low = split_rates(logits)
        from_start = decayed(sums_ref[levels], high, low)
        to_end = decayed(sums_ref[levels + 1], high, low)
        marks = marks_ref[rows, :]
        decay_ref[s] = from_start[length - 1 :, :] * marks[:1, 4:5]
        query = mixed_ref[rows, pl.ds(0, key_dim)] * scale
        key = mixed_ref[rows, pl.ds(key_dim, key_dim)]
        start_ref[rows, :] = (query * (from_start * marks[:, 1:2])).astype(BF16)
        end_key = (key * (to_end * marks[:, 2:3])).astype(BF16)
        end_ref[rows, :] = end_key
        value = mixed_ref[rows, pl.ds(value_at, value_dim)].astype(BF16)
        local_ref[s] = rows_product(value, end_key)
        start_state(s, first, last, target, local_ref, send_ref, recv_ref, send_sem, recv_sem)
        for copy in keeps(s, (1, 3, 4, 5)):
            copy.start()
        return carry

    lax.fori_loop(0, count, ends, 0)

    def mix(s, carry):
        rows = rows_of(s)
        pass_state(
            s, first, last, target, decay_ref[s], local_ref, send_ref, recv_ref, send_sem, recv_sem
        )
        query = mixed_ref[rows, pl.ds(0, key_dim)] * scale
        key = mixed_ref[rows, pl.ds(key_dim, key_dim)]
        high, low = split_rates(logits_ref[rows, :])
        scores = jnp.zeros((length, length), F32)
        for level in range(levels):
            decay = decayed(sums_ref[level], high, low)
            pair = back_product((query * decay).astype(BF16), (key * decay).astype(BF16))
            scores += pair * pairs_ref[level].astype(F32)
        row = lax.broadcasted_iota(jnp.int32, (length, length), 0)
        col = lax.broadcasted_iota(jnp.int32, (length, length), 1)
        own = jnp.sum(query * key, axis=1, keepdims=True)
        scores += jnp.where(row == col, own, 0.0)
        marks = marks_ref[rows, :]
        scores = jnp.where(marks[:, 0:1] == segment_ref[s], scores, 0.0).astype(BF16)
        scores_ref[s] = scores
        value = mixed_ref[rows, pl.ds(value_at, value_dim)].astype(BF16)
        attended = matmul(scores, value) + back_product(start_ref[rows, :], recv_ref[s])
        attended = attended * marks[:, 3:4]
        attended_ref[rows, :] = attended
        headed = attended * rms_scale(attended, HEAD_EPS) * gain_ref[...]
        outgate = mixed_ref[rows, pl.ds(gate_at, value_dim)]
        gated_ref[rows, :] = (headed * (outgate * jax.nn.sigmoid(outgate))).astype(BF16)
        for copy in keeps(s, (0, 2, 6)):
            copy.start()
        return carry

    lax.fori_loop(0, count, mix, 0)
    finish_states(count, last, target, send_ref, recv_ref, send_sem, recv_sem)
    lax.fori_loop(0, count, finish_keeps, 0)


def backward_kernel(
    key_dim,
    value_dim,
    *refs,
):
    given, refs = refs[:9], refs[9:]
    gaterank_ref, gain_ref, marks_ref, segment_ref, sums_ref, pairs_ref, *refs = refs
    grad_ref, gain_grad_ref, bias_grad_ref, gaterank_grad_ref, *refs = refs
    held, refs = refs[:9], refs[9:]
    mixed_ref, upstream_ref, attended_ref, start_ref, *rest_refs = held
    logits_ref, scores_ref, end_ref, decay_ref, enter_ref = rest_refs
    out_ref, local_ref, send_ref, recv_ref, send_sem, recv_sem, take_sem = refs
    count, _, length = segment_ref.shape

    def rows_of(s):
        return pl.ds(pl.multiple_of(s * length, length), length)

    def takes(s, kinds):
        rows = rows_of(s)
        for kind in kinds:
            at = rows if len(held[kind].shape) == 2 else s
            yield pltpu.make_async_copy(given[kind].at[at], held[kind].at[at], take_sem.at[s, kind])

    def start_takes(s, carry):
        for copy in takes(s, range(9)):
            copy.start()
        return carry

    lax.fori_loop(0, count, start_takes, 0)
    levels = pairs_ref.shape[0]
    parts, place = lax.axis_size("fsdp"), lax.axis_index("fsdp")
    first, last, target = place == parts - 1, place == 0, lax.rem(place + parts - 1, parts)
    rank = gaterank_ref.shape[0]
    scale = key_dim ** (-0.5)
    value_at = 2 * key_dim
    gate_at = value_at + value_dim
    rank_at = gate_at + value_dim

    greet_neighbours(place, parts)

    @pl.when(first)
    def _():
        recv_ref[...] = jnp.zeros_like(recv_ref)

    gain_grad_ref[...] = jnp.zeros_like(gain_grad_ref)
    bias_grad_ref[...] = jnp.zeros_like(bias_grad_ref)
    gaterank_grad_ref[...] = jnp.zeros_like(gaterank_grad_ref)

    def heads(s, carry):
        rows = rows_of(s)
        for copy in takes(s, range(4)):
            copy.wait()
        upstream = upstream_ref[rows, :]
        attended = attended_ref[rows, :]
        outgate = mixed_ref[rows, pl.ds(gate_at, value_dim)]
        gain = gain_ref[...]
        norm = rms_scale(attended, HEAD_EPS)
        normed = attended * norm
        sig = jax.nn.sigmoid(outgate)
        grad_gate = upstream * (normed * gain) * sig * (1.0 + outgate * (1.0 - sig))
        grad_ref[rows, pl.ds(gate_at, value_dim)] = grad_gate.astype(BF16)
        grad_headed = upstream * (outgate * sig)
        gain_grad_ref[...] += jnp.sum(grad_headed * normed, axis=0, keepdims=True)
        grad_out = rms_back(grad_headed * gain, attended, norm) * marks_ref[rows, pl.ds(3, 1)]
        grad_out = grad_out.astype(BF16)
        out_ref[rows, :] = grad_out
        local_ref[s] = rows_product(grad_out, start_ref[rows, :])
        start_state(s, first, last, target, local_ref, send_ref, recv_ref, send_sem, recv_sem)
        return carry

    lax.fori_loop(0, count, heads, 0)

    def mix(s, carry):
        rows = rows_of(s)
        for copy in takes(s, range(4, 9)):
            copy.wait()
        decay_row = decay_ref[s]
        pass_state(
            s, first, last, target, decay_row, local_ref, send_ref, recv_ref, send_sem, recv_sem
        )
        query = mixed_ref[rows, pl.ds(0, key_dim)] * scale
        key = mixed_ref[rows, pl.ds(key_dim, key_dim)]
        value = mixed_ref[rows, pl.ds(value_at, value_dim)].astype(BF16)
        marks = marks_ref[rows, :]
        logits = logits_ref[rows, :]
        high, low = split_rates(logits)
        grad_out = out_ref[rows, :]
        row = lax.broadcasted_iota(jnp.int32, (length, length), 0)
        col = lax.broadcasted_iota(jnp.int32, (length, length), 1)
        pair_grads = back_product(grad_out, value)
        pair_grads = jnp.where(marks[:, 0:1] == segment_ref[s], pair_grads, 0.0)
        own = jnp.sum(jnp.where(row == col, pair_grads, 0.0), axis=1, keepdims=True)
        grad_query = own * key
        grad_key = own * query
        grad_rates = jnp.zeros((length, key_dim), F32)
        for level in range(levels):
            decay = decayed(sums_ref[level], high, low)
            level_query = (query * decay).astype(BF16)
            level_key = (key * decay).astype(BF16)
            level_pairs = (pair_grads * pairs_ref[level].astype(F32)).astype(BF16)
            level_grad_query = matmul(level_pairs, level_key)
            level_grad_key = rows_product(level_pairs, level_query)
            grad_query += level_grad_query * decay
            grad_key += level_grad_key * decay
            flow = level_grad_query * level_query.astype(F32)
            flow += level_grad_key * level_key.astype(F32)
            grad_rates += rows_product(sums_ref[level], flow.astype(BF16))
        ending = recv_ref[s]
        entering = enter_ref[s]
        start_query = start_ref[rows, :]
        end_key = end_ref[rows, :]
        start_grad = matmul(grad_out, entering)
        end_grad = matmul(value, ending)
        grad_query += start_grad * (decayed(sums_ref[levels], high, low) * marks[:, 1:2])
        grad_key += end_grad * (decayed(sums_ref[levels + 1], high, low) * marks[:, 2:3])
        grad_rates += rows_product(
            sums_ref[levels], (start_grad * start_query.astype(F32)).astype(BF16)
        )
        grad_rates += rows_product(
            sums_ref[levels + 1], (end_grad * end_key.astype(F32)).astype(BF16)
        )
        grad_rates += decay_row * jnp.sum(
            ending.astype(F32) * entering.astype(F32), axis=0, keepdims=True
        )
        grad_value = rows_product(scores_ref[s], grad_out) + back_product(end_key, ending)
        grad_ref[rows, pl.ds(0, key_dim)] = (grad_query * scale).astype(BF16)
        grad_ref[rows, pl.ds(key_dim, key_dim)] = grad_key.astype(BF16)
        grad_ref[rows, pl.ds(value_at, value_dim)] = grad_value.astype(BF16)
        grad_logits = grad_rates / 16.0 * jax.nn.sigmoid(-logits)
        bias_grad_ref[...] += jnp.sum(grad_logits, axis=0, keepdims=True)
        lowrank = mixed_ref[rows, pl.ds(rank_at, rank)]
        gaterank_grad_ref[...] += dot(lowrank, grad_logits, ((0,), (0,)), HIGHEST)
        grad_lowrank = dot(grad_logits, gaterank_ref[...], ((1,), (1,)), HIGHEST)
        rest = grad_ref.shape[1] - rank_at - rank
        grad_ref[rows, pl.ds(rank_at, rank + rest)] = jnp.concatenate(
            [grad_lowrank, jnp.zeros((length, rest), F32)], axis=1
        ).astype(BF16)
        return carry

    lax.fori_loop(0, count, mix, 0)
    finish_states(count, last, target, send_ref, recv_ref, send_sem, recv_sem)


def state_scratch(count, value_dim, key_dim):
    return [
        pltpu.VMEM((count, value_dim, key_dim), F32),
        pltpu.VMEM((count, value_dim, key_dim), BF16),
        pltpu.VMEM((count, value_dim, key_dim), BF16),
        pltpu.SemaphoreType.DMA((count, PIECES)),
        pltpu.SemaphoreType.DMA((count, PIECES)),
    ]


def kernel_params(number, mebibytes=44):
    return pltpu.CompilerParams(
        collective_id=number, has_side_effects=True, vmem_limit_bytes=mebibytes * 2**20
    )


def head_copy(src, dst, send_sem, recv_sem, target):
    return pltpu.make_async_remote_copy(
        src_ref=src,
        dst_ref=dst,
        send_sem=send_sem,
        recv_sem=recv_sem,
        device_id={"head": target},
        device_id_type=pl.DeviceIdType.MESH,
    )


def greet_heads(targets):
    barrier = pltpu.get_barrier_semaphore()
    for target in targets:
        pl.semaphore_signal(
            barrier, inc=1, device_id={"head": target}, device_id_type=pl.DeviceIdType.MESH
        )
    pl.semaphore_wait(barrier, len(targets))


def square(me):
    return me + 1 - 2 * lax.rem(me, 2), me + 2 - 4 * (me // 2), H - 1 - me


def move_columns(weights, gain, out_ref, send_ref, send_sem, recv_sem, own_sem):
    me = lax.axis_index("head")
    place = 0
    for w in weights:
        n = w.shape[1] // H
        for h in range(H):
            part = w[:, pl.ds(h * n, n)].astype(F32) * gain
            send_ref[h, :, pl.ds(place, n)] = part.astype(BF16)
        place += n
    copies = []
    for ahead in range(1, H):
        peer = lax.rem(me + ahead, H)
        copy = head_copy(
            send_ref.at[peer],
            out_ref.at[me],
            send_sem.at[ahead],
            recv_sem.at[ahead],
            peer,
        )
        copy.start()
        copies.append(copy)
    own = pltpu.make_async_copy(send_ref.at[me], out_ref.at[me], own_sem)
    own.start()
    return copies + [own]


def mix_weights_kernel(*refs):
    *weights, extra_ref, gain_ref, out_ref, send_ref, send_sem, recv_sem, own_sem = refs
    me = lax.axis_index("head")
    greet_heads([lax.rem(me + ahead, H) for ahead in range(1, H)])
    spare = extra_ref.shape[1]
    for h in range(H):
        send_ref[h, :, pl.ds(send_ref.shape[2] - spare, spare)] = extra_ref[...]
    gain = gain_ref[...].astype(F32)
    for copy in move_columns(weights, gain, out_ref, send_ref, send_sem, recv_sem, own_sem):
        copy.wait()


def mix_weights(weights, extra, gain):
    rows = extra.shape[0]
    n = sum(w.shape[1] for w in weights) // H + extra.shape[1]
    return pl.pallas_call(
        mix_weights_kernel,
        out_shape=jax.ShapeDtypeStruct((H, rows, n), BF16),
        in_specs=[pl.BlockSpec(memory_space=pltpu.VMEM)] * (len(weights) + 2),
        out_specs=pl.BlockSpec(memory_space=pltpu.HBM),
        scratch_shapes=[
            pltpu.VMEM((H, rows, n), BF16),
            pltpu.SemaphoreType.DMA((H,)),
            pltpu.SemaphoreType.DMA((H,)),
            pltpu.SemaphoreType.DMA,
        ],
        compiler_params=kernel_params(3, 16),
        cost_estimate=pl.CostEstimate(flops=10**6, bytes_accessed=10**4, transcendentals=0),
        name="mix_weights",
    )(*weights, extra, gain)


class Share:
    def __init__(self, mine_ref, out_ref, send_sem, recv_sem, own_sem):
        self.refs = mine_ref, out_ref, send_sem, recv_sem, own_sem
        self.me = lax.axis_index("head")
        self.size = mine_ref.shape[0] // CHUNKS

    def copy(self, c, kind):
        mine, out, send_sem, recv_sem, _ = self.refs
        sides = square(self.me)[:2]
        rows = pl.ds(c * self.size, self.size)
        if kind < 2:
            src, dst, target = mine.at[rows], out.at[self.me, rows], sides[kind]
        else:
            origin, target = (sides[0], sides[1]) if c % 2 == 0 else (sides[1], sides[0])
            src = dst = out.at[origin, rows]
        return head_copy(src, dst, send_sem.at[c, kind], recv_sem.at[c, kind], target)

    def own(self, c):
        mine, out, _, _, own_sem = self.refs
        rows = pl.ds(c * self.size, self.size)
        return pltpu.make_async_copy(mine.at[rows], out.at[self.me, rows], own_sem.at[c])

    def start(self, c):
        self.copy(c, 0).start()
        self.copy(c, 1).start()
        self.own(c).start()

    def forward(self, c):
        self.copy(c, c % 2).wait_recv()
        self.copy(c, 2).start()

    def finish(self):
        for c in range(CHUNKS):
            self.copy(c, 1 - c % 2).wait_recv()
            self.copy(c, 2).wait_recv()
            self.own(c).wait()
            for kind in range(3):
                self.copy(c, kind).wait_send()


def share_scratch(rows, width):
    return [
        pltpu.VMEM((rows, width), BF16),
        pltpu.SemaphoreType.DMA((CHUNKS, 3)),
        pltpu.SemaphoreType.DMA((CHUNKS, 3)),
        pltpu.SemaphoreType.DMA((CHUNKS,)),
    ]


def share_kernel(
    tokens_ref,
    gate_ref,
    up_ref,
    gain_ref,
    out_ref,
    moved_ref,
    mine_ref,
    share_send,
    share_recv,
    share_own,
    send_ref,
    send_sem,
    recv_sem,
    own_sem,
):
    me = lax.axis_index("head")
    greet_heads([lax.rem(me + ahead, H) for ahead in range(1, H)])
    share = Share(mine_ref, out_ref, share_send, share_recv, share_own)
    for c in range(CHUNKS):
        rows = pl.ds(c * share.size, share.size)
        x = tokens_ref[rows, :].astype(F32)
        mine_ref[rows, :] = (x * rms_scale(x, EPS)).astype(BF16)
        share.start(c)
    gain = gain_ref[...].astype(F32)
    copies = move_columns(
        [gate_ref, up_ref], gain, moved_ref, send_ref, send_sem, recv_sem, own_sem
    )
    for c in range(CHUNKS):
        share.forward(c)
    share.finish()
    for copy in copies:
        copy.wait()


def share_tokens(tokens, w_gate, w_up, gain):
    rows, n = w_gate.shape[0], 2 * w_gate.shape[1] // H
    return pl.pallas_call(
        share_kernel,
        out_shape=[
            jax.ShapeDtypeStruct((H,) + tokens.shape, BF16),
            jax.ShapeDtypeStruct((H, rows, n), BF16),
        ],
        in_specs=[pl.BlockSpec(memory_space=pltpu.VMEM)] * 4,
        out_specs=[pl.BlockSpec(memory_space=pltpu.HBM)] * 2,
        scratch_shapes=share_scratch(*tokens.shape)
        + [
            pltpu.VMEM((H, rows, n), BF16),
            pltpu.SemaphoreType.DMA((H,)),
            pltpu.SemaphoreType.DMA((H,)),
            pltpu.SemaphoreType.DMA,
        ],
        compiler_params=kernel_params(4, 16),
        cost_estimate=pl.CostEstimate(flops=10**6, bytes_accessed=10**4, transcendentals=0),
        name="share_tokens",
    )(tokens, w_gate, w_up, gain)


def turn_rows(
    partial_ref,
    first_ref,
    relay_ref,
    second_ref,
    pass_ref,
    send_sem,
    recv_sem,
    done,
    share=None,
    fillers=(),
):
    me = lax.axis_index("head")
    side = square(me)
    far = side[2]
    size = first_ref.shape[0] // CHUNKS
    steps = CHUNKS + 3
    fillers = list(fillers)

    def copies(c):
        one, two = (side[0], side[1]) if c % 2 == 0 else (side[1], side[0])
        rows = pl.ds(c * size, size)
        sems = [(send_sem.at[c, kind], recv_sem.at[c, kind]) for kind in range(3)]
        return (
            head_copy(partial_ref.at[far, rows], relay_ref.at[rows], *sems[0], one),
            head_copy(partial_ref.at[one, rows], first_ref.at[rows], *sems[1], one),
            head_copy(pass_ref.at[rows], second_ref.at[rows], *sems[2], two),
            two,
            rows,
        )

    for c in range(CHUNKS):
        relay, first, *_ = copies(c)
        relay.start()
        first.start()
    for step in range(steps):
        for filler in fillers[step * len(fillers) // steps : (step + 1) * len(fillers) // steps]:
            filler()
        if step < CHUNKS:
            relay, _, second, two, rows = copies(step)
            relay.wait_recv()
            both = partial_ref[two, rows, :].astype(F32) + relay_ref[rows, :].astype(F32)
            pass_ref[rows, :] = both.astype(BF16)
            second.start()
        if 1 <= step <= CHUNKS:
            _, first, second, _, rows = copies(step - 1)
            first.wait_recv()
            second.wait_recv()
            total = partial_ref[me, rows, :].astype(F32) + first_ref[rows, :].astype(F32)
            made = done(rows, total + second_ref[rows, :].astype(F32))
            if share is not None:
                share.refs[0][rows, :] = made
                share.start(step - 1)
        if step >= 3 and share is not None:
            share.forward(step - 3)
    if share is not None:
        share.finish()
    for c in range(CHUNKS):
        for copy in copies(c)[:3]:
            copy.wait_send()


def turn_scratch(rows, width):
    return [pltpu.VMEM((rows, width), BF16) for _ in range(4)] + [
        pltpu.SemaphoreType.DMA((CHUNKS, 3)),
        pltpu.SemaphoreType.DMA((CHUNKS, 3)),
    ]


def hidden_kernel(partial_ref, tokens_ref, hidden_ref, out_ref, *scratch):
    greet_heads(square(lax.axis_index("head"))[:2])
    mine_ref, *sems = scratch[6:]

    def done(rows, total):
        hidden = tokens_ref[rows, :].astype(F32) + total
        hidden_ref[rows, :] = hidden
        return (hidden * rms_scale(hidden, EPS)).astype(BF16)

    turn_rows(partial_ref, *scratch[:6], done, Share(mine_ref, out_ref, *sems))


def share_hidden(partial, tokens):
    whole = pl.BlockSpec(memory_space=pltpu.VMEM)
    return pl.pallas_call(
        hidden_kernel,
        out_shape=[
            jax.ShapeDtypeStruct(tokens.shape, F32),
            jax.ShapeDtypeStruct((H,) + tokens.shape, BF16),
        ],
        in_specs=[whole] * 2,
        out_specs=[whole, pl.BlockSpec(memory_space=pltpu.HBM)],
        scratch_shapes=turn_scratch(*tokens.shape) + share_scratch(*tokens.shape),
        compiler_params=kernel_params(5, 18),
        cost_estimate=pl.CostEstimate(flops=10**6, bytes_accessed=10**4, transcendentals=0),
        name="share_hidden",
    )(partial, tokens)


class PairProduct:
    def __init__(self, left_ref, right_ref, out_ref, give_ref, take_ref, send_sem, recv_sem, own_sem):
        self.refs = left_ref, right_ref, out_ref, give_ref, take_ref
        self.sems = send_sem, recv_sem, own_sem
        self.core = lax.axis_index("core")
        self.groups, self.rows, self.width = out_ref.shape
        self.cut = self.width // 2 if self.width % (2 * LANES) == 0 else self.width

    def product(self, group, core, at):
        left, right, *_ = self.refs
        start = pl.multiple_of((group * CORES + core) * self.rows, LANES)
        return rows_product(left[:, pl.ds(start, self.rows)], right[:, pl.ds(at, self.cut)])

    def copy(self, group):
        give, take = self.refs[3:]
        return pltpu.make_async_remote_copy(
            src_ref=give.at[group],
            dst_ref=take.at[group],
            send_sem=self.sems[0].at[group],
            recv_sem=self.sems[1].at[group],
            device_id={"core": 1 - self.core},
            device_id_type=pl.DeviceIdType.MESH,
        )

    def store(self, group):
        return pltpu.make_async_copy(
            self.refs[3].at[group], self.refs[2].at[group], self.sems[2].at[group]
        )

    def give(self, group, at):
        product = self.product(group, 1 - self.core, at)
        self.refs[3][group, :, pl.ds(at, self.cut)] = product.astype(BF16)
        if at + self.cut == self.width:
            self.copy(group).start()

    def keep(self, group, at):
        give, take = self.refs[3:]
        if at == 0:
            self.copy(group).wait()
        both = self.product(group, self.core, at)
        both += take[group, :, pl.ds(at, self.cut)].astype(F32)
        give[group, :, pl.ds(at, self.cut)] = both.astype(BF16)
        if at + self.cut == self.width:
            self.store(group).start()

    def steps(self):
        places = [
            (group, at) for group in range(self.groups) for at in range(0, self.width, self.cut)
        ]
        return [functools.partial(self.give, *place) for place in places] + [
            functools.partial(self.keep, *place) for place in places
        ]

    def finish(self):
        for group in range(self.groups):
            self.store(group).wait()


def pair_shape(left, right, groups):
    return (groups, left.shape[1] // (CORES * groups), right.shape[1])


def pair_scratch(shape):
    return [
        pltpu.VMEM(shape, BF16),
        pltpu.VMEM(shape, BF16),
        pltpu.SemaphoreType.DMA((shape[0],)),
        pltpu.SemaphoreType.DMA((shape[0],)),
        pltpu.SemaphoreType.DMA((shape[0],)),
    ]


def pair_kernel(moving, left_ref, right_ref, *refs):
    g_ref, out_ref, moved_ref, *scratch = refs if moving else (None, refs[0], None, *refs[1:])
    core = 1 - lax.axis_index("core")
    me = lax.axis_index("head")
    peers = [lax.rem(me + ahead, H) for ahead in range(1, H)] if moving else []
    barrier = pltpu.get_barrier_semaphore()
    for target in [{"core": core}] + [{"head": peer} for peer in peers]:
        pl.semaphore_signal(
            barrier, inc=1, device_id=target, device_id_type=pl.DeviceIdType.MESH
        )
    pl.semaphore_wait(barrier, 1 + len(peers))
    copies = back_copies(g_ref, moved_ref, peers, *scratch[5:]) if moving else []
    for copy in copies:
        copy.start()
    pair = PairProduct(left_ref, right_ref, out_ref, *scratch[:5])
    for step in pair.steps():
        step()
    pair.finish()
    for copy in copies:
        copy.wait()


def pair_product(left, right, groups, number, moving=None):
    shape = pair_shape(left, right, groups)
    whole = pl.BlockSpec(memory_space=pltpu.VMEM)
    hbm = pl.BlockSpec(memory_space=pltpu.HBM)
    moves = [] if moving is None else [moving]
    return pl.pallas_call(
        functools.partial(pair_kernel, len(moves) > 0),
        out_shape=[jax.ShapeDtypeStruct(shape, BF16)]
        + [jax.ShapeDtypeStruct(m.shape, BF16) for m in moves],
        in_specs=[whole] * 2 + [hbm] * len(moves),
        out_specs=[hbm] * (1 + len(moves)),
        scratch_shapes=pair_scratch(shape) + back_scratch() * len(moves),
        compiler_params=kernel_params(number, 28),
        cost_estimate=pl.CostEstimate(flops=10**6, bytes_accessed=10**4, transcendentals=0),
        name="pair_product",
    )(left, right, *moves)


def branch_kernel(
    partial_ref,
    hidden_ref,
    upstream_ref,
    active_ref,
    down_ref,
    grad_ref,
    gain_grad_ref,
    down_out_ref,
    out_ref,
    *scratch,
):
    greet_heads(square(lax.axis_index("head"))[:2])
    mine_ref, *sems = scratch[6:10]
    gain_grad_ref[...] = jnp.zeros_like(gain_grad_ref)

    def done(rows, total):
        hidden = hidden_ref[rows, :]
        scale = rms_scale(hidden, EPS)
        gain_grad_ref[...] += jnp.sum(total * hidden * scale, axis=0, keepdims=True)
        grad = upstream_ref[rows, :].astype(F32) + rms_back(total, hidden, scale)
        grad_ref[rows, :] = grad
        return grad.astype(BF16)

    def down(at):
        rows = pl.ds(at, LANES)
        down_out_ref[rows, :] = matmul(active_ref[rows, :], down_ref[...]).astype(BF16)

    share = Share(mine_ref, out_ref, *sems)
    fillers = [functools.partial(down, at) for at in range(0, active_ref.shape[0], LANES)]
    turn_rows(partial_ref, *scratch[:6], done, share, fillers)


def share_branch(partial, hidden, upstream, active, down):
    whole = pl.BlockSpec(memory_space=pltpu.VMEM)
    return pl.pallas_call(
        branch_kernel,
        out_shape=[
            jax.ShapeDtypeStruct(hidden.shape, F32),
            jax.ShapeDtypeStruct((1, hidden.shape[1]), F32),
            jax.ShapeDtypeStruct((active.shape[0], down.shape[1]), BF16),
            jax.ShapeDtypeStruct((H,) + hidden.shape, BF16),
        ],
        in_specs=[whole] * 5,
        out_specs=[whole] * 3 + [pl.BlockSpec(memory_space=pltpu.HBM)],
        scratch_shapes=turn_scratch(*hidden.shape) + share_scratch(*hidden.shape),
        compiler_params=kernel_params(6, 34),
        cost_estimate=pl.CostEstimate(flops=10**6, bytes_accessed=10**4, transcendentals=0),
        name="share_branch",
    )(partial, hidden, upstream, active, down)


def tokens_kernel(partial_ref, tokens_ref, upstream_ref, grad_ref, gain_grad_ref, *scratch):
    greet_heads(square(lax.axis_index("head"))[:2])
    gain_grad_ref[...] = jnp.zeros_like(gain_grad_ref)

    def done(rows, total):
        tokens = tokens_ref[rows, :].astype(F32)
        scale = rms_scale(tokens, EPS)
        gain_grad_ref[...] += jnp.sum(total * tokens * scale, axis=0, keepdims=True)
        grad = upstream_ref[rows, :] + rms_back(total, tokens, scale)
        grad_ref[rows, :] = grad.astype(BF16)

    turn_rows(partial_ref, *scratch, done)


def tokens_back(partial, tokens, upstream):
    whole = pl.BlockSpec(memory_space=pltpu.VMEM)
    return pl.pallas_call(
        tokens_kernel,
        out_shape=[
            jax.ShapeDtypeStruct(tokens.shape, BF16),
            jax.ShapeDtypeStruct((1, tokens.shape[1]), F32),
        ],
        in_specs=[whole] * 3,
        out_specs=[whole] * 2,
        scratch_shapes=turn_scratch(*tokens.shape),
        compiler_params=kernel_params(8, 18),
        cost_estimate=pl.CostEstimate(flops=10**6, bytes_accessed=10**4, transcendentals=0),
        name="tokens_back",
    )(partial, tokens, upstream)


def hidden_units_kernel(cot_ref, down_ref, pre_ref, out_ref):
    units = down_ref.shape[0]
    grad = back_product(cot_ref[...], down_ref[...])
    gate, up = pre_ref[:, pl.ds(0, units)], pre_ref[:, pl.ds(units, units)]
    sig = jax.nn.sigmoid(gate)
    grad_sig = grad * sig
    out_ref[:, pl.ds(0, units)] = (grad_sig * up * (1.0 + gate * (1.0 - sig))).astype(BF16)
    out_ref[:, pl.ds(units, units)] = (grad_sig * gate).astype(BF16)


def hidden_units_back(cot, down, pre):
    rows, width = cot.shape
    size = 2 * LANES

    def rows_block(n):
        return pl.BlockSpec((size, n), lambda i: (i, 0))

    return pl.pallas_call(
        hidden_units_kernel,
        grid=(rows // size,),
        out_shape=jax.ShapeDtypeStruct(pre.shape, BF16),
        in_specs=[
            rows_block(width),
            pl.BlockSpec(down.shape, lambda i: (0, 0)),
            rows_block(pre.shape[1]),
        ],
        out_specs=rows_block(pre.shape[1]),
        compiler_params=pltpu.CompilerParams(vmem_limit_bytes=32 * 2**20),
        cost_estimate=pl.CostEstimate(flops=10**6, bytes_accessed=10**4, transcendentals=0),
        name="hidden_units_back",
    )(cot, down, pre)


def back_copies(g_ref, out_ref, peers, send_sem, recv_sem, own_sem):
    me = lax.axis_index("head")
    copies = [
        head_copy(g_ref.at[peer], out_ref.at[me], send_sem.at[ahead], recv_sem.at[ahead], peer)
        for ahead, peer in enumerate(peers)
    ]
    return copies + [pltpu.make_async_copy(g_ref.at[me], out_ref.at[me], own_sem)]


def back_scratch():
    return [pltpu.SemaphoreType.DMA((H,)), pltpu.SemaphoreType.DMA((H,)), pltpu.SemaphoreType.DMA]


def columns_kernel(g_ref, out_ref, *sems):
    me = lax.axis_index("head")
    peers = [lax.rem(me + ahead, H) for ahead in range(1, H)]
    greet_heads(peers)
    copies = back_copies(g_ref, out_ref, peers, *sems)
    for copy in copies:
        copy.start()
    for copy in copies:
        copy.wait()


def columns_back(g):
    return pl.pallas_call(
        columns_kernel,
        out_shape=jax.ShapeDtypeStruct(g.shape, BF16),
        in_specs=[pl.BlockSpec(memory_space=pltpu.HBM)],
        out_specs=pl.BlockSpec(memory_space=pltpu.HBM),
        scratch_shapes=back_scratch(),
        compiler_params=kernel_params(10, 16),
        cost_estimate=pl.CostEstimate(flops=10**6, bytes_accessed=10**4, transcendentals=0),
        name="columns_back",
    )(g)


def mix_forward(mixed, bias, gaterank, gain, marks, segment, sums, pairs, key_dim, value_dim):
    rows = mixed.shape[0]
    count, _, length = segment.shape
    shapes = (
        ((rows, value_dim), BF16),
        ((rows, value_dim), F32),
        ((rows, key_dim), F32),
        ((count, length, length), BF16),
        ((rows, key_dim), BF16),
        ((rows, key_dim), BF16),
        ((count, 1, key_dim), F32),
        ((count, value_dim, key_dim), BF16),
    )
    whole = pl.BlockSpec(memory_space=pltpu.VMEM)
    return pl.pallas_call(
        functools.partial(forward_kernel, key_dim, value_dim),
        out_shape=[jax.ShapeDtypeStruct(*s) for s in shapes],
        in_specs=[whole] * 8,
        out_specs=[whole] + [pl.BlockSpec(memory_space=pltpu.HBM)] * (len(shapes) - 1),
        scratch_shapes=[pltpu.VMEM(*s) for s in shapes[1:-1]]
        + state_scratch(count, value_dim, key_dim)
        + [pltpu.SemaphoreType.DMA((count, 7))],
        compiler_params=kernel_params(1, 26),
        cost_estimate=pl.CostEstimate(flops=10**6, bytes_accessed=10**4, transcendentals=0),
        name="mix_forward",
    )(mixed, bias, gaterank, gain, marks, segment, sums, pairs)


def mix_backward(
    mixed, kept, upstream, gaterank, gain, marks, segment, sums, pairs, key_dim, value_dim
):
    rows = mixed.shape[0]
    count = segment.shape[0]
    shapes = (
        (mixed.shape, BF16),
        ((1, value_dim), F32),
        ((1, key_dim), F32),
        (gaterank.shape, F32),
    )
    attended, logits, scores, start, end, decay, enter = kept
    given = (mixed, upstream, attended, start, logits, scores, end, decay, enter)
    whole = pl.BlockSpec(memory_space=pltpu.VMEM)
    return pl.pallas_call(
        functools.partial(backward_kernel, key_dim, value_dim),
        out_shape=[jax.ShapeDtypeStruct(*s) for s in shapes],
        in_specs=[pl.BlockSpec(memory_space=pltpu.HBM)] * 9 + [whole] * 6,
        out_specs=[whole] * len(shapes),
        scratch_shapes=[pltpu.VMEM(a.shape, a.dtype) for a in given]
        + [pltpu.VMEM((rows, value_dim), BF16)]
        + state_scratch(count, value_dim, key_dim)
        + [pltpu.SemaphoreType.DMA((count, 9))],
        compiler_params=kernel_params(2, 34),
        cost_estimate=pl.CostEstimate(flops=10**6, bytes_accessed=10**4, transcendentals=0),
        name="mix_backward",
    )(
        *given,
        gaterank,
        gain,
        marks,
        segment,
        sums,
        pairs,
    )


def per_device(
    tokens,
    doc_lengths,
    norm_gain,
    w_query,
    w_key,
    w_value,
    w_outgate,
    w_lowrank,
    w_gaterank,
    gate_bias,
    head_gain,
    w_output,
    ffn_gain,
    w_gate,
    w_up,
    w_down,
    cotangent,
):
    seqs_here, length, width = tokens.shape
    reps = lax.axis_size("rep")
    parts = lax.axis_size("fsdp")
    devices = reps * H * CORES * parts
    here = lax.axis_index("head")
    key_dim, value_dim = DK, DV
    rank = w_lowrank.shape[1]
    rows = width // devices
    count = H * seqs_here

    rank_at = 2 * key_dim + 2 * value_dim

    def core_sum(g):
        halves = g.reshape(g.shape[0], CORES, -1, g.shape[-1])
        core = lax.axis_index("core")
        other = lax.ppermute(halves[:, 1 - core], "core", ((0, 1), (1, 0)))
        return (halves[:, core].astype(F32) + other.astype(F32)).astype(BF16)

    def scatter_rows(g):
        if reps > 1:
            g = lax.psum_scatter(g, "rep", scatter_dimension=0, tiled=True)
        return lax.psum_scatter(g, "fsdp", scatter_dimension=1, tiled=True)

    def gather_columns(moved):
        whole = lax.all_gather(moved, ("core", "fsdp"), axis=1, tiled=True)
        if reps > 1:
            whole = lax.all_gather(whole, "rep", axis=0, tiled=False)
        return whole.reshape(width, -1)

    def gather_part(w):
        if reps == 1:
            return lax.all_gather(w, SHARE, axis=0, tiled=True)
        whole = lax.all_gather(w, EVERY, axis=0, tiled=True)
        size = whole.shape[0] // H
        return lax.dynamic_slice_in_dim(whole, here * size, size, 0)

    def pair_part(g):
        return core_sum(g[None])[0] if reps == 1 else g

    def scatter_part(g):
        if reps == 1:
            return lax.psum_scatter(g, "fsdp", scatter_dimension=0, tiled=True)
        whole = jnp.zeros((H * g.shape[0], g.shape[1]), BF16)
        whole = lax.dynamic_update_slice_in_dim(whole, g, here * g.shape[0], 0)
        return lax.psum_scatter(whole, EVERY, scatter_dimension=0, tiled=True)

    rank_at = 2 * key_dim + 2 * value_dim

    def with_gain(w, gain):
        return (w.astype(F32) * gain.astype(F32)[:, None]).astype(BF16)

    small = (
        w_gaterank,
        gate_bias.reshape(1, -1),
        head_gain.reshape(1, -1),
        (doc_lengths // 16).astype(BF16).reshape(1, -1),
        (doc_lengths % 16).astype(BF16).reshape(1, -1),
    )
    edges = [rank]
    extra = jnp.pad(with_gain(w_lowrank, norm_gain), ((0, 0), (0, LANES - rank)))
    for piece in small:
        high, wide = piece.shape
        extra += jnp.pad(piece, ((0, rows - high), (edges[-1], LANES - edges[-1] - wide)))
        edges.append(edges[-1] + wide)

    mix_moved = mix_weights((w_query, w_key, w_value, w_outgate), extra, norm_gain[:, None])
    inputs = tokens.reshape(-1, width)
    inputs, w_output, w_down, _ = after(inputs, w_output, w_down, mix_moved)
    mix_w = gather_columns(mix_moved)
    output_w = gather_part(w_output)
    down_w = gather_part(w_down)
    normed, ffn_moved = share_tokens(inputs, w_gate, w_up, ffn_gain[:, None])
    normed = normed.reshape(-1, width)

    small = mix_w[:, rank_at:].astype(F32).reshape(devices, rows, LANES)
    gaterank, bias, gain_head, long, short = (
        small[:, : rank if i == 0 else 1, edges[i] : edges[i + 1]] for i in range(len(edges) - 1)
    )
    gaterank = gaterank.transpose(1, 0, 2).reshape(rank, -1)
    bias = lax.dynamic_slice_in_dim(bias.reshape(1, -1), here * key_dim, key_dim, 1)
    gaterank = lax.dynamic_slice_in_dim(gaterank, here * key_dim, key_dim, 1)
    gain_head = gain_head.reshape(1, -1)
    lengths = (long * 16.0 + short).reshape(reps, H, CORES, parts, seqs_here, DOCS)
    lengths = lengths[lax.axis_index("rep"), :, lax.axis_index("core"), 0]
    lengths = lengths.reshape(count, DOCS).astype(jnp.int32)

    offset = lax.axis_index("fsdp") * length
    doc_ends = jnp.cumsum(lengths, axis=-1)
    places = offset + jnp.arange(length, dtype=jnp.int32)
    segment = jnp.sum((places[None, :, None] >= doc_ends[:, None, :]).astype(jnp.int32), axis=-1)
    before = jnp.sum((offset - 1 >= doc_ends).astype(jnp.int32), axis=-1)[:, None]
    last = segment[:, -1:]
    marks = jnp.stack(
        [
            segment,
            segment == before,
            segment == last,
            segment != DOCS - 1,
            jnp.broadcast_to(last == before, segment.shape),
        ],
        axis=2,
    )
    marks = jnp.pad(marks.astype(F32).reshape(count * length, 5), ((0, 0), (0, 3)))
    segment = segment.astype(F32).reshape(count, 1, length)

    mixed = matmul(normed, mix_w)
    sums, pairs = level_sums(length)
    sums, pairs = sums.astype(BF16), pairs.astype(BF16)
    gated, *kept = mix_forward(
        mixed, bias, gaterank, gain_head, marks, segment, sums, pairs, key_dim, value_dim
    )
    cot_rows, _ = after(cotangent.reshape(-1, width), normed)
    gated, cot_shared, output_w, down_w = after(gated, share_rows(cot_rows), output_w, down_w)
    ffn_moved, _ = after(ffn_moved, gated)
    ffn_w = gather_columns(ffn_moved)
    partial = matmul(gated, output_w).astype(BF16).reshape(H, -1, width)
    hidden, normed_two = share_hidden(partial, inputs)
    normed_two = normed_two.reshape(-1, width)

    pre = matmul(normed_two, ffn_w)
    gate_pre, up_pre = jnp.split(pre, 2, axis=1)
    sig_gate = jax.nn.sigmoid(gate_pre)
    activated = (gate_pre * sig_gate * up_pre).astype(BF16)

    grad_down_w = rows_product(activated, cot_shared).astype(BF16)
    down_w, grad_down_w = after(down_w, grad_down_w)
    grad_pre = hidden_units_back(cot_shared, down_w, pre)
    grad_pre, grad_down_w = after(grad_pre, pair_part(grad_down_w))
    grad_down_w = scatter_part(grad_down_w)
    (grad_ffn_w,) = pair_product(normed_two, grad_pre, reps * H, 7)
    grad_pre, grad_ffn_w = after(grad_pre, grad_ffn_w)
    partial = back_product(grad_pre, ffn_w).astype(BF16)

    grad_hidden, grad_gain_two, down_partial, branch = share_branch(
        partial.reshape(H, -1, width), hidden, cot_rows, activated, down_w
    )
    grad_ffn_w = scatter_rows(grad_ffn_w)
    branch = branch.reshape(-1, width)
    grad_gated = back_product(branch, output_w)
    gated, grad_gated = after(gated, grad_gated)
    grad_output_w = pair_part(rows_product(gated, branch).astype(BF16))
    grad_gated, grad_output_w, grad_down_w = after(grad_gated, grad_output_w, grad_down_w)
    grad_output_w = scatter_part(grad_output_w)
    pieces = move_rows(down_partial)
    grad_mixed, grad_gain_head, grad_bias, grad_gaterank = mix_backward(
        mixed,
        kept,
        grad_gated,
        gaterank,
        gain_head,
        marks,
        segment,
        sums,
        pairs,
        key_dim,
        value_dim,
    )
    grad_mixed, pieces, grad_down_w, grad_ffn_w = after(
        grad_mixed, pieces, grad_down_w, grad_ffn_w
    )
    output = (hidden + jnp.sum(pieces.astype(F32), axis=0)).astype(BF16).reshape(tokens.shape)
    grad_mix_w, grad_ffn_w = pair_product(normed, grad_mixed, reps * H, 11, grad_ffn_w)
    grad_mixed, grad_mix_w = after(grad_mixed, grad_mix_w)
    partial = back_product(grad_mixed, mix_w).astype(BF16)
    grad_mix_w = scatter_rows(grad_mix_w)
    partial, grad_output_w = after(partial, grad_output_w)
    tokens_grad, grad_gain_one = tokens_back(partial.reshape(H, -1, width), inputs, grad_hidden)
    tokens_grad = tokens_grad.reshape(tokens.shape)

    def weight_grad(moved, gain, start, w):
        n = w.shape[1] // H
        whole = moved[:, :, start : start + n].transpose(1, 0, 2).reshape(rows, -1)
        return whole.astype(F32) * gain.astype(F32)[:, None]

    w_gate_grad = weight_grad(grad_ffn_w, ffn_gain, 0, w_gate)
    w_up_grad = weight_grad(grad_ffn_w, ffn_gain, w_gate.shape[1] // H, w_up)
    grad_mix_w = columns_back(grad_mix_w)
    query_g = weight_grad(grad_mix_w, norm_gain, 0, w_query)
    key_g = weight_grad(grad_mix_w, norm_gain, key_dim, w_key)
    value_g = weight_grad(grad_mix_w, norm_gain, 2 * key_dim, w_value)
    outgate_g = weight_grad(grad_mix_w, norm_gain, 2 * key_dim + value_dim, w_outgate)
    lowrank_g = grad_mix_w[:, :, rank_at : rank_at + rank].astype(F32)
    lowrank_g = jnp.sum(lowrank_g, axis=0) * norm_gain.astype(F32)[:, None]

    def place(g, axis):
        shape = list(g.shape)
        shape[axis] *= H
        return lax.dynamic_update_slice_in_dim(jnp.zeros(shape, F32), g, here * key_dim, axis)

    small_grads = jnp.concatenate(
        [
            grad_gain_one.reshape(devices, -1),
            grad_gain_two.reshape(devices, -1),
            place(grad_bias.reshape(-1), 0).reshape(devices, -1),
            grad_gain_head.reshape(devices, -1),
            place(grad_gaterank, 1)
            .reshape(rank, devices, -1)
            .transpose(1, 0, 2)
            .reshape(devices, -1),
        ],
        axis=1,
    )
    small_grads = lax.all_to_all(small_grads, EVERY, split_axis=0, concat_axis=0, tiled=True)
    small_grads = jnp.sum(small_grads, axis=0)
    sizes = [norm_gain.shape[0], ffn_gain.shape[0], gate_bias.shape[0], head_gain.shape[0]]
    norm_g, ffn_g, bias_g, head_g, gaterank_g = jnp.split(
        small_grads, [sum(sizes[: i + 1]) for i in range(len(sizes))]
    )
    return (
        output,
        tokens_grad,
        norm_g / norm_gain.astype(F32),
        query_g,
        key_g,
        value_g,
        outgate_g,
        lowrank_g,
        gaterank_g.reshape(w_gaterank.shape),
        bias_g,
        head_g,
        grad_output_w.astype(F32),
        ffn_g / ffn_gain.astype(F32),
        w_gate_grad,
        w_up_grad,
        grad_down_w.astype(F32),
    )


def solution(mesh):
    dp, parts = mesh.shape["dp"], mesh.shape["fsdp"]
    fine = Mesh(mesh.devices.reshape(dp // (H * CORES), H, CORES, parts), EVERY)
    seq = ("rep", "head", "core")
    rows, vector = P(EVERY, None), P(EVERY)
    activations = P(seq, "fsdp", None)
    columns = P(None, EVERY)
    return jax.shard_map(
        per_device,
        mesh=fine,
        in_specs=(
            activations,
            P(seq, None),
            vector,
            rows,
            rows,
            rows,
            rows,
            rows,
            columns,
            vector,
            vector,
            rows,
            vector,
            rows,
            rows,
            rows,
            activations,
        ),
        out_specs=(
            activations,
            activations,
            vector,
            rows,
            rows,
            rows,
            rows,
            rows,
            columns,
            vector,
            vector,
            rows,
            vector,
            rows,
            rows,
            rows,
        ),
        check_vma=False,
    )
```

```python
import functools

import jax
import jax.experimental.pallas as pl
import jax.experimental.pallas.tpu as pltpu
import jax.numpy as jnp
from jax import lax
from jax.sharding import Mesh
from jax.sharding import PartitionSpec as P

H = 4
DK = 256
DV = 512
CORES = 2
DOCS = 8
PIECES = 2
LANES = 128
CHUNKS = 8

EPS = 1e-05
HEAD_EPS = 1.0
HIGHEST = lax.Precision.HIGHEST
F32 = jnp.float32
BF16 = jnp.bfloat16

SHARE = ("rep", "core", "fsdp")
EVERY = ("rep", "head", "core", "fsdp")


def dot(a, b, dims, precision=None):
    return lax.dot_general(a, b, (dims, ((), ())), precision=precision, preferred_element_type=F32)


def after(value, *others):
    return lax.optimization_barrier((value,) + others)


def matmul(a, b):
    return dot(a, b, ((1,), (0,)))


def rows_product(a, b):
    return dot(a, b, ((0,), (0,)))


def back_product(a, b):
    return dot(a, b, ((1,), (1,)))


def batched(form, a, b):
    return jnp.einsum(form, a, b, preferred_element_type=F32)


def rms_scale(values, epsilon):
    return lax.rsqrt(jnp.mean(values * values, axis=-1, keepdims=True) + epsilon)


def rms_back(upstream, values, scale):
    return scale * upstream - values * scale**3 * jnp.mean(upstream * values, axis=-1, keepdims=True)


def share_rows(part):
    spread = jnp.broadcast_to(part[None], (H,) + part.shape)
    whole = lax.all_to_all(spread, "head", split_axis=0, concat_axis=0, tiled=True)
    return whole.reshape(-1, part.shape[-1])


def move_rows(partial):
    pieces = partial.astype(BF16).reshape(H, -1, partial.shape[-1])
    return lax.all_to_all(pieces, "head", split_axis=0, concat_axis=0, tiled=True)


def sum_rows(partial):
    return jnp.sum(move_rows(partial).astype(F32), axis=0)


def level_sums(length):
    rows = jnp.arange(length)[:, None]
    cols = jnp.arange(length)[None, :]
    sums, pairs = [], []
    step = 1
    while step < length:
        bound = rows // (2 * step) * (2 * step) + step - 1
        upper = rows > bound
        sums.append(jnp.where(upper, (cols > bound) & (cols <= rows), (cols > rows) & (cols <= bound)))
        pairs.append(upper & (cols // (2 * step) == rows // (2 * step)) & (cols <= bound))
        step *= 2
    sums.append(cols <= rows)
    sums.append(cols > rows)
    return jnp.stack(sums), jnp.stack(pairs)


def log_sigmoid(x):
    return jnp.minimum(x, 0.0) - jnp.log1p(jnp.exp(-jnp.abs(x)))


def state_copy(send, recv, send_sem, recv_sem, seq, piece, target):
    size = send.shape[1] // PIECES
    part = pl.ds(piece * size, size)
    return pltpu.make_async_remote_copy(
        src_ref=send.at[seq, part],
        dst_ref=recv.at[seq, part],
        send_sem=send_sem.at[seq, piece],
        recv_sem=recv_sem.at[seq, piece],
        device_id={"fsdp": target},
        device_id_type=pl.DeviceIdType.MESH,
    )


def greet_neighbours(place, parts):
    barrier = pltpu.get_barrier_semaphore()
    for near, there in ((place - 1, place > 0), (place + 1, place < parts - 1)):

        @pl.when(there)
        def _(near=near):
            pl.semaphore_signal(
                barrier,
                inc=1,
                device_id={"fsdp": lax.rem(near + parts, parts)},
                device_id_type=pl.DeviceIdType.MESH,
            )

    peers = (place > 0).astype(jnp.int32) + (place < parts - 1).astype(jnp.int32)
    pl.semaphore_wait(barrier, peers)


def pass_state(s, first, last, target, decay, local, send, recv, send_sem, recv_sem):
    size = send.shape[1] // PIECES
    for piece in range(PIECES):
        part = pl.ds(piece * size, size)
        copy = state_copy(send, recv, send_sem, recv_sem, s, piece, target)

        @pl.when(jnp.logical_not(first))
        def _(copy=copy):
            copy.wait_recv()

        @pl.when(jnp.logical_not(jnp.logical_or(first, last)))
        def _(copy=copy, part=part):
            joined = decay * recv[s, part].astype(F32) + local[s, part]
            send[s, part] = joined.astype(BF16)
            copy.start()


def start_state(s, first, last, target, local, send, recv, send_sem, recv_sem):
    @pl.when(jnp.logical_and(first, jnp.logical_not(last)))
    def _():
        send[s] = local[s].astype(BF16)
        for piece in range(PIECES):
            state_copy(send, recv, send_sem, recv_sem, s, piece, target).start()


def finish_states(count, last, target, send, recv, send_sem, recv_sem):
    @pl.when(jnp.logical_not(last))
    def _():
        def one(s, carry):
            for piece in range(PIECES):
                state_copy(send, recv, send_sem, recv_sem, s, piece, target).wait_send()
            return carry

        lax.fori_loop(0, count, one, 0)


def split_rates(logits):
    rates = log_sigmoid(logits) / 16.0
    high = rates.astype(BF16)
    return high, (rates - high.astype(F32)).astype(BF16)


def decayed(sums, high, low):
    return jnp.exp(matmul(sums, high) + matmul(sums, low))


def forward_kernel(
    key_dim,
    value_dim,
    given_ref,
    bias_ref,
    gaterank_ref,
    gain_ref,
    marks_ref,
    segment_ref,
    sums_ref,
    pairs_ref,
    gated_ref,
    *refs,
):
    kept, (attended_ref, logits_ref, scores_ref, start_ref, end_ref, decay_ref) = refs[:7], refs[7:13]
    local_ref, send_ref, recv_ref, send_sem, recv_sem, keep_sem, mixed_ref, take_sem = refs[13:]
    count, _, length = segment_ref.shape
    levels = pairs_ref.shape[0]
    parts, place = lax.axis_size("fsdp"), lax.axis_index("fsdp")
    first, last, target = place == 0, place == parts - 1, lax.rem(place + 1, parts)

    def rows_of(s):
        return pl.ds(pl.multiple_of(s * length, length), length)

    def keeps(s, kinds):
        held = (attended_ref, logits_ref, scores_ref, start_ref, end_ref, decay_ref, recv_ref)
        rows = rows_of(s)
        for kind in kinds:
            at = rows if len(held[kind].shape) == 2 else s
            yield pltpu.make_async_copy(held[kind].at[at], kept[kind].at[at], keep_sem.at[s, kind])

    def take(s):
        rows = rows_of(s)
        return pltpu.make_async_copy(given_ref.at[rows], mixed_ref.at[rows], take_sem.at[s])

    def start_take(s, carry):
        take(s).start()
        return carry

    lax.fori_loop(0, count, start_take, 0)

    def finish_keeps(s, carry):
        for copy in keeps(s, range(7)):
            copy.wait()
        return carry

    rank = gaterank_ref.shape[0]
    scale = key_dim ** (-0.5)
    value_at = 2 * key_dim
    gate_at = value_at + value_dim
    rank_at = gate_at + value_dim

    greet_neighbours(place, parts)

    @pl.when(first)
    def _():
        recv_ref[...] = jnp.zeros_like(recv_ref)

    def ends(s, carry):
        rows = rows_of(s)
        take(s).wait()
        lowrank = mixed_ref[rows, pl.ds(rank_at, rank)]
        logits = dot(lowrank, gaterank_ref[...], ((1,), (0,)), HIGHEST) + bias_ref[...]
        logits_ref[rows, :] = logits
        high, low = split_rates(logits)
        from_start = decayed(sums_ref[levels], high, low)
        to_end = decayed(sums_ref[levels + 1], high, low)
        marks = marks_ref[rows, :]
        decay_ref[s] = from_start[length - 1 :, :] * marks[:1, 4:5]
        query = mixed_ref[rows, pl.ds(0, key_dim)] * scale
        key = mixed_ref[rows, pl.ds(key_dim, key_dim)]
        start_ref[rows, :] = (query * (from_start * marks[:, 1:2])).astype(BF16)
        end_key = (key * (to_end * marks[:, 2:3])).astype(BF16)
        end_ref[rows, :] = end_key
        value = mixed_ref[rows, pl.ds(value_at, value_dim)].astype(BF16)
        local_ref[s] = rows_product(value, end_key)
        start_state(s, first, last, target, local_ref, send_ref, recv_ref, send_sem, recv_sem)
        for copy in keeps(s, (1, 3, 4, 5)):
            copy.start()
        return carry

    lax.fori_loop(0, count, ends, 0)

    def mix(s, carry):
        rows = rows_of(s)
        pass_state(
            s, first, last, target, decay_ref[s], local_ref, send_ref, recv_ref, send_sem, recv_sem
        )
        query = mixed_ref[rows, pl.ds(0, key_dim)] * scale
        key = mixed_ref[rows, pl.ds(key_dim, key_dim)]
        high, low = split_rates(logits_ref[rows, :])
        scores = jnp.zeros((length, length), F32)
        for level in range(levels):
            decay = decayed(sums_ref[level], high, low)
            pair = back_product((query * decay).astype(BF16), (key * decay).astype(BF16))
            scores += pair * pairs_ref[level].astype(F32)
        row = lax.broadcasted_iota(jnp.int32, (length, length), 0)
        col = lax.broadcasted_iota(jnp.int32, (length, length), 1)
        own = jnp.sum(query * key, axis=1, keepdims=True)
        scores += jnp.where(row == col, own, 0.0)
        marks = marks_ref[rows, :]
        scores = jnp.where(marks[:, 0:1] == segment_ref[s], scores, 0.0).astype(BF16)
        scores_ref[s] = scores
        value = mixed_ref[rows, pl.ds(value_at, value_dim)].astype(BF16)
        attended = matmul(scores, value) + back_product(start_ref[rows, :], recv_ref[s])
        attended = attended * marks[:, 3:4]
        attended_ref[rows, :] = attended
        headed = attended * rms_scale(attended, HEAD_EPS) * gain_ref[...]
        outgate = mixed_ref[rows, pl.ds(gate_at, value_dim)]
        gated_ref[rows, :] = (headed * (outgate * jax.nn.sigmoid(outgate))).astype(BF16)
        for copy in keeps(s, (0, 2, 6)):
            copy.start()
        return carry

    lax.fori_loop(0, count, mix, 0)
    finish_states(count, last, target, send_ref, recv_ref, send_sem, recv_sem)
    lax.fori_loop(0, count, finish_keeps, 0)


def backward_kernel(
    key_dim,
    value_dim,
    *refs,
):
    given, refs = refs[:9], refs[9:]
    gaterank_ref, gain_ref, marks_ref, segment_ref, sums_ref, pairs_ref, *refs = refs
    grad_ref, gain_grad_ref, bias_grad_ref, gaterank_grad_ref, *refs = refs
    held, refs = refs[:9], refs[9:]
    mixed_ref, upstream_ref, attended_ref, start_ref, *rest_refs = held
    logits_ref, scores_ref, end_ref, decay_ref, enter_ref = rest_refs
    out_ref, local_ref, send_ref, recv_ref, send_sem, recv_sem, take_sem = refs
    count, _, length = segment_ref.shape

    def rows_of(s):
        return pl.ds(pl.multiple_of(s * length, length), length)

    def takes(s, kinds):
        rows = rows_of(s)
        for kind in kinds:
            at = rows if len(held[kind].shape) == 2 else s
            yield pltpu.make_async_copy(given[kind].at[at], held[kind].at[at], take_sem.at[s, kind])

    def start_takes(s, carry):
        for copy in takes(s, range(9)):
            copy.start()
        return carry

    lax.fori_loop(0, count, start_takes, 0)
    levels = pairs_ref.shape[0]
    parts, place = lax.axis_size("fsdp"), lax.axis_index("fsdp")
    first, last, target = place == parts - 1, place == 0, lax.rem(place + parts - 1, parts)
    rank = gaterank_ref.shape[0]
    scale = key_dim ** (-0.5)
    value_at = 2 * key_dim
    gate_at = value_at + value_dim
    rank_at = gate_at + value_dim

    greet_neighbours(place, parts)

    @pl.when(first)
    def _():
        recv_ref[...] = jnp.zeros_like(recv_ref)

    gain_grad_ref[...] = jnp.zeros_like(gain_grad_ref)
    bias_grad_ref[...] = jnp.zeros_like(bias_grad_ref)
    gaterank_grad_ref[...] = jnp.zeros_like(gaterank_grad_ref)

    def heads(s, carry):
        rows = rows_of(s)
        for copy in takes(s, range(4)):
            copy.wait()
        upstream = upstream_ref[rows, :]
        attended = attended_ref[rows, :]
        outgate = mixed_ref[rows, pl.ds(gate_at, value_dim)]
        gain = gain_ref[...]
        norm = rms_scale(attended, HEAD_EPS)
        normed = attended * norm
        sig = jax.nn.sigmoid(outgate)
        grad_gate = upstream * (normed * gain) * sig * (1.0 + outgate * (1.0 - sig))
        grad_ref[rows, pl.ds(gate_at, value_dim)] = grad_gate.astype(BF16)
        grad_headed = upstream * (outgate * sig)
        gain_grad_ref[...] += jnp.sum(grad_headed * normed, axis=0, keepdims=True)
        grad_out = rms_back(grad_headed * gain, attended, norm) * marks_ref[rows, pl.ds(3, 1)]
        grad_out = grad_out.astype(BF16)
        out_ref[rows, :] = grad_out
        local_ref[s] = rows_product(grad_out, start_ref[rows, :])
        start_state(s, first, last, target, local_ref, send_ref, recv_ref, send_sem, recv_sem)
        return carry

    lax.fori_loop(0, count, heads, 0)

    def mix(s, carry):
        rows = rows_of(s)
        for copy in takes(s, range(4, 9)):
            copy.wait()
        decay_row = decay_ref[s]
        pass_state(
            s, first, last, target, decay_row, local_ref, send_ref, recv_ref, send_sem, recv_sem
        )
        query = mixed_ref[rows, pl.ds(0, key_dim)] * scale
        key = mixed_ref[rows, pl.ds(key_dim, key_dim)]
        value = mixed_ref[rows, pl.ds(value_at, value_dim)].astype(BF16)
        marks = marks_ref[rows, :]
        logits = logits_ref[rows, :]
        high, low = split_rates(logits)
        grad_out = out_ref[rows, :]
        row = lax.broadcasted_iota(jnp.int32, (length, length), 0)
        col = lax.broadcasted_iota(jnp.int32, (length, length), 1)
        pair_grads = back_product(grad_out, value)
        pair_grads = jnp.where(marks[:, 0:1] == segment_ref[s], pair_grads, 0.0)
        own = jnp.sum(jnp.where(row == col, pair_grads, 0.0), axis=1, keepdims=True)
        grad_query = own * key
        grad_key = own * query
        grad_rates = jnp.zeros((length, key_dim), F32)
        for level in range(levels):
            decay = decayed(sums_ref[level], high, low)
            level_query = (query * decay).astype(BF16)
            level_key = (key * decay).astype(BF16)
            level_pairs = (pair_grads * pairs_ref[level].astype(F32)).astype(BF16)
            level_grad_query = matmul(level_pairs, level_key)
            level_grad_key = rows_product(level_pairs, level_query)
            grad_query += level_grad_query * decay
            grad_key += level_grad_key * decay
            flow = level_grad_query * level_query.astype(F32)
            flow += level_grad_key * level_key.astype(F32)
            grad_rates += rows_product(sums_ref[level], flow.astype(BF16))
        ending = recv_ref[s]
        entering = enter_ref[s]
        start_query = start_ref[rows, :]
        end_key = end_ref[rows, :]
        start_grad = matmul(grad_out, entering)
        end_grad = matmul(value, ending)
        grad_query += start_grad * (decayed(sums_ref[levels], high, low) * marks[:, 1:2])
        grad_key += end_grad * (decayed(sums_ref[levels + 1], high, low) * marks[:, 2:3])
        grad_rates += rows_product(
            sums_ref[levels], (start_grad * start_query.astype(F32)).astype(BF16)
        )
        grad_rates += rows_product(
            sums_ref[levels + 1], (end_grad * end_key.astype(F32)).astype(BF16)
        )
        grad_rates += decay_row * jnp.sum(
            ending.astype(F32) * entering.astype(F32), axis=0, keepdims=True
        )
        grad_value = rows_product(scores_ref[s], grad_out) + back_product(end_key, ending)
        grad_ref[rows, pl.ds(0, key_dim)] = (grad_query * scale).astype(BF16)
        grad_ref[rows, pl.ds(key_dim, key_dim)] = grad_key.astype(BF16)
        grad_ref[rows, pl.ds(value_at, value_dim)] = grad_value.astype(BF16)
        grad_logits = grad_rates / 16.0 * jax.nn.sigmoid(-logits)
        bias_grad_ref[...] += jnp.sum(grad_logits, axis=0, keepdims=True)
        lowrank = mixed_ref[rows, pl.ds(rank_at, rank)]
        gaterank_grad_ref[...] += dot(lowrank, grad_logits, ((0,), (0,)), HIGHEST)
        grad_lowrank = dot(grad_logits, gaterank_ref[...], ((1,), (1,)), HIGHEST)
        rest = grad_ref.shape[1] - rank_at - rank
        grad_ref[rows, pl.ds(rank_at, rank + rest)] = jnp.concatenate(
            [grad_lowrank, jnp.zeros((length, rest), F32)], axis=1
        ).astype(BF16)
        return carry

    lax.fori_loop(0, count, mix, 0)
    finish_states(count, last, target, send_ref, recv_ref, send_sem, recv_sem)


def state_scratch(count, value_dim, key_dim):
    return [
        pltpu.VMEM((count, value_dim, key_dim), F32),
        pltpu.VMEM((count, value_dim, key_dim), BF16),
        pltpu.VMEM((count, value_dim, key_dim), BF16),
        pltpu.SemaphoreType.DMA((count, PIECES)),
        pltpu.SemaphoreType.DMA((count, PIECES)),
    ]


def kernel_params(number, mebibytes=44):
    return pltpu.CompilerParams(
        collective_id=number, has_side_effects=True, vmem_limit_bytes=mebibytes * 2**20
    )


def head_copy(src, dst, send_sem, recv_sem, target):
    return pltpu.make_async_remote_copy(
        src_ref=src,
        dst_ref=dst,
        send_sem=send_sem,
        recv_sem=recv_sem,
        device_id={"head": target},
        device_id_type=pl.DeviceIdType.MESH,
    )


def greet_heads(targets):
    barrier = pltpu.get_barrier_semaphore()
    for target in targets:
        pl.semaphore_signal(
            barrier, inc=1, device_id={"head": target}, device_id_type=pl.DeviceIdType.MESH
        )
    pl.semaphore_wait(barrier, len(targets))


def square(me):
    return me + 1 - 2 * lax.rem(me, 2), me + 2 - 4 * (me // 2), H - 1 - me


def move_columns(weights, gain, out_ref, send_ref, send_sem, recv_sem, own_sem):
    me = lax.axis_index("head")
    place = 0
    for w in weights:
        n = w.shape[1] // H
        for h in range(H):
            part = w[:, pl.ds(h * n, n)].astype(F32) * gain
            send_ref[h, :, pl.ds(place, n)] = part.astype(BF16)
        place += n
    copies = []
    for ahead in range(1, H):
        peer = lax.rem(me + ahead, H)
        copy = head_copy(
            send_ref.at[peer],
            out_ref.at[me],
            send_sem.at[ahead],
            recv_sem.at[ahead],
            peer,
        )
        copy.start()
        copies.append(copy)
    own = pltpu.make_async_copy(send_ref.at[me], out_ref.at[me], own_sem)
    own.start()
    return copies + [own]


def mix_weights_kernel(*refs):
    *weights, extra_ref, gain_ref, out_ref, send_ref, send_sem, recv_sem, own_sem = refs
    me = lax.axis_index("head")
    greet_heads([lax.rem(me + ahead, H) for ahead in range(1, H)])
    spare = extra_ref.shape[1]
    for h in range(H):
        send_ref[h, :, pl.ds(send_ref.shape[2] - spare, spare)] = extra_ref[...]
    gain = gain_ref[...].astype(F32)
    for copy in move_columns(weights, gain, out_ref, send_ref, send_sem, recv_sem, own_sem):
        copy.wait()


def mix_weights(weights, extra, gain):
    rows = extra.shape[0]
    n = sum(w.shape[1] for w in weights) // H + extra.shape[1]
    return pl.pallas_call(
        mix_weights_kernel,
        out_shape=jax.ShapeDtypeStruct((H, rows, n), BF16),
        in_specs=[pl.BlockSpec(memory_space=pltpu.VMEM)] * (len(weights) + 2),
        out_specs=pl.BlockSpec(memory_space=pl.ANY),
        scratch_shapes=[
            pltpu.VMEM((H, rows, n), BF16),
            pltpu.SemaphoreType.DMA((H,)),
            pltpu.SemaphoreType.DMA((H,)),
            pltpu.SemaphoreType.DMA,
        ],
        compiler_params=kernel_params(3, 16),
        cost_estimate=pl.CostEstimate(flops=10**6, bytes_accessed=10**4, transcendentals=0),
        name="mix_weights",
    )(*weights, extra, gain)


class Share:
    def __init__(self, mine_ref, out_ref, send_sem, recv_sem, own_sem):
        self.refs = mine_ref, out_ref, send_sem, recv_sem, own_sem
        self.me = lax.axis_index("head")
        self.size = mine_ref.shape[0] // CHUNKS

    def copy(self, c, kind):
        mine, out, send_sem, recv_sem, _ = self.refs
        sides = square(self.me)[:2]
        rows = pl.ds(c * self.size, self.size)
        if kind < 2:
            src, dst, target = mine.at[rows], out.at[self.me, rows], sides[kind]
        else:
            origin, target = (sides[0], sides[1]) if c % 2 == 0 else (sides[1], sides[0])
            src = dst = out.at[origin, rows]
        return head_copy(src, dst, send_sem.at[c, kind], recv_sem.at[c, kind], target)

    def own(self, c):
        mine, out, _, _, own_sem = self.refs
        rows = pl.ds(c * self.size, self.size)
        return pltpu.make_async_copy(mine.at[rows], out.at[self.me, rows], own_sem.at[c])

    def start(self, c):
        self.copy(c, 0).start()
        self.copy(c, 1).start()
        self.own(c).start()

    def forward(self, c):
        self.copy(c, c % 2).wait_recv()
        self.copy(c, 2).start()

    def finish(self):
        for c in range(CHUNKS):
            self.copy(c, 1 - c % 2).wait_recv()
            self.copy(c, 2).wait_recv()
            self.own(c).wait()
            for kind in range(3):
                self.copy(c, kind).wait_send()


def share_scratch(rows, width):
    return [
        pltpu.VMEM((rows, width), BF16),
        pltpu.SemaphoreType.DMA((CHUNKS, 3)),
        pltpu.SemaphoreType.DMA((CHUNKS, 3)),
        pltpu.SemaphoreType.DMA((CHUNKS,)),
    ]


def share_kernel(
    tokens_ref,
    gate_ref,
    up_ref,
    gain_ref,
    out_ref,
    moved_ref,
    mine_ref,
    share_send,
    share_recv,
    share_own,
    send_ref,
    send_sem,
    recv_sem,
    own_sem,
):
    me = lax.axis_index("head")
    greet_heads([lax.rem(me + ahead, H) for ahead in range(1, H)])
    share = Share(mine_ref, out_ref, share_send, share_recv, share_own)
    for c in range(CHUNKS):
        rows = pl.ds(c * share.size, share.size)
        x = tokens_ref[rows, :].astype(F32)
        mine_ref[rows, :] = (x * rms_scale(x, EPS)).astype(BF16)
        share.start(c)
    gain = gain_ref[...].astype(F32)
    copies = move_columns(
        [gate_ref, up_ref], gain, moved_ref, send_ref, send_sem, recv_sem, own_sem
    )
    for c in range(CHUNKS):
        share.forward(c)
    share.finish()
    for copy in copies:
        copy.wait()


def share_tokens(tokens, w_gate, w_up, gain):
    rows, n = w_gate.shape[0], 2 * w_gate.shape[1] // H
    return pl.pallas_call(
        share_kernel,
        out_shape=[
            jax.ShapeDtypeStruct((H,) + tokens.shape, BF16),
            jax.ShapeDtypeStruct((H, rows, n), BF16),
        ],
        in_specs=[pl.BlockSpec(memory_space=pltpu.VMEM)] * 4,
        out_specs=[pl.BlockSpec(memory_space=pl.ANY)] * 2,
        scratch_shapes=share_scratch(*tokens.shape)
        + [
            pltpu.VMEM((H, rows, n), BF16),
            pltpu.SemaphoreType.DMA((H,)),
            pltpu.SemaphoreType.DMA((H,)),
            pltpu.SemaphoreType.DMA,
        ],
        compiler_params=kernel_params(4, 16),
        cost_estimate=pl.CostEstimate(flops=10**6, bytes_accessed=10**4, transcendentals=0),
        name="share_tokens",
    )(tokens, w_gate, w_up, gain)


def turn_rows(
    partial_ref,
    first_ref,
    relay_ref,
    second_ref,
    pass_ref,
    send_sem,
    recv_sem,
    done,
    share=None,
    fillers=(),
):
    me = lax.axis_index("head")
    side = square(me)
    far = side[2]
    size = first_ref.shape[0] // CHUNKS
    steps = CHUNKS + 3
    fillers = list(fillers)

    def copies(c):
        one, two = (side[0], side[1]) if c % 2 == 0 else (side[1], side[0])
        rows = pl.ds(c * size, size)
        sems = [(send_sem.at[c, kind], recv_sem.at[c, kind]) for kind in range(3)]
        return (
            head_copy(partial_ref.at[far, rows], relay_ref.at[rows], *sems[0], one),
            head_copy(partial_ref.at[one, rows], first_ref.at[rows], *sems[1], one),
            head_copy(pass_ref.at[rows], second_ref.at[rows], *sems[2], two),
            two,
            rows,
        )

    for c in range(CHUNKS):
        relay, first, *_ = copies(c)
        relay.start()
        first.start()
    for step in range(steps):
        for filler in fillers[step * len(fillers) // steps : (step + 1) * len(fillers) // steps]:
            filler()
        if step < CHUNKS:
            relay, _, second, two, rows = copies(step)
            relay.wait_recv()
            both = partial_ref[two, rows, :].astype(F32) + relay_ref[rows, :].astype(F32)
            pass_ref[rows, :] = both.astype(BF16)
            second.start()
        if 1 <= step <= CHUNKS:
            _, first, second, _, rows = copies(step - 1)
            first.wait_recv()
            second.wait_recv()
            total = partial_ref[me, rows, :].astype(F32) + first_ref[rows, :].astype(F32)
            made = done(rows, total + second_ref[rows, :].astype(F32))
            if share is not None:
                share.refs[0][rows, :] = made
                share.start(step - 1)
        if step >= 3 and share is not None:
            share.forward(step - 3)
    if share is not None:
        share.finish()
    for c in range(CHUNKS):
        for copy in copies(c)[:3]:
            copy.wait_send()


def turn_scratch(rows, width):
    return [pltpu.VMEM((rows, width), BF16) for _ in range(4)] + [
        pltpu.SemaphoreType.DMA((CHUNKS, 3)),
        pltpu.SemaphoreType.DMA((CHUNKS, 3)),
    ]


def hidden_kernel(partial_ref, tokens_ref, hidden_ref, out_ref, *scratch):
    greet_heads(square(lax.axis_index("head"))[:2])
    mine_ref, *sems = scratch[6:]

    def done(rows, total):
        hidden = tokens_ref[rows, :].astype(F32) + total
        hidden_ref[rows, :] = hidden
        return (hidden * rms_scale(hidden, EPS)).astype(BF16)

    turn_rows(partial_ref, *scratch[:6], done, Share(mine_ref, out_ref, *sems))


def share_hidden(partial, tokens):
    whole = pl.BlockSpec(memory_space=pltpu.VMEM)
    return pl.pallas_call(
        hidden_kernel,
        out_shape=[
            jax.ShapeDtypeStruct(tokens.shape, F32),
            jax.ShapeDtypeStruct((H,) + tokens.shape, BF16),
        ],
        in_specs=[whole] * 2,
        out_specs=[whole, pl.BlockSpec(memory_space=pl.ANY)],
        scratch_shapes=turn_scratch(*tokens.shape) + share_scratch(*tokens.shape),
        compiler_params=kernel_params(5, 18),
        cost_estimate=pl.CostEstimate(flops=10**6, bytes_accessed=10**4, transcendentals=0),
        name="share_hidden",
    )(partial, tokens)


class PairProduct:
    def __init__(self, left_ref, right_ref, out_ref, give_ref, take_ref, send_sem, recv_sem, own_sem):
        self.refs = left_ref, right_ref, out_ref, give_ref, take_ref
        self.sems = send_sem, recv_sem, own_sem
        self.core = lax.axis_index("core")
        self.groups, self.rows, self.width = out_ref.shape
        self.cut = self.width // 2 if self.width % (2 * LANES) == 0 else self.width

    def product(self, group, core, at):
        left, right, *_ = self.refs
        start = pl.multiple_of((group * CORES + core) * self.rows, LANES)
        return rows_product(left[:, pl.ds(start, self.rows)], right[:, pl.ds(at, self.cut)])

    def copy(self, group):
        give, take = self.refs[3:]
        return pltpu.make_async_remote_copy(
            src_ref=give.at[group],
            dst_ref=take.at[group],
            send_sem=self.sems[0].at[group],
            recv_sem=self.sems[1].at[group],
            device_id={"core": 1 - self.core},
            device_id_type=pl.DeviceIdType.MESH,
        )

    def store(self, group):
        return pltpu.make_async_copy(
            self.refs[3].at[group], self.refs[2].at[group], self.sems[2].at[group]
        )

    def give(self, group, at):
        product = self.product(group, 1 - self.core, at)
        self.refs[3][group, :, pl.ds(at, self.cut)] = product.astype(BF16)
        if at + self.cut == self.width:
            self.copy(group).start()

    def keep(self, group, at):
        give, take = self.refs[3:]
        if at == 0:
            self.copy(group).wait()
        both = self.product(group, self.core, at)
        both += take[group, :, pl.ds(at, self.cut)].astype(F32)
        give[group, :, pl.ds(at, self.cut)] = both.astype(BF16)
        if at + self.cut == self.width:
            self.store(group).start()

    def steps(self):
        places = [
            (group, at) for group in range(self.groups) for at in range(0, self.width, self.cut)
        ]
        return [functools.partial(self.give, *place) for place in places] + [
            functools.partial(self.keep, *place) for place in places
        ]

    def finish(self):
        for group in range(self.groups):
            self.store(group).wait()


def pair_shape(left, right, groups):
    return (groups, left.shape[1] // (CORES * groups), right.shape[1])


def pair_scratch(shape):
    return [
        pltpu.VMEM(shape, BF16),
        pltpu.VMEM(shape, BF16),
        pltpu.SemaphoreType.DMA((shape[0],)),
        pltpu.SemaphoreType.DMA((shape[0],)),
        pltpu.SemaphoreType.DMA((shape[0],)),
    ]


def pair_kernel(moving, left_ref, right_ref, *refs):
    g_ref, out_ref, moved_ref, *scratch = refs if moving else (None, refs[0], None, *refs[1:])
    core = 1 - lax.axis_index("core")
    me = lax.axis_index("head")
    peers = [lax.rem(me + ahead, H) for ahead in range(1, H)] if moving else []
    barrier = pltpu.get_barrier_semaphore()
    for target in [{"core": core}] + [{"head": peer} for peer in peers]:
        pl.semaphore_signal(
            barrier, inc=1, device_id=target, device_id_type=pl.DeviceIdType.MESH
        )
    pl.semaphore_wait(barrier, 1 + len(peers))
    copies = back_copies(g_ref, moved_ref, peers, *scratch[5:]) if moving else []
    for copy in copies:
        copy.start()
    pair = PairProduct(left_ref, right_ref, out_ref, *scratch[:5])
    for step in pair.steps():
        step()
    pair.finish()
    for copy in copies:
        copy.wait()


def pair_product(left, right, groups, number, moving=None):
    shape = pair_shape(left, right, groups)
    whole = pl.BlockSpec(memory_space=pltpu.VMEM)
    hbm = pl.BlockSpec(memory_space=pl.ANY)
    moves = [] if moving is None else [moving]
    return pl.pallas_call(
        functools.partial(pair_kernel, len(moves) > 0),
        out_shape=[jax.ShapeDtypeStruct(shape, BF16)]
        + [jax.ShapeDtypeStruct(m.shape, BF16) for m in moves],
        in_specs=[whole] * 2 + [hbm] * len(moves),
        out_specs=[hbm] * (1 + len(moves)),
        scratch_shapes=pair_scratch(shape) + back_scratch() * len(moves),
        compiler_params=kernel_params(number, 58),
        cost_estimate=pl.CostEstimate(flops=10**6, bytes_accessed=10**4, transcendentals=0),
        name="pair_product",
    )(left, right, *moves)


def branch_kernel(
    partial_ref,
    hidden_ref,
    upstream_ref,
    active_ref,
    down_ref,
    rest_ref,
    grad_ref,
    gain_grad_ref,
    down_out_ref,
    out_ref,
    *scratch,
):
    greet_heads(square(lax.axis_index("head"))[:2])
    mine_ref, *sems = scratch[6:10]
    gain_grad_ref[...] = jnp.zeros_like(gain_grad_ref)

    def done(rows, total):
        hidden = hidden_ref[rows, :]
        scale = rms_scale(hidden, EPS)
        gain_grad_ref[...] += jnp.sum(total * hidden * scale, axis=0, keepdims=True)
        grad = upstream_ref[rows, :].astype(F32) + rms_back(total, hidden, scale)
        grad_ref[rows, :] = grad
        return grad.astype(BF16)

    def down(at):
        rows = pl.ds(at, LANES)
        half = down_ref.shape[1]
        for place, ref in ((0, down_ref), (half, rest_ref)):
            product = matmul(active_ref[rows, :], ref[...])
            down_out_ref[rows, pl.ds(place, half)] = product.astype(BF16)

    share = Share(mine_ref, out_ref, *sems)
    fillers = [functools.partial(down, at) for at in range(0, active_ref.shape[0], LANES)]
    turn_rows(partial_ref, *scratch[:6], done, share, fillers)


def share_branch(partial, hidden, upstream, active, down, rest):
    whole = pl.BlockSpec(memory_space=pltpu.VMEM)
    return pl.pallas_call(
        branch_kernel,
        out_shape=[
            jax.ShapeDtypeStruct(hidden.shape, F32),
            jax.ShapeDtypeStruct((1, hidden.shape[1]), F32),
            jax.ShapeDtypeStruct((active.shape[0], hidden.shape[1]), BF16),
            jax.ShapeDtypeStruct((H,) + hidden.shape, BF16),
        ],
        in_specs=[whole] * 6,
        out_specs=[whole] * 3 + [pl.BlockSpec(memory_space=pl.ANY)],
        scratch_shapes=turn_scratch(*hidden.shape) + share_scratch(*hidden.shape),
        compiler_params=kernel_params(6, 34),
        cost_estimate=pl.CostEstimate(flops=10**6, bytes_accessed=10**4, transcendentals=0),
        name="share_branch",
    )(partial, hidden, upstream, active, down, rest)


def tokens_kernel(partial_ref, tokens_ref, upstream_ref, grad_ref, gain_grad_ref, *scratch):
    greet_heads(square(lax.axis_index("head"))[:2])
    gain_grad_ref[...] = jnp.zeros_like(gain_grad_ref)

    def done(rows, total):
        tokens = tokens_ref[rows, :].astype(F32)
        scale = rms_scale(tokens, EPS)
        gain_grad_ref[...] += jnp.sum(total * tokens * scale, axis=0, keepdims=True)
        grad = upstream_ref[rows, :] + rms_back(total, tokens, scale)
        grad_ref[rows, :] = grad.astype(BF16)

    turn_rows(partial_ref, *scratch, done)


def tokens_back(partial, tokens, upstream):
    whole = pl.BlockSpec(memory_space=pltpu.VMEM)
    return pl.pallas_call(
        tokens_kernel,
        out_shape=[
            jax.ShapeDtypeStruct(tokens.shape, BF16),
            jax.ShapeDtypeStruct((1, tokens.shape[1]), F32),
        ],
        in_specs=[whole] * 3,
        out_specs=[whole] * 2,
        scratch_shapes=turn_scratch(*tokens.shape),
        compiler_params=kernel_params(8, 18),
        cost_estimate=pl.CostEstimate(flops=10**6, bytes_accessed=10**4, transcendentals=0),
        name="tokens_back",
    )(partial, tokens, upstream)


def hidden_units_kernel(cot_ref, down_ref, rest_ref, pre_ref, out_ref):
    units, half = down_ref.shape
    grad = back_product(cot_ref[:, pl.ds(0, half)], down_ref[...])
    grad += back_product(cot_ref[:, pl.ds(half, half)], rest_ref[...])
    gate, up = pre_ref[:, pl.ds(0, units)], pre_ref[:, pl.ds(units, units)]
    sig = jax.nn.sigmoid(gate)
    grad_sig = grad * sig
    out_ref[:, pl.ds(0, units)] = (grad_sig * up * (1.0 + gate * (1.0 - sig))).astype(BF16)
    out_ref[:, pl.ds(units, units)] = (grad_sig * gate).astype(BF16)


def hidden_units_back(cot, down, rest, pre):
    rows, width = cot.shape
    size = 2 * LANES

    def rows_block(n):
        return pl.BlockSpec((size, n), lambda i: (i, 0))

    return pl.pallas_call(
        hidden_units_kernel,
        grid=(rows // size,),
        out_shape=jax.ShapeDtypeStruct(pre.shape, BF16),
        in_specs=[
            rows_block(width),
            pl.BlockSpec(down.shape, lambda i: (0, 0)),
            pl.BlockSpec(rest.shape, lambda i: (0, 0)),
            rows_block(pre.shape[1]),
        ],
        out_specs=rows_block(pre.shape[1]),
        compiler_params=pltpu.CompilerParams(vmem_limit_bytes=58 * 2**20),
        cost_estimate=pl.CostEstimate(flops=10**6, bytes_accessed=10**4, transcendentals=0),
        name="hidden_units_back",
    )(cot, down, rest, pre)


def back_copies(g_ref, out_ref, peers, send_sem, recv_sem, own_sem):
    me = lax.axis_index("head")
    copies = [
        head_copy(g_ref.at[peer], out_ref.at[me], send_sem.at[ahead], recv_sem.at[ahead], peer)
        for ahead, peer in enumerate(peers)
    ]
    return copies + [pltpu.make_async_copy(g_ref.at[me], out_ref.at[me], own_sem)]


def back_scratch():
    return [pltpu.SemaphoreType.DMA((H,)), pltpu.SemaphoreType.DMA((H,)), pltpu.SemaphoreType.DMA]


def mix_forward(mixed, bias, gaterank, gain, marks, segment, sums, pairs, key_dim, value_dim):
    rows = mixed.shape[0]
    count, _, length = segment.shape
    shapes = (
        ((rows, value_dim), BF16),
        ((rows, value_dim), F32),
        ((rows, key_dim), F32),
        ((count, length, length), BF16),
        ((rows, key_dim), BF16),
        ((rows, key_dim), BF16),
        ((count, 1, key_dim), F32),
        ((count, value_dim, key_dim), BF16),
    )
    whole = pl.BlockSpec(memory_space=pltpu.VMEM)
    return pl.pallas_call(
        functools.partial(forward_kernel, key_dim, value_dim),
        out_shape=[jax.ShapeDtypeStruct(*s) for s in shapes],
        in_specs=[pl.BlockSpec(memory_space=pl.ANY)] + [whole] * 7,
        out_specs=[whole] + [pl.BlockSpec(memory_space=pl.ANY)] * (len(shapes) - 1),
        scratch_shapes=[pltpu.VMEM(*s) for s in shapes[1:-1]]
        + state_scratch(count, value_dim, key_dim)
        + [
            pltpu.SemaphoreType.DMA((count, 7)),
            pltpu.VMEM(mixed.shape, mixed.dtype),
            pltpu.SemaphoreType.DMA((count,)),
        ],
        compiler_params=kernel_params(1, 58),
        cost_estimate=pl.CostEstimate(flops=10**6, bytes_accessed=10**4, transcendentals=0),
        name="mix_forward",
    )(mixed, bias, gaterank, gain, marks, segment, sums, pairs)


def mix_backward(
    mixed, kept, upstream, gaterank, gain, marks, segment, sums, pairs, key_dim, value_dim
):
    rows = mixed.shape[0]
    count = segment.shape[0]
    shapes = (
        (mixed.shape, BF16),
        ((1, value_dim), F32),
        ((1, key_dim), F32),
        (gaterank.shape, F32),
    )
    attended, logits, scores, start, end, decay, enter = kept
    given = (mixed, upstream, attended, start, logits, scores, end, decay, enter)
    whole = pl.BlockSpec(memory_space=pltpu.VMEM)
    return pl.pallas_call(
        functools.partial(backward_kernel, key_dim, value_dim),
        out_shape=[jax.ShapeDtypeStruct(*s) for s in shapes],
        in_specs=[pl.BlockSpec(memory_space=pl.ANY)] * 9 + [whole] * 6,
        out_specs=[whole] * len(shapes),
        scratch_shapes=[pltpu.VMEM(a.shape, a.dtype) for a in given]
        + [pltpu.VMEM((rows, value_dim), BF16)]
        + state_scratch(count, value_dim, key_dim)
        + [pltpu.SemaphoreType.DMA((count, 9))],
        compiler_params=kernel_params(2, 58),
        cost_estimate=pl.CostEstimate(flops=10**6, bytes_accessed=10**4, transcendentals=0),
        name="mix_backward",
    )(
        *given,
        gaterank,
        gain,
        marks,
        segment,
        sums,
        pairs,
    )


def per_device(
    tokens,
    doc_lengths,
    norm_gain,
    w_query,
    w_key,
    w_value,
    w_outgate,
    w_lowrank,
    w_gaterank,
    gate_bias,
    head_gain,
    w_output,
    ffn_gain,
    w_gate,
    w_up,
    w_down,
    cotangent,
):
    seqs_here, length, width = tokens.shape
    reps = lax.axis_size("rep")
    parts = lax.axis_size("fsdp")
    devices = reps * H * CORES * parts
    here = lax.axis_index("head")
    key_dim, value_dim = DK, DV
    rank = w_lowrank.shape[1]
    rows = width // devices
    count = H * seqs_here

    rank_at = 2 * key_dim + 2 * value_dim

    def core_sum(g):
        halves = g.reshape(g.shape[0], CORES, -1, g.shape[-1])
        core = lax.axis_index("core")
        other = lax.ppermute(halves[:, 1 - core], "core", ((0, 1), (1, 0)))
        return (halves[:, core].astype(F32) + other.astype(F32)).astype(BF16)

    def scatter_rows(g):
        if reps > 1:
            g = lax.psum_scatter(g, "rep", scatter_dimension=0, tiled=True)
        return lax.psum_scatter(g, "fsdp", scatter_dimension=1, tiled=True)

    def gather_columns(moved):
        whole = lax.all_gather(moved, ("core", "fsdp"), axis=1, tiled=True)
        if reps > 1:
            whole = lax.all_gather(whole, "rep", axis=0, tiled=False)
        return whole.reshape(width, -1)

    def gather_part(w):
        if reps == 1:
            return lax.all_gather(w, SHARE, axis=0, tiled=True)
        whole = lax.all_gather(w, EVERY, axis=0, tiled=True)
        size = whole.shape[0] // H
        return lax.dynamic_slice_in_dim(whole, here * size, size, 0)

    def pair_part(g):
        return core_sum(g[None])[0] if reps == 1 else g

    def scatter_part(g):
        if reps == 1:
            return lax.psum_scatter(g, "fsdp", scatter_dimension=0, tiled=True)
        whole = jnp.zeros((H * g.shape[0], g.shape[1]), BF16)
        whole = lax.dynamic_update_slice_in_dim(whole, g, here * g.shape[0], 0)
        return lax.psum_scatter(whole, EVERY, scatter_dimension=0, tiled=True)

    rank_at = 2 * key_dim + 2 * value_dim

    def with_gain(w, gain):
        return (w.astype(F32) * gain.astype(F32)[:, None]).astype(BF16)

    small = (
        w_gaterank,
        gate_bias.reshape(1, -1),
        head_gain.reshape(1, -1),
        (doc_lengths // 16).astype(BF16).reshape(1, -1),
        (doc_lengths % 16).astype(BF16).reshape(1, -1),
    )
    edges = [rank]
    extra = jnp.pad(with_gain(w_lowrank, norm_gain), ((0, 0), (0, LANES - rank)))
    for piece in small:
        high, wide = piece.shape
        extra += jnp.pad(piece, ((0, rows - high), (edges[-1], LANES - edges[-1] - wide)))
        edges.append(edges[-1] + wide)

    mix_moved = mix_weights((w_query, w_key, w_value, w_outgate), extra, norm_gain[:, None])
    inputs = tokens.reshape(-1, width)
    inputs, _ = after(inputs, mix_moved)
    output_w = gather_part(w_output)
    mix_moved, output_w = after(mix_moved, output_w)
    mix_w = gather_columns(mix_moved)
    w_down, _ = after(w_down, mix_moved)
    down_w = gather_part(w_down[:, : width // 2])
    normed, ffn_moved = share_tokens(inputs, w_gate, w_up, ffn_gain[:, None])
    normed = normed.reshape(-1, width)

    small = mix_w[:, rank_at:].astype(F32).reshape(devices, rows, LANES)
    gaterank, bias, gain_head, long, short = (
        small[:, : rank if i == 0 else 1, edges[i] : edges[i + 1]] for i in range(len(edges) - 1)
    )
    gaterank = gaterank.transpose(1, 0, 2).reshape(rank, -1)
    bias = lax.dynamic_slice_in_dim(bias.reshape(1, -1), here * key_dim, key_dim, 1)
    gaterank = lax.dynamic_slice_in_dim(gaterank, here * key_dim, key_dim, 1)
    gain_head = gain_head.reshape(1, -1)
    lengths = (long * 16.0 + short).reshape(reps, H, CORES, parts, seqs_here, DOCS)
    lengths = lengths[lax.axis_index("rep"), :, lax.axis_index("core"), 0]
    lengths = lengths.reshape(count, DOCS).astype(jnp.int32)

    offset = lax.axis_index("fsdp") * length
    doc_ends = jnp.cumsum(lengths, axis=-1)
    places = offset + jnp.arange(length, dtype=jnp.int32)
    segment = jnp.sum((places[None, :, None] >= doc_ends[:, None, :]).astype(jnp.int32), axis=-1)
    before = jnp.sum((offset - 1 >= doc_ends).astype(jnp.int32), axis=-1)[:, None]
    last = segment[:, -1:]
    marks = jnp.stack(
        [
            segment,
            segment == before,
            segment == last,
            segment != DOCS - 1,
            jnp.broadcast_to(last == before, segment.shape),
        ],
        axis=2,
    )
    marks = jnp.pad(marks.astype(F32).reshape(count * length, 5), ((0, 0), (0, 3)))
    segment = segment.astype(F32).reshape(count, 1, length)

    mixed = matmul(normed, mix_w)
    sums, pairs = level_sums(length)
    sums, pairs = sums.astype(BF16), pairs.astype(BF16)
    gated, *kept = mix_forward(
        mixed, bias, gaterank, gain_head, marks, segment, sums, pairs, key_dim, value_dim
    )
    cot_rows, _ = after(cotangent.reshape(-1, width), normed)
    gated, cot_shared, down_w = after(gated, share_rows(cot_rows), down_w)
    ffn_moved, w_down_rest, _ = after(ffn_moved, w_down[:, width // 2 :], gated)
    ffn_w = gather_columns(ffn_moved)
    down_rest = gather_part(w_down_rest)
    partial = matmul(gated, output_w).astype(BF16).reshape(H, -1, width)
    hidden, normed_two = share_hidden(partial, inputs)
    normed_two = normed_two.reshape(-1, width)

    pre = matmul(normed_two, ffn_w)
    gate_pre, up_pre = jnp.split(pre, 2, axis=1)
    sig_gate = jax.nn.sigmoid(gate_pre)
    activated = (gate_pre * sig_gate * up_pre).astype(BF16)

    grad_down_w = rows_product(activated, cot_shared).astype(BF16)
    down_w, grad_down_w = after(down_w, grad_down_w)
    grad_pre = hidden_units_back(cot_shared, down_w, down_rest, pre)
    grad_pre, grad_down_w = after(grad_pre, pair_part(grad_down_w))
    grad_down_w = scatter_part(grad_down_w)
    (grad_ffn_w,) = pair_product(normed_two, grad_pre, reps * H, 7)
    grad_pre, grad_ffn_w = after(grad_pre, grad_ffn_w)
    partial = back_product(grad_pre, ffn_w).astype(BF16)

    grad_hidden, grad_gain_two, down_partial, branch = share_branch(
        partial.reshape(H, -1, width), hidden, cot_rows, activated, down_w, down_rest
    )
    grad_ffn_w = scatter_rows(grad_ffn_w)
    branch = branch.reshape(-1, width)
    grad_gated = back_product(branch, output_w)
    gated, grad_gated = after(gated, grad_gated)
    grad_output_w = pair_part(rows_product(gated, branch).astype(BF16))
    grad_gated, grad_output_w, grad_down_w = after(grad_gated, grad_output_w, grad_down_w)
    grad_output_w = scatter_part(grad_output_w)
    pieces = move_rows(down_partial)
    grad_mixed, grad_gain_head, grad_bias, grad_gaterank = mix_backward(
        mixed,
        kept,
        grad_gated,
        gaterank,
        gain_head,
        marks,
        segment,
        sums,
        pairs,
        key_dim,
        value_dim,
    )
    grad_mixed, pieces, grad_down_w, grad_ffn_w = after(
        grad_mixed, pieces, grad_down_w, grad_ffn_w
    )
    output = (hidden + jnp.sum(pieces.astype(F32), axis=0)).astype(BF16).reshape(tokens.shape)
    grad_mix_w, grad_ffn_w = pair_product(normed, grad_mixed, reps * H, 11, grad_ffn_w)
    grad_mixed, grad_mix_w = after(grad_mixed, grad_mix_w)
    partial = back_product(grad_mixed, mix_w).astype(BF16)
    grad_mix_w = scatter_rows(grad_mix_w)
    partial, grad_output_w = after(partial, grad_output_w)
    tokens_grad, grad_gain_one = tokens_back(partial.reshape(H, -1, width), inputs, grad_hidden)
    tokens_grad = tokens_grad.reshape(tokens.shape)

    def weight_grad(moved, gain, start, w):
        n = w.shape[1] // H
        whole = moved[:, :, start : start + n].transpose(1, 0, 2).reshape(rows, -1)
        return whole.astype(F32) * gain.astype(F32)[:, None]

    w_gate_grad = weight_grad(grad_ffn_w, ffn_gain, 0, w_gate)
    w_up_grad = weight_grad(grad_ffn_w, ffn_gain, w_gate.shape[1] // H, w_up)
    grad_mix_w = lax.all_to_all(grad_mix_w, "head", split_axis=0, concat_axis=0, tiled=True)
    query_g = weight_grad(grad_mix_w, norm_gain, 0, w_query)
    key_g = weight_grad(grad_mix_w, norm_gain, key_dim, w_key)
    value_g = weight_grad(grad_mix_w, norm_gain, 2 * key_dim, w_value)
    outgate_g = weight_grad(grad_mix_w, norm_gain, 2 * key_dim + value_dim, w_outgate)
    lowrank_g = grad_mix_w[:, :, rank_at : rank_at + rank].astype(F32)
    lowrank_g = jnp.sum(lowrank_g, axis=0) * norm_gain.astype(F32)[:, None]

    def place(g, axis):
        shape = list(g.shape)
        shape[axis] *= H
        return lax.dynamic_update_slice_in_dim(jnp.zeros(shape, F32), g, here * key_dim, axis)

    small_grads = jnp.concatenate(
        [
            grad_gain_one.reshape(devices, -1),
            grad_gain_two.reshape(devices, -1),
            place(grad_bias.reshape(-1), 0).reshape(devices, -1),
            grad_gain_head.reshape(devices, -1),
            place(grad_gaterank, 1)
            .reshape(rank, devices, -1)
            .transpose(1, 0, 2)
            .reshape(devices, -1),
        ],
        axis=1,
    )
    small_grads = lax.all_to_all(small_grads, EVERY, split_axis=0, concat_axis=0, tiled=True)
    small_grads = jnp.sum(small_grads, axis=0)
    sizes = [norm_gain.shape[0], ffn_gain.shape[0], gate_bias.shape[0], head_gain.shape[0]]
    norm_g, ffn_g, bias_g, head_g, gaterank_g = jnp.split(
        small_grads, [sum(sizes[: i + 1]) for i in range(len(sizes))]
    )
    return (
        output,
        tokens_grad,
        norm_g / norm_gain.astype(F32),
        query_g,
        key_g,
        value_g,
        outgate_g,
        lowrank_g,
        gaterank_g.reshape(w_gaterank.shape),
        bias_g,
        head_g,
        grad_output_w.astype(F32),
        ffn_g / ffn_gain.astype(F32),
        w_gate_grad,
        w_up_grad,
        grad_down_w.astype(F32),
    )


def solution(mesh):
    dp, parts = mesh.shape["dp"], mesh.shape["fsdp"]
    fine = Mesh(mesh.devices.reshape(dp // (H * CORES), H, CORES, parts), EVERY)
    seq = ("rep", "head", "core")
    rows, vector = P(EVERY, None), P(EVERY)
    activations = P(seq, "fsdp", None)
    columns = P(None, EVERY)
    return jax.shard_map(
        per_device,
        mesh=fine,
        in_specs=(
            activations,
            P(seq, None),
            vector,
            rows,
            rows,
            rows,
            rows,
            rows,
            columns,
            vector,
            vector,
            rows,
            vector,
            rows,
            rows,
            rows,
            activations,
        ),
        out_specs=(
            activations,
            activations,
            vector,
            rows,
            rows,
            rows,
            rows,
            rows,
            columns,
            vector,
            vector,
            rows,
            vector,
            rows,
            rows,
            rows,
        ),
        check_vma=False,
    )
```

```python
import functools

import jax
import jax.experimental.pallas as pl
import jax.experimental.pallas.tpu as pltpu
import jax.numpy as jnp
from jax import lax
from jax.sharding import Mesh
from jax.sharding import PartitionSpec as P

H = 4
DK = 256
DV = 512
CORES = 2
DOCS = 8
PIECES = 4
LANES = 128
CHUNKS = 8

EPS = 1e-05
HEAD_EPS = 1.0
HIGHEST = lax.Precision.HIGHEST
F32 = jnp.float32
BF16 = jnp.bfloat16

SHARE = ("rep", "core", "fsdp")
EVERY = ("rep", "head", "core", "fsdp")


def dot(a, b, dims, precision=None):
    return lax.dot_general(a, b, (dims, ((), ())), precision=precision, preferred_element_type=F32)


def after(value, *others):
    return lax.optimization_barrier((value,) + others)


def matmul(a, b):
    return dot(a, b, ((1,), (0,)))


def rows_product(a, b):
    return dot(a, b, ((0,), (0,)))


def back_product(a, b):
    return dot(a, b, ((1,), (1,)))


def batched(form, a, b):
    return jnp.einsum(form, a, b, preferred_element_type=F32)


def rms_scale(values, epsilon):
    return lax.rsqrt(jnp.mean(values * values, axis=-1, keepdims=True) + epsilon)


def rms_back(upstream, values, scale):
    return scale * upstream - values * scale**3 * jnp.mean(upstream * values, axis=-1, keepdims=True)


def share_rows(part):
    spread = jnp.broadcast_to(part[None], (H,) + part.shape)
    whole = lax.all_to_all(spread, "head", split_axis=0, concat_axis=0, tiled=True)
    return whole.reshape(-1, part.shape[-1])


def move_rows(partial):
    pieces = partial.astype(BF16).reshape(H, -1, partial.shape[-1])
    return lax.all_to_all(pieces, "head", split_axis=0, concat_axis=0, tiled=True)


def sum_rows(partial):
    return jnp.sum(move_rows(partial).astype(F32), axis=0)


def level_sums(length):
    rows = jnp.arange(length)[:, None]
    cols = jnp.arange(length)[None, :]
    sums, pairs = [], []
    step = 1
    while step < length:
        bound = rows // (2 * step) * (2 * step) + step - 1
        upper = rows > bound
        sums.append(jnp.where(upper, (cols > bound) & (cols <= rows), (cols > rows) & (cols <= bound)))
        pairs.append(upper & (cols // (2 * step) == rows // (2 * step)) & (cols <= bound))
        step *= 2
    sums.append(cols <= rows)
    sums.append(cols > rows)
    return jnp.stack(sums), jnp.stack(pairs)


def log_sigmoid(x):
    return jnp.minimum(x, 0.0) - jnp.log1p(jnp.exp(-jnp.abs(x)))


def state_copy(send, recv, send_sem, recv_sem, seq, piece, target):
    size = send.shape[1] // PIECES
    part = pl.ds(piece * size, size)
    return pltpu.make_async_remote_copy(
        src_ref=send.at[seq, part],
        dst_ref=recv.at[seq, part],
        send_sem=send_sem.at[seq, piece],
        recv_sem=recv_sem.at[seq, piece],
        device_id={"fsdp": target},
        device_id_type=pl.DeviceIdType.MESH,
    )


def greet_neighbours(place, parts):
    barrier = pltpu.get_barrier_semaphore()
    for near, there in ((place - 1, place > 0), (place + 1, place < parts - 1)):

        @pl.when(there)
        def _(near=near):
            pl.semaphore_signal(
                barrier,
                inc=1,
                device_id={"fsdp": lax.rem(near + parts, parts)},
                device_id_type=pl.DeviceIdType.MESH,
            )

    peers = (place > 0).astype(jnp.int32) + (place < parts - 1).astype(jnp.int32)
    pl.semaphore_wait(barrier, peers)


def pass_state(s, first, last, target, decay, local, send, recv, send_sem, recv_sem):
    size = send.shape[1] // PIECES
    for piece in range(PIECES):
        part = pl.ds(piece * size, size)
        copy = state_copy(send, recv, send_sem, recv_sem, s, piece, target)

        @pl.when(jnp.logical_not(first))
        def _(copy=copy):
            copy.wait_recv()

        @pl.when(jnp.logical_not(jnp.logical_or(first, last)))
        def _(copy=copy, part=part):
            joined = decay * recv[s, part].astype(F32) + local[s, part]
            send[s, part] = joined.astype(BF16)
            copy.start()


def start_state(s, first, last, target, local, send, recv, send_sem, recv_sem):
    @pl.when(jnp.logical_and(first, jnp.logical_not(last)))
    def _():
        send[s] = local[s].astype(BF16)
        for piece in range(PIECES):
            state_copy(send, recv, send_sem, recv_sem, s, piece, target).start()


def finish_states(count, last, target, send, recv, send_sem, recv_sem):
    @pl.when(jnp.logical_not(last))
    def _():
        def one(s, carry):
            for piece in range(PIECES):
                state_copy(send, recv, send_sem, recv_sem, s, piece, target).wait_send()
            return carry

        lax.fori_loop(0, count, one, 0)


def split_rates(logits):
    rates = log_sigmoid(logits) / 16.0
    high = rates.astype(BF16)
    return high, (rates - high.astype(F32)).astype(BF16)


def decayed(sums, high, low):
    return jnp.exp(matmul(sums, high) + matmul(sums, low))


def forward_kernel(
    key_dim,
    value_dim,
    given_ref,
    bias_ref,
    gaterank_ref,
    gain_ref,
    marks_ref,
    segment_ref,
    sums_ref,
    pairs_ref,
    gated_ref,
    *refs,
):
    kept, (attended_ref, logits_ref, scores_ref, start_ref, end_ref, decay_ref) = refs[:7], refs[7:13]
    local_ref, send_ref, recv_ref, send_sem, recv_sem, keep_sem, mixed_ref, take_sem = refs[13:]
    count, _, length = segment_ref.shape
    levels = pairs_ref.shape[0]
    parts, place = lax.axis_size("fsdp"), lax.axis_index("fsdp")
    first, last, target = place == 0, place == parts - 1, lax.rem(place + 1, parts)

    def rows_of(s):
        return pl.ds(pl.multiple_of(s * length, length), length)

    def keeps(s, kinds):
        held = (attended_ref, logits_ref, scores_ref, start_ref, end_ref, decay_ref, recv_ref)
        rows = rows_of(s)
        for kind in kinds:
            at = rows if len(held[kind].shape) == 2 else s
            yield pltpu.make_async_copy(held[kind].at[at], kept[kind].at[at], keep_sem.at[s, kind])

    def take(s):
        rows = rows_of(s)
        return pltpu.make_async_copy(given_ref.at[rows], mixed_ref.at[rows], take_sem.at[s])

    def start_take(s, carry):
        take(s).start()
        return carry

    lax.fori_loop(0, count, start_take, 0)

    def finish_keeps(s, carry):
        for copy in keeps(s, range(7)):
            copy.wait()
        return carry

    rank = gaterank_ref.shape[0]
    scale = key_dim ** (-0.5)
    value_at = 2 * key_dim
    gate_at = value_at + value_dim
    rank_at = gate_at + value_dim

    greet_neighbours(place, parts)

    @pl.when(first)
    def _():
        recv_ref[...] = jnp.zeros_like(recv_ref)

    def ends(s, carry):
        rows = rows_of(s)
        take(s).wait()
        lowrank = mixed_ref[rows, pl.ds(rank_at, rank)]
        logits = dot(lowrank, gaterank_ref[...], ((1,), (0,)), HIGHEST) + bias_ref[...]
        logits_ref[rows, :] = logits
        high, low = split_rates(logits)
        from_start = decayed(sums_ref[levels], high, low)
        to_end = decayed(sums_ref[levels + 1], high, low)
        marks = marks_ref[rows, :]
        decay_ref[s] = from_start[length - 1 :, :] * marks[:1, 4:5]
        query = mixed_ref[rows, pl.ds(0, key_dim)] * scale
        key = mixed_ref[rows, pl.ds(key_dim, key_dim)]
        start_ref[rows, :] = (query * (from_start * marks[:, 1:2])).astype(BF16)
        end_key = (key * (to_end * marks[:, 2:3])).astype(BF16)
        end_ref[rows, :] = end_key
        value = mixed_ref[rows, pl.ds(value_at, value_dim)].astype(BF16)
        local_ref[s] = rows_product(value, end_key)
        start_state(s, first, last, target, local_ref, send_ref, recv_ref, send_sem, recv_sem)
        for copy in keeps(s, (1, 3, 4, 5)):
            copy.start()
        return carry

    lax.fori_loop(0, count, ends, 0)

    def mix(s, carry):
        rows = rows_of(s)
        pass_state(
            s, first, last, target, decay_ref[s], local_ref, send_ref, recv_ref, send_sem, recv_sem
        )
        query = mixed_ref[rows, pl.ds(0, key_dim)] * scale
        key = mixed_ref[rows, pl.ds(key_dim, key_dim)]
        high, low = split_rates(logits_ref[rows, :])
        scores = jnp.zeros((length, length), F32)
        for level in range(levels):
            decay = decayed(sums_ref[level], high, low)
            pair = back_product((query * decay).astype(BF16), (key * decay).astype(BF16))
            scores += pair * pairs_ref[level].astype(F32)
        row = lax.broadcasted_iota(jnp.int32, (length, length), 0)
        col = lax.broadcasted_iota(jnp.int32, (length, length), 1)
        own = jnp.sum(query * key, axis=1, keepdims=True)
        scores += jnp.where(row == col, own, 0.0)
        marks = marks_ref[rows, :]
        scores = jnp.where(marks[:, 0:1] == segment_ref[s], scores, 0.0).astype(BF16)
        scores_ref[s] = scores
        value = mixed_ref[rows, pl.ds(value_at, value_dim)].astype(BF16)
        attended = matmul(scores, value) + back_product(start_ref[rows, :], recv_ref[s])
        attended = attended * marks[:, 3:4]
        attended_ref[rows, :] = attended
        headed = attended * rms_scale(attended, HEAD_EPS) * gain_ref[...]
        outgate = mixed_ref[rows, pl.ds(gate_at, value_dim)]
        gated_ref[rows, :] = (headed * (outgate * jax.nn.sigmoid(outgate))).astype(BF16)
        for copy in keeps(s, (0, 2, 6)):
            copy.start()
        return carry

    lax.fori_loop(0, count, mix, 0)
    finish_states(count, last, target, send_ref, recv_ref, send_sem, recv_sem)
    lax.fori_loop(0, count, finish_keeps, 0)


def backward_kernel(
    key_dim,
    value_dim,
    *refs,
):
    given, refs = refs[:9], refs[9:]
    gaterank_ref, gain_ref, marks_ref, segment_ref, sums_ref, pairs_ref, *refs = refs
    grad_ref, gain_grad_ref, bias_grad_ref, gaterank_grad_ref, *refs = refs
    held, refs = refs[:9], refs[9:]
    mixed_ref, upstream_ref, attended_ref, start_ref, *rest_refs = held
    logits_ref, scores_ref, end_ref, decay_ref, enter_ref = rest_refs
    out_ref, local_ref, send_ref, recv_ref, send_sem, recv_sem, take_sem = refs
    count, _, length = segment_ref.shape

    def rows_of(s):
        return pl.ds(pl.multiple_of(s * length, length), length)

    def takes(s, kinds):
        rows = rows_of(s)
        for kind in kinds:
            at = rows if len(held[kind].shape) == 2 else s
            yield pltpu.make_async_copy(given[kind].at[at], held[kind].at[at], take_sem.at[s, kind])

    def start_takes(s, carry):
        for copy in takes(s, range(9)):
            copy.start()
        return carry

    lax.fori_loop(0, count, start_takes, 0)
    levels = pairs_ref.shape[0]
    parts, place = lax.axis_size("fsdp"), lax.axis_index("fsdp")
    first, last, target = place == parts - 1, place == 0, lax.rem(place + parts - 1, parts)
    rank = gaterank_ref.shape[0]
    scale = key_dim ** (-0.5)
    value_at = 2 * key_dim
    gate_at = value_at + value_dim
    rank_at = gate_at + value_dim

    greet_neighbours(place, parts)

    @pl.when(first)
    def _():
        recv_ref[...] = jnp.zeros_like(recv_ref)

    gain_grad_ref[...] = jnp.zeros_like(gain_grad_ref)
    bias_grad_ref[...] = jnp.zeros_like(bias_grad_ref)
    gaterank_grad_ref[...] = jnp.zeros_like(gaterank_grad_ref)

    def heads(s, carry):
        rows = rows_of(s)
        for copy in takes(s, range(4)):
            copy.wait()
        upstream = upstream_ref[rows, :]
        attended = attended_ref[rows, :]
        outgate = mixed_ref[rows, pl.ds(gate_at, value_dim)]
        gain = gain_ref[...]
        norm = rms_scale(attended, HEAD_EPS)
        normed = attended * norm
        sig = jax.nn.sigmoid(outgate)
        grad_gate = upstream * (normed * gain) * sig * (1.0 + outgate * (1.0 - sig))
        grad_ref[rows, pl.ds(gate_at, value_dim)] = grad_gate.astype(BF16)
        grad_headed = upstream * (outgate * sig)
        gain_grad_ref[...] += jnp.sum(grad_headed * normed, axis=0, keepdims=True)
        grad_out = rms_back(grad_headed * gain, attended, norm) * marks_ref[rows, pl.ds(3, 1)]
        grad_out = grad_out.astype(BF16)
        out_ref[rows, :] = grad_out
        local_ref[s] = rows_product(grad_out, start_ref[rows, :])
        start_state(s, first, last, target, local_ref, send_ref, recv_ref, send_sem, recv_sem)
        return carry

    lax.fori_loop(0, count, heads, 0)

    def mix(s, carry):
        rows = rows_of(s)
        for copy in takes(s, range(4, 9)):
            copy.wait()
        decay_row = decay_ref[s]
        pass_state(
            s, first, last, target, decay_row, local_ref, send_ref, recv_ref, send_sem, recv_sem
        )
        query = mixed_ref[rows, pl.ds(0, key_dim)] * scale
        key = mixed_ref[rows, pl.ds(key_dim, key_dim)]
        value = mixed_ref[rows, pl.ds(value_at, value_dim)].astype(BF16)
        marks = marks_ref[rows, :]
        logits = logits_ref[rows, :]
        high, low = split_rates(logits)
        grad_out = out_ref[rows, :]
        row = lax.broadcasted_iota(jnp.int32, (length, length), 0)
        col = lax.broadcasted_iota(jnp.int32, (length, length), 1)
        pair_grads = back_product(grad_out, value)
        pair_grads = jnp.where(marks[:, 0:1] == segment_ref[s], pair_grads, 0.0)
        own = jnp.sum(jnp.where(row == col, pair_grads, 0.0), axis=1, keepdims=True)
        grad_query = own * key
        grad_key = own * query
        grad_rates = jnp.zeros((length, key_dim), F32)
        for level in range(levels):
            decay = decayed(sums_ref[level], high, low)
            level_query = (query * decay).astype(BF16)
            level_key = (key * decay).astype(BF16)
            level_pairs = (pair_grads * pairs_ref[level].astype(F32)).astype(BF16)
            level_grad_query = matmul(level_pairs, level_key)
            level_grad_key = rows_product(level_pairs, level_query)
            grad_query += level_grad_query * decay
            grad_key += level_grad_key * decay
            flow = level_grad_query * level_query.astype(F32)
            flow += level_grad_key * level_key.astype(F32)
            grad_rates += rows_product(sums_ref[level], flow.astype(BF16))
        ending = recv_ref[s]
        entering = enter_ref[s]
        start_query = start_ref[rows, :]
        end_key = end_ref[rows, :]
        start_grad = matmul(grad_out, entering)
        end_grad = matmul(value, ending)
        grad_query += start_grad * (decayed(sums_ref[levels], high, low) * marks[:, 1:2])
        grad_key += end_grad * (decayed(sums_ref[levels + 1], high, low) * marks[:, 2:3])
        grad_rates += rows_product(
            sums_ref[levels], (start_grad * start_query.astype(F32)).astype(BF16)
        )
        grad_rates += rows_product(
            sums_ref[levels + 1], (end_grad * end_key.astype(F32)).astype(BF16)
        )
        grad_rates += decay_row * jnp.sum(
            ending.astype(F32) * entering.astype(F32), axis=0, keepdims=True
        )
        grad_value = rows_product(scores_ref[s], grad_out) + back_product(end_key, ending)
        grad_ref[rows, pl.ds(0, key_dim)] = (grad_query * scale).astype(BF16)
        grad_ref[rows, pl.ds(key_dim, key_dim)] = grad_key.astype(BF16)
        grad_ref[rows, pl.ds(value_at, value_dim)] = grad_value.astype(BF16)
        grad_logits = grad_rates / 16.0 * jax.nn.sigmoid(-logits)
        bias_grad_ref[...] += jnp.sum(grad_logits, axis=0, keepdims=True)
        lowrank = mixed_ref[rows, pl.ds(rank_at, rank)]
        gaterank_grad_ref[...] += dot(lowrank, grad_logits, ((0,), (0,)), HIGHEST)
        grad_lowrank = dot(grad_logits, gaterank_ref[...], ((1,), (1,)), HIGHEST)
        rest = grad_ref.shape[1] - rank_at - rank
        grad_ref[rows, pl.ds(rank_at, rank + rest)] = jnp.concatenate(
            [grad_lowrank, jnp.zeros((length, rest), F32)], axis=1
        ).astype(BF16)
        return carry

    lax.fori_loop(0, count, mix, 0)
    finish_states(count, last, target, send_ref, recv_ref, send_sem, recv_sem)


def state_scratch(count, value_dim, key_dim):
    return [
        pltpu.VMEM((count, value_dim, key_dim), F32),
        pltpu.VMEM((count, value_dim, key_dim), BF16),
        pltpu.VMEM((count, value_dim, key_dim), BF16),
        pltpu.SemaphoreType.DMA((count, PIECES)),
        pltpu.SemaphoreType.DMA((count, PIECES)),
    ]


def kernel_params(number, mebibytes=44):
    return pltpu.CompilerParams(
        collective_id=number, has_side_effects=True, vmem_limit_bytes=mebibytes * 2**20
    )


def head_copy(src, dst, send_sem, recv_sem, target):
    return pltpu.make_async_remote_copy(
        src_ref=src,
        dst_ref=dst,
        send_sem=send_sem,
        recv_sem=recv_sem,
        device_id={"head": target},
        device_id_type=pl.DeviceIdType.MESH,
    )


def greet_heads(targets):
    barrier = pltpu.get_barrier_semaphore()
    for target in targets:
        pl.semaphore_signal(
            barrier, inc=1, device_id={"head": target}, device_id_type=pl.DeviceIdType.MESH
        )
    pl.semaphore_wait(barrier, len(targets))


def square(me):
    return me + 1 - 2 * lax.rem(me, 2), me + 2 - 4 * (me // 2), H - 1 - me


def move_columns(weights, gain, out_ref, send_ref, send_sem, recv_sem, own_sem):
    me = lax.axis_index("head")
    place = 0
    for w in weights:
        n = w.shape[1] // H
        for h in range(H):
            part = w[:, pl.ds(h * n, n)].astype(F32) * gain
            send_ref[h, :, pl.ds(place, n)] = part.astype(BF16)
        place += n
    copies = []
    for ahead in range(1, H):
        peer = lax.rem(me + ahead, H)
        copy = head_copy(
            send_ref.at[peer],
            out_ref.at[me],
            send_sem.at[ahead],
            recv_sem.at[ahead],
            peer,
        )
        copy.start()
        copies.append(copy)
    own = pltpu.make_async_copy(send_ref.at[me], out_ref.at[me], own_sem)
    own.start()
    return copies + [own]


def mix_weights_kernel(*refs):
    *weights, extra_ref, gain_ref, out_ref, send_ref, send_sem, recv_sem, own_sem = refs
    me = lax.axis_index("head")
    greet_heads([lax.rem(me + ahead, H) for ahead in range(1, H)])
    spare = extra_ref.shape[1]
    for h in range(H):
        send_ref[h, :, pl.ds(send_ref.shape[2] - spare, spare)] = extra_ref[...]
    gain = gain_ref[...].astype(F32)
    for copy in move_columns(weights, gain, out_ref, send_ref, send_sem, recv_sem, own_sem):
        copy.wait()


def mix_weights(weights, extra, gain):
    rows = extra.shape[0]
    n = sum(w.shape[1] for w in weights) // H + extra.shape[1]
    return pl.pallas_call(
        mix_weights_kernel,
        out_shape=jax.ShapeDtypeStruct((H, rows, n), BF16),
        in_specs=[pl.BlockSpec(memory_space=pltpu.VMEM)] * (len(weights) + 2),
        out_specs=pl.BlockSpec(memory_space=pl.ANY),
        scratch_shapes=[
            pltpu.VMEM((H, rows, n), BF16),
            pltpu.SemaphoreType.DMA((H,)),
            pltpu.SemaphoreType.DMA((H,)),
            pltpu.SemaphoreType.DMA,
        ],
        compiler_params=kernel_params(3, 16),
        cost_estimate=pl.CostEstimate(flops=10**6, bytes_accessed=10**4, transcendentals=0),
        name="mix_weights",
    )(*weights, extra, gain)


class Share:
    def __init__(self, mine_ref, out_ref, send_sem, recv_sem, own_sem):
        self.refs = mine_ref, out_ref, send_sem, recv_sem, own_sem
        self.me = lax.axis_index("head")
        self.size = mine_ref.shape[0] // CHUNKS

    def copy(self, c, kind):
        mine, out, send_sem, recv_sem, _ = self.refs
        sides = square(self.me)[:2]
        rows = pl.ds(c * self.size, self.size)
        if kind < 2:
            src, dst, target = mine.at[rows], out.at[self.me, rows], sides[kind]
        else:
            origin, target = (sides[0], sides[1]) if c % 2 == 0 else (sides[1], sides[0])
            src = dst = out.at[origin, rows]
        return head_copy(src, dst, send_sem.at[c, kind], recv_sem.at[c, kind], target)

    def own(self, c):
        mine, out, _, _, own_sem = self.refs
        rows = pl.ds(c * self.size, self.size)
        return pltpu.make_async_copy(mine.at[rows], out.at[self.me, rows], own_sem.at[c])

    def start(self, c):
        self.copy(c, 0).start()
        self.copy(c, 1).start()
        self.own(c).start()

    def forward(self, c):
        self.copy(c, c % 2).wait_recv()
        self.copy(c, 2).start()

    def finish(self):
        for c in range(CHUNKS):
            self.copy(c, 1 - c % 2).wait_recv()
            self.copy(c, 2).wait_recv()
            self.own(c).wait()
            for kind in range(3):
                self.copy(c, kind).wait_send()


def share_scratch(rows, width):
    return [
        pltpu.VMEM((rows, width), BF16),
        pltpu.SemaphoreType.DMA((CHUNKS, 3)),
        pltpu.SemaphoreType.DMA((CHUNKS, 3)),
        pltpu.SemaphoreType.DMA((CHUNKS,)),
    ]


def share_kernel(
    tokens_ref,
    gate_ref,
    up_ref,
    gain_ref,
    out_ref,
    moved_ref,
    mine_ref,
    share_send,
    share_recv,
    share_own,
    send_ref,
    send_sem,
    recv_sem,
    own_sem,
):
    me = lax.axis_index("head")
    greet_heads([lax.rem(me + ahead, H) for ahead in range(1, H)])
    share = Share(mine_ref, out_ref, share_send, share_recv, share_own)
    for c in range(CHUNKS):
        rows = pl.ds(c * share.size, share.size)
        x = tokens_ref[rows, :].astype(F32)
        mine_ref[rows, :] = (x * rms_scale(x, EPS)).astype(BF16)
        share.start(c)
    gain = gain_ref[...].astype(F32)
    copies = move_columns(
        [gate_ref, up_ref], gain, moved_ref, send_ref, send_sem, recv_sem, own_sem
    )
    for c in range(CHUNKS):
        share.forward(c)
    share.finish()
    for copy in copies:
        copy.wait()


def share_tokens(tokens, w_gate, w_up, gain):
    rows, n = w_gate.shape[0], 2 * w_gate.shape[1] // H
    return pl.pallas_call(
        share_kernel,
        out_shape=[
            jax.ShapeDtypeStruct((H,) + tokens.shape, BF16),
            jax.ShapeDtypeStruct((H, rows, n), BF16),
        ],
        in_specs=[pl.BlockSpec(memory_space=pltpu.VMEM)] * 4,
        out_specs=[pl.BlockSpec(memory_space=pl.ANY)] * 2,
        scratch_shapes=share_scratch(*tokens.shape)
        + [
            pltpu.VMEM((H, rows, n), BF16),
            pltpu.SemaphoreType.DMA((H,)),
            pltpu.SemaphoreType.DMA((H,)),
            pltpu.SemaphoreType.DMA,
        ],
        compiler_params=kernel_params(4, 16),
        cost_estimate=pl.CostEstimate(flops=10**6, bytes_accessed=10**4, transcendentals=0),
        name="share_tokens",
    )(tokens, w_gate, w_up, gain)


def turn_rows(
    partial_ref,
    first_ref,
    relay_ref,
    second_ref,
    pass_ref,
    send_sem,
    recv_sem,
    done,
    share=None,
    fillers=(),
):
    me = lax.axis_index("head")
    side = square(me)
    far = side[2]
    size = first_ref.shape[0] // CHUNKS
    steps = CHUNKS + 3
    fillers = list(fillers)

    def copies(c):
        one, two = (side[0], side[1]) if c % 2 == 0 else (side[1], side[0])
        rows = pl.ds(c * size, size)
        sems = [(send_sem.at[c, kind], recv_sem.at[c, kind]) for kind in range(3)]
        return (
            head_copy(partial_ref.at[far, rows], relay_ref.at[rows], *sems[0], one),
            head_copy(partial_ref.at[one, rows], first_ref.at[rows], *sems[1], one),
            head_copy(pass_ref.at[rows], second_ref.at[rows], *sems[2], two),
            two,
            rows,
        )

    for c in range(CHUNKS):
        relay, first, *_ = copies(c)
        relay.start()
        first.start()
    for step in range(steps):
        for filler in fillers[step * len(fillers) // steps : (step + 1) * len(fillers) // steps]:
            filler()
        if step < CHUNKS:
            relay, _, second, two, rows = copies(step)
            relay.wait_recv()
            both = partial_ref[two, rows, :].astype(F32) + relay_ref[rows, :].astype(F32)
            pass_ref[rows, :] = both.astype(BF16)
            second.start()
        if 1 <= step <= CHUNKS:
            _, first, second, _, rows = copies(step - 1)
            first.wait_recv()
            second.wait_recv()
            total = partial_ref[me, rows, :].astype(F32) + first_ref[rows, :].astype(F32)
            made = done(rows, total + second_ref[rows, :].astype(F32))
            if share is not None:
                share.refs[0][rows, :] = made
                share.start(step - 1)
        if step >= 3 and share is not None:
            share.forward(step - 3)
    if share is not None:
        share.finish()
    for c in range(CHUNKS):
        for copy in copies(c)[:3]:
            copy.wait_send()


def turn_scratch(rows, width):
    return [pltpu.VMEM((rows, width), BF16) for _ in range(4)] + [
        pltpu.SemaphoreType.DMA((CHUNKS, 3)),
        pltpu.SemaphoreType.DMA((CHUNKS, 3)),
    ]


def hidden_kernel(partial_ref, tokens_ref, hidden_ref, out_ref, *scratch):
    greet_heads(square(lax.axis_index("head"))[:2])
    mine_ref, *sems = scratch[6:]

    def done(rows, total):
        hidden = tokens_ref[rows, :].astype(F32) + total
        hidden_ref[rows, :] = hidden
        return (hidden * rms_scale(hidden, EPS)).astype(BF16)

    turn_rows(partial_ref, *scratch[:6], done, Share(mine_ref, out_ref, *sems))


def share_hidden(partial, tokens):
    whole = pl.BlockSpec(memory_space=pltpu.VMEM)
    return pl.pallas_call(
        hidden_kernel,
        out_shape=[
            jax.ShapeDtypeStruct(tokens.shape, F32),
            jax.ShapeDtypeStruct((H,) + tokens.shape, BF16),
        ],
        in_specs=[whole] * 2,
        out_specs=[whole, pl.BlockSpec(memory_space=pl.ANY)],
        scratch_shapes=turn_scratch(*tokens.shape) + share_scratch(*tokens.shape),
        compiler_params=kernel_params(5, 18),
        cost_estimate=pl.CostEstimate(flops=10**6, bytes_accessed=10**4, transcendentals=0),
        name="share_hidden",
    )(partial, tokens)


class PairProduct:
    def __init__(self, left_ref, right_ref, out_ref, give_ref, take_ref, send_sem, recv_sem, own_sem):
        self.refs = left_ref, right_ref, out_ref, give_ref, take_ref
        self.sems = send_sem, recv_sem, own_sem
        self.core = lax.axis_index("core")
        self.groups, self.rows, self.width = out_ref.shape
        self.cut = self.width // 2 if self.width % (2 * LANES) == 0 else self.width

    def product(self, group, core, at):
        left, right, *_ = self.refs
        start = pl.multiple_of((group * CORES + core) * self.rows, LANES)
        return rows_product(left[:, pl.ds(start, self.rows)], right[:, pl.ds(at, self.cut)])

    def copy(self, group):
        give, take = self.refs[3:]
        return pltpu.make_async_remote_copy(
            src_ref=give.at[group],
            dst_ref=take.at[group],
            send_sem=self.sems[0].at[group],
            recv_sem=self.sems[1].at[group],
            device_id={"core": 1 - self.core},
            device_id_type=pl.DeviceIdType.MESH,
        )

    def store(self, group):
        return pltpu.make_async_copy(
            self.refs[3].at[group], self.refs[2].at[group], self.sems[2].at[group]
        )

    def give(self, group, at):
        product = self.product(group, 1 - self.core, at)
        self.refs[3][group, :, pl.ds(at, self.cut)] = product.astype(BF16)
        if at + self.cut == self.width:
            self.copy(group).start()

    def keep(self, group, at):
        give, take = self.refs[3:]
        if at == 0:
            self.copy(group).wait()
        both = self.product(group, self.core, at)
        both += take[group, :, pl.ds(at, self.cut)].astype(F32)
        give[group, :, pl.ds(at, self.cut)] = both.astype(BF16)
        if at + self.cut == self.width:
            self.store(group).start()

    def steps(self):
        places = [
            (group, at) for group in range(self.groups) for at in range(0, self.width, self.cut)
        ]
        return [functools.partial(self.give, *place) for place in places] + [
            functools.partial(self.keep, *place) for place in places
        ]

    def finish(self):
        for group in range(self.groups):
            self.store(group).wait()


def pair_shape(left, right, groups):
    return (groups, left.shape[1] // (CORES * groups), right.shape[1])


def pair_scratch(shape):
    return [
        pltpu.VMEM(shape, BF16),
        pltpu.VMEM(shape, BF16),
        pltpu.SemaphoreType.DMA((shape[0],)),
        pltpu.SemaphoreType.DMA((shape[0],)),
        pltpu.SemaphoreType.DMA((shape[0],)),
    ]


def pair_kernel(left_ref, right_ref, out_ref, *scratch):
    barrier = pltpu.get_barrier_semaphore()
    other = 1 - lax.axis_index("core")
    pl.semaphore_signal(
        barrier, inc=1, device_id={"core": other}, device_id_type=pl.DeviceIdType.MESH
    )
    pl.semaphore_wait(barrier, 1)
    pair = PairProduct(left_ref, right_ref, out_ref, *scratch)
    for step in pair.steps():
        step()
    pair.finish()


def pair_product(left, right, groups, number):
    shape = pair_shape(left, right, groups)
    whole = pl.BlockSpec(memory_space=pltpu.VMEM)
    return pl.pallas_call(
        pair_kernel,
        out_shape=jax.ShapeDtypeStruct(shape, BF16),
        in_specs=[whole] * 2,
        out_specs=pl.BlockSpec(memory_space=pl.ANY),
        scratch_shapes=pair_scratch(shape),
        compiler_params=kernel_params(number, 58),
        cost_estimate=pl.CostEstimate(flops=10**6, bytes_accessed=10**4, transcendentals=0),
        name="pair_product",
    )(left, right)


def branch_kernel(
    partial_ref,
    hidden_ref,
    upstream_ref,
    active_ref,
    down_ref,
    rest_ref,
    grad_ref,
    gain_grad_ref,
    down_out_ref,
    out_ref,
    *scratch,
):
    greet_heads(square(lax.axis_index("head"))[:2])
    mine_ref, *sems = scratch[6:10]
    gain_grad_ref[...] = jnp.zeros_like(gain_grad_ref)

    def done(rows, total):
        hidden = hidden_ref[rows, :]
        scale = rms_scale(hidden, EPS)
        gain_grad_ref[...] += jnp.sum(total * hidden * scale, axis=0, keepdims=True)
        grad = upstream_ref[rows, :].astype(F32) + rms_back(total, hidden, scale)
        grad_ref[rows, :] = grad
        return grad.astype(BF16)

    def down(at):
        rows = pl.ds(at, LANES)
        half = down_ref.shape[1]
        for place, ref in ((0, down_ref), (half, rest_ref)):
            product = matmul(active_ref[rows, :], ref[...])
            down_out_ref[rows, pl.ds(place, half)] = product.astype(BF16)

    share = Share(mine_ref, out_ref, *sems)
    fillers = [functools.partial(down, at) for at in range(0, active_ref.shape[0], LANES)]
    turn_rows(partial_ref, *scratch[:6], done, share, fillers)


def share_branch(partial, hidden, upstream, active, down, rest):
    whole = pl.BlockSpec(memory_space=pltpu.VMEM)
    return pl.pallas_call(
        branch_kernel,
        out_shape=[
            jax.ShapeDtypeStruct(hidden.shape, F32),
            jax.ShapeDtypeStruct((1, hidden.shape[1]), F32),
            jax.ShapeDtypeStruct((active.shape[0], hidden.shape[1]), BF16),
            jax.ShapeDtypeStruct((H,) + hidden.shape, BF16),
        ],
        in_specs=[whole] * 6,
        out_specs=[whole] * 3 + [pl.BlockSpec(memory_space=pl.ANY)],
        scratch_shapes=turn_scratch(*hidden.shape) + share_scratch(*hidden.shape),
        compiler_params=kernel_params(6, 34),
        cost_estimate=pl.CostEstimate(flops=10**6, bytes_accessed=10**4, transcendentals=0),
        name="share_branch",
    )(partial, hidden, upstream, active, down, rest)


def tokens_kernel(partial_ref, tokens_ref, upstream_ref, grad_ref, gain_grad_ref, *scratch):
    greet_heads(square(lax.axis_index("head"))[:2])
    gain_grad_ref[...] = jnp.zeros_like(gain_grad_ref)

    def done(rows, total):
        tokens = tokens_ref[rows, :].astype(F32)
        scale = rms_scale(tokens, EPS)
        gain_grad_ref[...] += jnp.sum(total * tokens * scale, axis=0, keepdims=True)
        grad = upstream_ref[rows, :] + rms_back(total, tokens, scale)
        grad_ref[rows, :] = grad.astype(BF16)

    turn_rows(partial_ref, *scratch, done)


def tokens_back(partial, tokens, upstream):
    whole = pl.BlockSpec(memory_space=pltpu.VMEM)
    return pl.pallas_call(
        tokens_kernel,
        out_shape=[
            jax.ShapeDtypeStruct(tokens.shape, BF16),
            jax.ShapeDtypeStruct((1, tokens.shape[1]), F32),
        ],
        in_specs=[whole] * 3,
        out_specs=[whole] * 2,
        scratch_shapes=turn_scratch(*tokens.shape),
        compiler_params=kernel_params(8, 18),
        cost_estimate=pl.CostEstimate(flops=10**6, bytes_accessed=10**4, transcendentals=0),
        name="tokens_back",
    )(partial, tokens, upstream)


def hidden_units_kernel(cot_ref, down_ref, rest_ref, pre_ref, out_ref):
    units, half = down_ref.shape
    grad = back_product(cot_ref[:, pl.ds(0, half)], down_ref[...])
    grad += back_product(cot_ref[:, pl.ds(half, half)], rest_ref[...])
    gate, up = pre_ref[:, pl.ds(0, units)], pre_ref[:, pl.ds(units, units)]
    sig = jax.nn.sigmoid(gate)
    grad_sig = grad * sig
    out_ref[:, pl.ds(0, units)] = (grad_sig * up * (1.0 + gate * (1.0 - sig))).astype(BF16)
    out_ref[:, pl.ds(units, units)] = (grad_sig * gate).astype(BF16)


def hidden_units_back(cot, down, rest, pre):
    rows, width = cot.shape
    size = 2 * LANES

    def rows_block(n):
        return pl.BlockSpec((size, n), lambda i: (i, 0))

    return pl.pallas_call(
        hidden_units_kernel,
        grid=(rows // size,),
        out_shape=jax.ShapeDtypeStruct(pre.shape, BF16),
        in_specs=[
            rows_block(width),
            pl.BlockSpec(down.shape, lambda i: (0, 0)),
            pl.BlockSpec(rest.shape, lambda i: (0, 0)),
            rows_block(pre.shape[1]),
        ],
        out_specs=rows_block(pre.shape[1]),
        compiler_params=pltpu.CompilerParams(vmem_limit_bytes=58 * 2**20),
        cost_estimate=pl.CostEstimate(flops=10**6, bytes_accessed=10**4, transcendentals=0),
        name="hidden_units_back",
    )(cot, down, rest, pre)


def mix_forward(mixed, bias, gaterank, gain, marks, segment, sums, pairs, key_dim, value_dim):
    rows = mixed.shape[0]
    count, _, length = segment.shape
    shapes = (
        ((rows, value_dim), BF16),
        ((rows, value_dim), F32),
        ((rows, key_dim), F32),
        ((count, length, length), BF16),
        ((rows, key_dim), BF16),
        ((rows, key_dim), BF16),
        ((count, 1, key_dim), F32),
        ((count, value_dim, key_dim), BF16),
    )
    whole = pl.BlockSpec(memory_space=pltpu.VMEM)
    return pl.pallas_call(
        functools.partial(forward_kernel, key_dim, value_dim),
        out_shape=[jax.ShapeDtypeStruct(*s) for s in shapes],
        in_specs=[pl.BlockSpec(memory_space=pl.ANY)] + [whole] * 7,
        out_specs=[whole] + [pl.BlockSpec(memory_space=pl.ANY)] * (len(shapes) - 1),
        scratch_shapes=[pltpu.VMEM(*s) for s in shapes[1:-1]]
        + state_scratch(count, value_dim, key_dim)
        + [
            pltpu.SemaphoreType.DMA((count, 7)),
            pltpu.VMEM(mixed.shape, mixed.dtype),
            pltpu.SemaphoreType.DMA((count,)),
        ],
        compiler_params=kernel_params(1, 58),
        cost_estimate=pl.CostEstimate(flops=10**6, bytes_accessed=10**4, transcendentals=0),
        name="mix_forward",
    )(mixed, bias, gaterank, gain, marks, segment, sums, pairs)


def mix_backward(
    mixed, kept, upstream, gaterank, gain, marks, segment, sums, pairs, key_dim, value_dim
):
    rows = mixed.shape[0]
    count = segment.shape[0]
    shapes = (
        (mixed.shape, BF16),
        ((1, value_dim), F32),
        ((1, key_dim), F32),
        (gaterank.shape, F32),
    )
    attended, logits, scores, start, end, decay, enter = kept
    given = (mixed, upstream, attended, start, logits, scores, end, decay, enter)
    whole = pl.BlockSpec(memory_space=pltpu.VMEM)
    return pl.pallas_call(
        functools.partial(backward_kernel, key_dim, value_dim),
        out_shape=[jax.ShapeDtypeStruct(*s) for s in shapes],
        in_specs=[pl.BlockSpec(memory_space=pl.ANY)] * 9 + [whole] * 6,
        out_specs=[whole] * len(shapes),
        scratch_shapes=[pltpu.VMEM(a.shape, a.dtype) for a in given]
        + [pltpu.VMEM((rows, value_dim), BF16)]
        + state_scratch(count, value_dim, key_dim)
        + [pltpu.SemaphoreType.DMA((count, 9))],
        compiler_params=kernel_params(2, 58),
        cost_estimate=pl.CostEstimate(flops=10**6, bytes_accessed=10**4, transcendentals=0),
        name="mix_backward",
    )(
        *given,
        gaterank,
        gain,
        marks,
        segment,
        sums,
        pairs,
    )


def per_device(
    tokens,
    doc_lengths,
    norm_gain,
    w_query,
    w_key,
    w_value,
    w_outgate,
    w_lowrank,
    w_gaterank,
    gate_bias,
    head_gain,
    w_output,
    ffn_gain,
    w_gate,
    w_up,
    w_down,
    cotangent,
):
    seqs_here, length, width = tokens.shape
    reps = lax.axis_size("rep")
    parts = lax.axis_size("fsdp")
    devices = reps * H * CORES * parts
    here = lax.axis_index("head")
    key_dim, value_dim = DK, DV
    rank = w_lowrank.shape[1]
    rows = width // devices
    count = H * seqs_here

    rank_at = 2 * key_dim + 2 * value_dim

    def core_sum(g):
        halves = g.reshape(g.shape[0], CORES, -1, g.shape[-1])
        core = lax.axis_index("core")
        other = lax.ppermute(halves[:, 1 - core], "core", ((0, 1), (1, 0)))
        return (halves[:, core].astype(F32) + other.astype(F32)).astype(BF16)

    def scatter_rows(g):
        if reps > 1:
            g = lax.psum_scatter(g, "rep", scatter_dimension=0, tiled=True)
        return lax.psum_scatter(g, "fsdp", scatter_dimension=1, tiled=True)

    def gather_columns(moved):
        whole = lax.all_gather(moved, ("core", "fsdp"), axis=1, tiled=True)
        if reps > 1:
            whole = lax.all_gather(whole, "rep", axis=0, tiled=False)
        return whole.reshape(width, -1)

    def gather_part(w):
        if reps == 1:
            return lax.all_gather(w, SHARE, axis=0, tiled=True)
        whole = lax.all_gather(w, EVERY, axis=0, tiled=True)
        size = whole.shape[0] // H
        return lax.dynamic_slice_in_dim(whole, here * size, size, 0)

    def pair_part(g):
        return core_sum(g[None])[0] if reps == 1 else g

    def scatter_part(g):
        if reps == 1:
            return lax.psum_scatter(g, "fsdp", scatter_dimension=0, tiled=True)
        whole = jnp.zeros((H * g.shape[0], g.shape[1]), BF16)
        whole = lax.dynamic_update_slice_in_dim(whole, g, here * g.shape[0], 0)
        return lax.psum_scatter(whole, EVERY, scatter_dimension=0, tiled=True)

    rank_at = 2 * key_dim + 2 * value_dim

    def with_gain(w, gain):
        return (w.astype(F32) * gain.astype(F32)[:, None]).astype(BF16)

    small = (
        w_gaterank,
        gate_bias.reshape(1, -1),
        head_gain.reshape(1, -1),
        (doc_lengths // 16).astype(BF16).reshape(1, -1),
        (doc_lengths % 16).astype(BF16).reshape(1, -1),
    )
    edges = [rank]
    extra = jnp.pad(with_gain(w_lowrank, norm_gain), ((0, 0), (0, LANES - rank)))
    for piece in small:
        high, wide = piece.shape
        extra += jnp.pad(piece, ((0, rows - high), (edges[-1], LANES - edges[-1] - wide)))
        edges.append(edges[-1] + wide)

    mix_moved = mix_weights((w_query, w_key, w_value, w_outgate), extra, norm_gain[:, None])
    inputs = tokens.reshape(-1, width)
    inputs, _ = after(inputs, mix_moved)
    output_w = gather_part(w_output)
    mix_moved, output_w = after(mix_moved, output_w)
    mix_w = gather_columns(mix_moved)
    w_down, _ = after(w_down, mix_moved)
    down_w = gather_part(w_down[:, : width // 2])
    normed, ffn_moved = share_tokens(inputs, w_gate, w_up, ffn_gain[:, None])
    normed = normed.reshape(-1, width)

    small = mix_w[:, rank_at:].astype(F32).reshape(devices, rows, LANES)
    gaterank, bias, gain_head, long, short = (
        small[:, : rank if i == 0 else 1, edges[i] : edges[i + 1]] for i in range(len(edges) - 1)
    )
    gaterank = gaterank.transpose(1, 0, 2).reshape(rank, -1)
    bias = lax.dynamic_slice_in_dim(bias.reshape(1, -1), here * key_dim, key_dim, 1)
    gaterank = lax.dynamic_slice_in_dim(gaterank, here * key_dim, key_dim, 1)
    gain_head = gain_head.reshape(1, -1)
    lengths = (long * 16.0 + short).reshape(reps, H, CORES, parts, seqs_here, DOCS)
    lengths = lengths[lax.axis_index("rep"), :, lax.axis_index("core"), 0]
    lengths = lengths.reshape(count, DOCS).astype(jnp.int32)

    offset = lax.axis_index("fsdp") * length
    doc_ends = jnp.cumsum(lengths, axis=-1)
    places = offset + jnp.arange(length, dtype=jnp.int32)
    segment = jnp.sum((places[None, :, None] >= doc_ends[:, None, :]).astype(jnp.int32), axis=-1)
    before = jnp.sum((offset - 1 >= doc_ends).astype(jnp.int32), axis=-1)[:, None]
    last = segment[:, -1:]
    marks = jnp.stack(
        [
            segment,
            segment == before,
            segment == last,
            segment != DOCS - 1,
            jnp.broadcast_to(last == before, segment.shape),
        ],
        axis=2,
    )
    marks = jnp.pad(marks.astype(F32).reshape(count * length, 5), ((0, 0), (0, 3)))
    segment = segment.astype(F32).reshape(count, 1, length)

    mixed = matmul(normed, mix_w)
    sums, pairs = level_sums(length)
    sums, pairs = sums.astype(BF16), pairs.astype(BF16)
    gated, *kept = mix_forward(
        mixed, bias, gaterank, gain_head, marks, segment, sums, pairs, key_dim, value_dim
    )
    cot_rows, _ = after(cotangent.reshape(-1, width), normed)
    gated, cot_shared, down_w = after(gated, share_rows(cot_rows), down_w)
    ffn_moved, w_down_rest, _ = after(ffn_moved, w_down[:, width // 2 :], gated)
    ffn_w = gather_columns(ffn_moved)
    down_rest = gather_part(w_down_rest)
    partial = matmul(gated, output_w).astype(BF16).reshape(H, -1, width)
    hidden, normed_two = share_hidden(partial, inputs)
    normed_two = normed_two.reshape(-1, width)

    pre = matmul(normed_two, ffn_w)
    gate_pre, up_pre = jnp.split(pre, 2, axis=1)
    sig_gate = jax.nn.sigmoid(gate_pre)
    activated = (gate_pre * sig_gate * up_pre).astype(BF16)

    grad_down_w = rows_product(activated, cot_shared).astype(BF16)
    down_w, grad_down_w = after(down_w, grad_down_w)
    grad_pre = hidden_units_back(cot_shared, down_w, down_rest, pre)
    grad_pre, grad_down_w = after(grad_pre, pair_part(grad_down_w))
    grad_down_w = scatter_part(grad_down_w)
    grad_ffn_w = pair_product(normed_two, grad_pre, reps * H, 7)
    grad_pre, grad_ffn_w = after(grad_pre, grad_ffn_w)
    partial = back_product(grad_pre, ffn_w).astype(BF16)

    grad_hidden, grad_gain_two, down_partial, branch = share_branch(
        partial.reshape(H, -1, width), hidden, cot_rows, activated, down_w, down_rest
    )
    grad_ffn_w = scatter_rows(grad_ffn_w)
    branch = branch.reshape(-1, width)
    grad_gated = back_product(branch, output_w)
    gated, grad_gated = after(gated, grad_gated)
    grad_output_w = pair_part(rows_product(gated, branch).astype(BF16))
    grad_gated, grad_output_w, grad_down_w = after(grad_gated, grad_output_w, grad_down_w)
    grad_output_w = scatter_part(grad_output_w)
    pieces = move_rows(down_partial)
    grad_mixed, grad_gain_head, grad_bias, grad_gaterank = mix_backward(
        mixed,
        kept,
        grad_gated,
        gaterank,
        gain_head,
        marks,
        segment,
        sums,
        pairs,
        key_dim,
        value_dim,
    )
    grad_mixed, pieces, grad_down_w, grad_ffn_w = after(
        grad_mixed, pieces, grad_down_w, grad_ffn_w
    )
    output = (hidden + jnp.sum(pieces.astype(F32), axis=0)).astype(BF16).reshape(tokens.shape)
    grad_mix_w = pair_product(normed, grad_mixed, reps * H, 11)
    grad_mixed, grad_mix_w = after(grad_mixed, grad_mix_w)
    partial = back_product(grad_mixed, mix_w).astype(BF16)
    grad_mix_w = scatter_rows(grad_mix_w)
    grad_ffn_w = lax.all_to_all(grad_ffn_w, "head", split_axis=0, concat_axis=0, tiled=True)
    partial, grad_output_w, grad_ffn_w = after(partial, grad_output_w, grad_ffn_w)
    tokens_grad, grad_gain_one = tokens_back(partial.reshape(H, -1, width), inputs, grad_hidden)
    tokens_grad = tokens_grad.reshape(tokens.shape)

    def weight_grad(moved, gain, start, w):
        n = w.shape[1] // H
        whole = moved[:, :, start : start + n].transpose(1, 0, 2).reshape(rows, -1)
        return whole.astype(F32) * gain.astype(F32)[:, None]

    w_gate_grad = weight_grad(grad_ffn_w, ffn_gain, 0, w_gate)
    w_up_grad = weight_grad(grad_ffn_w, ffn_gain, w_gate.shape[1] // H, w_up)
    grad_mix_w = lax.all_to_all(grad_mix_w, "head", split_axis=0, concat_axis=0, tiled=True)
    query_g = weight_grad(grad_mix_w, norm_gain, 0, w_query)
    key_g = weight_grad(grad_mix_w, norm_gain, key_dim, w_key)
    value_g = weight_grad(grad_mix_w, norm_gain, 2 * key_dim, w_value)
    outgate_g = weight_grad(grad_mix_w, norm_gain, 2 * key_dim + value_dim, w_outgate)
    lowrank_g = grad_mix_w[:, :, rank_at : rank_at + rank].astype(F32)
    lowrank_g = jnp.sum(lowrank_g, axis=0) * norm_gain.astype(F32)[:, None]

    def place(g, axis):
        shape = list(g.shape)
        shape[axis] *= H
        return lax.dynamic_update_slice_in_dim(jnp.zeros(shape, F32), g, here * key_dim, axis)

    small_grads = jnp.concatenate(
        [
            grad_gain_one.reshape(devices, -1),
            grad_gain_two.reshape(devices, -1),
            place(grad_bias.reshape(-1), 0).reshape(devices, -1),
            grad_gain_head.reshape(devices, -1),
            place(grad_gaterank, 1)
            .reshape(rank, devices, -1)
            .transpose(1, 0, 2)
            .reshape(devices, -1),
        ],
        axis=1,
    )
    small_grads = lax.all_to_all(small_grads, EVERY, split_axis=0, concat_axis=0, tiled=True)
    small_grads = jnp.sum(small_grads, axis=0)
    sizes = [norm_gain.shape[0], ffn_gain.shape[0], gate_bias.shape[0], head_gain.shape[0]]
    norm_g, ffn_g, bias_g, head_g, gaterank_g = jnp.split(
        small_grads, [sum(sizes[: i + 1]) for i in range(len(sizes))]
    )
    return (
        output,
        tokens_grad,
        norm_g / norm_gain.astype(F32),
        query_g,
        key_g,
        value_g,
        outgate_g,
        lowrank_g,
        gaterank_g.reshape(w_gaterank.shape),
        bias_g,
        head_g,
        grad_output_w.astype(F32),
        ffn_g / ffn_gain.astype(F32),
        w_gate_grad,
        w_up_grad,
        grad_down_w.astype(F32),
    )


def solution(mesh):
    dp, parts = mesh.shape["dp"], mesh.shape["fsdp"]
    fine = Mesh(mesh.devices.reshape(dp // (H * CORES), H, CORES, parts), EVERY)
    seq = ("rep", "head", "core")
    rows, vector = P(EVERY, None), P(EVERY)
    activations = P(seq, "fsdp", None)
    columns = P(None, EVERY)
    return jax.shard_map(
        per_device,
        mesh=fine,
        in_specs=(
            activations,
            P(seq, None),
            vector,
            rows,
            rows,
            rows,
            rows,
            rows,
            columns,
            vector,
            vector,
            rows,
            vector,
            rows,
            rows,
            rows,
            activations,
        ),
        out_specs=(
            activations,
            activations,
            vector,
            rows,
            rows,
            rows,
            rows,
            rows,
            columns,
            vector,
            vector,
            rows,
            vector,
            rows,
            rows,
            rows,
        ),
        check_vma=False,
    )
```

```python
import functools

import jax
import jax.experimental.pallas as pl
import jax.experimental.pallas.tpu as pltpu
import jax.numpy as jnp
from jax import lax
from jax.sharding import Mesh
from jax.sharding import PartitionSpec as P

H = 4
DK = 256
DV = 512
CORES = 2
DOCS = 8
PIECES = 4
LANES = 128
CHUNKS = 8

EPS = 1e-05
HEAD_EPS = 1.0
HIGHEST = lax.Precision.HIGHEST
F32 = jnp.float32
BF16 = jnp.bfloat16

SHARE = ("rep", "core", "fsdp")
EVERY = ("rep", "head", "core", "fsdp")


def dot(a, b, dims, precision=None):
    return lax.dot_general(a, b, (dims, ((), ())), precision=precision, preferred_element_type=F32)


def after(value, *others):
    return lax.optimization_barrier((value,) + others)


def matmul(a, b):
    return dot(a, b, ((1,), (0,)))


def rows_product(a, b):
    return dot(a, b, ((0,), (0,)))


def back_product(a, b):
    return dot(a, b, ((1,), (1,)))


def batched(form, a, b):
    return jnp.einsum(form, a, b, preferred_element_type=F32)


def rms_scale(values, epsilon):
    return lax.rsqrt(jnp.mean(values * values, axis=-1, keepdims=True) + epsilon)


def rms_back(upstream, values, scale):
    return scale * upstream - values * scale**3 * jnp.mean(upstream * values, axis=-1, keepdims=True)


def share_rows(part):
    spread = jnp.broadcast_to(part[None], (H,) + part.shape)
    whole = lax.all_to_all(spread, "head", split_axis=0, concat_axis=0, tiled=True)
    return whole.reshape(-1, part.shape[-1])


def move_rows(partial):
    pieces = partial.astype(BF16).reshape(H, -1, partial.shape[-1])
    return lax.all_to_all(pieces, "head", split_axis=0, concat_axis=0, tiled=True)


def sum_rows(partial):
    return jnp.sum(move_rows(partial).astype(F32), axis=0)


def level_sums(length):
    rows = jnp.arange(length)[:, None]
    cols = jnp.arange(length)[None, :]
    sums, pairs = [], []
    step = 1
    while step < length:
        bound = rows // (2 * step) * (2 * step) + step - 1
        upper = rows > bound
        sums.append(jnp.where(upper, (cols > bound) & (cols <= rows), (cols > rows) & (cols <= bound)))
        pairs.append(upper & (cols // (2 * step) == rows // (2 * step)) & (cols <= bound))
        step *= 2
    sums.append(cols <= rows)
    sums.append(cols > rows)
    return jnp.stack(sums), jnp.stack(pairs)


def log_sigmoid(x):
    return jnp.minimum(x, 0.0) - jnp.log1p(jnp.exp(-jnp.abs(x)))


def state_copy(send, recv, send_sem, recv_sem, seq, piece, target):
    size = send.shape[1] // PIECES
    part = pl.ds(piece * size, size)
    return pltpu.make_async_remote_copy(
        src_ref=send.at[seq, part],
        dst_ref=recv.at[seq, part],
        send_sem=send_sem.at[seq, piece],
        recv_sem=recv_sem.at[seq, piece],
        device_id={"fsdp": target},
        device_id_type=pl.DeviceIdType.MESH,
    )


def greet_neighbours(place, parts):
    barrier = pltpu.get_barrier_semaphore()
    for near, there in ((place - 1, place > 0), (place + 1, place < parts - 1)):

        @pl.when(there)
        def _(near=near):
            pl.semaphore_signal(
                barrier,
                inc=1,
                device_id={"fsdp": lax.rem(near + parts, parts)},
                device_id_type=pl.DeviceIdType.MESH,
            )

    peers = (place > 0).astype(jnp.int32) + (place < parts - 1).astype(jnp.int32)
    pl.semaphore_wait(barrier, peers)


def pass_state(s, first, last, target, decay, local, send, recv, send_sem, recv_sem):
    size = send.shape[1] // PIECES
    for piece in range(PIECES):
        part = pl.ds(piece * size, size)
        copy = state_copy(send, recv, send_sem, recv_sem, s, piece, target)

        @pl.when(jnp.logical_not(first))
        def _(copy=copy):
            copy.wait_recv()

        @pl.when(jnp.logical_not(jnp.logical_or(first, last)))
        def _(copy=copy, part=part):
            joined = decay * recv[s, part].astype(F32) + local[s, part]
            send[s, part] = joined.astype(BF16)
            copy.start()


def start_state(s, first, last, target, local, send, recv, send_sem, recv_sem):
    @pl.when(jnp.logical_and(first, jnp.logical_not(last)))
    def _():
        send[s] = local[s].astype(BF16)
        for piece in range(PIECES):
            state_copy(send, recv, send_sem, recv_sem, s, piece, target).start()


def finish_states(count, last, target, send, recv, send_sem, recv_sem):
    @pl.when(jnp.logical_not(last))
    def _():
        def one(s, carry):
            for piece in range(PIECES):
                state_copy(send, recv, send_sem, recv_sem, s, piece, target).wait_send()
            return carry

        lax.fori_loop(0, count, one, 0)


def split_rates(logits):
    rates = log_sigmoid(logits) / 16.0
    high = rates.astype(BF16)
    return high, (rates - high.astype(F32)).astype(BF16)


def decayed(sums, high, low):
    return jnp.exp(matmul(sums, high) + matmul(sums, low))


def forward_kernel(
    key_dim,
    value_dim,
    given_ref,
    bias_ref,
    gaterank_ref,
    gain_ref,
    marks_ref,
    segment_ref,
    sums_ref,
    pairs_ref,
    gated_ref,
    *refs,
):
    kept, (attended_ref, logits_ref, scores_ref, start_ref, end_ref, decay_ref) = refs[:7], refs[7:13]
    local_ref, send_ref, recv_ref, send_sem, recv_sem, keep_sem, mixed_ref, take_sem = refs[13:]
    count, _, length = segment_ref.shape
    levels = pairs_ref.shape[0]
    parts, place = lax.axis_size("fsdp"), lax.axis_index("fsdp")
    first, last, target = place == 0, place == parts - 1, lax.rem(place + 1, parts)

    def rows_of(s):
        return pl.ds(pl.multiple_of(s * length, length), length)

    def keeps(s, kinds):
        held = (attended_ref, logits_ref, scores_ref, start_ref, end_ref, decay_ref, recv_ref)
        rows = rows_of(s)
        for kind in kinds:
            at = rows if len(held[kind].shape) == 2 else s
            yield pltpu.make_async_copy(held[kind].at[at], kept[kind].at[at], keep_sem.at[s, kind])

    def take(s):
        rows = rows_of(s)
        return pltpu.make_async_copy(given_ref.at[rows], mixed_ref.at[rows], take_sem.at[s])

    def start_take(s, carry):
        take(s).start()
        return carry

    lax.fori_loop(0, count, start_take, 0)

    def finish_keeps(s, carry):
        for copy in keeps(s, range(7)):
            copy.wait()
        return carry

    rank = gaterank_ref.shape[0]
    scale = key_dim ** (-0.5)
    value_at = 2 * key_dim
    gate_at = value_at + value_dim
    rank_at = gate_at + value_dim

    greet_neighbours(place, parts)

    @pl.when(first)
    def _():
        recv_ref[...] = jnp.zeros_like(recv_ref)

    def ends(s, carry):
        rows = rows_of(s)
        take(s).wait()
        lowrank = mixed_ref[rows, pl.ds(rank_at, rank)]
        logits = dot(lowrank, gaterank_ref[...], ((1,), (0,)), HIGHEST) + bias_ref[...]
        logits_ref[rows, :] = logits
        high, low = split_rates(logits)
        from_start = decayed(sums_ref[levels], high, low)
        to_end = decayed(sums_ref[levels + 1], high, low)
        marks = marks_ref[rows, :]
        decay_ref[s] = from_start[length - 1 :, :] * marks[:1, 4:5]
        query = mixed_ref[rows, pl.ds(0, key_dim)] * scale
        key = mixed_ref[rows, pl.ds(key_dim, key_dim)]
        start_ref[rows, :] = (query * (from_start * marks[:, 1:2])).astype(BF16)
        end_key = (key * (to_end * marks[:, 2:3])).astype(BF16)
        end_ref[rows, :] = end_key
        value = mixed_ref[rows, pl.ds(value_at, value_dim)].astype(BF16)
        local_ref[s] = rows_product(value, end_key)
        start_state(s, first, last, target, local_ref, send_ref, recv_ref, send_sem, recv_sem)
        for copy in keeps(s, (1, 3, 4, 5)):
            copy.start()
        return carry

    lax.fori_loop(0, count, ends, 0)

    def mix(s, carry):
        rows = rows_of(s)
        pass_state(
            s, first, last, target, decay_ref[s], local_ref, send_ref, recv_ref, send_sem, recv_sem
        )
        query = mixed_ref[rows, pl.ds(0, key_dim)] * scale
        key = mixed_ref[rows, pl.ds(key_dim, key_dim)]
        high, low = split_rates(logits_ref[rows, :])
        scores = jnp.zeros((length, length), F32)
        for level in range(levels):
            decay = decayed(sums_ref[level], high, low)
            pair = back_product((query * decay).astype(BF16), (key * decay).astype(BF16))
            scores += pair * pairs_ref[level].astype(F32)
        row = lax.broadcasted_iota(jnp.int32, (length, length), 0)
        col = lax.broadcasted_iota(jnp.int32, (length, length), 1)
        own = jnp.sum(query * key, axis=1, keepdims=True)
        scores += jnp.where(row == col, own, 0.0)
        marks = marks_ref[rows, :]
        scores = jnp.where(marks[:, 0:1] == segment_ref[s], scores, 0.0).astype(BF16)
        scores_ref[s] = scores
        value = mixed_ref[rows, pl.ds(value_at, value_dim)].astype(BF16)
        attended = matmul(scores, value) + back_product(start_ref[rows, :], recv_ref[s])
        attended = attended * marks[:, 3:4]
        attended_ref[rows, :] = attended
        headed = attended * rms_scale(attended, HEAD_EPS) * gain_ref[...]
        outgate = mixed_ref[rows, pl.ds(gate_at, value_dim)]
        gated_ref[rows, :] = (headed * (outgate * jax.nn.sigmoid(outgate))).astype(BF16)
        for copy in keeps(s, (0, 2, 6)):
            copy.start()
        return carry

    lax.fori_loop(0, count, mix, 0)
    finish_states(count, last, target, send_ref, recv_ref, send_sem, recv_sem)
    lax.fori_loop(0, count, finish_keeps, 0)


def backward_kernel(
    key_dim,
    value_dim,
    *refs,
):
    given, refs = refs[:9], refs[9:]
    gaterank_ref, gain_ref, marks_ref, segment_ref, sums_ref, pairs_ref, *refs = refs
    grad_ref, gain_grad_ref, bias_grad_ref, gaterank_grad_ref, *refs = refs
    held, refs = refs[:9], refs[9:]
    mixed_ref, upstream_ref, attended_ref, start_ref, *rest_refs = held
    logits_ref, scores_ref, end_ref, decay_ref, enter_ref = rest_refs
    out_ref, local_ref, send_ref, recv_ref, send_sem, recv_sem, take_sem = refs
    count, _, length = segment_ref.shape

    def rows_of(s):
        return pl.ds(pl.multiple_of(s * length, length), length)

    def takes(s, kinds):
        rows = rows_of(s)
        for kind in kinds:
            at = rows if len(held[kind].shape) == 2 else s
            yield pltpu.make_async_copy(given[kind].at[at], held[kind].at[at], take_sem.at[s, kind])

    def start_takes(s, carry):
        for copy in takes(s, range(9)):
            copy.start()
        return carry

    lax.fori_loop(0, count, start_takes, 0)
    levels = pairs_ref.shape[0]
    parts, place = lax.axis_size("fsdp"), lax.axis_index("fsdp")
    first, last, target = place == parts - 1, place == 0, lax.rem(place + parts - 1, parts)
    rank = gaterank_ref.shape[0]
    scale = key_dim ** (-0.5)
    value_at = 2 * key_dim
    gate_at = value_at + value_dim
    rank_at = gate_at + value_dim

    greet_neighbours(place, parts)

    @pl.when(first)
    def _():
        recv_ref[...] = jnp.zeros_like(recv_ref)

    gain_grad_ref[...] = jnp.zeros_like(gain_grad_ref)
    bias_grad_ref[...] = jnp.zeros_like(bias_grad_ref)
    gaterank_grad_ref[...] = jnp.zeros_like(gaterank_grad_ref)

    def heads(s, carry):
        rows = rows_of(s)
        for copy in takes(s, range(4)):
            copy.wait()
        upstream = upstream_ref[rows, :]
        attended = attended_ref[rows, :]
        outgate = mixed_ref[rows, pl.ds(gate_at, value_dim)]
        gain = gain_ref[...]
        norm = rms_scale(attended, HEAD_EPS)
        normed = attended * norm
        sig = jax.nn.sigmoid(outgate)
        grad_gate = upstream * (normed * gain) * sig * (1.0 + outgate * (1.0 - sig))
        grad_ref[rows, pl.ds(gate_at, value_dim)] = grad_gate.astype(BF16)
        grad_headed = upstream * (outgate * sig)
        gain_grad_ref[...] += jnp.sum(grad_headed * normed, axis=0, keepdims=True)
        grad_out = rms_back(grad_headed * gain, attended, norm) * marks_ref[rows, pl.ds(3, 1)]
        grad_out = grad_out.astype(BF16)
        out_ref[rows, :] = grad_out
        local_ref[s] = rows_product(grad_out, start_ref[rows, :])
        start_state(s, first, last, target, local_ref, send_ref, recv_ref, send_sem, recv_sem)
        return carry

    lax.fori_loop(0, count, heads, 0)

    def mix(s, carry):
        rows = rows_of(s)
        for copy in takes(s, range(4, 9)):
            copy.wait()
        decay_row = decay_ref[s]
        pass_state(
            s, first, last, target, decay_row, local_ref, send_ref, recv_ref, send_sem, recv_sem
        )
        query = mixed_ref[rows, pl.ds(0, key_dim)] * scale
        key = mixed_ref[rows, pl.ds(key_dim, key_dim)]
        value = mixed_ref[rows, pl.ds(value_at, value_dim)].astype(BF16)
        marks = marks_ref[rows, :]
        logits = logits_ref[rows, :]
        high, low = split_rates(logits)
        grad_out = out_ref[rows, :]
        row = lax.broadcasted_iota(jnp.int32, (length, length), 0)
        col = lax.broadcasted_iota(jnp.int32, (length, length), 1)
        pair_grads = back_product(grad_out, value)
        pair_grads = jnp.where(marks[:, 0:1] == segment_ref[s], pair_grads, 0.0)
        own = jnp.sum(jnp.where(row == col, pair_grads, 0.0), axis=1, keepdims=True)
        grad_query = own * key
        grad_key = own * query
        grad_rates = jnp.zeros((length, key_dim), F32)
        for level in range(levels):
            decay = decayed(sums_ref[level], high, low)
            level_query = (query * decay).astype(BF16)
            level_key = (key * decay).astype(BF16)
            level_pairs = (pair_grads * pairs_ref[level].astype(F32)).astype(BF16)
            level_grad_query = matmul(level_pairs, level_key)
            level_grad_key = rows_product(level_pairs, level_query)
            grad_query += level_grad_query * decay
            grad_key += level_grad_key * decay
            flow = level_grad_query * level_query.astype(F32)
            flow += level_grad_key * level_key.astype(F32)
            grad_rates += rows_product(sums_ref[level], flow.astype(BF16))
        ending = recv_ref[s]
        entering = enter_ref[s]
        start_query = start_ref[rows, :]
        end_key = end_ref[rows, :]
        start_grad = matmul(grad_out, entering)
        end_grad = matmul(value, ending)
        grad_query += start_grad * (decayed(sums_ref[levels], high, low) * marks[:, 1:2])
        grad_key += end_grad * (decayed(sums_ref[levels + 1], high, low) * marks[:, 2:3])
        grad_rates += rows_product(
            sums_ref[levels], (start_grad * start_query.astype(F32)).astype(BF16)
        )
        grad_rates += rows_product(
            sums_ref[levels + 1], (end_grad * end_key.astype(F32)).astype(BF16)
        )
        grad_rates += decay_row * jnp.sum(
            ending.astype(F32) * entering.astype(F32), axis=0, keepdims=True
        )
        grad_value = rows_product(scores_ref[s], grad_out) + back_product(end_key, ending)
        grad_ref[rows, pl.ds(0, key_dim)] = (grad_query * scale).astype(BF16)
        grad_ref[rows, pl.ds(key_dim, key_dim)] = grad_key.astype(BF16)
        grad_ref[rows, pl.ds(value_at, value_dim)] = grad_value.astype(BF16)
        grad_logits = grad_rates / 16.0 * jax.nn.sigmoid(-logits)
        bias_grad_ref[...] += jnp.sum(grad_logits, axis=0, keepdims=True)
        lowrank = mixed_ref[rows, pl.ds(rank_at, rank)]
        gaterank_grad_ref[...] += dot(lowrank, grad_logits, ((0,), (0,)), HIGHEST)
        grad_lowrank = dot(grad_logits, gaterank_ref[...], ((1,), (1,)), HIGHEST)
        rest = grad_ref.shape[1] - rank_at - rank
        grad_ref[rows, pl.ds(rank_at, rank + rest)] = jnp.concatenate(
            [grad_lowrank, jnp.zeros((length, rest), F32)], axis=1
        ).astype(BF16)
        return carry

    lax.fori_loop(0, count, mix, 0)
    finish_states(count, last, target, send_ref, recv_ref, send_sem, recv_sem)


def state_scratch(count, value_dim, key_dim):
    return [
        pltpu.VMEM((count, value_dim, key_dim), F32),
        pltpu.VMEM((count, value_dim, key_dim), BF16),
        pltpu.VMEM((count, value_dim, key_dim), BF16),
        pltpu.SemaphoreType.DMA((count, PIECES)),
        pltpu.SemaphoreType.DMA((count, PIECES)),
    ]


def kernel_params(number, mebibytes=44):
    return pltpu.CompilerParams(
        collective_id=number, has_side_effects=True, vmem_limit_bytes=mebibytes * 2**20
    )


def head_copy(src, dst, send_sem, recv_sem, target):
    return pltpu.make_async_remote_copy(
        src_ref=src,
        dst_ref=dst,
        send_sem=send_sem,
        recv_sem=recv_sem,
        device_id={"head": target},
        device_id_type=pl.DeviceIdType.MESH,
    )


def greet_heads(targets):
    barrier = pltpu.get_barrier_semaphore()
    for target in targets:
        pl.semaphore_signal(
            barrier, inc=1, device_id={"head": target}, device_id_type=pl.DeviceIdType.MESH
        )
    pl.semaphore_wait(barrier, len(targets))


def square(me):
    return me + 1 - 2 * lax.rem(me, 2), me + 2 - 4 * (me // 2), H - 1 - me


def move_columns(weights, gain, out_ref, send_ref, send_sem, recv_sem, own_sem):
    me = lax.axis_index("head")
    place = 0
    for w in weights:
        n = w.shape[1] // H
        for h in range(H):
            part = w[:, pl.ds(h * n, n)].astype(F32) * gain
            send_ref[h, :, pl.ds(place, n)] = part.astype(BF16)
        place += n
    copies = []
    for ahead in range(1, H):
        peer = lax.rem(me + ahead, H)
        copy = head_copy(
            send_ref.at[peer],
            out_ref.at[me],
            send_sem.at[ahead],
            recv_sem.at[ahead],
            peer,
        )
        copy.start()
        copies.append(copy)
    own = pltpu.make_async_copy(send_ref.at[me], out_ref.at[me], own_sem)
    own.start()
    return copies + [own]


def mix_weights_kernel(*refs):
    *weights, extra_ref, gain_ref, out_ref, send_ref, send_sem, recv_sem, own_sem = refs
    me = lax.axis_index("head")
    greet_heads([lax.rem(me + ahead, H) for ahead in range(1, H)])
    spare = extra_ref.shape[1]
    for h in range(H):
        send_ref[h, :, pl.ds(send_ref.shape[2] - spare, spare)] = extra_ref[...]
    gain = gain_ref[...].astype(F32)
    for copy in move_columns(weights, gain, out_ref, send_ref, send_sem, recv_sem, own_sem):
        copy.wait()


def mix_weights(weights, extra, gain):
    rows = extra.shape[0]
    n = sum(w.shape[1] for w in weights) // H + extra.shape[1]
    return pl.pallas_call(
        mix_weights_kernel,
        out_shape=jax.ShapeDtypeStruct((H, rows, n), BF16),
        in_specs=[pl.BlockSpec(memory_space=pltpu.VMEM)] * (len(weights) + 2),
        out_specs=pl.BlockSpec(memory_space=pl.ANY),
        scratch_shapes=[
            pltpu.VMEM((H, rows, n), BF16),
            pltpu.SemaphoreType.DMA((H,)),
            pltpu.SemaphoreType.DMA((H,)),
            pltpu.SemaphoreType.DMA,
        ],
        compiler_params=kernel_params(3, 16),
        cost_estimate=pl.CostEstimate(flops=10**6, bytes_accessed=10**4, transcendentals=0),
        name="mix_weights",
    )(*weights, extra, gain)


class Share:
    def __init__(self, mine_ref, out_ref, send_sem, recv_sem, own_sem):
        self.refs = mine_ref, out_ref, send_sem, recv_sem, own_sem
        self.me = lax.axis_index("head")
        self.size = mine_ref.shape[0] // CHUNKS

    def copy(self, c, kind):
        mine, out, send_sem, recv_sem, _ = self.refs
        sides = square(self.me)[:2]
        rows = pl.ds(c * self.size, self.size)
        if kind < 2:
            src, dst, target = mine.at[rows], out.at[self.me, rows], sides[kind]
        else:
            origin, target = (sides[0], sides[1]) if c % 2 == 0 else (sides[1], sides[0])
            src = dst = out.at[origin, rows]
        return head_copy(src, dst, send_sem.at[c, kind], recv_sem.at[c, kind], target)

    def own(self, c):
        mine, out, _, _, own_sem = self.refs
        rows = pl.ds(c * self.size, self.size)
        return pltpu.make_async_copy(mine.at[rows], out.at[self.me, rows], own_sem.at[c])

    def start(self, c):
        self.copy(c, 0).start()
        self.copy(c, 1).start()
        self.own(c).start()

    def forward(self, c):
        self.copy(c, c % 2).wait_recv()
        self.copy(c, 2).start()

    def finish(self):
        for c in range(CHUNKS):
            self.copy(c, 1 - c % 2).wait_recv()
            self.copy(c, 2).wait_recv()
            self.own(c).wait()
            for kind in range(3):
                self.copy(c, kind).wait_send()


def share_scratch(rows, width):
    return [
        pltpu.VMEM((rows, width), BF16),
        pltpu.SemaphoreType.DMA((CHUNKS, 3)),
        pltpu.SemaphoreType.DMA((CHUNKS, 3)),
        pltpu.SemaphoreType.DMA((CHUNKS,)),
    ]


def share_kernel(
    tokens_ref,
    gate_ref,
    up_ref,
    gain_ref,
    out_ref,
    moved_ref,
    mine_ref,
    share_send,
    share_recv,
    share_own,
    send_ref,
    send_sem,
    recv_sem,
    own_sem,
):
    me = lax.axis_index("head")
    greet_heads([lax.rem(me + ahead, H) for ahead in range(1, H)])
    share = Share(mine_ref, out_ref, share_send, share_recv, share_own)
    for c in range(CHUNKS):
        rows = pl.ds(c * share.size, share.size)
        x = tokens_ref[rows, :].astype(F32)
        mine_ref[rows, :] = (x * rms_scale(x, EPS)).astype(BF16)
        share.start(c)
    gain = gain_ref[...].astype(F32)
    copies = move_columns(
        [gate_ref, up_ref], gain, moved_ref, send_ref, send_sem, recv_sem, own_sem
    )
    for c in range(CHUNKS):
        share.forward(c)
    share.finish()
    for copy in copies:
        copy.wait()


def share_tokens(tokens, w_gate, w_up, gain):
    rows, n = w_gate.shape[0], 2 * w_gate.shape[1] // H
    return pl.pallas_call(
        share_kernel,
        out_shape=[
            jax.ShapeDtypeStruct((H,) + tokens.shape, BF16),
            jax.ShapeDtypeStruct((H, rows, n), BF16),
        ],
        in_specs=[pl.BlockSpec(memory_space=pltpu.VMEM)] * 4,
        out_specs=[pl.BlockSpec(memory_space=pl.ANY)] * 2,
        scratch_shapes=share_scratch(*tokens.shape)
        + [
            pltpu.VMEM((H, rows, n), BF16),
            pltpu.SemaphoreType.DMA((H,)),
            pltpu.SemaphoreType.DMA((H,)),
            pltpu.SemaphoreType.DMA,
        ],
        compiler_params=kernel_params(4, 16),
        cost_estimate=pl.CostEstimate(flops=10**6, bytes_accessed=10**4, transcendentals=0),
        name="share_tokens",
    )(tokens, w_gate, w_up, gain)


def turn_rows(
    partial_ref,
    first_ref,
    relay_ref,
    second_ref,
    pass_ref,
    send_sem,
    recv_sem,
    done,
    share=None,
    fillers=(),
):
    me = lax.axis_index("head")
    side = square(me)
    far = side[2]
    size = first_ref.shape[0] // CHUNKS
    steps = CHUNKS + 3
    fillers = list(fillers)

    def copies(c):
        one, two = (side[0], side[1]) if c % 2 == 0 else (side[1], side[0])
        rows = pl.ds(c * size, size)
        sems = [(send_sem.at[c, kind], recv_sem.at[c, kind]) for kind in range(3)]
        return (
            head_copy(partial_ref.at[far, rows], relay_ref.at[rows], *sems[0], one),
            head_copy(partial_ref.at[one, rows], first_ref.at[rows], *sems[1], one),
            head_copy(pass_ref.at[rows], second_ref.at[rows], *sems[2], two),
            two,
            rows,
        )

    for c in range(CHUNKS):
        relay, first, *_ = copies(c)
        relay.start()
        first.start()
    for step in range(steps):
        for filler in fillers[step * len(fillers) // steps : (step + 1) * len(fillers) // steps]:
            filler()
        if step < CHUNKS:
            relay, _, second, two, rows = copies(step)
            relay.wait_recv()
            both = partial_ref[two, rows, :].astype(F32) + relay_ref[rows, :].astype(F32)
            pass_ref[rows, :] = both.astype(BF16)
            second.start()
        if 1 <= step <= CHUNKS:
            _, first, second, _, rows = copies(step - 1)
            first.wait_recv()
            second.wait_recv()
            total = partial_ref[me, rows, :].astype(F32) + first_ref[rows, :].astype(F32)
            made = done(rows, total + second_ref[rows, :].astype(F32))
            if share is not None:
                share.refs[0][rows, :] = made
                share.start(step - 1)
        if step >= 3 and share is not None:
            share.forward(step - 3)
    if share is not None:
        share.finish()
    for c in range(CHUNKS):
        for copy in copies(c)[:3]:
            copy.wait_send()


def turn_scratch(rows, width):
    return [pltpu.VMEM((rows, width), BF16) for _ in range(4)] + [
        pltpu.SemaphoreType.DMA((CHUNKS, 3)),
        pltpu.SemaphoreType.DMA((CHUNKS, 3)),
    ]


def hidden_kernel(partial_ref, tokens_ref, hidden_ref, out_ref, *scratch):
    greet_heads(square(lax.axis_index("head"))[:2])
    mine_ref, *sems = scratch[6:]

    def done(rows, total):
        hidden = tokens_ref[rows, :].astype(F32) + total
        hidden_ref[rows, :] = hidden
        return (hidden * rms_scale(hidden, EPS)).astype(BF16)

    turn_rows(partial_ref, *scratch[:6], done, Share(mine_ref, out_ref, *sems))


def share_hidden(partial, tokens):
    whole = pl.BlockSpec(memory_space=pltpu.VMEM)
    return pl.pallas_call(
        hidden_kernel,
        out_shape=[
            jax.ShapeDtypeStruct(tokens.shape, F32),
            jax.ShapeDtypeStruct((H,) + tokens.shape, BF16),
        ],
        in_specs=[whole] * 2,
        out_specs=[whole, pl.BlockSpec(memory_space=pl.ANY)],
        scratch_shapes=turn_scratch(*tokens.shape) + share_scratch(*tokens.shape),
        compiler_params=kernel_params(5, 18),
        cost_estimate=pl.CostEstimate(flops=10**6, bytes_accessed=10**4, transcendentals=0),
        name="share_hidden",
    )(partial, tokens)


class PairProduct:
    def __init__(self, left_ref, right_ref, out_ref, give_ref, take_ref, send_sem, recv_sem, own_sem):
        self.refs = left_ref, right_ref, out_ref, give_ref, take_ref
        self.sems = send_sem, recv_sem, own_sem
        self.core = lax.axis_index("core")
        self.groups, self.rows, self.width = out_ref.shape
        self.cut = self.width // 2 if self.width % (2 * LANES) == 0 else self.width

    def product(self, group, core, at):
        left, right, *_ = self.refs
        start = pl.multiple_of((group * CORES + core) * self.rows, LANES)
        return rows_product(left[:, pl.ds(start, self.rows)], right[:, pl.ds(at, self.cut)])

    def copy(self, group):
        give, take = self.refs[3:]
        return pltpu.make_async_remote_copy(
            src_ref=give.at[group],
            dst_ref=take.at[group],
            send_sem=self.sems[0].at[group],
            recv_sem=self.sems[1].at[group],
            device_id={"core": 1 - self.core},
            device_id_type=pl.DeviceIdType.MESH,
        )

    def store(self, group):
        return pltpu.make_async_copy(
            self.refs[3].at[group], self.refs[2].at[group], self.sems[2].at[group]
        )

    def give(self, group, at):
        product = self.product(group, 1 - self.core, at)
        self.refs[3][group, :, pl.ds(at, self.cut)] = product.astype(BF16)
        if at + self.cut == self.width:
            self.copy(group).start()

    def keep(self, group, at):
        give, take = self.refs[3:]
        if at == 0:
            self.copy(group).wait()
        both = self.product(group, self.core, at)
        both += take[group, :, pl.ds(at, self.cut)].astype(F32)
        give[group, :, pl.ds(at, self.cut)] = both.astype(BF16)
        if at + self.cut == self.width:
            self.store(group).start()

    def steps(self):
        places = [
            (group, at) for group in range(self.groups) for at in range(0, self.width, self.cut)
        ]
        return [functools.partial(self.give, *place) for place in places] + [
            functools.partial(self.keep, *place) for place in places
        ]

    def finish(self):
        for group in range(self.groups):
            self.store(group).wait()


def pair_shape(left, right, groups):
    return (groups, left.shape[1] // (CORES * groups), right.shape[1])


def pair_scratch(shape):
    return [
        pltpu.VMEM(shape, BF16),
        pltpu.VMEM(shape, BF16),
        pltpu.SemaphoreType.DMA((shape[0],)),
        pltpu.SemaphoreType.DMA((shape[0],)),
        pltpu.SemaphoreType.DMA((shape[0],)),
    ]


def pair_kernel(left_ref, right_ref, out_ref, *scratch):
    barrier = pltpu.get_barrier_semaphore()
    other = 1 - lax.axis_index("core")
    pl.semaphore_signal(
        barrier, inc=1, device_id={"core": other}, device_id_type=pl.DeviceIdType.MESH
    )
    pl.semaphore_wait(barrier, 1)
    pair = PairProduct(left_ref, right_ref, out_ref, *scratch)
    for step in pair.steps():
        step()
    pair.finish()


def pair_product(left, right, groups, number):
    shape = pair_shape(left, right, groups)
    whole = pl.BlockSpec(memory_space=pltpu.VMEM)
    return pl.pallas_call(
        pair_kernel,
        out_shape=jax.ShapeDtypeStruct(shape, BF16),
        in_specs=[whole] * 2,
        out_specs=pl.BlockSpec(memory_space=pl.ANY),
        scratch_shapes=pair_scratch(shape),
        compiler_params=kernel_params(number, 58),
        cost_estimate=pl.CostEstimate(flops=10**6, bytes_accessed=10**4, transcendentals=0),
        name="pair_product",
    )(left, right)


def branch_kernel(
    partial_ref,
    hidden_ref,
    upstream_ref,
    active_ref,
    down_ref,
    rest_ref,
    grad_ref,
    gain_grad_ref,
    down_out_ref,
    out_ref,
    *scratch,
):
    greet_heads(square(lax.axis_index("head"))[:2])
    mine_ref, *sems = scratch[6:10]
    gain_grad_ref[...] = jnp.zeros_like(gain_grad_ref)

    def done(rows, total):
        hidden = hidden_ref[rows, :]
        scale = rms_scale(hidden, EPS)
        gain_grad_ref[...] += jnp.sum(total * hidden * scale, axis=0, keepdims=True)
        grad = upstream_ref[rows, :].astype(F32) + rms_back(total, hidden, scale)
        grad_ref[rows, :] = grad
        return grad.astype(BF16)

    def down(at):
        rows = pl.ds(at, LANES)
        half = down_ref.shape[1]
        for place, ref in ((0, down_ref), (half, rest_ref)):
            product = matmul(active_ref[rows, :], ref[...])
            down_out_ref[rows, pl.ds(place, half)] = product.astype(BF16)

    share = Share(mine_ref, out_ref, *sems)
    fillers = [functools.partial(down, at) for at in range(0, active_ref.shape[0], LANES)]
    turn_rows(partial_ref, *scratch[:6], done, share, fillers)


def share_branch(partial, hidden, upstream, active, down, rest):
    whole = pl.BlockSpec(memory_space=pltpu.VMEM)
    return pl.pallas_call(
        branch_kernel,
        out_shape=[
            jax.ShapeDtypeStruct(hidden.shape, F32),
            jax.ShapeDtypeStruct((1, hidden.shape[1]), F32),
            jax.ShapeDtypeStruct((active.shape[0], hidden.shape[1]), BF16),
            jax.ShapeDtypeStruct((H,) + hidden.shape, BF16),
        ],
        in_specs=[whole] * 6,
        out_specs=[whole] * 3 + [pl.BlockSpec(memory_space=pl.ANY)],
        scratch_shapes=turn_scratch(*hidden.shape) + share_scratch(*hidden.shape),
        compiler_params=kernel_params(6, 34),
        cost_estimate=pl.CostEstimate(flops=10**6, bytes_accessed=10**4, transcendentals=0),
        name="share_branch",
    )(partial, hidden, upstream, active, down, rest)


def tokens_kernel(partial_ref, tokens_ref, upstream_ref, grad_ref, gain_grad_ref, *scratch):
    greet_heads(square(lax.axis_index("head"))[:2])
    gain_grad_ref[...] = jnp.zeros_like(gain_grad_ref)

    def done(rows, total):
        tokens = tokens_ref[rows, :].astype(F32)
        scale = rms_scale(tokens, EPS)
        gain_grad_ref[...] += jnp.sum(total * tokens * scale, axis=0, keepdims=True)
        grad = upstream_ref[rows, :] + rms_back(total, tokens, scale)
        grad_ref[rows, :] = grad.astype(BF16)

    turn_rows(partial_ref, *scratch, done)


def tokens_back(partial, tokens, upstream):
    whole = pl.BlockSpec(memory_space=pltpu.VMEM)
    return pl.pallas_call(
        tokens_kernel,
        out_shape=[
            jax.ShapeDtypeStruct(tokens.shape, BF16),
            jax.ShapeDtypeStruct((1, tokens.shape[1]), F32),
        ],
        in_specs=[whole] * 3,
        out_specs=[whole] * 2,
        scratch_shapes=turn_scratch(*tokens.shape),
        compiler_params=kernel_params(8, 18),
        cost_estimate=pl.CostEstimate(flops=10**6, bytes_accessed=10**4, transcendentals=0),
        name="tokens_back",
    )(partial, tokens, upstream)


def hidden_units_kernel(cot_ref, down_ref, rest_ref, pre_ref, out_ref):
    units, half = down_ref.shape
    grad = back_product(cot_ref[:, pl.ds(0, half)], down_ref[...])
    grad += back_product(cot_ref[:, pl.ds(half, half)], rest_ref[...])
    gate, up = pre_ref[:, pl.ds(0, units)], pre_ref[:, pl.ds(units, units)]
    sig = jax.nn.sigmoid(gate)
    grad_sig = grad * sig
    out_ref[:, pl.ds(0, units)] = (grad_sig * up * (1.0 + gate * (1.0 - sig))).astype(BF16)
    out_ref[:, pl.ds(units, units)] = (grad_sig * gate).astype(BF16)


def hidden_units_back(cot, down, rest, pre):
    rows, width = cot.shape
    size = 2 * LANES

    def rows_block(n):
        return pl.BlockSpec((size, n), lambda i: (i, 0))

    return pl.pallas_call(
        hidden_units_kernel,
        grid=(rows // size,),
        out_shape=jax.ShapeDtypeStruct(pre.shape, BF16),
        in_specs=[
            rows_block(width),
            pl.BlockSpec(down.shape, lambda i: (0, 0)),
            pl.BlockSpec(rest.shape, lambda i: (0, 0)),
            rows_block(pre.shape[1]),
        ],
        out_specs=rows_block(pre.shape[1]),
        compiler_params=pltpu.CompilerParams(vmem_limit_bytes=58 * 2**20),
        cost_estimate=pl.CostEstimate(flops=10**6, bytes_accessed=10**4, transcendentals=0),
        name="hidden_units_back",
    )(cot, down, rest, pre)


def columns_kernel(widths, total_width, moved_ref, gain_ref, *outs):
    gain = gain_ref[...].astype(F32)
    place = 0
    for out, width in zip(outs, widths):
        for p in range(H):
            piece = moved_ref[p, :, pl.ds(place, width)].astype(F32)
            out[:, pl.ds(p * width, width)] = piece * gain
        place += width
    if total_width:
        total = moved_ref[0, :, pl.ds(place, total_width)].astype(F32)
        for p in range(1, H):
            total += moved_ref[p, :, pl.ds(place, total_width)].astype(F32)
        outs[-1][...] = total * gain


def lay_columns(moved, gain, widths, total_width=0):
    rows = moved.shape[1]
    shapes = [(rows, H * width) for width in widths]
    if total_width:
        shapes.append((rows, total_width))
    whole = pl.BlockSpec(memory_space=pltpu.VMEM)
    return pl.pallas_call(
        functools.partial(columns_kernel, tuple(widths), total_width),
        out_shape=[jax.ShapeDtypeStruct(shape, F32) for shape in shapes],
        in_specs=[whole] * 2,
        out_specs=[whole] * len(shapes),
        compiler_params=pltpu.CompilerParams(vmem_limit_bytes=16 * 2**20),
        cost_estimate=pl.CostEstimate(flops=10**6, bytes_accessed=10**4, transcendentals=0),
        name="lay_columns",
    )(moved, gain)


def mix_forward(mixed, bias, gaterank, gain, marks, segment, sums, pairs, key_dim, value_dim):
    rows = mixed.shape[0]
    count, _, length = segment.shape
    shapes = (
        ((rows, value_dim), BF16),
        ((rows, value_dim), F32),
        ((rows, key_dim), F32),
        ((count, length, length), BF16),
        ((rows, key_dim), BF16),
        ((rows, key_dim), BF16),
        ((count, 1, key_dim), F32),
        ((count, value_dim, key_dim), BF16),
    )
    whole = pl.BlockSpec(memory_space=pltpu.VMEM)
    return pl.pallas_call(
        functools.partial(forward_kernel, key_dim, value_dim),
        out_shape=[jax.ShapeDtypeStruct(*s) for s in shapes],
        in_specs=[pl.BlockSpec(memory_space=pl.ANY)] + [whole] * 7,
        out_specs=[whole] + [pl.BlockSpec(memory_space=pl.ANY)] * (len(shapes) - 1),
        scratch_shapes=[pltpu.VMEM(*s) for s in shapes[1:-1]]
        + state_scratch(count, value_dim, key_dim)
        + [
            pltpu.SemaphoreType.DMA((count, 7)),
            pltpu.VMEM(mixed.shape, mixed.dtype),
            pltpu.SemaphoreType.DMA((count,)),
        ],
        compiler_params=kernel_params(1, 58),
        cost_estimate=pl.CostEstimate(flops=10**6, bytes_accessed=10**4, transcendentals=0),
        name="mix_forward",
    )(mixed, bias, gaterank, gain, marks, segment, sums, pairs)


def mix_backward(
    mixed, kept, upstream, gaterank, gain, marks, segment, sums, pairs, key_dim, value_dim
):
    rows = mixed.shape[0]
    count = segment.shape[0]
    shapes = (
        (mixed.shape, BF16),
        ((1, value_dim), F32),
        ((1, key_dim), F32),
        (gaterank.shape, F32),
    )
    attended, logits, scores, start, end, decay, enter = kept
    given = (mixed, upstream, attended, start, logits, scores, end, decay, enter)
    whole = pl.BlockSpec(memory_space=pltpu.VMEM)
    return pl.pallas_call(
        functools.partial(backward_kernel, key_dim, value_dim),
        out_shape=[jax.ShapeDtypeStruct(*s) for s in shapes],
        in_specs=[pl.BlockSpec(memory_space=pl.ANY)] * 9 + [whole] * 6,
        out_specs=[whole] * len(shapes),
        scratch_shapes=[pltpu.VMEM(a.shape, a.dtype) for a in given]
        + [pltpu.VMEM((rows, value_dim), BF16)]
        + state_scratch(count, value_dim, key_dim)
        + [pltpu.SemaphoreType.DMA((count, 9))],
        compiler_params=kernel_params(2, 58),
        cost_estimate=pl.CostEstimate(flops=10**6, bytes_accessed=10**4, transcendentals=0),
        name="mix_backward",
    )(
        *given,
        gaterank,
        gain,
        marks,
        segment,
        sums,
        pairs,
    )


def per_device(
    tokens,
    doc_lengths,
    norm_gain,
    w_query,
    w_key,
    w_value,
    w_outgate,
    w_lowrank,
    w_gaterank,
    gate_bias,
    head_gain,
    w_output,
    ffn_gain,
    w_gate,
    w_up,
    w_down,
    cotangent,
):
    seqs_here, length, width = tokens.shape
    reps = lax.axis_size("rep")
    parts = lax.axis_size("fsdp")
    devices = reps * H * CORES * parts
    here = lax.axis_index("head")
    key_dim, value_dim = DK, DV
    rank = w_lowrank.shape[1]
    rows = width // devices
    count = H * seqs_here

    rank_at = 2 * key_dim + 2 * value_dim

    def core_sum(g):
        halves = g.reshape(g.shape[0], CORES, -1, g.shape[-1])
        core = lax.axis_index("core")
        other = lax.ppermute(halves[:, 1 - core], "core", ((0, 1), (1, 0)))
        return (halves[:, core].astype(F32) + other.astype(F32)).astype(BF16)

    def scatter_rows(g):
        if reps > 1:
            g = lax.psum_scatter(g, "rep", scatter_dimension=0, tiled=True)
        return lax.psum_scatter(g, "fsdp", scatter_dimension=1, tiled=True)

    def gather_columns(moved):
        whole = lax.all_gather(moved, ("core", "fsdp"), axis=1, tiled=True)
        if reps > 1:
            whole = lax.all_gather(whole, "rep", axis=0, tiled=False)
        return whole.reshape(width, -1)

    def gather_part(w):
        if reps == 1:
            return lax.all_gather(w, SHARE, axis=0, tiled=True)
        whole = lax.all_gather(w, EVERY, axis=0, tiled=True)
        size = whole.shape[0] // H
        return lax.dynamic_slice_in_dim(whole, here * size, size, 0)

    def pair_part(g):
        return core_sum(g[None])[0] if reps == 1 else g

    def scatter_part(g):
        if reps == 1:
            return lax.psum_scatter(g, "fsdp", scatter_dimension=0, tiled=True)
        whole = jnp.zeros((H * g.shape[0], g.shape[1]), BF16)
        whole = lax.dynamic_update_slice_in_dim(whole, g, here * g.shape[0], 0)
        return lax.psum_scatter(whole, EVERY, scatter_dimension=0, tiled=True)

    rank_at = 2 * key_dim + 2 * value_dim

    def with_gain(w, gain):
        return (w.astype(F32) * gain.astype(F32)[:, None]).astype(BF16)

    small = (
        w_gaterank,
        gate_bias.reshape(1, -1),
        head_gain.reshape(1, -1),
        (doc_lengths // 16).astype(BF16).reshape(1, -1),
        (doc_lengths % 16).astype(BF16).reshape(1, -1),
    )
    edges = [rank]
    extra = jnp.pad(with_gain(w_lowrank, norm_gain), ((0, 0), (0, LANES - rank)))
    for piece in small:
        high, wide = piece.shape
        extra += jnp.pad(piece, ((0, rows - high), (edges[-1], LANES - edges[-1] - wide)))
        edges.append(edges[-1] + wide)

    mix_moved = mix_weights((w_query, w_key, w_value, w_outgate), extra, norm_gain[:, None])
    inputs = tokens.reshape(-1, width)
    inputs, _ = after(inputs, mix_moved)
    output_w = gather_part(w_output)
    mix_moved, output_w = after(mix_moved, output_w)
    mix_w = gather_columns(mix_moved)
    w_down, _ = after(w_down, mix_moved)
    down_w = gather_part(w_down[:, : width // 2])
    normed, ffn_moved = share_tokens(inputs, w_gate, w_up, ffn_gain[:, None])
    normed = normed.reshape(-1, width)

    small = mix_w[:, rank_at:].astype(F32).reshape(devices, rows, LANES)
    gaterank, bias, gain_head, long, short = (
        small[:, : rank if i == 0 else 1, edges[i] : edges[i + 1]] for i in range(len(edges) - 1)
    )
    gaterank = gaterank.transpose(1, 0, 2).reshape(rank, -1)
    bias = lax.dynamic_slice_in_dim(bias.reshape(1, -1), here * key_dim, key_dim, 1)
    gaterank = lax.dynamic_slice_in_dim(gaterank, here * key_dim, key_dim, 1)
    gain_head = gain_head.reshape(1, -1)
    lengths = (long * 16.0 + short).reshape(reps, H, CORES, parts, seqs_here, DOCS)
    lengths = lengths[lax.axis_index("rep"), :, lax.axis_index("core"), 0]
    lengths = lengths.reshape(count, DOCS).astype(jnp.int32)

    offset = lax.axis_index("fsdp") * length
    doc_ends = jnp.cumsum(lengths, axis=-1)
    places = offset + jnp.arange(length, dtype=jnp.int32)
    segment = jnp.sum((places[None, :, None] >= doc_ends[:, None, :]).astype(jnp.int32), axis=-1)
    before = jnp.sum((offset - 1 >= doc_ends).astype(jnp.int32), axis=-1)[:, None]
    last = segment[:, -1:]
    marks = jnp.stack(
        [
            segment,
            segment == before,
            segment == last,
            segment != DOCS - 1,
            jnp.broadcast_to(last == before, segment.shape),
        ],
        axis=2,
    )
    marks = jnp.pad(marks.astype(F32).reshape(count * length, 5), ((0, 0), (0, 3)))
    segment = segment.astype(F32).reshape(count, 1, length)

    mixed = matmul(normed, mix_w)
    sums, pairs = level_sums(length)
    sums, pairs = sums.astype(BF16), pairs.astype(BF16)
    gated, *kept = mix_forward(
        mixed, bias, gaterank, gain_head, marks, segment, sums, pairs, key_dim, value_dim
    )
    cot_rows, _ = after(cotangent.reshape(-1, width), normed)
    gated, cot_shared, down_w = after(gated, share_rows(cot_rows), down_w)
    ffn_moved, w_down_rest, _ = after(ffn_moved, w_down[:, width // 2 :], gated)
    ffn_w = gather_columns(ffn_moved)
    down_rest = gather_part(w_down_rest)
    partial = matmul(gated, output_w).astype(BF16).reshape(H, -1, width)
    hidden, normed_two = share_hidden(partial, inputs)
    normed_two = normed_two.reshape(-1, width)

    pre = matmul(normed_two, ffn_w)
    gate_pre, up_pre = jnp.split(pre, 2, axis=1)
    sig_gate = jax.nn.sigmoid(gate_pre)
    activated = (gate_pre * sig_gate * up_pre).astype(BF16)

    grad_down_w = rows_product(activated, cot_shared).astype(BF16)
    down_w, grad_down_w = after(down_w, grad_down_w)
    grad_pre = hidden_units_back(cot_shared, down_w, down_rest, pre)
    grad_pre, grad_down_w = after(grad_pre, pair_part(grad_down_w))
    grad_down_w = scatter_part(grad_down_w)
    grad_ffn_w = pair_product(normed_two, grad_pre, reps * H, 7)
    grad_pre, grad_ffn_w = after(grad_pre, grad_ffn_w)
    partial = back_product(grad_pre, ffn_w).astype(BF16)

    grad_hidden, grad_gain_two, down_partial, branch = share_branch(
        partial.reshape(H, -1, width), hidden, cot_rows, activated, down_w, down_rest
    )
    grad_ffn_w = scatter_rows(grad_ffn_w)
    branch = branch.reshape(-1, width)
    grad_gated = back_product(branch, output_w)
    gated, grad_gated = after(gated, grad_gated)
    grad_output_w = pair_part(rows_product(gated, branch).astype(BF16))
    grad_gated, grad_output_w, grad_down_w = after(grad_gated, grad_output_w, grad_down_w)
    grad_output_w = scatter_part(grad_output_w)
    pieces = move_rows(down_partial)
    grad_mixed, grad_gain_head, grad_bias, grad_gaterank = mix_backward(
        mixed,
        kept,
        grad_gated,
        gaterank,
        gain_head,
        marks,
        segment,
        sums,
        pairs,
        key_dim,
        value_dim,
    )
    grad_mixed, pieces, grad_down_w, grad_ffn_w = after(
        grad_mixed, pieces, grad_down_w, grad_ffn_w
    )
    output = (hidden + jnp.sum(pieces.astype(F32), axis=0)).astype(BF16).reshape(tokens.shape)
    grad_mix_w = pair_product(normed, grad_mixed, reps * H, 11)
    grad_mixed, grad_mix_w = after(grad_mixed, grad_mix_w)
    partial = back_product(grad_mixed, mix_w).astype(BF16)
    grad_mix_w = scatter_rows(grad_mix_w)
    grad_ffn_w = lax.all_to_all(grad_ffn_w, "head", split_axis=0, concat_axis=0, tiled=True)
    partial, grad_output_w, grad_ffn_w = after(partial, grad_output_w, grad_ffn_w)
    tokens_grad, grad_gain_one = tokens_back(partial.reshape(H, -1, width), inputs, grad_hidden)
    tokens_grad = tokens_grad.reshape(tokens.shape)

    units = w_gate.shape[1] // H
    w_gate_grad, w_up_grad = lay_columns(grad_ffn_w, ffn_gain[:, None], (units, units))
    grad_mix_w, _ = after(grad_mix_w, grad_gain_one)
    grad_mix_w = lax.all_to_all(grad_mix_w, "head", split_axis=0, concat_axis=0, tiled=True)
    query_g, key_g, value_g, outgate_g, lowrank_g = lay_columns(
        grad_mix_w, norm_gain[:, None], (key_dim, key_dim, value_dim, value_dim), rank
    )

    def place(g, axis):
        shape = list(g.shape)
        shape[axis] *= H
        return lax.dynamic_update_slice_in_dim(jnp.zeros(shape, F32), g, here * key_dim, axis)

    small_grads = jnp.concatenate(
        [
            grad_gain_one.reshape(devices, -1),
            grad_gain_two.reshape(devices, -1),
            place(grad_bias.reshape(-1), 0).reshape(devices, -1),
            grad_gain_head.reshape(devices, -1),
            place(grad_gaterank, 1)
            .reshape(rank, devices, -1)
            .transpose(1, 0, 2)
            .reshape(devices, -1),
        ],
        axis=1,
    )
    small_grads, _ = after(small_grads, grad_mix_w)
    small_grads = lax.all_to_all(small_grads, EVERY, split_axis=0, concat_axis=0, tiled=True)
    small_grads = jnp.sum(small_grads, axis=0)
    sizes = [norm_gain.shape[0], ffn_gain.shape[0], gate_bias.shape[0], head_gain.shape[0]]
    norm_g, ffn_g, bias_g, head_g, gaterank_g = jnp.split(
        small_grads, [sum(sizes[: i + 1]) for i in range(len(sizes))]
    )
    return (
        output,
        tokens_grad,
        norm_g / norm_gain.astype(F32),
        query_g,
        key_g,
        value_g,
        outgate_g,
        lowrank_g,
        gaterank_g.reshape(w_gaterank.shape),
        bias_g,
        head_g,
        grad_output_w.astype(F32),
        ffn_g / ffn_gain.astype(F32),
        w_gate_grad,
        w_up_grad,
        grad_down_w.astype(F32),
    )


def solution(mesh):
    dp, parts = mesh.shape["dp"], mesh.shape["fsdp"]
    fine = Mesh(mesh.devices.reshape(dp // (H * CORES), H, CORES, parts), EVERY)
    seq = ("rep", "head", "core")
    rows, vector = P(EVERY, None), P(EVERY)
    activations = P(seq, "fsdp", None)
    columns = P(None, EVERY)
    return jax.shard_map(
        per_device,
        mesh=fine,
        in_specs=(
            activations,
            P(seq, None),
            vector,
            rows,
            rows,
            rows,
            rows,
            rows,
            columns,
            vector,
            vector,
            rows,
            vector,
            rows,
            rows,
            rows,
            activations,
        ),
        out_specs=(
            activations,
            activations,
            vector,
            rows,
            rows,
            rows,
            rows,
            rows,
            columns,
            vector,
            vector,
            rows,
            vector,
            rows,
            rows,
            rows,
        ),
        check_vma=False,
    )
```

```python
import functools

import jax
import jax.experimental.pallas as pl
import jax.experimental.pallas.tpu as pltpu
import jax.numpy as jnp
from jax import lax
from jax.sharding import Mesh
from jax.sharding import PartitionSpec as P

H = 4
DK = 256
DV = 512
CORES = 2
DOCS = 8
PIECES = 4
LANES = 128
CHUNKS = 8

EPS = 1e-05
HEAD_EPS = 1.0
HIGHEST = lax.Precision.HIGHEST
F32 = jnp.float32
BF16 = jnp.bfloat16

SHARE = ("rep", "core", "fsdp")
EVERY = ("rep", "head", "core", "fsdp")


def dot(a, b, dims, precision=None):
    return lax.dot_general(a, b, (dims, ((), ())), precision=precision, preferred_element_type=F32)


def after(value, *others):
    return lax.optimization_barrier((value,) + others)


def matmul(a, b):
    return dot(a, b, ((1,), (0,)))


def rows_product(a, b):
    return dot(a, b, ((0,), (0,)))


def back_product(a, b):
    return dot(a, b, ((1,), (1,)))


def batched(form, a, b):
    return jnp.einsum(form, a, b, preferred_element_type=F32)


def rms_scale(values, epsilon):
    return lax.rsqrt(jnp.mean(values * values, axis=-1, keepdims=True) + epsilon)


def rms_back(upstream, values, scale):
    return scale * upstream - values * scale**3 * jnp.mean(upstream * values, axis=-1, keepdims=True)


def share_rows(part):
    spread = jnp.broadcast_to(part[None], (H,) + part.shape)
    whole = lax.all_to_all(spread, "head", split_axis=0, concat_axis=0, tiled=True)
    return whole.reshape(-1, part.shape[-1])


def move_rows(partial):
    pieces = partial.astype(BF16).reshape(H, -1, partial.shape[-1])
    return lax.all_to_all(pieces, "head", split_axis=0, concat_axis=0, tiled=True)


def sum_rows(partial):
    return jnp.sum(move_rows(partial).astype(F32), axis=0)


def level_sums(length):
    rows = jnp.arange(length)[:, None]
    cols = jnp.arange(length)[None, :]
    sums, pairs = [], []
    step = 1
    while step < length:
        bound = rows // (2 * step) * (2 * step) + step - 1
        upper = rows > bound
        sums.append(jnp.where(upper, (cols > bound) & (cols <= rows), (cols > rows) & (cols <= bound)))
        pairs.append(upper & (cols // (2 * step) == rows // (2 * step)) & (cols <= bound))
        step *= 2
    sums.append(cols <= rows)
    sums.append(cols > rows)
    return jnp.stack(sums), jnp.stack(pairs)


def log_sigmoid(x):
    return jnp.minimum(x, 0.0) - jnp.log1p(jnp.exp(-jnp.abs(x)))


def state_copy(send, recv, send_sem, recv_sem, seq, piece, target):
    size = send.shape[1] // PIECES
    part = pl.ds(piece * size, size)
    return pltpu.make_async_remote_copy(
        src_ref=send.at[seq, part],
        dst_ref=recv.at[seq, part],
        send_sem=send_sem.at[seq, piece],
        recv_sem=recv_sem.at[seq, piece],
        device_id={"fsdp": target},
        device_id_type=pl.DeviceIdType.MESH,
    )


def greet_neighbours(place, parts):
    barrier = pltpu.get_barrier_semaphore()
    for near, there in ((place - 1, place > 0), (place + 1, place < parts - 1)):

        @pl.when(there)
        def _(near=near):
            pl.semaphore_signal(
                barrier,
                inc=1,
                device_id={"fsdp": lax.rem(near + parts, parts)},
                device_id_type=pl.DeviceIdType.MESH,
            )

    peers = (place > 0).astype(jnp.int32) + (place < parts - 1).astype(jnp.int32)
    pl.semaphore_wait(barrier, peers)


def pass_state(s, first, last, target, decay, local, send, recv, send_sem, recv_sem):
    size = send.shape[1] // PIECES
    for piece in range(PIECES):
        part = pl.ds(piece * size, size)
        copy = state_copy(send, recv, send_sem, recv_sem, s, piece, target)

        @pl.when(jnp.logical_not(first))
        def _(copy=copy):
            copy.wait_recv()

        @pl.when(jnp.logical_not(jnp.logical_or(first, last)))
        def _(copy=copy, part=part):
            joined = decay * recv[s, part].astype(F32) + local[s, part]
            send[s, part] = joined.astype(BF16)
            copy.start()


def start_state(s, first, last, target, local, send, recv, send_sem, recv_sem):
    @pl.when(jnp.logical_and(first, jnp.logical_not(last)))
    def _():
        send[s] = local[s].astype(BF16)
        for piece in range(PIECES):
            state_copy(send, recv, send_sem, recv_sem, s, piece, target).start()


def finish_states(count, last, target, send, recv, send_sem, recv_sem):
    @pl.when(jnp.logical_not(last))
    def _():
        def one(s, carry):
            for piece in range(PIECES):
                state_copy(send, recv, send_sem, recv_sem, s, piece, target).wait_send()
            return carry

        lax.fori_loop(0, count, one, 0)


def split_rates(logits):
    rates = log_sigmoid(logits) / 16.0
    high = rates.astype(BF16)
    return high, (rates - high.astype(F32)).astype(BF16)


def decayed(sums, high, low):
    return jnp.exp(matmul(sums, high) + matmul(sums, low))


def forward_kernel(
    key_dim,
    value_dim,
    given_ref,
    bias_ref,
    gaterank_ref,
    gain_ref,
    marks_ref,
    segment_ref,
    sums_ref,
    pairs_ref,
    gated_ref,
    *refs,
):
    kept, (attended_ref, logits_ref, scores_ref, start_ref, end_ref, decay_ref) = refs[:7], refs[7:13]
    local_ref, send_ref, recv_ref, send_sem, recv_sem, keep_sem, mixed_ref, take_sem = refs[13:]
    count, _, length = segment_ref.shape
    levels = pairs_ref.shape[0]
    parts, place = lax.axis_size("fsdp"), lax.axis_index("fsdp")
    first, last, target = place == 0, place == parts - 1, lax.rem(place + 1, parts)

    def rows_of(s):
        return pl.ds(pl.multiple_of(s * length, length), length)

    def keeps(s, kinds):
        held = (attended_ref, logits_ref, scores_ref, start_ref, end_ref, decay_ref, recv_ref)
        rows = rows_of(s)
        for kind in kinds:
            at = rows if len(held[kind].shape) == 2 else s
            yield pltpu.make_async_copy(held[kind].at[at], kept[kind].at[at], keep_sem.at[s, kind])

    def take(s):
        rows = rows_of(s)
        return pltpu.make_async_copy(given_ref.at[rows], mixed_ref.at[rows], take_sem.at[s])

    def start_take(s, carry):
        take(s).start()
        return carry

    lax.fori_loop(0, count, start_take, 0)

    def finish_keeps(s, carry):
        for copy in keeps(s, range(7)):
            copy.wait()
        return carry

    rank = gaterank_ref.shape[0]
    scale = key_dim ** (-0.5)
    value_at = 2 * key_dim
    gate_at = value_at + value_dim
    rank_at = gate_at + value_dim

    greet_neighbours(place, parts)

    @pl.when(first)
    def _():
        recv_ref[...] = jnp.zeros_like(recv_ref)

    def ends(s, carry):
        rows = rows_of(s)
        take(s).wait()
        lowrank = mixed_ref[rows, pl.ds(rank_at, rank)]
        logits = dot(lowrank, gaterank_ref[...], ((1,), (0,)), HIGHEST) + bias_ref[...]
        logits_ref[rows, :] = logits
        high, low = split_rates(logits)
        from_start = decayed(sums_ref[levels], high, low)
        to_end = decayed(sums_ref[levels + 1], high, low)
        marks = marks_ref[rows, :]
        decay_ref[s] = from_start[length - 1 :, :] * marks[:1, 4:5]
        query = mixed_ref[rows, pl.ds(0, key_dim)] * scale
        key = mixed_ref[rows, pl.ds(key_dim, key_dim)]
        start_ref[rows, :] = (query * (from_start * marks[:, 1:2])).astype(BF16)
        end_key = (key * (to_end * marks[:, 2:3])).astype(BF16)
        end_ref[rows, :] = end_key
        value = mixed_ref[rows, pl.ds(value_at, value_dim)].astype(BF16)
        local_ref[s] = rows_product(value, end_key)
        start_state(s, first, last, target, local_ref, send_ref, recv_ref, send_sem, recv_sem)
        for copy in keeps(s, (1, 3, 4, 5)):
            copy.start()
        return carry

    lax.fori_loop(0, count, ends, 0)

    def mix(s, carry):
        rows = rows_of(s)
        pass_state(
            s, first, last, target, decay_ref[s], local_ref, send_ref, recv_ref, send_sem, recv_sem
        )
        query = mixed_ref[rows, pl.ds(0, key_dim)] * scale
        key = mixed_ref[rows, pl.ds(key_dim, key_dim)]
        high, low = split_rates(logits_ref[rows, :])
        scores = jnp.zeros((length, length), F32)
        for level in range(levels):
            decay = decayed(sums_ref[level], high, low)
            pair = back_product((query * decay).astype(BF16), (key * decay).astype(BF16))
            scores += pair * pairs_ref[level].astype(F32)
        row = lax.broadcasted_iota(jnp.int32, (length, length), 0)
        col = lax.broadcasted_iota(jnp.int32, (length, length), 1)
        own = jnp.sum(query * key, axis=1, keepdims=True)
        scores += jnp.where(row == col, own, 0.0)
        marks = marks_ref[rows, :]
        scores = jnp.where(marks[:, 0:1] == segment_ref[s], scores, 0.0).astype(BF16)
        scores_ref[s] = scores
        value = mixed_ref[rows, pl.ds(value_at, value_dim)].astype(BF16)
        attended = matmul(scores, value) + back_product(start_ref[rows, :], recv_ref[s])
        attended = attended * marks[:, 3:4]
        attended_ref[rows, :] = attended
        headed = attended * rms_scale(attended, HEAD_EPS) * gain_ref[...]
        outgate = mixed_ref[rows, pl.ds(gate_at, value_dim)]
        gated_ref[rows, :] = (headed * (outgate * jax.nn.sigmoid(outgate))).astype(BF16)
        for copy in keeps(s, (0, 2, 6)):
            copy.start()
        return carry

    lax.fori_loop(0, count, mix, 0)
    finish_states(count, last, target, send_ref, recv_ref, send_sem, recv_sem)
    lax.fori_loop(0, count, finish_keeps, 0)


def backward_kernel(
    key_dim,
    value_dim,
    *refs,
):
    given, refs = refs[:9], refs[9:]
    gaterank_ref, gain_ref, marks_ref, segment_ref, sums_ref, pairs_ref, *refs = refs
    grad_ref, gain_grad_ref, bias_grad_ref, gaterank_grad_ref, *refs = refs
    held, refs = refs[:9], refs[9:]
    mixed_ref, upstream_ref, attended_ref, start_ref, *rest_refs = held
    logits_ref, scores_ref, end_ref, decay_ref, enter_ref = rest_refs
    out_ref, local_ref, send_ref, recv_ref, send_sem, recv_sem, take_sem = refs
    count, _, length = segment_ref.shape

    def rows_of(s):
        return pl.ds(pl.multiple_of(s * length, length), length)

    def takes(s, kinds):
        rows = rows_of(s)
        for kind in kinds:
            at = rows if len(held[kind].shape) == 2 else s
            yield pltpu.make_async_copy(given[kind].at[at], held[kind].at[at], take_sem.at[s, kind])

    def start_takes(s, carry):
        for copy in takes(s, range(9)):
            copy.start()
        return carry

    lax.fori_loop(0, count, start_takes, 0)
    levels = pairs_ref.shape[0]
    parts, place = lax.axis_size("fsdp"), lax.axis_index("fsdp")
    first, last, target = place == parts - 1, place == 0, lax.rem(place + parts - 1, parts)
    rank = gaterank_ref.shape[0]
    scale = key_dim ** (-0.5)
    value_at = 2 * key_dim
    gate_at = value_at + value_dim
    rank_at = gate_at + value_dim

    greet_neighbours(place, parts)

    @pl.when(first)
    def _():
        recv_ref[...] = jnp.zeros_like(recv_ref)

    gain_grad_ref[...] = jnp.zeros_like(gain_grad_ref)
    bias_grad_ref[...] = jnp.zeros_like(bias_grad_ref)
    gaterank_grad_ref[...] = jnp.zeros_like(gaterank_grad_ref)

    def heads(s, carry):
        rows = rows_of(s)
        for copy in takes(s, range(4)):
            copy.wait()
        upstream = upstream_ref[rows, :]
        attended = attended_ref[rows, :]
        outgate = mixed_ref[rows, pl.ds(gate_at, value_dim)]
        gain = gain_ref[...]
        norm = rms_scale(attended, HEAD_EPS)
        normed = attended * norm
        sig = jax.nn.sigmoid(outgate)
        grad_gate = upstream * (normed * gain) * sig * (1.0 + outgate * (1.0 - sig))
        grad_ref[rows, pl.ds(gate_at, value_dim)] = grad_gate.astype(BF16)
        grad_headed = upstream * (outgate * sig)
        gain_grad_ref[...] += jnp.sum(grad_headed * normed, axis=0, keepdims=True)
        grad_out = rms_back(grad_headed * gain, attended, norm) * marks_ref[rows, pl.ds(3, 1)]
        grad_out = grad_out.astype(BF16)
        out_ref[rows, :] = grad_out
        local_ref[s] = rows_product(grad_out, start_ref[rows, :])
        start_state(s, first, last, target, local_ref, send_ref, recv_ref, send_sem, recv_sem)
        return carry

    lax.fori_loop(0, count, heads, 0)

    def mix(s, carry):
        rows = rows_of(s)
        for copy in takes(s, range(4, 9)):
            copy.wait()
        decay_row = decay_ref[s]
        pass_state(
            s, first, last, target, decay_row, local_ref, send_ref, recv_ref, send_sem, recv_sem
        )
        query = mixed_ref[rows, pl.ds(0, key_dim)] * scale
        key = mixed_ref[rows, pl.ds(key_dim, key_dim)]
        value = mixed_ref[rows, pl.ds(value_at, value_dim)].astype(BF16)
        marks = marks_ref[rows, :]
        logits = logits_ref[rows, :]
        high, low = split_rates(logits)
        grad_out = out_ref[rows, :]
        row = lax.broadcasted_iota(jnp.int32, (length, length), 0)
        col = lax.broadcasted_iota(jnp.int32, (length, length), 1)
        pair_grads = back_product(grad_out, value)
        pair_grads = jnp.where(marks[:, 0:1] == segment_ref[s], pair_grads, 0.0)
        own = jnp.sum(jnp.where(row == col, pair_grads, 0.0), axis=1, keepdims=True)
        grad_query = own * key
        grad_key = own * query
        grad_rates = jnp.zeros((length, key_dim), F32)
        for level in range(levels):
            decay = decayed(sums_ref[level], high, low)
            level_query = (query * decay).astype(BF16)
            level_key = (key * decay).astype(BF16)
            level_pairs = (pair_grads * pairs_ref[level].astype(F32)).astype(BF16)
            level_grad_query = matmul(level_pairs, level_key)
            level_grad_key = rows_product(level_pairs, level_query)
            grad_query += level_grad_query * decay
            grad_key += level_grad_key * decay
            flow = level_grad_query * level_query.astype(F32)
            flow += level_grad_key * level_key.astype(F32)
            grad_rates += rows_product(sums_ref[level], flow.astype(BF16))
        ending = recv_ref[s]
        entering = enter_ref[s]
        start_query = start_ref[rows, :]
        end_key = end_ref[rows, :]
        start_grad = matmul(grad_out, entering)
        end_grad = matmul(value, ending)
        grad_query += start_grad * (decayed(sums_ref[levels], high, low) * marks[:, 1:2])
        grad_key += end_grad * (decayed(sums_ref[levels + 1], high, low) * marks[:, 2:3])
        grad_rates += rows_product(
            sums_ref[levels], (start_grad * start_query.astype(F32)).astype(BF16)
        )
        grad_rates += rows_product(
            sums_ref[levels + 1], (end_grad * end_key.astype(F32)).astype(BF16)
        )
        grad_rates += decay_row * jnp.sum(
            ending.astype(F32) * entering.astype(F32), axis=0, keepdims=True
        )
        grad_value = rows_product(scores_ref[s], grad_out) + back_product(end_key, ending)
        grad_ref[rows, pl.ds(0, key_dim)] = (grad_query * scale).astype(BF16)
        grad_ref[rows, pl.ds(key_dim, key_dim)] = grad_key.astype(BF16)
        grad_ref[rows, pl.ds(value_at, value_dim)] = grad_value.astype(BF16)
        grad_logits = grad_rates / 16.0 * jax.nn.sigmoid(-logits)
        bias_grad_ref[...] += jnp.sum(grad_logits, axis=0, keepdims=True)
        lowrank = mixed_ref[rows, pl.ds(rank_at, rank)]
        gaterank_grad_ref[...] += dot(lowrank, grad_logits, ((0,), (0,)), HIGHEST)
        grad_lowrank = dot(grad_logits, gaterank_ref[...], ((1,), (1,)), HIGHEST)
        rest = grad_ref.shape[1] - rank_at - rank
        grad_ref[rows, pl.ds(rank_at, rank + rest)] = jnp.concatenate(
            [grad_lowrank, jnp.zeros((length, rest), F32)], axis=1
        ).astype(BF16)
        return carry

    lax.fori_loop(0, count, mix, 0)
    finish_states(count, last, target, send_ref, recv_ref, send_sem, recv_sem)


def state_scratch(count, value_dim, key_dim):
    return [
        pltpu.VMEM((count, value_dim, key_dim), F32),
        pltpu.VMEM((count, value_dim, key_dim), BF16),
        pltpu.VMEM((count, value_dim, key_dim), BF16),
        pltpu.SemaphoreType.DMA((count, PIECES)),
        pltpu.SemaphoreType.DMA((count, PIECES)),
    ]


def kernel_params(number, mebibytes=44):
    return pltpu.CompilerParams(
        collective_id=number, has_side_effects=True, vmem_limit_bytes=mebibytes * 2**20
    )


def head_copy(src, dst, send_sem, recv_sem, target):
    return pltpu.make_async_remote_copy(
        src_ref=src,
        dst_ref=dst,
        send_sem=send_sem,
        recv_sem=recv_sem,
        device_id={"head": target},
        device_id_type=pl.DeviceIdType.MESH,
    )


def greet_heads(targets):
    barrier = pltpu.get_barrier_semaphore()
    for target in targets:
        pl.semaphore_signal(
            barrier, inc=1, device_id={"head": target}, device_id_type=pl.DeviceIdType.MESH
        )
    pl.semaphore_wait(barrier, len(targets))


def square(me):
    return me + 1 - 2 * lax.rem(me, 2), me + 2 - 4 * (me // 2), H - 1 - me


def move_columns(weights, gain, out_ref, send_ref, send_sem, recv_sem, own_sem):
    me = lax.axis_index("head")
    place = 0
    for w in weights:
        n = w.shape[1] // H
        for h in range(H):
            part = w[:, pl.ds(h * n, n)].astype(F32) * gain
            send_ref[h, :, pl.ds(place, n)] = part.astype(BF16)
        place += n
    copies = []
    for ahead in range(1, H):
        peer = lax.rem(me + ahead, H)
        copy = head_copy(
            send_ref.at[peer],
            out_ref.at[me],
            send_sem.at[ahead],
            recv_sem.at[ahead],
            peer,
        )
        copy.start()
        copies.append(copy)
    own = pltpu.make_async_copy(send_ref.at[me], out_ref.at[me], own_sem)
    own.start()
    return copies + [own]


def mix_weights_kernel(*refs):
    *weights, extra_ref, gain_ref, out_ref, send_ref, send_sem, recv_sem, own_sem = refs
    me = lax.axis_index("head")
    greet_heads([lax.rem(me + ahead, H) for ahead in range(1, H)])
    spare = extra_ref.shape[1]
    for h in range(H):
        send_ref[h, :, pl.ds(send_ref.shape[2] - spare, spare)] = extra_ref[...]
    gain = gain_ref[...].astype(F32)
    for copy in move_columns(weights, gain, out_ref, send_ref, send_sem, recv_sem, own_sem):
        copy.wait()


def mix_weights(weights, extra, gain):
    rows = extra.shape[0]
    n = sum(w.shape[1] for w in weights) // H + extra.shape[1]
    return pl.pallas_call(
        mix_weights_kernel,
        out_shape=jax.ShapeDtypeStruct((H, rows, n), BF16),
        in_specs=[pl.BlockSpec(memory_space=pltpu.VMEM)] * (len(weights) + 2),
        out_specs=pl.BlockSpec(memory_space=pl.ANY),
        scratch_shapes=[
            pltpu.VMEM((H, rows, n), BF16),
            pltpu.SemaphoreType.DMA((H,)),
            pltpu.SemaphoreType.DMA((H,)),
            pltpu.SemaphoreType.DMA,
        ],
        compiler_params=kernel_params(3, 16),
        cost_estimate=pl.CostEstimate(flops=10**6, bytes_accessed=10**4, transcendentals=0),
        name="mix_weights",
    )(*weights, extra, gain)


class Share:
    def __init__(self, mine_ref, out_ref, send_sem, recv_sem, own_sem):
        self.refs = mine_ref, out_ref, send_sem, recv_sem, own_sem
        self.me = lax.axis_index("head")
        self.size = mine_ref.shape[0] // CHUNKS

    def copy(self, c, kind):
        mine, out, send_sem, recv_sem, _ = self.refs
        sides = square(self.me)[:2]
        rows = pl.ds(c * self.size, self.size)
        if kind < 2:
            src, dst, target = mine.at[rows], out.at[self.me, rows], sides[kind]
        else:
            origin, target = (sides[0], sides[1]) if c % 2 == 0 else (sides[1], sides[0])
            src = dst = out.at[origin, rows]
        return head_copy(src, dst, send_sem.at[c, kind], recv_sem.at[c, kind], target)

    def own(self, c):
        mine, out, _, _, own_sem = self.refs
        rows = pl.ds(c * self.size, self.size)
        return pltpu.make_async_copy(mine.at[rows], out.at[self.me, rows], own_sem.at[c])

    def start(self, c):
        self.copy(c, 0).start()
        self.copy(c, 1).start()
        self.own(c).start()

    def forward(self, c):
        self.copy(c, c % 2).wait_recv()
        self.copy(c, 2).start()

    def finish(self):
        for c in range(CHUNKS):
            self.copy(c, 1 - c % 2).wait_recv()
            self.copy(c, 2).wait_recv()
            self.own(c).wait()
            for kind in range(3):
                self.copy(c, kind).wait_send()


def share_scratch(rows, width):
    return [
        pltpu.VMEM((rows, width), BF16),
        pltpu.SemaphoreType.DMA((CHUNKS, 3)),
        pltpu.SemaphoreType.DMA((CHUNKS, 3)),
        pltpu.SemaphoreType.DMA((CHUNKS,)),
    ]


def share_kernel(
    tokens_ref,
    gate_ref,
    up_ref,
    gain_ref,
    out_ref,
    moved_ref,
    mine_ref,
    share_send,
    share_recv,
    share_own,
    send_ref,
    send_sem,
    recv_sem,
    own_sem,
):
    me = lax.axis_index("head")
    greet_heads([lax.rem(me + ahead, H) for ahead in range(1, H)])
    share = Share(mine_ref, out_ref, share_send, share_recv, share_own)
    for c in range(CHUNKS):
        rows = pl.ds(c * share.size, share.size)
        x = tokens_ref[rows, :].astype(F32)
        mine_ref[rows, :] = (x * rms_scale(x, EPS)).astype(BF16)
        share.start(c)
    gain = gain_ref[...].astype(F32)
    copies = move_columns(
        [gate_ref, up_ref], gain, moved_ref, send_ref, send_sem, recv_sem, own_sem
    )
    for c in range(CHUNKS):
        share.forward(c)
    share.finish()
    for copy in copies:
        copy.wait()


def share_tokens(tokens, w_gate, w_up, gain):
    rows, n = w_gate.shape[0], 2 * w_gate.shape[1] // H
    return pl.pallas_call(
        share_kernel,
        out_shape=[
            jax.ShapeDtypeStruct((H,) + tokens.shape, BF16),
            jax.ShapeDtypeStruct((H, rows, n), BF16),
        ],
        in_specs=[pl.BlockSpec(memory_space=pltpu.VMEM)] * 4,
        out_specs=[pl.BlockSpec(memory_space=pl.ANY)] * 2,
        scratch_shapes=share_scratch(*tokens.shape)
        + [
            pltpu.VMEM((H, rows, n), BF16),
            pltpu.SemaphoreType.DMA((H,)),
            pltpu.SemaphoreType.DMA((H,)),
            pltpu.SemaphoreType.DMA,
        ],
        compiler_params=kernel_params(4, 16),
        cost_estimate=pl.CostEstimate(flops=10**6, bytes_accessed=10**4, transcendentals=0),
        name="share_tokens",
    )(tokens, w_gate, w_up, gain)


def turn_rows(
    partial_ref,
    first_ref,
    relay_ref,
    second_ref,
    pass_ref,
    send_sem,
    recv_sem,
    done,
    share=None,
    fillers=(),
):
    me = lax.axis_index("head")
    side = square(me)
    far = side[2]
    size = first_ref.shape[0] // CHUNKS
    steps = CHUNKS + 3
    fillers = list(fillers)

    def copies(c):
        one, two = (side[0], side[1]) if c % 2 == 0 else (side[1], side[0])
        rows = pl.ds(c * size, size)
        sems = [(send_sem.at[c, kind], recv_sem.at[c, kind]) for kind in range(3)]
        return (
            head_copy(partial_ref.at[far, rows], relay_ref.at[rows], *sems[0], one),
            head_copy(partial_ref.at[one, rows], first_ref.at[rows], *sems[1], one),
            head_copy(pass_ref.at[rows], second_ref.at[rows], *sems[2], two),
            two,
            rows,
        )

    for c in range(CHUNKS):
        relay, first, *_ = copies(c)
        relay.start()
        first.start()
    for step in range(steps):
        for filler in fillers[step * len(fillers) // steps : (step + 1) * len(fillers) // steps]:
            filler()
        if step < CHUNKS:
            relay, _, second, two, rows = copies(step)
            relay.wait_recv()
            both = partial_ref[two, rows, :].astype(F32) + relay_ref[rows, :].astype(F32)
            pass_ref[rows, :] = both.astype(BF16)
            second.start()
        if 1 <= step <= CHUNKS:
            _, first, second, _, rows = copies(step - 1)
            first.wait_recv()
            second.wait_recv()
            total = partial_ref[me, rows, :].astype(F32) + first_ref[rows, :].astype(F32)
            made = done(rows, total + second_ref[rows, :].astype(F32))
            if share is not None:
                share.refs[0][rows, :] = made
                share.start(step - 1)
        if step >= 3 and share is not None:
            share.forward(step - 3)
    if share is not None:
        share.finish()
    for c in range(CHUNKS):
        for copy in copies(c)[:3]:
            copy.wait_send()


def turn_scratch(rows, width):
    return [pltpu.VMEM((rows, width), BF16) for _ in range(4)] + [
        pltpu.SemaphoreType.DMA((CHUNKS, 3)),
        pltpu.SemaphoreType.DMA((CHUNKS, 3)),
    ]


def hidden_kernel(partial_ref, tokens_ref, hidden_ref, out_ref, *scratch):
    greet_heads(square(lax.axis_index("head"))[:2])
    mine_ref, *sems = scratch[6:]

    def done(rows, total):
        hidden = tokens_ref[rows, :].astype(F32) + total
        hidden_ref[rows, :] = hidden
        return (hidden * rms_scale(hidden, EPS)).astype(BF16)

    turn_rows(partial_ref, *scratch[:6], done, Share(mine_ref, out_ref, *sems))


def share_hidden(partial, tokens):
    whole = pl.BlockSpec(memory_space=pltpu.VMEM)
    return pl.pallas_call(
        hidden_kernel,
        out_shape=[
            jax.ShapeDtypeStruct(tokens.shape, F32),
            jax.ShapeDtypeStruct((H,) + tokens.shape, BF16),
        ],
        in_specs=[whole] * 2,
        out_specs=[whole, pl.BlockSpec(memory_space=pl.ANY)],
        scratch_shapes=turn_scratch(*tokens.shape) + share_scratch(*tokens.shape),
        compiler_params=kernel_params(5, 18),
        cost_estimate=pl.CostEstimate(flops=10**6, bytes_accessed=10**4, transcendentals=0),
        name="share_hidden",
    )(partial, tokens)


class PairProduct:
    def __init__(self, left_ref, right_ref, out_ref, give_ref, take_ref, send_sem, recv_sem, own_sem):
        self.refs = left_ref, right_ref, out_ref, give_ref, take_ref
        self.sems = send_sem, recv_sem, own_sem
        self.core = lax.axis_index("core")
        self.groups, self.rows, self.width = out_ref.shape
        self.cut = self.width // 2 if self.width % (2 * LANES) == 0 else self.width

    def product(self, group, core, at):
        left, right, *_ = self.refs
        start = pl.multiple_of((group * CORES + core) * self.rows, LANES)
        return rows_product(left[:, pl.ds(start, self.rows)], right[:, pl.ds(at, self.cut)])

    def copy(self, group):
        give, take = self.refs[3:]
        return pltpu.make_async_remote_copy(
            src_ref=give.at[group],
            dst_ref=take.at[group],
            send_sem=self.sems[0].at[group],
            recv_sem=self.sems[1].at[group],
            device_id={"core": 1 - self.core},
            device_id_type=pl.DeviceIdType.MESH,
        )

    def store(self, group):
        return pltpu.make_async_copy(
            self.refs[3].at[group], self.refs[2].at[group], self.sems[2].at[group]
        )

    def give(self, group, at):
        product = self.product(group, 1 - self.core, at)
        self.refs[3][group, :, pl.ds(at, self.cut)] = product.astype(BF16)
        if at + self.cut == self.width:
            self.copy(group).start()

    def keep(self, group, at):
        give, take = self.refs[3:]
        if at == 0:
            self.copy(group).wait()
        both = self.product(group, self.core, at)
        both += take[group, :, pl.ds(at, self.cut)].astype(F32)
        give[group, :, pl.ds(at, self.cut)] = both.astype(BF16)
        if at + self.cut == self.width:
            self.store(group).start()

    def steps(self):
        places = [
            (group, at) for group in range(self.groups) for at in range(0, self.width, self.cut)
        ]
        return [functools.partial(self.give, *place) for place in places] + [
            functools.partial(self.keep, *place) for place in places
        ]

    def finish(self):
        for group in range(self.groups):
            self.store(group).wait()


def pair_shape(left, right, groups):
    return (groups, left.shape[1] // (CORES * groups), right.shape[1])


def pair_scratch(shape):
    return [
        pltpu.VMEM(shape, BF16),
        pltpu.VMEM(shape, BF16),
        pltpu.SemaphoreType.DMA((shape[0],)),
        pltpu.SemaphoreType.DMA((shape[0],)),
        pltpu.SemaphoreType.DMA((shape[0],)),
    ]


def pair_kernel(left_ref, right_ref, out_ref, *scratch):
    barrier = pltpu.get_barrier_semaphore()
    other = 1 - lax.axis_index("core")
    pl.semaphore_signal(
        barrier, inc=1, device_id={"core": other}, device_id_type=pl.DeviceIdType.MESH
    )
    pl.semaphore_wait(barrier, 1)
    pair = PairProduct(left_ref, right_ref, out_ref, *scratch)
    for step in pair.steps():
        step()
    pair.finish()


def pair_product(left, right, groups, number):
    shape = pair_shape(left, right, groups)
    whole = pl.BlockSpec(memory_space=pltpu.VMEM)
    return pl.pallas_call(
        pair_kernel,
        out_shape=jax.ShapeDtypeStruct(shape, BF16),
        in_specs=[whole] * 2,
        out_specs=pl.BlockSpec(memory_space=pl.ANY),
        scratch_shapes=pair_scratch(shape),
        compiler_params=kernel_params(number, 58),
        cost_estimate=pl.CostEstimate(flops=10**6, bytes_accessed=10**4, transcendentals=0),
        name="pair_product",
    )(left, right)


def branch_kernel(
    partial_ref,
    hidden_ref,
    upstream_ref,
    active_ref,
    down_ref,
    rest_ref,
    grad_ref,
    gain_grad_ref,
    down_out_ref,
    out_ref,
    *scratch,
):
    greet_heads(square(lax.axis_index("head"))[:2])
    mine_ref, *sems = scratch[6:10]
    gain_grad_ref[...] = jnp.zeros_like(gain_grad_ref)

    def done(rows, total):
        hidden = hidden_ref[rows, :]
        scale = rms_scale(hidden, EPS)
        gain_grad_ref[...] += jnp.sum(total * hidden * scale, axis=0, keepdims=True)
        grad = upstream_ref[rows, :].astype(F32) + rms_back(total, hidden, scale)
        grad_ref[rows, :] = grad
        return grad.astype(BF16)

    def down(at):
        rows = pl.ds(at, LANES)
        half = down_ref.shape[1]
        for place, ref in ((0, down_ref), (half, rest_ref)):
            product = matmul(active_ref[rows, :], ref[...])
            down_out_ref[rows, pl.ds(place, half)] = product.astype(BF16)

    share = Share(mine_ref, out_ref, *sems)
    fillers = [functools.partial(down, at) for at in range(0, active_ref.shape[0], LANES)]
    turn_rows(partial_ref, *scratch[:6], done, share, fillers)


def share_branch(partial, hidden, upstream, active, down, rest):
    whole = pl.BlockSpec(memory_space=pltpu.VMEM)
    return pl.pallas_call(
        branch_kernel,
        out_shape=[
            jax.ShapeDtypeStruct(hidden.shape, F32),
            jax.ShapeDtypeStruct((1, hidden.shape[1]), F32),
            jax.ShapeDtypeStruct((active.shape[0], hidden.shape[1]), BF16),
            jax.ShapeDtypeStruct((H,) + hidden.shape, BF16),
        ],
        in_specs=[whole] * 6,
        out_specs=[whole] * 3 + [pl.BlockSpec(memory_space=pl.ANY)],
        scratch_shapes=turn_scratch(*hidden.shape) + share_scratch(*hidden.shape),
        compiler_params=kernel_params(6, 34),
        cost_estimate=pl.CostEstimate(flops=10**6, bytes_accessed=10**4, transcendentals=0),
        name="share_branch",
    )(partial, hidden, upstream, active, down, rest)


def tokens_kernel(partial_ref, tokens_ref, upstream_ref, grad_ref, gain_grad_ref, *scratch):
    greet_heads(square(lax.axis_index("head"))[:2])
    gain_grad_ref[...] = jnp.zeros_like(gain_grad_ref)

    def done(rows, total):
        tokens = tokens_ref[rows, :].astype(F32)
        scale = rms_scale(tokens, EPS)
        gain_grad_ref[...] += jnp.sum(total * tokens * scale, axis=0, keepdims=True)
        grad = upstream_ref[rows, :] + rms_back(total, tokens, scale)
        grad_ref[rows, :] = grad.astype(BF16)

    turn_rows(partial_ref, *scratch, done)


def tokens_back(partial, tokens, upstream):
    whole = pl.BlockSpec(memory_space=pltpu.VMEM)
    return pl.pallas_call(
        tokens_kernel,
        out_shape=[
            jax.ShapeDtypeStruct(tokens.shape, BF16),
            jax.ShapeDtypeStruct((1, tokens.shape[1]), F32),
        ],
        in_specs=[whole] * 3,
        out_specs=[whole] * 2,
        scratch_shapes=turn_scratch(*tokens.shape),
        compiler_params=kernel_params(8, 18),
        cost_estimate=pl.CostEstimate(flops=10**6, bytes_accessed=10**4, transcendentals=0),
        name="tokens_back",
    )(partial, tokens, upstream)


def hidden_units_kernel(cot_ref, down_ref, rest_ref, pre_ref, out_ref):
    units, half = down_ref.shape
    grad = back_product(cot_ref[:, pl.ds(0, half)], down_ref[...])
    grad += back_product(cot_ref[:, pl.ds(half, half)], rest_ref[...])
    gate, up = pre_ref[:, pl.ds(0, units)], pre_ref[:, pl.ds(units, units)]
    sig = jax.nn.sigmoid(gate)
    grad_sig = grad * sig
    out_ref[:, pl.ds(0, units)] = (grad_sig * up * (1.0 + gate * (1.0 - sig))).astype(BF16)
    out_ref[:, pl.ds(units, units)] = (grad_sig * gate).astype(BF16)


def hidden_units_back(cot, down, rest, pre):
    rows, width = cot.shape
    size = 2 * LANES

    def rows_block(n):
        return pl.BlockSpec((size, n), lambda i: (i, 0))

    return pl.pallas_call(
        hidden_units_kernel,
        grid=(rows // size,),
        out_shape=jax.ShapeDtypeStruct(pre.shape, BF16),
        in_specs=[
            rows_block(width),
            pl.BlockSpec(down.shape, lambda i: (0, 0)),
            pl.BlockSpec(rest.shape, lambda i: (0, 0)),
            rows_block(pre.shape[1]),
        ],
        out_specs=rows_block(pre.shape[1]),
        compiler_params=pltpu.CompilerParams(vmem_limit_bytes=58 * 2**20),
        cost_estimate=pl.CostEstimate(flops=10**6, bytes_accessed=10**4, transcendentals=0),
        name="hidden_units_back",
    )(cot, down, rest, pre)


def columns_kernel(widths, total_width, moved_ref, gain_ref, *outs):
    gain = gain_ref[...].astype(F32)
    place = 0
    for out, width in zip(outs, widths):
        for p in range(H):
            piece = moved_ref[p, :, pl.ds(place, width)].astype(F32)
            out[:, pl.ds(p * width, width)] = piece * gain
        place += width
    if total_width:
        total = moved_ref[0, :, pl.ds(place, total_width)].astype(F32)
        for p in range(1, H):
            total += moved_ref[p, :, pl.ds(place, total_width)].astype(F32)
        outs[-1][...] = total * gain


def lay_columns(moved, gain, widths, total_width=0):
    rows = moved.shape[1]
    shapes = [(rows, H * width) for width in widths]
    if total_width:
        shapes.append((rows, total_width))
    whole = pl.BlockSpec(memory_space=pltpu.VMEM)
    return pl.pallas_call(
        functools.partial(columns_kernel, tuple(widths), total_width),
        out_shape=[jax.ShapeDtypeStruct(shape, F32) for shape in shapes],
        in_specs=[whole] * 2,
        out_specs=[whole] * len(shapes),
        compiler_params=pltpu.CompilerParams(vmem_limit_bytes=16 * 2**20),
        cost_estimate=pl.CostEstimate(flops=10**6, bytes_accessed=10**4, transcendentals=0),
        name="lay_columns",
    )(moved, gain)


def mix_forward(mixed, bias, gaterank, gain, marks, segment, sums, pairs, key_dim, value_dim):
    rows = mixed.shape[0]
    count, _, length = segment.shape
    shapes = (
        ((rows, value_dim), BF16),
        ((rows, value_dim), F32),
        ((rows, key_dim), F32),
        ((count, length, length), BF16),
        ((rows, key_dim), BF16),
        ((rows, key_dim), BF16),
        ((count, 1, key_dim), F32),
        ((count, value_dim, key_dim), BF16),
    )
    whole = pl.BlockSpec(memory_space=pltpu.VMEM)
    return pl.pallas_call(
        functools.partial(forward_kernel, key_dim, value_dim),
        out_shape=[jax.ShapeDtypeStruct(*s) for s in shapes],
        in_specs=[pl.BlockSpec(memory_space=pl.ANY)] + [whole] * 7,
        out_specs=[whole] + [pl.BlockSpec(memory_space=pl.ANY)] * (len(shapes) - 1),
        scratch_shapes=[pltpu.VMEM(*s) for s in shapes[1:-1]]
        + state_scratch(count, value_dim, key_dim)
        + [
            pltpu.SemaphoreType.DMA((count, 7)),
            pltpu.VMEM(mixed.shape, mixed.dtype),
            pltpu.SemaphoreType.DMA((count,)),
        ],
        compiler_params=kernel_params(1, 58),
        cost_estimate=pl.CostEstimate(flops=10**6, bytes_accessed=10**4, transcendentals=0),
        name="mix_forward",
    )(mixed, bias, gaterank, gain, marks, segment, sums, pairs)


def mix_backward(
    mixed, kept, upstream, gaterank, gain, marks, segment, sums, pairs, key_dim, value_dim
):
    rows = mixed.shape[0]
    count = segment.shape[0]
    shapes = (
        (mixed.shape, BF16),
        ((1, value_dim), F32),
        ((1, key_dim), F32),
        (gaterank.shape, F32),
    )
    attended, logits, scores, start, end, decay, enter = kept
    given = (mixed, upstream, attended, start, logits, scores, end, decay, enter)
    whole = pl.BlockSpec(memory_space=pltpu.VMEM)
    return pl.pallas_call(
        functools.partial(backward_kernel, key_dim, value_dim),
        out_shape=[jax.ShapeDtypeStruct(*s) for s in shapes],
        in_specs=[pl.BlockSpec(memory_space=pl.ANY)] * 9 + [whole] * 6,
        out_specs=[whole] * len(shapes),
        scratch_shapes=[pltpu.VMEM(a.shape, a.dtype) for a in given]
        + [pltpu.VMEM((rows, value_dim), BF16)]
        + state_scratch(count, value_dim, key_dim)
        + [pltpu.SemaphoreType.DMA((count, 9))],
        compiler_params=kernel_params(2, 58),
        cost_estimate=pl.CostEstimate(flops=10**6, bytes_accessed=10**4, transcendentals=0),
        name="mix_backward",
    )(
        *given,
        gaterank,
        gain,
        marks,
        segment,
        sums,
        pairs,
    )


def per_device(
    tokens,
    doc_lengths,
    norm_gain,
    w_query,
    w_key,
    w_value,
    w_outgate,
    w_lowrank,
    w_gaterank,
    gate_bias,
    head_gain,
    w_output,
    ffn_gain,
    w_gate,
    w_up,
    w_down,
    cotangent,
):
    seqs_here, length, width = tokens.shape
    reps = lax.axis_size("rep")
    parts = lax.axis_size("fsdp")
    devices = reps * H * CORES * parts
    here = lax.axis_index("head")
    key_dim, value_dim = DK, DV
    rank = w_lowrank.shape[1]
    rows = width // devices
    count = H * seqs_here

    rank_at = 2 * key_dim + 2 * value_dim

    def core_sum(g):
        halves = g.reshape(g.shape[0], CORES, -1, g.shape[-1])
        core = lax.axis_index("core")
        other = lax.ppermute(halves[:, 1 - core], "core", ((0, 1), (1, 0)))
        return (halves[:, core].astype(F32) + other.astype(F32)).astype(BF16)

    def scatter_rows(g):
        if reps > 1:
            g = lax.psum_scatter(g, "rep", scatter_dimension=0, tiled=True)
        return lax.psum_scatter(g, "fsdp", scatter_dimension=1, tiled=True)

    def gather_columns(moved):
        whole = lax.all_gather(moved, ("core", "fsdp"), axis=1, tiled=True)
        if reps > 1:
            whole = lax.all_gather(whole, "rep", axis=0, tiled=False)
        return whole.reshape(width, -1)

    def gather_part(w):
        if reps == 1:
            return lax.all_gather(w, SHARE, axis=0, tiled=True)
        whole = lax.all_gather(w, EVERY, axis=0, tiled=True)
        size = whole.shape[0] // H
        return lax.dynamic_slice_in_dim(whole, here * size, size, 0)

    def pair_part(g):
        return core_sum(g[None])[0] if reps == 1 else g

    def scatter_part(g):
        if reps == 1:
            return lax.psum_scatter(g, "fsdp", scatter_dimension=0, tiled=True)
        whole = jnp.zeros((H * g.shape[0], g.shape[1]), BF16)
        whole = lax.dynamic_update_slice_in_dim(whole, g, here * g.shape[0], 0)
        return lax.psum_scatter(whole, EVERY, scatter_dimension=0, tiled=True)

    rank_at = 2 * key_dim + 2 * value_dim

    def with_gain(w, gain):
        return (w.astype(F32) * gain.astype(F32)[:, None]).astype(BF16)

    small = (
        w_gaterank,
        gate_bias.reshape(1, -1),
        head_gain.reshape(1, -1),
        (doc_lengths // 16).astype(BF16).reshape(1, -1),
        (doc_lengths % 16).astype(BF16).reshape(1, -1),
    )
    edges = [rank]
    extra = jnp.pad(with_gain(w_lowrank, norm_gain), ((0, 0), (0, LANES - rank)))
    for piece in small:
        high, wide = piece.shape
        extra += jnp.pad(piece, ((0, rows - high), (edges[-1], LANES - edges[-1] - wide)))
        edges.append(edges[-1] + wide)

    mix_moved = mix_weights((w_query, w_key, w_value, w_outgate), extra, norm_gain[:, None])
    inputs = tokens.reshape(-1, width)
    inputs, _ = after(inputs, mix_moved)
    output_w = gather_part(w_output)
    mix_moved, output_w = after(mix_moved, output_w)
    mix_w = gather_columns(mix_moved)
    w_down, _ = after(w_down, mix_moved)
    down_w = gather_part(w_down[:, : width // 2])
    normed, ffn_moved = share_tokens(inputs, w_gate, w_up, ffn_gain[:, None])
    normed = normed.reshape(-1, width)

    small = mix_w[:, rank_at:].astype(F32).reshape(devices, rows, LANES)
    gaterank, bias, gain_head, long, short = (
        small[:, : rank if i == 0 else 1, edges[i] : edges[i + 1]] for i in range(len(edges) - 1)
    )
    gaterank = gaterank.transpose(1, 0, 2).reshape(rank, -1)
    bias = lax.dynamic_slice_in_dim(bias.reshape(1, -1), here * key_dim, key_dim, 1)
    gaterank = lax.dynamic_slice_in_dim(gaterank, here * key_dim, key_dim, 1)
    gain_head = gain_head.reshape(1, -1)
    lengths = (long * 16.0 + short).reshape(reps, H, CORES, parts, seqs_here, DOCS)
    lengths = lengths[lax.axis_index("rep"), :, lax.axis_index("core"), 0]
    lengths = lengths.reshape(count, DOCS).astype(jnp.int32)

    offset = lax.axis_index("fsdp") * length
    doc_ends = jnp.cumsum(lengths, axis=-1)
    places = offset + jnp.arange(length, dtype=jnp.int32)
    segment = jnp.sum((places[None, :, None] >= doc_ends[:, None, :]).astype(jnp.int32), axis=-1)
    before = jnp.sum((offset - 1 >= doc_ends).astype(jnp.int32), axis=-1)[:, None]
    last = segment[:, -1:]
    marks = jnp.stack(
        [
            segment,
            segment == before,
            segment == last,
            segment != DOCS - 1,
            jnp.broadcast_to(last == before, segment.shape),
        ],
        axis=2,
    )
    marks = jnp.pad(marks.astype(F32).reshape(count * length, 5), ((0, 0), (0, 3)))
    segment = segment.astype(F32).reshape(count, 1, length)

    mixed = matmul(normed, mix_w)
    sums, pairs = level_sums(length)
    sums, pairs = sums.astype(BF16), pairs.astype(BF16)
    gated, *kept = mix_forward(
        mixed, bias, gaterank, gain_head, marks, segment, sums, pairs, key_dim, value_dim
    )
    cot_rows, _ = after(cotangent.reshape(-1, width), normed)
    gated, cot_shared, down_w = after(gated, share_rows(cot_rows), down_w)
    ffn_moved, w_down_rest, _ = after(ffn_moved, w_down[:, width // 2 :], gated)
    ffn_w = gather_columns(ffn_moved)
    down_rest = gather_part(w_down_rest)
    partial = matmul(gated, output_w).astype(BF16).reshape(H, -1, width)
    hidden, normed_two = share_hidden(partial, inputs)
    normed_two = normed_two.reshape(-1, width)

    pre = matmul(normed_two, ffn_w)
    gate_pre, up_pre = jnp.split(pre, 2, axis=1)
    sig_gate = jax.nn.sigmoid(gate_pre)
    activated = (gate_pre * sig_gate * up_pre).astype(BF16)

    grad_down_w = rows_product(activated, cot_shared).astype(BF16)
    down_w, grad_down_w = after(down_w, grad_down_w)
    grad_pre = hidden_units_back(cot_shared, down_w, down_rest, pre)
    grad_pre, grad_down_w = after(grad_pre, pair_part(grad_down_w))
    grad_down_w = scatter_part(grad_down_w)
    grad_ffn_w = pair_product(normed_two, grad_pre, reps * H, 7)
    grad_pre, grad_ffn_w = after(grad_pre, grad_ffn_w)
    partial = back_product(grad_pre, ffn_w).astype(BF16)

    grad_hidden, grad_gain_two, down_partial, branch = share_branch(
        partial.reshape(H, -1, width), hidden, cot_rows, activated, down_w, down_rest
    )
    grad_ffn_w = scatter_rows(grad_ffn_w)
    branch = branch.reshape(-1, width)
    grad_gated = back_product(branch, output_w)
    gated, grad_gated = after(gated, grad_gated)
    grad_output_w = pair_part(rows_product(gated, branch).astype(BF16))
    grad_gated, grad_output_w, grad_down_w = after(grad_gated, grad_output_w, grad_down_w)
    grad_output_w = scatter_part(grad_output_w)
    pieces = move_rows(down_partial)
    grad_mixed, grad_gain_head, grad_bias, grad_gaterank = mix_backward(
        mixed,
        kept,
        grad_gated,
        gaterank,
        gain_head,
        marks,
        segment,
        sums,
        pairs,
        key_dim,
        value_dim,
    )
    grad_mixed, pieces, grad_down_w, grad_ffn_w = after(
        grad_mixed, pieces, grad_down_w, grad_ffn_w
    )
    output = (hidden + jnp.sum(pieces.astype(F32), axis=0)).astype(BF16).reshape(tokens.shape)
    grad_mix_w = pair_product(normed, grad_mixed, reps * H, 11)
    grad_mixed, grad_mix_w = after(grad_mixed, grad_mix_w)
    partial = back_product(grad_mixed, mix_w).astype(BF16)
    grad_mix_w = scatter_rows(grad_mix_w)
    grad_ffn_w = lax.all_to_all(grad_ffn_w, "head", split_axis=0, concat_axis=0, tiled=True)
    def place(g, axis):
        shape = list(g.shape)
        shape[axis] *= H
        return lax.dynamic_update_slice_in_dim(jnp.zeros(shape, F32), g, here * key_dim, axis)

    small_grads = jnp.concatenate(
        [
            grad_gain_two.reshape(devices, -1),
            place(grad_bias.reshape(-1), 0).reshape(devices, -1),
            grad_gain_head.reshape(devices, -1),
            place(grad_gaterank, 1)
            .reshape(rank, devices, -1)
            .transpose(1, 0, 2)
            .reshape(devices, -1),
        ],
        axis=1,
    )
    partial, grad_output_w, grad_ffn_w, small_grads = after(
        partial, grad_output_w, grad_ffn_w, small_grads
    )
    tokens_grad, grad_gain_one = tokens_back(partial.reshape(H, -1, width), inputs, grad_hidden)
    tokens_grad = tokens_grad.reshape(tokens.shape)

    units = w_gate.shape[1] // H
    w_gate_grad, w_up_grad = lay_columns(grad_ffn_w, ffn_gain[:, None], (units, units))
    grad_mix_w, _ = after(grad_mix_w, grad_gain_one)
    grad_mix_w = lax.all_to_all(grad_mix_w, "head", split_axis=0, concat_axis=0, tiled=True)
    query_g, key_g, value_g, outgate_g, lowrank_g = lay_columns(
        grad_mix_w, norm_gain[:, None], (key_dim, key_dim, value_dim, value_dim), rank
    )

    small_grads = jnp.concatenate([grad_gain_one.reshape(devices, -1), small_grads], axis=1)
    small_grads, _ = after(small_grads, grad_mix_w)
    small_grads = lax.all_to_all(small_grads, EVERY, split_axis=0, concat_axis=0, tiled=True)
    small_grads = jnp.sum(small_grads, axis=0)
    sizes = [norm_gain.shape[0], ffn_gain.shape[0], gate_bias.shape[0], head_gain.shape[0]]
    norm_g, ffn_g, bias_g, head_g, gaterank_g = jnp.split(
        small_grads, [sum(sizes[: i + 1]) for i in range(len(sizes))]
    )
    return (
        output,
        tokens_grad,
        norm_g / norm_gain.astype(F32),
        query_g,
        key_g,
        value_g,
        outgate_g,
        lowrank_g,
        gaterank_g.reshape(w_gaterank.shape),
        bias_g,
        head_g,
        grad_output_w.astype(F32),
        ffn_g / ffn_gain.astype(F32),
        w_gate_grad,
        w_up_grad,
        grad_down_w.astype(F32),
    )


def solution(mesh):
    dp, parts = mesh.shape["dp"], mesh.shape["fsdp"]
    fine = Mesh(mesh.devices.reshape(dp // (H * CORES), H, CORES, parts), EVERY)
    seq = ("rep", "head", "core")
    rows, vector = P(EVERY, None), P(EVERY)
    activations = P(seq, "fsdp", None)
    columns = P(None, EVERY)
    return jax.shard_map(
        per_device,
        mesh=fine,
        in_specs=(
            activations,
            P(seq, None),
            vector,
            rows,
            rows,
            rows,
            rows,
            rows,
            columns,
            vector,
            vector,
            rows,
            vector,
            rows,
            rows,
            rows,
            activations,
        ),
        out_specs=(
            activations,
            activations,
            vector,
            rows,
            rows,
            rows,
            rows,
            rows,
            columns,
            vector,
            vector,
            rows,
            vector,
            rows,
            rows,
            rows,
        ),
        check_vma=False,
    )
```

```python
import functools

import jax
import jax.experimental.pallas as pl
import jax.experimental.pallas.tpu as pltpu
import jax.numpy as jnp
from jax import lax
from jax.sharding import Mesh
from jax.sharding import PartitionSpec as P

H = 4
DK = 256
DV = 512
CORES = 2
DOCS = 8
PIECES = 4
LANES = 128
CHUNKS = 8

EPS = 1e-05
HEAD_EPS = 1.0
HIGHEST = lax.Precision.HIGHEST
F32 = jnp.float32
BF16 = jnp.bfloat16

SHARE = ("rep", "core", "fsdp")
EVERY = ("rep", "head", "core", "fsdp")


def dot(a, b, dims, precision=None):
    return lax.dot_general(a, b, (dims, ((), ())), precision=precision, preferred_element_type=F32)


def after(value, *others):
    return lax.optimization_barrier((value,) + others)


def matmul(a, b):
    return dot(a, b, ((1,), (0,)))


def rows_product(a, b):
    return dot(a, b, ((0,), (0,)))


def back_product(a, b):
    return dot(a, b, ((1,), (1,)))


def batched(form, a, b):
    return jnp.einsum(form, a, b, preferred_element_type=F32)


def rms_scale(values, epsilon):
    return lax.rsqrt(jnp.mean(values * values, axis=-1, keepdims=True) + epsilon)


def rms_back(upstream, values, scale):
    return scale * upstream - values * scale**3 * jnp.mean(upstream * values, axis=-1, keepdims=True)


def share_rows(part):
    spread = jnp.broadcast_to(part[None], (H,) + part.shape)
    whole = lax.all_to_all(spread, "head", split_axis=0, concat_axis=0, tiled=True)
    return whole.reshape(-1, part.shape[-1])


def move_rows(partial):
    pieces = partial.astype(BF16).reshape(H, -1, partial.shape[-1])
    return lax.all_to_all(pieces, "head", split_axis=0, concat_axis=0, tiled=True)


def sum_rows(partial):
    return jnp.sum(move_rows(partial).astype(F32), axis=0)


def level_sums(length):
    rows = jnp.arange(length)[:, None]
    cols = jnp.arange(length)[None, :]
    sums, pairs = [], []
    step = 1
    while step < length:
        bound = rows // (2 * step) * (2 * step) + step - 1
        upper = rows > bound
        sums.append(jnp.where(upper, (cols > bound) & (cols <= rows), (cols > rows) & (cols <= bound)))
        pairs.append(upper & (cols // (2 * step) == rows // (2 * step)) & (cols <= bound))
        step *= 2
    sums.append(cols <= rows)
    sums.append(cols > rows)
    return jnp.stack(sums), jnp.stack(pairs)


def log_sigmoid(x):
    return jnp.minimum(x, 0.0) - jnp.log1p(jnp.exp(-jnp.abs(x)))


def state_copy(send, recv, send_sem, recv_sem, seq, piece, target):
    size = send.shape[1] // PIECES
    part = pl.ds(piece * size, size)
    return pltpu.make_async_remote_copy(
        src_ref=send.at[seq, part],
        dst_ref=recv.at[seq, part],
        send_sem=send_sem.at[seq, piece],
        recv_sem=recv_sem.at[seq, piece],
        device_id={"fsdp": target},
        device_id_type=pl.DeviceIdType.MESH,
    )


def greet_neighbours(place, parts):
    barrier = pltpu.get_barrier_semaphore()
    for near, there in ((place - 1, place > 0), (place + 1, place < parts - 1)):

        @pl.when(there)
        def _(near=near):
            pl.semaphore_signal(
                barrier,
                inc=1,
                device_id={"fsdp": lax.rem(near + parts, parts)},
                device_id_type=pl.DeviceIdType.MESH,
            )

    peers = (place > 0).astype(jnp.int32) + (place < parts - 1).astype(jnp.int32)
    pl.semaphore_wait(barrier, peers)


def pass_state(s, first, last, target, decay, local, send, recv, send_sem, recv_sem):
    size = send.shape[1] // PIECES
    for piece in range(PIECES):
        part = pl.ds(piece * size, size)
        copy = state_copy(send, recv, send_sem, recv_sem, s, piece, target)

        @pl.when(jnp.logical_not(first))
        def _(copy=copy):
            copy.wait_recv()

        @pl.when(jnp.logical_not(jnp.logical_or(first, last)))
        def _(copy=copy, part=part):
            joined = decay * recv[s, part].astype(F32) + local[s, part]
            send[s, part] = joined.astype(BF16)
            copy.start()


def start_state(s, first, last, target, local, send, recv, send_sem, recv_sem):
    @pl.when(jnp.logical_and(first, jnp.logical_not(last)))
    def _():
        send[s] = local[s].astype(BF16)
        for piece in range(PIECES):
            state_copy(send, recv, send_sem, recv_sem, s, piece, target).start()


def finish_states(count, last, target, send, recv, send_sem, recv_sem):
    @pl.when(jnp.logical_not(last))
    def _():
        def one(s, carry):
            for piece in range(PIECES):
                state_copy(send, recv, send_sem, recv_sem, s, piece, target).wait_send()
            return carry

        lax.fori_loop(0, count, one, 0)


def split_rates(logits):
    rates = log_sigmoid(logits) / 16.0
    high = rates.astype(BF16)
    return high, (rates - high.astype(F32)).astype(BF16)


def decayed(sums, high, low):
    return jnp.exp(matmul(sums, high) + matmul(sums, low))


def forward_kernel(
    key_dim,
    value_dim,
    given_ref,
    bias_ref,
    gaterank_ref,
    gain_ref,
    marks_ref,
    segment_ref,
    sums_ref,
    pairs_ref,
    gated_ref,
    *refs,
):
    kept, (attended_ref, logits_ref, scores_ref, start_ref, end_ref, decay_ref) = refs[:7], refs[7:13]
    local_ref, send_ref, recv_ref, send_sem, recv_sem, keep_sem, mixed_ref, take_sem = refs[13:]
    count, _, length = segment_ref.shape
    levels = pairs_ref.shape[0]
    parts, place = lax.axis_size("fsdp"), lax.axis_index("fsdp")
    first, last, target = place == 0, place == parts - 1, lax.rem(place + 1, parts)

    def rows_of(s):
        return pl.ds(pl.multiple_of(s * length, length), length)

    def keeps(s, kinds):
        held = (attended_ref, logits_ref, scores_ref, start_ref, end_ref, decay_ref, recv_ref)
        rows = rows_of(s)
        for kind in kinds:
            at = rows if len(held[kind].shape) == 2 else s
            yield pltpu.make_async_copy(held[kind].at[at], kept[kind].at[at], keep_sem.at[s, kind])

    def take(s):
        rows = rows_of(s)
        return pltpu.make_async_copy(given_ref.at[rows], mixed_ref.at[rows], take_sem.at[s])

    def start_take(s, carry):
        take(s).start()
        return carry

    lax.fori_loop(0, count, start_take, 0)

    def finish_keeps(s, carry):
        for copy in keeps(s, range(7)):
            copy.wait()
        return carry

    rank = gaterank_ref.shape[0]
    scale = key_dim ** (-0.5)
    value_at = 2 * key_dim
    gate_at = value_at + value_dim
    rank_at = gate_at + value_dim

    greet_neighbours(place, parts)

    @pl.when(first)
    def _():
        recv_ref[...] = jnp.zeros_like(recv_ref)

    def ends(s, carry):
        rows = rows_of(s)
        take(s).wait()
        lowrank = mixed_ref[rows, pl.ds(rank_at, rank)]
        logits = dot(lowrank, gaterank_ref[...], ((1,), (0,)), HIGHEST) + bias_ref[...]
        logits_ref[rows, :] = logits
        high, low = split_rates(logits)
        from_start = decayed(sums_ref[levels], high, low)
        to_end = decayed(sums_ref[levels + 1], high, low)
        marks = marks_ref[rows, :]
        decay_ref[s] = from_start[length - 1 :, :] * marks[:1, 4:5]
        query = mixed_ref[rows, pl.ds(0, key_dim)] * scale
        key = mixed_ref[rows, pl.ds(key_dim, key_dim)]
        start_ref[rows, :] = (query * (from_start * marks[:, 1:2])).astype(BF16)
        end_key = (key * (to_end * marks[:, 2:3])).astype(BF16)
        end_ref[rows, :] = end_key
        value = mixed_ref[rows, pl.ds(value_at, value_dim)].astype(BF16)
        local_ref[s] = rows_product(value, end_key)
        start_state(s, first, last, target, local_ref, send_ref, recv_ref, send_sem, recv_sem)
        for copy in keeps(s, (1, 3, 4, 5)):
            copy.start()
        return carry

    lax.fori_loop(0, count, ends, 0)

    def mix(s, carry):
        rows = rows_of(s)
        pass_state(
            s, first, last, target, decay_ref[s], local_ref, send_ref, recv_ref, send_sem, recv_sem
        )
        query = mixed_ref[rows, pl.ds(0, key_dim)] * scale
        key = mixed_ref[rows, pl.ds(key_dim, key_dim)]
        high, low = split_rates(logits_ref[rows, :])
        scores = jnp.zeros((length, length), F32)
        for level in range(levels):
            decay = decayed(sums_ref[level], high, low)
            pair = back_product((query * decay).astype(BF16), (key * decay).astype(BF16))
            scores += pair * pairs_ref[level].astype(F32)
        row = lax.broadcasted_iota(jnp.int32, (length, length), 0)
        col = lax.broadcasted_iota(jnp.int32, (length, length), 1)
        own = jnp.sum(query * key, axis=1, keepdims=True)
        scores += jnp.where(row == col, own, 0.0)
        marks = marks_ref[rows, :]
        scores = jnp.where(marks[:, 0:1] == segment_ref[s], scores, 0.0).astype(BF16)
        scores_ref[s] = scores
        value = mixed_ref[rows, pl.ds(value_at, value_dim)].astype(BF16)
        attended = matmul(scores, value) + back_product(start_ref[rows, :], recv_ref[s])
        attended = attended * marks[:, 3:4]
        attended_ref[rows, :] = attended
        headed = attended * rms_scale(attended, HEAD_EPS) * gain_ref[...]
        outgate = mixed_ref[rows, pl.ds(gate_at, value_dim)]
        gated_ref[rows, :] = (headed * (outgate * jax.nn.sigmoid(outgate))).astype(BF16)
        for copy in keeps(s, (0, 2, 6)):
            copy.start()
        return carry

    lax.fori_loop(0, count, mix, 0)
    finish_states(count, last, target, send_ref, recv_ref, send_sem, recv_sem)
    lax.fori_loop(0, count, finish_keeps, 0)


def backward_kernel(
    key_dim,
    value_dim,
    *refs,
):
    given, refs = refs[:9], refs[9:]
    gaterank_ref, gain_ref, marks_ref, segment_ref, sums_ref, pairs_ref, *refs = refs
    grad_ref, gain_grad_ref, bias_grad_ref, gaterank_grad_ref, *refs = refs
    held, refs = refs[:9], refs[9:]
    mixed_ref, upstream_ref, attended_ref, start_ref, *rest_refs = held
    logits_ref, scores_ref, end_ref, decay_ref, enter_ref = rest_refs
    out_ref, local_ref, send_ref, recv_ref, send_sem, recv_sem, take_sem = refs
    count, _, length = segment_ref.shape

    def rows_of(s):
        return pl.ds(pl.multiple_of(s * length, length), length)

    def takes(s, kinds):
        rows = rows_of(s)
        for kind in kinds:
            at = rows if len(held[kind].shape) == 2 else s
            yield pltpu.make_async_copy(given[kind].at[at], held[kind].at[at], take_sem.at[s, kind])

    def start_takes(s, carry):
        for copy in takes(s, range(9)):
            copy.start()
        return carry

    lax.fori_loop(0, count, start_takes, 0)
    levels = pairs_ref.shape[0]
    parts, place = lax.axis_size("fsdp"), lax.axis_index("fsdp")
    first, last, target = place == parts - 1, place == 0, lax.rem(place + parts - 1, parts)
    rank = gaterank_ref.shape[0]
    scale = key_dim ** (-0.5)
    value_at = 2 * key_dim
    gate_at = value_at + value_dim
    rank_at = gate_at + value_dim

    greet_neighbours(place, parts)

    @pl.when(first)
    def _():
        recv_ref[...] = jnp.zeros_like(recv_ref)

    gain_grad_ref[...] = jnp.zeros_like(gain_grad_ref)
    bias_grad_ref[...] = jnp.zeros_like(bias_grad_ref)
    gaterank_grad_ref[...] = jnp.zeros_like(gaterank_grad_ref)

    def heads(s, carry):
        rows = rows_of(s)
        for copy in takes(s, range(4)):
            copy.wait()
        upstream = upstream_ref[rows, :]
        attended = attended_ref[rows, :]
        outgate = mixed_ref[rows, pl.ds(gate_at, value_dim)]
        gain = gain_ref[...]
        norm = rms_scale(attended, HEAD_EPS)
        normed = attended * norm
        sig = jax.nn.sigmoid(outgate)
        grad_gate = upstream * (normed * gain) * sig * (1.0 + outgate * (1.0 - sig))
        grad_ref[rows, pl.ds(gate_at, value_dim)] = grad_gate.astype(BF16)
        grad_headed = upstream * (outgate * sig)
        gain_grad_ref[...] += jnp.sum(grad_headed * normed, axis=0, keepdims=True)
        grad_out = rms_back(grad_headed * gain, attended, norm) * marks_ref[rows, pl.ds(3, 1)]
        grad_out = grad_out.astype(BF16)
        out_ref[rows, :] = grad_out
        local_ref[s] = rows_product(grad_out, start_ref[rows, :])
        start_state(s, first, last, target, local_ref, send_ref, recv_ref, send_sem, recv_sem)
        return carry

    lax.fori_loop(0, count, heads, 0)

    def mix(s, carry):
        rows = rows_of(s)
        for copy in takes(s, range(4, 9)):
            copy.wait()
        decay_row = decay_ref[s]
        pass_state(
            s, first, last, target, decay_row, local_ref, send_ref, recv_ref, send_sem, recv_sem
        )
        query = mixed_ref[rows, pl.ds(0, key_dim)] * scale
        key = mixed_ref[rows, pl.ds(key_dim, key_dim)]
        value = mixed_ref[rows, pl.ds(value_at, value_dim)].astype(BF16)
        marks = marks_ref[rows, :]
        logits = logits_ref[rows, :]
        high, low = split_rates(logits)
        grad_out = out_ref[rows, :]
        row = lax.broadcasted_iota(jnp.int32, (length, length), 0)
        col = lax.broadcasted_iota(jnp.int32, (length, length), 1)
        pair_grads = back_product(grad_out, value)
        pair_grads = jnp.where(marks[:, 0:1] == segment_ref[s], pair_grads, 0.0)
        own = jnp.sum(jnp.where(row == col, pair_grads, 0.0), axis=1, keepdims=True)
        grad_query = own * key
        grad_key = own * query
        grad_rates = jnp.zeros((length, key_dim), F32)
        for level in range(levels):
            decay = decayed(sums_ref[level], high, low)
            level_query = (query * decay).astype(BF16)
            level_key = (key * decay).astype(BF16)
            level_pairs = (pair_grads * pairs_ref[level].astype(F32)).astype(BF16)
            level_grad_query = matmul(level_pairs, level_key)
            level_grad_key = rows_product(level_pairs, level_query)
            grad_query += level_grad_query * decay
            grad_key += level_grad_key * decay
            flow = level_grad_query * level_query.astype(F32)
            flow += level_grad_key * level_key.astype(F32)
            grad_rates += rows_product(sums_ref[level], flow.astype(BF16))
        ending = recv_ref[s]
        entering = enter_ref[s]
        start_query = start_ref[rows, :]
        end_key = end_ref[rows, :]
        start_grad = matmul(grad_out, entering)
        end_grad = matmul(value, ending)
        grad_query += start_grad * (decayed(sums_ref[levels], high, low) * marks[:, 1:2])
        grad_key += end_grad * (decayed(sums_ref[levels + 1], high, low) * marks[:, 2:3])
        grad_rates += rows_product(
            sums_ref[levels], (start_grad * start_query.astype(F32)).astype(BF16)
        )
        grad_rates += rows_product(
            sums_ref[levels + 1], (end_grad * end_key.astype(F32)).astype(BF16)
        )
        grad_rates += decay_row * jnp.sum(
            ending.astype(F32) * entering.astype(F32), axis=0, keepdims=True
        )
        grad_value = rows_product(scores_ref[s], grad_out) + back_product(end_key, ending)
        grad_ref[rows, pl.ds(0, key_dim)] = (grad_query * scale).astype(BF16)
        grad_ref[rows, pl.ds(key_dim, key_dim)] = grad_key.astype(BF16)
        grad_ref[rows, pl.ds(value_at, value_dim)] = grad_value.astype(BF16)
        grad_logits = grad_rates / 16.0 * jax.nn.sigmoid(-logits)
        bias_grad_ref[...] += jnp.sum(grad_logits, axis=0, keepdims=True)
        lowrank = mixed_ref[rows, pl.ds(rank_at, rank)]
        gaterank_grad_ref[...] += dot(lowrank, grad_logits, ((0,), (0,)), HIGHEST)
        grad_lowrank = dot(grad_logits, gaterank_ref[...], ((1,), (1,)), HIGHEST)
        rest = grad_ref.shape[1] - rank_at - rank
        grad_ref[rows, pl.ds(rank_at, rank + rest)] = jnp.concatenate(
            [grad_lowrank, jnp.zeros((length, rest), F32)], axis=1
        ).astype(BF16)
        return carry

    lax.fori_loop(0, count, mix, 0)
    finish_states(count, last, target, send_ref, recv_ref, send_sem, recv_sem)


def state_scratch(count, value_dim, key_dim):
    return [
        pltpu.VMEM((count, value_dim, key_dim), F32),
        pltpu.VMEM((count, value_dim, key_dim), BF16),
        pltpu.VMEM((count, value_dim, key_dim), BF16),
        pltpu.SemaphoreType.DMA((count, PIECES)),
        pltpu.SemaphoreType.DMA((count, PIECES)),
    ]


def kernel_params(number, mebibytes=44):
    return pltpu.CompilerParams(
        collective_id=number, has_side_effects=True, vmem_limit_bytes=mebibytes * 2**20
    )


def head_copy(src, dst, send_sem, recv_sem, target):
    return pltpu.make_async_remote_copy(
        src_ref=src,
        dst_ref=dst,
        send_sem=send_sem,
        recv_sem=recv_sem,
        device_id={"head": target},
        device_id_type=pl.DeviceIdType.MESH,
    )


def greet_heads(targets):
    barrier = pltpu.get_barrier_semaphore()
    for target in targets:
        pl.semaphore_signal(
            barrier, inc=1, device_id={"head": target}, device_id_type=pl.DeviceIdType.MESH
        )
    pl.semaphore_wait(barrier, len(targets))


def square(me):
    return me + 1 - 2 * lax.rem(me, 2), me + 2 - 4 * (me // 2), H - 1 - me


def move_columns(weights, gain, out_ref, send_ref, send_sem, recv_sem, own_sem):
    me = lax.axis_index("head")
    place = 0
    for w in weights:
        n = w.shape[1] // H
        for h in range(H):
            part = w[:, pl.ds(h * n, n)].astype(F32) * gain
            send_ref[h, :, pl.ds(place, n)] = part.astype(BF16)
        place += n
    copies = []
    for ahead in range(1, H):
        peer = lax.rem(me + ahead, H)
        copy = head_copy(
            send_ref.at[peer],
            out_ref.at[me],
            send_sem.at[ahead],
            recv_sem.at[ahead],
            peer,
        )
        copy.start()
        copies.append(copy)
    own = pltpu.make_async_copy(send_ref.at[me], out_ref.at[me], own_sem)
    own.start()
    return copies + [own]


def mix_weights_kernel(*refs):
    *weights, extra_ref, gain_ref, out_ref, send_ref, send_sem, recv_sem, own_sem = refs
    me = lax.axis_index("head")
    greet_heads([lax.rem(me + ahead, H) for ahead in range(1, H)])
    spare = extra_ref.shape[1]
    for h in range(H):
        send_ref[h, :, pl.ds(send_ref.shape[2] - spare, spare)] = extra_ref[...]
    gain = gain_ref[...].astype(F32)
    for copy in move_columns(weights, gain, out_ref, send_ref, send_sem, recv_sem, own_sem):
        copy.wait()


def mix_weights(weights, extra, gain):
    rows = extra.shape[0]
    n = sum(w.shape[1] for w in weights) // H + extra.shape[1]
    return pl.pallas_call(
        mix_weights_kernel,
        out_shape=jax.ShapeDtypeStruct((H, rows, n), BF16),
        in_specs=[pl.BlockSpec(memory_space=pltpu.VMEM)] * (len(weights) + 2),
        out_specs=pl.BlockSpec(memory_space=pl.ANY),
        scratch_shapes=[
            pltpu.VMEM((H, rows, n), BF16),
            pltpu.SemaphoreType.DMA((H,)),
            pltpu.SemaphoreType.DMA((H,)),
            pltpu.SemaphoreType.DMA,
        ],
        compiler_params=kernel_params(3, 16),
        cost_estimate=pl.CostEstimate(flops=10**6, bytes_accessed=10**4, transcendentals=0),
        name="mix_weights",
    )(*weights, extra, gain)


class Share:
    def __init__(self, mine_ref, out_ref, send_sem, recv_sem, own_sem):
        self.refs = mine_ref, out_ref, send_sem, recv_sem, own_sem
        self.me = lax.axis_index("head")
        self.size = mine_ref.shape[0] // CHUNKS

    def copy(self, c, kind):
        mine, out, send_sem, recv_sem, _ = self.refs
        sides = square(self.me)[:2]
        rows = pl.ds(c * self.size, self.size)
        if kind < 2:
            src, dst, target = mine.at[rows], out.at[self.me, rows], sides[kind]
        else:
            origin, target = (sides[0], sides[1]) if c % 2 == 0 else (sides[1], sides[0])
            src = dst = out.at[origin, rows]
        return head_copy(src, dst, send_sem.at[c, kind], recv_sem.at[c, kind], target)

    def own(self, c):
        mine, out, _, _, own_sem = self.refs
        rows = pl.ds(c * self.size, self.size)
        return pltpu.make_async_copy(mine.at[rows], out.at[self.me, rows], own_sem.at[c])

    def start(self, c):
        self.copy(c, 0).start()
        self.copy(c, 1).start()
        self.own(c).start()

    def forward(self, c):
        self.copy(c, c % 2).wait_recv()
        self.copy(c, 2).start()

    def finish(self):
        for c in range(CHUNKS):
            self.copy(c, 1 - c % 2).wait_recv()
            self.copy(c, 2).wait_recv()
            self.own(c).wait()
            for kind in range(3):
                self.copy(c, kind).wait_send()


def share_scratch(rows, width):
    return [
        pltpu.VMEM((rows, width), BF16),
        pltpu.SemaphoreType.DMA((CHUNKS, 3)),
        pltpu.SemaphoreType.DMA((CHUNKS, 3)),
        pltpu.SemaphoreType.DMA((CHUNKS,)),
    ]


def share_kernel(
    tokens_ref,
    gate_ref,
    up_ref,
    gain_ref,
    out_ref,
    moved_ref,
    mine_ref,
    share_send,
    share_recv,
    share_own,
    send_ref,
    send_sem,
    recv_sem,
    own_sem,
):
    me = lax.axis_index("head")
    greet_heads([lax.rem(me + ahead, H) for ahead in range(1, H)])
    share = Share(mine_ref, out_ref, share_send, share_recv, share_own)
    for c in range(CHUNKS):
        rows = pl.ds(c * share.size, share.size)
        x = tokens_ref[rows, :].astype(F32)
        mine_ref[rows, :] = (x * rms_scale(x, EPS)).astype(BF16)
        share.start(c)
    gain = gain_ref[...].astype(F32)
    copies = move_columns(
        [gate_ref, up_ref], gain, moved_ref, send_ref, send_sem, recv_sem, own_sem
    )
    for c in range(CHUNKS):
        share.forward(c)
    share.finish()
    for copy in copies:
        copy.wait()


def share_tokens(tokens, w_gate, w_up, gain):
    rows, n = w_gate.shape[0], 2 * w_gate.shape[1] // H
    return pl.pallas_call(
        share_kernel,
        out_shape=[
            jax.ShapeDtypeStruct((H,) + tokens.shape, BF16),
            jax.ShapeDtypeStruct((H, rows, n), BF16),
        ],
        in_specs=[pl.BlockSpec(memory_space=pltpu.VMEM)] * 4,
        out_specs=[pl.BlockSpec(memory_space=pl.ANY)] * 2,
        scratch_shapes=share_scratch(*tokens.shape)
        + [
            pltpu.VMEM((H, rows, n), BF16),
            pltpu.SemaphoreType.DMA((H,)),
            pltpu.SemaphoreType.DMA((H,)),
            pltpu.SemaphoreType.DMA,
        ],
        compiler_params=kernel_params(4, 16),
        cost_estimate=pl.CostEstimate(flops=10**6, bytes_accessed=10**4, transcendentals=0),
        name="share_tokens",
    )(tokens, w_gate, w_up, gain)


def turn_rows(
    partial_ref,
    first_ref,
    relay_ref,
    second_ref,
    pass_ref,
    send_sem,
    recv_sem,
    done,
    share=None,
    fillers=(),
):
    me = lax.axis_index("head")
    side = square(me)
    far = side[2]
    size = first_ref.shape[0] // CHUNKS
    steps = CHUNKS + 3
    fillers = list(fillers)

    def copies(c):
        one, two = (side[0], side[1]) if c % 2 == 0 else (side[1], side[0])
        rows = pl.ds(c * size, size)
        sems = [(send_sem.at[c, kind], recv_sem.at[c, kind]) for kind in range(3)]
        return (
            head_copy(partial_ref.at[far, rows], relay_ref.at[rows], *sems[0], one),
            head_copy(partial_ref.at[one, rows], first_ref.at[rows], *sems[1], one),
            head_copy(pass_ref.at[rows], second_ref.at[rows], *sems[2], two),
            two,
            rows,
        )

    for c in range(CHUNKS):
        relay, first, *_ = copies(c)
        relay.start()
        first.start()
    for step in range(steps):
        for filler in fillers[step * len(fillers) // steps : (step + 1) * len(fillers) // steps]:
            filler()
        if step < CHUNKS:
            relay, _, second, two, rows = copies(step)
            relay.wait_recv()
            both = partial_ref[two, rows, :].astype(F32) + relay_ref[rows, :].astype(F32)
            pass_ref[rows, :] = both.astype(BF16)
            second.start()
        if 1 <= step <= CHUNKS:
            _, first, second, _, rows = copies(step - 1)
            first.wait_recv()
            second.wait_recv()
            total = partial_ref[me, rows, :].astype(F32) + first_ref[rows, :].astype(F32)
            made = done(rows, total + second_ref[rows, :].astype(F32))
            if share is not None:
                share.refs[0][rows, :] = made
                share.start(step - 1)
        if step >= 3 and share is not None:
            share.forward(step - 3)
    if share is not None:
        share.finish()
    for c in range(CHUNKS):
        for copy in copies(c)[:3]:
            copy.wait_send()


def turn_scratch(rows, width):
    return [pltpu.VMEM((rows, width), BF16) for _ in range(4)] + [
        pltpu.SemaphoreType.DMA((CHUNKS, 3)),
        pltpu.SemaphoreType.DMA((CHUNKS, 3)),
    ]


def hidden_kernel(partial_ref, tokens_ref, hidden_ref, out_ref, *scratch):
    greet_heads(square(lax.axis_index("head"))[:2])
    mine_ref, *sems = scratch[6:]

    def done(rows, total):
        hidden = tokens_ref[rows, :].astype(F32) + total
        hidden_ref[rows, :] = hidden
        return (hidden * rms_scale(hidden, EPS)).astype(BF16)

    turn_rows(partial_ref, *scratch[:6], done, Share(mine_ref, out_ref, *sems))


def share_hidden(partial, tokens):
    whole = pl.BlockSpec(memory_space=pltpu.VMEM)
    return pl.pallas_call(
        hidden_kernel,
        out_shape=[
            jax.ShapeDtypeStruct(tokens.shape, F32),
            jax.ShapeDtypeStruct((H,) + tokens.shape, BF16),
        ],
        in_specs=[whole] * 2,
        out_specs=[whole, pl.BlockSpec(memory_space=pl.ANY)],
        scratch_shapes=turn_scratch(*tokens.shape) + share_scratch(*tokens.shape),
        compiler_params=kernel_params(5, 18),
        cost_estimate=pl.CostEstimate(flops=10**6, bytes_accessed=10**4, transcendentals=0),
        name="share_hidden",
    )(partial, tokens)


class PairProduct:
    def __init__(self, left_ref, right_ref, out_ref, give_ref, take_ref, send_sem, recv_sem, own_sem):
        self.refs = left_ref, right_ref, out_ref, give_ref, take_ref
        self.sems = send_sem, recv_sem, own_sem
        self.core = lax.axis_index("core")
        self.groups, self.rows, self.width = out_ref.shape
        self.cut = self.width // 2 if self.width % (2 * LANES) == 0 else self.width

    def product(self, group, core, at):
        left, right, *_ = self.refs
        start = pl.multiple_of((group * CORES + core) * self.rows, LANES)
        return rows_product(left[:, pl.ds(start, self.rows)], right[:, pl.ds(at, self.cut)])

    def copy(self, group):
        give, take = self.refs[3:]
        return pltpu.make_async_remote_copy(
            src_ref=give.at[group],
            dst_ref=take.at[group],
            send_sem=self.sems[0].at[group],
            recv_sem=self.sems[1].at[group],
            device_id={"core": 1 - self.core},
            device_id_type=pl.DeviceIdType.MESH,
        )

    def store(self, group):
        return pltpu.make_async_copy(
            self.refs[3].at[group], self.refs[2].at[group], self.sems[2].at[group]
        )

    def give(self, group, at):
        product = self.product(group, 1 - self.core, at)
        self.refs[3][group, :, pl.ds(at, self.cut)] = product.astype(BF16)
        if at + self.cut == self.width:
            self.copy(group).start()

    def keep(self, group, at):
        give, take = self.refs[3:]
        if at == 0:
            self.copy(group).wait()
        both = self.product(group, self.core, at)
        both += take[group, :, pl.ds(at, self.cut)].astype(F32)
        give[group, :, pl.ds(at, self.cut)] = both.astype(BF16)
        if at + self.cut == self.width:
            self.store(group).start()

    def steps(self):
        places = [
            (group, at) for group in range(self.groups) for at in range(0, self.width, self.cut)
        ]
        return [functools.partial(self.give, *place) for place in places] + [
            functools.partial(self.keep, *place) for place in places
        ]

    def finish(self):
        for group in range(self.groups):
            self.store(group).wait()


def pair_shape(left, right, groups):
    return (groups, left.shape[1] // (CORES * groups), right.shape[1])


def pair_scratch(shape):
    return [
        pltpu.VMEM(shape, BF16),
        pltpu.VMEM(shape, BF16),
        pltpu.SemaphoreType.DMA((shape[0],)),
        pltpu.SemaphoreType.DMA((shape[0],)),
        pltpu.SemaphoreType.DMA((shape[0],)),
    ]


def pair_kernel(left_ref, right_ref, out_ref, *scratch):
    barrier = pltpu.get_barrier_semaphore()
    other = 1 - lax.axis_index("core")
    pl.semaphore_signal(
        barrier, inc=1, device_id={"core": other}, device_id_type=pl.DeviceIdType.MESH
    )
    pl.semaphore_wait(barrier, 1)
    pair = PairProduct(left_ref, right_ref, out_ref, *scratch)
    for step in pair.steps():
        step()
    pair.finish()


def pair_product(left, right, groups, number):
    shape = pair_shape(left, right, groups)
    whole = pl.BlockSpec(memory_space=pltpu.VMEM)
    return pl.pallas_call(
        pair_kernel,
        out_shape=jax.ShapeDtypeStruct(shape, BF16),
        in_specs=[whole] * 2,
        out_specs=pl.BlockSpec(memory_space=pl.ANY),
        scratch_shapes=pair_scratch(shape),
        compiler_params=kernel_params(number, 58),
        cost_estimate=pl.CostEstimate(flops=10**6, bytes_accessed=10**4, transcendentals=0),
        name="pair_product",
    )(left, right)


def branch_kernel(
    partial_ref,
    hidden_ref,
    upstream_ref,
    active_ref,
    down_ref,
    rest_ref,
    grad_ref,
    gain_grad_ref,
    down_out_ref,
    out_ref,
    *scratch,
):
    greet_heads(square(lax.axis_index("head"))[:2])
    mine_ref, *sems = scratch[6:10]
    gain_grad_ref[...] = jnp.zeros_like(gain_grad_ref)

    def done(rows, total):
        hidden = hidden_ref[rows, :]
        scale = rms_scale(hidden, EPS)
        gain_grad_ref[...] += jnp.sum(total * hidden * scale, axis=0, keepdims=True)
        grad = upstream_ref[rows, :].astype(F32) + rms_back(total, hidden, scale)
        grad_ref[rows, :] = grad
        return grad.astype(BF16)

    def down(at):
        rows = pl.ds(at, LANES)
        half = down_ref.shape[1]
        for place, ref in ((0, down_ref), (half, rest_ref)):
            product = matmul(active_ref[rows, :], ref[...])
            down_out_ref[rows, pl.ds(place, half)] = product.astype(BF16)

    share = Share(mine_ref, out_ref, *sems)
    fillers = [functools.partial(down, at) for at in range(0, active_ref.shape[0], LANES)]
    turn_rows(partial_ref, *scratch[:6], done, share, fillers)


def share_branch(partial, hidden, upstream, active, down, rest):
    whole = pl.BlockSpec(memory_space=pltpu.VMEM)
    return pl.pallas_call(
        branch_kernel,
        out_shape=[
            jax.ShapeDtypeStruct(hidden.shape, F32),
            jax.ShapeDtypeStruct((1, hidden.shape[1]), F32),
            jax.ShapeDtypeStruct((active.shape[0], hidden.shape[1]), BF16),
            jax.ShapeDtypeStruct((H,) + hidden.shape, BF16),
        ],
        in_specs=[whole] * 6,
        out_specs=[whole] * 3 + [pl.BlockSpec(memory_space=pl.ANY)],
        scratch_shapes=turn_scratch(*hidden.shape) + share_scratch(*hidden.shape),
        compiler_params=kernel_params(6, 30),
        cost_estimate=pl.CostEstimate(flops=10**6, bytes_accessed=10**4, transcendentals=0),
        name="share_branch",
    )(partial, hidden, upstream, active, down, rest)


def tokens_kernel(partial_ref, tokens_ref, upstream_ref, grad_ref, gain_grad_ref, *scratch):
    greet_heads(square(lax.axis_index("head"))[:2])
    gain_grad_ref[...] = jnp.zeros_like(gain_grad_ref)

    def done(rows, total):
        tokens = tokens_ref[rows, :].astype(F32)
        scale = rms_scale(tokens, EPS)
        gain_grad_ref[...] += jnp.sum(total * tokens * scale, axis=0, keepdims=True)
        grad = upstream_ref[rows, :] + rms_back(total, tokens, scale)
        grad_ref[rows, :] = grad.astype(BF16)

    turn_rows(partial_ref, *scratch, done)


def tokens_back(partial, tokens, upstream):
    whole = pl.BlockSpec(memory_space=pltpu.VMEM)
    return pl.pallas_call(
        tokens_kernel,
        out_shape=[
            jax.ShapeDtypeStruct(tokens.shape, BF16),
            jax.ShapeDtypeStruct((1, tokens.shape[1]), F32),
        ],
        in_specs=[whole] * 3,
        out_specs=[whole] * 2,
        scratch_shapes=turn_scratch(*tokens.shape),
        compiler_params=kernel_params(8, 18),
        cost_estimate=pl.CostEstimate(flops=10**6, bytes_accessed=10**4, transcendentals=0),
        name="tokens_back",
    )(partial, tokens, upstream)


def hidden_units_kernel(cot_ref, down_ref, rest_ref, pre_ref, out_ref):
    units, half = down_ref.shape
    grad = back_product(cot_ref[:, pl.ds(0, half)], down_ref[...])
    grad += back_product(cot_ref[:, pl.ds(half, half)], rest_ref[...])
    gate, up = pre_ref[:, pl.ds(0, units)], pre_ref[:, pl.ds(units, units)]
    sig = jax.nn.sigmoid(gate)
    grad_sig = grad * sig
    out_ref[:, pl.ds(0, units)] = (grad_sig * up * (1.0 + gate * (1.0 - sig))).astype(BF16)
    out_ref[:, pl.ds(units, units)] = (grad_sig * gate).astype(BF16)


def hidden_units_back(cot, down, rest, pre):
    rows, width = cot.shape
    size = 2 * LANES

    def rows_block(n):
        return pl.BlockSpec((size, n), lambda i: (i, 0))

    return pl.pallas_call(
        hidden_units_kernel,
        grid=(rows // size,),
        out_shape=jax.ShapeDtypeStruct(pre.shape, BF16),
        in_specs=[
            rows_block(width),
            pl.BlockSpec(down.shape, lambda i: (0, 0)),
            pl.BlockSpec(rest.shape, lambda i: (0, 0)),
            rows_block(pre.shape[1]),
        ],
        out_specs=rows_block(pre.shape[1]),
        compiler_params=pltpu.CompilerParams(vmem_limit_bytes=58 * 2**20),
        cost_estimate=pl.CostEstimate(flops=10**6, bytes_accessed=10**4, transcendentals=0),
        name="hidden_units_back",
    )(cot, down, rest, pre)


def columns_kernel(widths, total_width, moved_ref, gain_ref, *outs):
    gain = gain_ref[...].astype(F32)
    place = 0
    for out, width in zip(outs, widths):
        for p in range(H):
            piece = moved_ref[p, :, pl.ds(place, width)].astype(F32)
            out[:, pl.ds(p * width, width)] = piece * gain
        place += width
    if total_width:
        total = moved_ref[0, :, pl.ds(place, total_width)].astype(F32)
        for p in range(1, H):
            total += moved_ref[p, :, pl.ds(place, total_width)].astype(F32)
        outs[-1][...] = total * gain


def lay_columns(moved, gain, widths, total_width=0):
    rows = moved.shape[1]
    shapes = [(rows, H * width) for width in widths]
    if total_width:
        shapes.append((rows, total_width))
    whole = pl.BlockSpec(memory_space=pltpu.VMEM)
    return pl.pallas_call(
        functools.partial(columns_kernel, tuple(widths), total_width),
        out_shape=[jax.ShapeDtypeStruct(shape, F32) for shape in shapes],
        in_specs=[whole] * 2,
        out_specs=[whole] * len(shapes),
        compiler_params=pltpu.CompilerParams(vmem_limit_bytes=16 * 2**20),
        cost_estimate=pl.CostEstimate(flops=10**6, bytes_accessed=10**4, transcendentals=0),
        name="lay_columns",
    )(moved, gain)


def mix_forward(mixed, bias, gaterank, gain, marks, segment, sums, pairs, key_dim, value_dim):
    rows = mixed.shape[0]
    count, _, length = segment.shape
    shapes = (
        ((rows, value_dim), BF16),
        ((rows, value_dim), F32),
        ((rows, key_dim), F32),
        ((count, length, length), BF16),
        ((rows, key_dim), BF16),
        ((rows, key_dim), BF16),
        ((count, 1, key_dim), F32),
        ((count, value_dim, key_dim), BF16),
    )
    whole = pl.BlockSpec(memory_space=pltpu.VMEM)
    return pl.pallas_call(
        functools.partial(forward_kernel, key_dim, value_dim),
        out_shape=[jax.ShapeDtypeStruct(*s) for s in shapes],
        in_specs=[pl.BlockSpec(memory_space=pl.ANY)] + [whole] * 7,
        out_specs=[whole] + [pl.BlockSpec(memory_space=pl.ANY)] * (len(shapes) - 1),
        scratch_shapes=[pltpu.VMEM(*s) for s in shapes[1:-1]]
        + state_scratch(count, value_dim, key_dim)
        + [
            pltpu.SemaphoreType.DMA((count, 7)),
            pltpu.VMEM(mixed.shape, mixed.dtype),
            pltpu.SemaphoreType.DMA((count,)),
        ],
        compiler_params=kernel_params(1, 58),
        cost_estimate=pl.CostEstimate(flops=10**6, bytes_accessed=10**4, transcendentals=0),
        name="mix_forward",
    )(mixed, bias, gaterank, gain, marks, segment, sums, pairs)


def mix_backward(
    mixed, kept, upstream, gaterank, gain, marks, segment, sums, pairs, key_dim, value_dim
):
    rows = mixed.shape[0]
    count = segment.shape[0]
    shapes = (
        (mixed.shape, BF16),
        ((1, value_dim), F32),
        ((1, key_dim), F32),
        (gaterank.shape, F32),
    )
    attended, logits, scores, start, end, decay, enter = kept
    given = (mixed, upstream, attended, start, logits, scores, end, decay, enter)
    whole = pl.BlockSpec(memory_space=pltpu.VMEM)
    return pl.pallas_call(
        functools.partial(backward_kernel, key_dim, value_dim),
        out_shape=[jax.ShapeDtypeStruct(*s) for s in shapes],
        in_specs=[pl.BlockSpec(memory_space=pl.ANY)] * 9 + [whole] * 6,
        out_specs=[whole] * len(shapes),
        scratch_shapes=[pltpu.VMEM(a.shape, a.dtype) for a in given]
        + [pltpu.VMEM((rows, value_dim), BF16)]
        + state_scratch(count, value_dim, key_dim)
        + [pltpu.SemaphoreType.DMA((count, 9))],
        compiler_params=kernel_params(2, 58),
        cost_estimate=pl.CostEstimate(flops=10**6, bytes_accessed=10**4, transcendentals=0),
        name="mix_backward",
    )(
        *given,
        gaterank,
        gain,
        marks,
        segment,
        sums,
        pairs,
    )


def per_device(
    tokens,
    doc_lengths,
    norm_gain,
    w_query,
    w_key,
    w_value,
    w_outgate,
    w_lowrank,
    w_gaterank,
    gate_bias,
    head_gain,
    w_output,
    ffn_gain,
    w_gate,
    w_up,
    w_down,
    cotangent,
):
    seqs_here, length, width = tokens.shape
    reps = lax.axis_size("rep")
    parts = lax.axis_size("fsdp")
    devices = reps * H * CORES * parts
    here = lax.axis_index("head")
    key_dim, value_dim = DK, DV
    rank = w_lowrank.shape[1]
    rows = width // devices
    count = H * seqs_here

    rank_at = 2 * key_dim + 2 * value_dim

    def core_sum(g):
        halves = g.reshape(g.shape[0], CORES, -1, g.shape[-1])
        core = lax.axis_index("core")
        other = lax.ppermute(halves[:, 1 - core], "core", ((0, 1), (1, 0)))
        return (halves[:, core].astype(F32) + other.astype(F32)).astype(BF16)

    def scatter_rows(g):
        if reps > 1:
            g = lax.psum_scatter(g, "rep", scatter_dimension=0, tiled=True)
        return lax.psum_scatter(g, "fsdp", scatter_dimension=1, tiled=True)

    def gather_columns(moved):
        whole = lax.all_gather(moved, ("core", "fsdp"), axis=1, tiled=True)
        if reps > 1:
            whole = lax.all_gather(whole, "rep", axis=0, tiled=False)
        return whole.reshape(width, -1)

    def gather_part(w):
        if reps == 1:
            return lax.all_gather(w, SHARE, axis=0, tiled=True)
        whole = lax.all_gather(w, EVERY, axis=0, tiled=True)
        size = whole.shape[0] // H
        return lax.dynamic_slice_in_dim(whole, here * size, size, 0)

    def pair_part(g):
        return core_sum(g[None])[0] if reps == 1 else g

    def scatter_part(g):
        if reps == 1:
            return lax.psum_scatter(g, "fsdp", scatter_dimension=0, tiled=True)
        whole = jnp.zeros((H * g.shape[0], g.shape[1]), BF16)
        whole = lax.dynamic_update_slice_in_dim(whole, g, here * g.shape[0], 0)
        return lax.psum_scatter(whole, EVERY, scatter_dimension=0, tiled=True)

    rank_at = 2 * key_dim + 2 * value_dim

    def with_gain(w, gain):
        return (w.astype(F32) * gain.astype(F32)[:, None]).astype(BF16)

    small = (
        w_gaterank,
        gate_bias.reshape(1, -1),
        head_gain.reshape(1, -1),
        (doc_lengths // 16).astype(BF16).reshape(1, -1),
        (doc_lengths % 16).astype(BF16).reshape(1, -1),
    )
    edges = [rank]
    extra = jnp.pad(with_gain(w_lowrank, norm_gain), ((0, 0), (0, LANES - rank)))
    for piece in small:
        high, wide = piece.shape
        extra += jnp.pad(piece, ((0, rows - high), (edges[-1], LANES - edges[-1] - wide)))
        edges.append(edges[-1] + wide)

    mix_moved = mix_weights((w_query, w_key, w_value, w_outgate), extra, norm_gain[:, None])
    inputs = tokens.reshape(-1, width)
    inputs, _ = after(inputs, mix_moved)
    output_w = gather_part(w_output)
    mix_moved, output_w = after(mix_moved, output_w)
    mix_w = gather_columns(mix_moved)
    w_down, _ = after(w_down, mix_moved)
    down_w = gather_part(w_down[:, : width // 2])
    normed, ffn_moved = share_tokens(inputs, w_gate, w_up, ffn_gain[:, None])
    normed = normed.reshape(-1, width)

    small = mix_w[:, rank_at:].astype(F32).reshape(devices, rows, LANES)
    gaterank, bias, gain_head, long, short = (
        small[:, : rank if i == 0 else 1, edges[i] : edges[i + 1]] for i in range(len(edges) - 1)
    )
    gaterank = gaterank.transpose(1, 0, 2).reshape(rank, -1)
    bias = lax.dynamic_slice_in_dim(bias.reshape(1, -1), here * key_dim, key_dim, 1)
    gaterank = lax.dynamic_slice_in_dim(gaterank, here * key_dim, key_dim, 1)
    gain_head = gain_head.reshape(1, -1)
    lengths = (long * 16.0 + short).reshape(reps, H, CORES, parts, seqs_here, DOCS)
    lengths = lengths[lax.axis_index("rep"), :, lax.axis_index("core"), 0]
    lengths = lengths.reshape(count, DOCS).astype(jnp.int32)

    offset = lax.axis_index("fsdp") * length
    doc_ends = jnp.cumsum(lengths, axis=-1)
    places = offset + jnp.arange(length, dtype=jnp.int32)
    segment = jnp.sum((places[None, :, None] >= doc_ends[:, None, :]).astype(jnp.int32), axis=-1)
    before = jnp.sum((offset - 1 >= doc_ends).astype(jnp.int32), axis=-1)[:, None]
    last = segment[:, -1:]
    marks = jnp.stack(
        [
            segment,
            segment == before,
            segment == last,
            segment != DOCS - 1,
            jnp.broadcast_to(last == before, segment.shape),
        ],
        axis=2,
    )
    marks = jnp.pad(marks.astype(F32).reshape(count * length, 5), ((0, 0), (0, 3)))
    segment = segment.astype(F32).reshape(count, 1, length)

    mixed = matmul(normed, mix_w)
    sums, pairs = level_sums(length)
    sums, pairs = sums.astype(BF16), pairs.astype(BF16)
    gated, *kept = mix_forward(
        mixed, bias, gaterank, gain_head, marks, segment, sums, pairs, key_dim, value_dim
    )
    cot_rows, _ = after(cotangent.reshape(-1, width), normed)
    gated, cot_shared, down_w = after(gated, share_rows(cot_rows), down_w)
    ffn_moved, w_down_rest, _ = after(ffn_moved, w_down[:, width // 2 :], gated)
    ffn_w = gather_columns(ffn_moved)
    down_rest = gather_part(w_down_rest)
    partial = matmul(gated, output_w).astype(BF16).reshape(H, -1, width)
    hidden, normed_two = share_hidden(partial, inputs)
    normed_two = normed_two.reshape(-1, width)

    pre = matmul(normed_two, ffn_w)
    gate_pre, up_pre = jnp.split(pre, 2, axis=1)
    sig_gate = jax.nn.sigmoid(gate_pre)
    activated = (gate_pre * sig_gate * up_pre).astype(BF16)

    grad_down_w = rows_product(activated, cot_shared).astype(BF16)
    down_w, grad_down_w = after(down_w, grad_down_w)
    grad_pre = hidden_units_back(cot_shared, down_w, down_rest, pre)
    grad_pre, grad_down_w = after(grad_pre, pair_part(grad_down_w))
    grad_down_w = scatter_part(grad_down_w)
    grad_ffn_w = pair_product(normed_two, grad_pre, reps * H, 7)
    grad_pre, grad_ffn_w = after(grad_pre, grad_ffn_w)
    partial = back_product(grad_pre, ffn_w).astype(BF16)

    grad_hidden, grad_gain_two, down_partial, branch = share_branch(
        partial.reshape(H, -1, width), hidden, cot_rows, activated, down_w, down_rest
    )
    grad_ffn_w = scatter_rows(grad_ffn_w)
    branch = branch.reshape(-1, width)
    grad_gated = back_product(branch, output_w)
    gated, grad_gated = after(gated, grad_gated)
    grad_output_w = pair_part(rows_product(gated, branch).astype(BF16))
    grad_gated, grad_output_w, grad_down_w = after(grad_gated, grad_output_w, grad_down_w)
    grad_output_w = scatter_part(grad_output_w)
    pieces = move_rows(down_partial)
    grad_mixed, grad_gain_head, grad_bias, grad_gaterank = mix_backward(
        mixed,
        kept,
        grad_gated,
        gaterank,
        gain_head,
        marks,
        segment,
        sums,
        pairs,
        key_dim,
        value_dim,
    )
    grad_mixed, pieces, grad_down_w, grad_ffn_w = after(
        grad_mixed, pieces, grad_down_w, grad_ffn_w
    )
    output = (hidden + jnp.sum(pieces.astype(F32), axis=0)).astype(BF16).reshape(tokens.shape)
    grad_mix_w = pair_product(normed, grad_mixed, reps * H, 11)
    grad_mixed, grad_mix_w = after(grad_mixed, grad_mix_w)
    partial = back_product(grad_mixed, mix_w).astype(BF16)
    grad_mix_w = scatter_rows(grad_mix_w)
    grad_ffn_w = lax.all_to_all(grad_ffn_w, "head", split_axis=0, concat_axis=0, tiled=True)
    def place(g, axis):
        shape = list(g.shape)
        shape[axis] *= H
        return lax.dynamic_update_slice_in_dim(jnp.zeros(shape, F32), g, here * key_dim, axis)

    small_grads = jnp.concatenate(
        [
            grad_gain_two.reshape(devices, -1),
            place(grad_bias.reshape(-1), 0).reshape(devices, -1),
            grad_gain_head.reshape(devices, -1),
            place(grad_gaterank, 1)
            .reshape(rank, devices, -1)
            .transpose(1, 0, 2)
            .reshape(devices, -1),
        ],
        axis=1,
    )
    partial, grad_output_w, grad_ffn_w, small_grads = after(
        partial, grad_output_w, grad_ffn_w, small_grads
    )
    tokens_grad, grad_gain_one = tokens_back(partial.reshape(H, -1, width), inputs, grad_hidden)
    tokens_grad = tokens_grad.reshape(tokens.shape)

    units = w_gate.shape[1] // H
    w_gate_grad, w_up_grad = lay_columns(grad_ffn_w, ffn_gain[:, None], (units, units))
    grad_mix_w, _ = after(grad_mix_w, grad_gain_one)
    grad_mix_w = lax.all_to_all(grad_mix_w, "head", split_axis=0, concat_axis=0, tiled=True)
    query_g, key_g, value_g, outgate_g, lowrank_g = lay_columns(
        grad_mix_w, norm_gain[:, None], (key_dim, key_dim, value_dim, value_dim), rank
    )

    small_grads = jnp.concatenate([grad_gain_one.reshape(devices, -1), small_grads], axis=1)
    small_grads, _ = after(small_grads, grad_mix_w)
    small_grads = lax.all_to_all(small_grads, EVERY, split_axis=0, concat_axis=0, tiled=True)
    small_grads = jnp.sum(small_grads, axis=0)
    sizes = [norm_gain.shape[0], ffn_gain.shape[0], gate_bias.shape[0], head_gain.shape[0]]
    norm_g, ffn_g, bias_g, head_g, gaterank_g = jnp.split(
        small_grads, [sum(sizes[: i + 1]) for i in range(len(sizes))]
    )
    return (
        output,
        tokens_grad,
        norm_g / norm_gain.astype(F32),
        query_g,
        key_g,
        value_g,
        outgate_g,
        lowrank_g,
        gaterank_g.reshape(w_gaterank.shape),
        bias_g,
        head_g,
        grad_output_w.astype(F32),
        ffn_g / ffn_gain.astype(F32),
        w_gate_grad,
        w_up_grad,
        grad_down_w.astype(F32),
    )


def solution(mesh):
    dp, parts = mesh.shape["dp"], mesh.shape["fsdp"]
    fine = Mesh(mesh.devices.reshape(dp // (H * CORES), H, CORES, parts), EVERY)
    seq = ("rep", "head", "core")
    rows, vector = P(EVERY, None), P(EVERY)
    activations = P(seq, "fsdp", None)
    columns = P(None, EVERY)
    return jax.shard_map(
        per_device,
        mesh=fine,
        in_specs=(
            activations,
            P(seq, None),
            vector,
            rows,
            rows,
            rows,
            rows,
            rows,
            columns,
            vector,
            vector,
            rows,
            vector,
            rows,
            rows,
            rows,
            activations,
        ),
        out_specs=(
            activations,
            activations,
            vector,
            rows,
            rows,
            rows,
            rows,
            rows,
            columns,
            vector,
            vector,
            rows,
            vector,
            rows,
            rows,
            rows,
        ),
        check_vma=False,
    )
```
